32 devices in a mesh: dp: 4 (over x, core), bank: 8 (over z, y).
Axes of the slice: x: 2, y: 2, z: 4, core: 2. Of those that a mesh axis runs over, the one named last changes fastest.
Arguments:
- feature_map: bfloat16 [16384, 2048], P(('dp', 'bank')), may hold values from -6 to 6
- bank: bfloat16 [4096, 2048], P('bank'), may hold values from -6 to 6
- region_time: int32 [1024], P('dp'), may hold values from 0 to 4095, as said below
- roi_index: int32 [1024, 16], P(('dp', 'bank')), may hold values from 0 to 511, as said below
- roi_weight: bfloat16 [1024, 16], P(('dp', 'bank')), may hold values from 0.029907227 to 0.099609375
- conv_a: bfloat16 [6144, 512], P('bank'), may hold values from -0.078125 to 0.078125
- scale_a: float32 [512], replicated, may hold values from 0.1 to 1.9
- shift_a: float32 [512], replicated, may hold values from -3 to 3
- conv_b: bfloat16 [4608, 512], P('bank'), may hold values from -0.09375 to 0.09375
- scale_b: float32 [512], replicated, may hold values from 0.1 to 1.9
- shift_b: float32 [512], replicated, may hold values from -3 to 3
- conv_c: bfloat16 [512, 2048], P('bank'), may hold values from -0.25 to 0.25
- scale_c: float32 [2048], replicated, may hold values from 0.1 to 1.9
- shift_c: float32 [2048], replicated, may hold values from -3 to 3
- w_reduce: bfloat16 [2048, 512], replicated, may hold values from -0.125 to 0.125
- w_bank: bfloat16 [2048, 512], replicated, may hold values from -0.125 to 0.125
- w_query: bfloat16 [512, 512], replicated, may hold values from -0.25 to 0.25
- w_key: bfloat16 [512, 512], replicated, may hold values from -0.25 to 0.25
- w_value: bfloat16 [512, 512], replicated, may hold values from -0.25 to 0.25
- ln_gain: float32 [512], replicated, may hold values from 0.1 to 1.9
- ln_shift: float32 [512], replicated, may hold values from -3 to 3
- w_out: bfloat16 [512, 512], replicated, may hold values from -0.25 to 0.25
- w_head: bfloat16 [2560, 80], replicated, may hold values from -0.125 to 0.125
- logit_grad: bfloat16 [1024, 80], P('dp'), may hold values from -6 to 6
Outputs:
- logits: bfloat16 [1024, 80], P(('dp', 'bank'))
- map_grad: bfloat16 [16384, 2048], P(('dp', 'bank'))
- bank_grad: bfloat16 [4096, 2048], P('bank')
- conv_a_grad: float32 [6144, 512], P('bank')
- scale_a_grad: float32 [512], P('bank')
- shift_a_grad: float32 [512], P('bank')
- conv_b_grad: float32 [4608, 512], P('bank')
- scale_b_grad: float32 [512], P('bank')
- shift_b_grad: float32 [512], P('bank')
- conv_c_grad: float32 [512, 2048], P('bank')
- scale_c_grad: float32 [2048], P('bank')
- shift_c_grad: float32 [2048], P('bank')
- reduce_weight_grad: float32 [2048, 512], P('bank')
- bank_weight_grad: float32 [2048, 512], P('bank')
- query_weight_grad: float32 [512, 512], P('bank')
- key_weight_grad: float32 [512, 512], P('bank')
- value_weight_grad: float32 [512, 512], P('bank')
- gain_grad: float32 [512], P('bank')
- shift_grad: float32 [512], P('bank')
- out_weight_grad: float32 [512, 512], P('bank')
- head_weight_grad: float32 [2560, 80], P('bank')
The draws below stay inside these ranges and needn't reach their ends.
Inputs may be any that keep to these rules, and one draw needn't show every extreme that they name: `region_time`: times lean toward the start of the bank; the first three regions of every block of 256 sit at times 4096 // 2, 4095 and 0. `roi_index`: A region's 16 entries are the distinct positions of a 4 x 4 window of rows and columns in one frame of one clip of its device's block of 512 positions, row by row; in every block of 32 regions the first reads the last window of the last frame of the last clip and the second the first window of the first frame of the first clip.
All inputs are finite; a program needn't handle non-finite values.
Results may differ from the reference program's by a relative error of at most 0.028.
Values may be sent and summed in bfloat16 or wider, within the bound.
No kernel may reach another device: no remote copies, remote signals or barrier semaphores. Data moves between devices by JAX's collectives and lax.ppermute only.
A program may use at most 192 MiB of HBM per device.

```python
import jax
import jax.numpy as jnp
from jax import lax

FEAT = 2048
HID = 512
CLASSES = 80
CLIPS_DEV = 2
FRAMES = 4
SIDE = 8
TAPS = 16
ROI_DEV = 32
POS_DEV = 512
POSITIONS = 16384
R_DEV = 256
REGIONS = 1024
BANK = 4096
HALF = 2048
N_DP = 4
N_BANK = 8


def draw_region_time(key, part):
    key = jax.random.fold_in(key, 11)
    spread = jax.random.randint(key, (REGIONS,), 0, BANK, dtype=jnp.int32)
    times = spread * spread // BANK
    within = jnp.arange(REGIONS, dtype=jnp.int32) % R_DEV
    times = jnp.where(within == 0, BANK // 2, times)
    times = jnp.where(within == 1, BANK - 1, times)
    times = jnp.where(within == 2, 0, times)
    return times.astype(jnp.int32)


def draw_roi_index(key, part):
    key = jax.random.fold_in(key, 17)
    key_clip, key_frame, key_top, key_left = jax.random.split(key, 4)
    clip = jax.random.randint(key_clip, (REGIONS,), 0, CLIPS_DEV, dtype=jnp.int32)
    frame = jax.random.randint(key_frame, (REGIONS,), 0, FRAMES, dtype=jnp.int32)
    top = jax.random.randint(key_top, (REGIONS,), 0, SIDE - 3, dtype=jnp.int32)
    left = jax.random.randint(key_left, (REGIONS,), 0, SIDE - 3, dtype=jnp.int32)
    within = jnp.arange(REGIONS, dtype=jnp.int32) % ROI_DEV
    clip = jnp.where(within == 0, CLIPS_DEV - 1, jnp.where(within == 1, 0, clip))
    frame = jnp.where(within == 0, FRAMES - 1, jnp.where(within == 1, 0, frame))
    top = jnp.where(within == 0, SIDE - 4, jnp.where(within == 1, 0, top))
    left = jnp.where(within == 0, SIDE - 4, jnp.where(within == 1, 0, left))
    base = ((clip * FRAMES + frame) * SIDE + top) * SIDE + left
    offsets = (jnp.arange(4, dtype=jnp.int32)[:, None] * SIDE + jnp.arange(4, dtype=jnp.int32)[None, :]).reshape(16)
    return (base[:, None] + offsets[None, :]).astype(jnp.int32)


def levels(stream_key, shape, pieces, smallest, largest):
    def one(axis_at, shards_of):
        heights = jax.random.uniform(jax.random.fold_in(jax.random.fold_in(stream_key, 6), axis_at), (shards_of,), jnp.float32, smallest / len(pieces), largest / len(pieces))
        return jnp.repeat(jnp.exp(heights), shape[axis_at] // shards_of).reshape((-1,) + (1,) * (len(shape) - axis_at - 1))

    level = one(*pieces[0])
    for cut in pieces[1:]:
        level = level * one(*cut)
    return level


def noise(own_key, dims, scale, bound, cuts=(), kind=jnp.bfloat16):
    drawn = jax.random.normal(own_key, dims, jnp.float32) * scale
    if len(cuts) > 0:
        drawn = levels(own_key, dims, cuts, -0.22, 0.18) * drawn
    return jnp.clip(drawn, min=-bound, max=bound).astype(kind)


def setup_inputs(seed: int = 0) -> dict:
    key_list = jax.random.split(jax.random.key(seed), 25)
    feature_map = noise(key_list[0], (POSITIONS, FEAT), 1.0, 6.0, ((0, 32),))
    bank = noise(key_list[1], (BANK, FEAT), 1.0, 6.0, ((0, 8),))
    region_time = draw_region_time(jax.random.fold_in(key_list[24], 71), 0)
    roi_index = draw_roi_index(jax.random.fold_in(key_list[24], 71), 0)
    roi_weight = jnp.clip(0.029907227 + 0.06970215 * jax.random.uniform(key_list[4], (REGIONS, TAPS), jnp.float32) ** levels(key_list[4], (REGIONS, TAPS), ((0, 32),), -0.2, 0.2), 0.029907227, 0.099609375).astype(jnp.bfloat16)
    conv_a = noise(key_list[5], (3 * FEAT, HID), (3 * FEAT) ** -0.5, 0.078125, ((0, 8),))
    scale_a = jnp.clip(1.0 + 0.18 * jax.random.normal(key_list[6], (HID,), jnp.float32), 0.1, 1.9)
    shift_a = noise(key_list[7], (HID,), 0.5, 3.0, (), jnp.float32)
    conv_b = noise(key_list[8], (9 * HID, HID), (9 * HID) ** -0.5, 0.09375, ((0, 8),))
    scale_b = jnp.clip(1.0 + 0.18 * jax.random.normal(key_list[9], (HID,), jnp.float32), 0.1, 1.9)
    shift_b = noise(key_list[10], (HID,), 0.5, 3.0, (), jnp.float32)
    conv_c = noise(key_list[11], (HID, FEAT), HID ** -0.5, 0.25, ((0, 8),))
    scale_c = jnp.clip(1.0 + 0.18 * jax.random.normal(key_list[12], (FEAT,), jnp.float32), 0.1, 1.9)
    shift_c = noise(key_list[13], (FEAT,), 0.5, 3.0, (), jnp.float32)
    w_reduce = noise(key_list[14], (FEAT, HID), FEAT ** -0.5, 0.125)
    w_bank = noise(key_list[15], (FEAT, HID), FEAT ** -0.5, 0.125)
    w_query = noise(key_list[16], (HID, HID), HID ** -0.5, 0.25)
    w_key = noise(key_list[17], (HID, HID), HID ** -0.5, 0.25)
    w_value = noise(key_list[18], (HID, HID), HID ** -0.5, 0.25)
    ln_gain = jnp.clip(1.0 + 0.18 * jax.random.normal(key_list[19], (HID,), jnp.float32), 0.1, 1.9)
    ln_shift = noise(key_list[20], (HID,), 0.5, 3.0, (), jnp.float32)
    w_out = noise(key_list[21], (HID, HID), HID ** -0.5, 0.25)
    w_head = noise(key_list[22], (FEAT + HID, CLASSES), (FEAT + HID) ** -0.5, 0.125)
    logit_grad = noise(key_list[23], (REGIONS, CLASSES), 1.0, 6.0, ((0, 4),))
    return dict(feature_map=feature_map, bank=bank, region_time=region_time, roi_index=roi_index, roi_weight=roi_weight, conv_a=conv_a, scale_a=scale_a, shift_a=shift_a, conv_b=conv_b, scale_b=scale_b, shift_b=shift_b, conv_c=conv_c, scale_c=scale_c, shift_c=shift_c, w_reduce=w_reduce, w_bank=w_bank, w_query=w_query, w_key=w_key, w_value=w_value, ln_gain=ln_gain, ln_shift=ln_shift, w_out=w_out, w_head=w_head, logit_grad=logit_grad)


@jax.custom_vjp
def low(v):
    return lax.optimization_barrier(v.astype(jnp.bfloat16)).astype(jnp.float32)

@jax.custom_vjp
def low_back(v):
    return v

def low_keep(v):
    return (low(v), None)

def low_pass(kept, grad):
    return (grad,)

def back_keep(v):
    return (v, None)

def back_low(kept, grad):
    return (low(grad),)
low.defvjp(low_keep, low_pass)
low_back.defvjp(back_keep, back_low)
epsilon = 1e-05
masked_score = -1e+30
places = [(-1, -1), (-1, 0), (-1, 1), (0, -1), (0, 0), (0, 1), (1, -1), (1, 0), (1, 1)]

def product(left, right):
    return jnp.dot(left, right, precision=lax.Precision.HIGHEST, preferred_element_type=jnp.float32)

def shifted(field, axis, step):
    if step == 0:
        return field
    length = field.shape[axis]
    widths = [(0, 0)] * field.ndim
    if step > 0:
        widths[axis] = (0, step)
        return lax.slice_in_dim(jnp.pad(field, widths), step, step + length, axis=axis)
    widths[axis] = (-step, 0)
    return lax.slice_in_dim(jnp.pad(field, widths), 0, length, axis=axis)

def frame_stack(field):
    return jnp.concatenate([shifted(field, 1, offset - 1) for offset in range(3)], axis=-1)

def space_stack(field):
    return jnp.concatenate([shifted(shifted(field, 2, rise), 3, slide) for rise, slide in places], axis=-1)

def bottleneck(map_block, conv_a, scale_a, shift_a, conv_b, scale_b, shift_b, conv_c, scale_c, shift_c):
    layout = (CLIPS_DEV, FRAMES, SIDE, SIDE)
    stack_a = frame_stack(map_block.reshape(layout + (FEAT,))).reshape(POS_DEV, 3 * FEAT)
    pre_a = low_back(product(stack_a, conv_a))
    act_a = low(jax.nn.gelu(pre_a * scale_a + shift_a))
    stack_b = space_stack(act_a.reshape(layout + (HID,))).reshape(POS_DEV, 9 * HID)
    pre_b = low_back(product(stack_b, conv_b))
    act_b = low(jax.nn.gelu(pre_b * scale_b + shift_b))
    pre_c = low_back(product(act_b, conv_c))
    return low(jax.nn.gelu(map_block + pre_c * scale_c + shift_c))

def forward(feature_map, bank, conv_a, scale_a, shift_a, conv_b, scale_b, shift_b, conv_c, scale_c, shift_c, w_reduce, w_bank, w_query, w_key, w_value, ln_gain, ln_shift, w_out, w_head, region_time, roi_index, roi_weight):
    score_scale = HID ** (-0.5)
    block_count = N_DP * N_BANK

    def pool_block(block_args):
        map_block, index_block, weight_block = block_args
        out_low = bottleneck(map_block, conv_a, scale_a, shift_a, conv_b, scale_b, shift_b, conv_c, scale_c, shift_c)
        return lax.optimization_barrier(jnp.sum(weight_block[:, :, None] * out_low[index_block], axis=1))
    pooled = lax.map(jax.checkpoint(pool_block), (feature_map.reshape(block_count, POS_DEV, FEAT), roi_index.reshape(block_count, ROI_DEV, TAPS), roi_weight.reshape(block_count, ROI_DEV, TAPS)))
    regions = low(low_back(pooled.reshape(REGIONS, FEAT)))
    reduced = low_back(product(regions, w_reduce))
    queries = low(low_back(product(low(reduced), w_query)))
    memory = low_back(product(bank, w_bank))
    memory_low = low(memory)
    keys = low(low_back(product(memory_low, w_key)))
    values = low(low_back(product(memory_low, w_value)))
    positions = jnp.arange(BANK, dtype=jnp.int32)
    block_rows = min(512, R_DEV)
    query_blocks = queries.reshape(REGIONS // block_rows, block_rows, HID)
    time_blocks = region_time.reshape(REGIONS // block_rows, block_rows)

    def attend(block_args):
        query_part, time_part = block_args
        scores = low_back(product(query_part, keys.T)) * score_scale
        visible = jnp.abs(time_part[:, None] - positions[None, :]) <= HALF
        scores = jnp.where(visible, scores, masked_score)
        row_top = lax.optimization_barrier(jnp.max(scores, axis=1, keepdims=True))
        weights = jnp.exp(scores - row_top)
        total = lax.optimization_barrier(jnp.sum(weights, axis=1))
        return (product(low(weights), values), total)
    numer, total = lax.map(jax.checkpoint(attend), (query_blocks, time_blocks))
    numer = low_back(numer.reshape(REGIONS, HID))
    total = total.reshape(REGIONS)
    attended = numer / total[:, None]
    row_mean = lax.optimization_barrier(jnp.mean(attended, axis=1, keepdims=True))
    centred = attended - row_mean
    row_var = lax.optimization_barrier(jnp.mean(centred * centred, axis=1, keepdims=True))
    normed = centred * lax.rsqrt(row_var + epsilon) * ln_gain + ln_shift
    hidden = low(jax.nn.gelu(normed))
    branch = low_back(product(hidden, w_out))
    merged = reduced + branch
    joined = low(jnp.concatenate([regions, merged], axis=1))
    return product(joined, w_head)

def reference(feature_map, bank, region_time, roi_index, roi_weight, conv_a, scale_a, shift_a, conv_b, scale_b, shift_b, conv_c, scale_c, shift_c, w_reduce, w_bank, w_query, w_key, w_value, ln_gain, ln_shift, w_out, w_head, logit_grad):
    inputs = [value.astype(jnp.float32) for value in (feature_map, bank, conv_a, scale_a, shift_a, conv_b, scale_b, shift_b, conv_c, scale_c, shift_c, w_reduce, w_bank, w_query, w_key, w_value, ln_gain, ln_shift, w_out, w_head)]
    pool_weights = roi_weight.astype(jnp.float32)

    def run(*values_in):
        return forward(*values_in, region_time, roi_index, pool_weights)
    logits, pullback = jax.vjp(run, *inputs)
    grads = pullback(logit_grad.astype(jnp.float32))
    return (logits.astype(jnp.bfloat16), grads[0].astype(jnp.bfloat16), grads[1].astype(jnp.bfloat16), grads[2], grads[3], grads[4], grads[5], grads[6], grads[7], grads[8], grads[9], grads[10], grads[11], grads[12], grads[13], grads[14], grads[15], grads[16], grads[17], grads[18], grads[19])
```

```python
import jax
import jax.numpy as jnp
from jax import lax
from jax.sharding import PartitionSpec as P

FRAMES = 4
SIDE = 8


epsilon = 1e-05
masked_score = -1e30
places = [(-1, -1), (-1, 0), (-1, 1), (0, -1), (0, 0), (0, 1), (1, -1), (1, 0), (1, 1)]


def product(left, right):
    return jnp.dot(left, right, preferred_element_type=jnp.float32)


def inner_rows(left, right):
    return lax.dot_general(
        left, right, (((0,), (0,)), ((), ())), preferred_element_type=jnp.float32
    )


def outer_cols(left, right):
    return lax.dot_general(
        left, right, (((1,), (1,)), ((), ())), preferred_element_type=jnp.float32
    )


def rows_of(left, right, first_col, col_count):
    return inner_rows(lax.dynamic_slice_in_dim(left, first_col, col_count, 1), right)


def shifted(field, axis, step):
    if step == 0:
        return field
    length = field.shape[axis]
    widths = [(0, 0)] * field.ndim
    if step > 0:
        widths[axis] = (0, step)
        return lax.slice_in_dim(jnp.pad(field, widths), step, step + length, axis=axis)
    widths[axis] = (-step, 0)
    return lax.slice_in_dim(jnp.pad(field, widths), 0, length, axis=axis)


def frame_stack(field):
    return jnp.concatenate([shifted(field, 1, offset - 1) for offset in range(3)], axis=-1)


def frame_unstack(stacked, width):
    summed = shifted(stacked[..., :width], 1, 1)
    for offset in range(1, 3):
        summed = summed + shifted(
            stacked[..., offset * width : (offset + 1) * width], 1, 1 - offset
        )
    return summed


def space_stack(field):
    return jnp.concatenate(
        [shifted(shifted(field, 2, rise), 3, slide) for rise, slide in places], axis=-1
    )


def space_unstack(stacked, width):
    summed = None
    for number, (rise, slide) in enumerate(places):
        back = shifted(
            shifted(stacked[..., number * width : (number + 1) * width], 3, -slide), 2, -rise
        )
        summed = back if summed is None else summed + back
    return summed


def norm_act(attended, ln_gain, ln_shift):
    row_mean = jnp.mean(attended, axis=1, keepdims=True)
    centred = attended - row_mean
    row_var = jnp.mean(centred * centred, axis=1, keepdims=True)
    normed = centred * lax.rsqrt(row_var + epsilon) * ln_gain + ln_shift
    return jax.nn.gelu(normed)


def gelu_back(linear, upstream):
    unused, pullback = jax.vjp(jax.nn.gelu, linear)
    return pullback(upstream)[0]


class SubAxis:
    def __init__(self, name, size, stride):
        self.name, self.size, self.stride = name, size, stride

    def place(self):
        return lax.rem(lax.axis_index(self.name) // self.stride, self.size)

    def swap(self, value, step):
        count = lax.axis_size(self.name)
        pairs = [(i, i ^ (step * self.stride)) for i in range(count)]
        return lax.ppermute(value, self.name, pairs)


def sub_axes(dp_count, bank_count):
    inner = 2 if bank_count <= 8 else 8
    return (
        SubAxis("bank", bank_count // inner, inner),
        SubAxis("bank", inner, 1),
        SubAxis("dp", dp_count // 2, 2),
        SubAxis("dp", 2, 1),
    )


def low(value):
    return value.astype(jnp.bfloat16)


def wide(value):
    return value.astype(jnp.float32)


def block_at(value, place, dim):
    return lax.dynamic_index_in_dim(value, place, dim, keepdims=False)


def reduce_over(value, axis, dim):
    me = axis.place()
    parts = [axis.swap(block_at(value, me ^ step, dim), step) for step in range(1, axis.size)]
    total = wide(block_at(value, me, dim))
    for part in parts:
        total = total + wide(part)
    return total


def reduce_all(value, axes):
    outer, inner, across, core = axes
    value = low(reduce_over(value, core, 3))
    half = outer.size // 2
    first = low(reduce_over(value[:half], across, 2))
    second = low(reduce_over(value[half:], inner, 1))
    first = low(reduce_over(first, inner, 1))
    second = low(reduce_over(second, across, 1))
    return reduce_over(jnp.concatenate([first, second], 0), outer, 0)


def sum_everywhere(value, names):
    for name in names:
        step = 1
        while step < lax.axis_size(name):
            pairs = [(i, i ^ step) for i in range(lax.axis_size(name))]
            value = value + lax.ppermute(value, name, pairs)
            step *= 2
    return value


def thirds(column):
    top = low(column)
    rest = column - wide(top)
    middle = low(rest)
    return jnp.concatenate([top, middle, low(rest - wide(middle))], axis=-1)


def from_thirds(columns):
    return jnp.sum(wide(columns), axis=-1, keepdims=True)


def to_owners(value):
    return lax.all_to_all(value, "bank", split_axis=0, concat_axis=0, tiled=True)


def to_group(value):
    count = lax.axis_size("bank")
    return to_owners(jnp.broadcast_to(value[None], (count,) + value.shape))


def body(
    feature_map,
    bank,
    region_time,
    roi_index,
    roi_weight,
    conv_a,
    scale_a,
    shift_a,
    conv_b,
    scale_b,
    shift_b,
    conv_c,
    scale_c,
    shift_c,
    w_reduce,
    w_bank,
    w_query,
    w_key,
    w_value,
    ln_gain,
    ln_shift,
    w_out,
    w_head,
    logit_grad,
):
    site_count = feature_map.shape[0]
    feature_count = feature_map.shape[1]
    channels = w_query.shape[0]
    keys_here = bank.shape[0]
    own_count = roi_index.shape[0]
    bank_count = lax.axis_size("bank")
    bank_place = lax.axis_index("bank")
    dp_count = lax.axis_size("dp")
    dp_place = lax.axis_index("dp")
    axes = sub_axes(dp_count, bank_count)
    first_row = bank_place * own_count
    score_scale = channels ** (-0.5)
    half_span = keys_here * bank_count // 2
    clip_count = site_count // (FRAMES * SIDE * SIDE)
    layout = (clip_count, FRAMES, SIDE, SIDE)
    grid = tuple(axis.size for axis in axes)
    blocks = bank_count * dp_count

    def own_quarter(shard):
        rows = shard.shape[0] // dp_count
        return lax.dynamic_slice_in_dim(shard, dp_place * rows, rows, 0)

    quarter_a, quarter_b, quarter_c = own_quarter(conv_a), own_quarter(conv_b), own_quarter(conv_c)
    rows_a, rows_b, rows_c = quarter_a.shape[0], quarter_b.shape[0], quarter_c.shape[0]
    wide_c = feature_count // channels
    packed = jnp.concatenate([quarter_a, quarter_b, quarter_c.reshape(rows_c * wide_c, channels)], 0)
    gathered = lax.all_gather(packed, ("bank", "dp"), axis=0, tiled=False)
    full_a = gathered[:, :rows_a].reshape(blocks * rows_a, channels)
    full_b = gathered[:, rows_a : rows_a + rows_b].reshape(blocks * rows_b, channels)
    full_c = gathered[:, rows_a + rows_b :].reshape(blocks * rows_c, feature_count)
    memory = product(bank, w_bank)
    memory_low = low(memory)
    keys = low(product(memory_low, w_key))
    values = low(product(memory_low, w_value))
    stack_a = frame_stack(feature_map.reshape(layout + (feature_count,))).reshape(
        site_count, 3 * feature_count
    )
    matches = roi_index[:, :, None] == jnp.arange(site_count, dtype=jnp.int32)[None, None, :]
    pooling = low(jnp.sum(jnp.where(matches, wide(roi_weight)[:, :, None], 0.0), axis=1))
    own_logit_grad = lax.dynamic_slice_in_dim(logit_grad, first_row, own_count, 0)
    joined_grad = outer_cols(own_logit_grad, w_head)
    direct_grad = joined_grad[:, :feature_count]
    merged_grad = joined_grad[:, feature_count:]
    branch_grad = low(merged_grad)
    hidden_grad = outer_cols(branch_grad, w_out)

    pre_a = product(stack_a, full_a)
    lin_a = pre_a * scale_a + shift_a
    act_a = low(jax.nn.gelu(lin_a))
    stack_b = space_stack(act_a.reshape(layout + (channels,))).reshape(site_count, 9 * channels)
    pre_b = product(stack_b, full_b)
    lin_b = pre_b * scale_b + shift_b
    act_b = low(jax.nn.gelu(lin_b))
    pre_c = product(act_b, full_c)
    lin_c = wide(feature_map) + pre_c * scale_c + shift_c
    out_low = low(jax.nn.gelu(lin_c))
    regions = low(product(pooling, out_low))
    reduced = product(regions, w_reduce)
    reduced_low = low(reduced)
    own_queries = low(product(reduced_low, w_query))
    queries = to_group(own_queries).reshape(bank_count * own_count, channels)

    positions = bank_place * keys_here + jnp.arange(keys_here, dtype=jnp.int32)
    visible = jnp.abs(region_time[:, None] - positions[None, :]) <= half_span
    scores = jnp.where(visible, outer_cols(queries, keys) * score_scale, masked_score)
    local_top = jnp.max(scores, axis=1, keepdims=True)
    local_weights = jnp.exp(scores - local_top)
    local_total = jnp.sum(local_weights, axis=1, keepdims=True)
    local_numer = product(low(local_weights), values)
    message = jnp.concatenate(
        [low(local_numer), thirds(local_top), thirds(local_total), jnp.zeros((scores.shape[0], 122), jnp.bfloat16)], 1
    )
    arrived = to_owners(message.reshape(bank_count, own_count, channels + 128))
    tops = from_thirds(arrived[:, :, channels : channels + 3])
    top = jnp.max(tops, axis=0)
    factors = jnp.exp(tops - top[None])
    total = jnp.sum(factors * from_thirds(arrived[:, :, channels + 3 : channels + 6]), axis=0)
    numer = jnp.sum(factors * wide(arrived[:, :, :channels]), axis=0)
    attended = numer / total
    hidden, act_pull = jax.vjp(norm_act, attended, ln_gain, ln_shift)
    hidden_low = low(hidden)
    attended_grad, gain_part, shift_part = act_pull(hidden_grad)
    own_numer_grad = low(attended_grad / total)
    own_centre = jnp.sum(attended_grad * attended, axis=1, keepdims=True) / total
    message = jnp.concatenate(
        [own_numer_grad, thirds(top), thirds(own_centre), jnp.zeros((own_count, 122), jnp.bfloat16)], 1
    )
    arrived = to_group(message).reshape(bank_count * own_count, channels + 128)
    numer_grad = arrived[:, :channels]
    row_top = from_thirds(arrived[:, channels : channels + 3])
    centre = from_thirds(arrived[:, channels + 3 : channels + 6])
    weights = jnp.exp(scores - row_top)
    weights_low = low(weights)
    prob_grad = outer_cols(numer_grad, values)
    score_grad = low(weights * (prob_grad - centre) * score_scale)
    query_part = low(product(score_grad, keys))
    arrived = to_owners(query_part.reshape(bank_count, own_count, channels))
    query_grad = low(jnp.sum(wide(arrived), axis=0))
    key_part = low(inner_rows(score_grad, queries))
    value_part = low(inner_rows(weights_low, numer_grad))
    reduced_grad = low(merged_grad + outer_cols(query_grad, w_query))
    regions_grad = low(direct_grad + outer_cols(reduced_grad, w_reduce))

    merged = reduced + product(hidden_low, w_out)
    joined = jnp.concatenate([regions, low(merged)], axis=1)
    logits_out = low(product(joined, w_head))

    out_grad = inner_rows(pooling, regions_grad)
    lin_c_grad = gelu_back(lin_c, out_grad)
    pre_c_grad = low(lin_c_grad * scale_c)
    part_c = low(inner_rows(act_b, pre_c_grad)).reshape(grid + (rows_c, feature_count))
    lin_b_grad = gelu_back(lin_b, outer_cols(pre_c_grad, full_c))
    pre_b_grad = low(lin_b_grad * scale_b)
    part_b = low(inner_rows(stack_b, pre_b_grad)).reshape(grid + (rows_b, channels))
    act_a_grad = space_unstack(
        outer_cols(pre_b_grad, full_b).reshape(layout + (9 * channels,)), channels
    )
    lin_a_grad = gelu_back(lin_a, act_a_grad.reshape(site_count, channels))
    pre_a_grad = low(lin_a_grad * scale_a)
    part_a = low(inner_rows(stack_a, pre_a_grad)).reshape(grid + (rows_a, channels))
    stack_a_grad = outer_cols(pre_a_grad, full_a).reshape(layout + (3 * feature_count,))
    map_grad = low(
        lin_c_grad + frame_unstack(stack_a_grad, feature_count).reshape(site_count, feature_count)
    )

    region_parts = [
        low(part).reshape(blocks, part.shape[0] // blocks, part.shape[1])
        for part in (
            inner_rows(regions, reduced_grad),
            inner_rows(reduced_low, query_grad),
            inner_rows(hidden_low, branch_grad),
            inner_rows(joined, own_logit_grad),
        )
    ]
    part_r = jnp.concatenate(region_parts[:3], axis=1)
    head_part = region_parts[3]
    rows_r, rows_h, classes = part_r.shape[1], head_part.shape[1], head_part.shape[2]

    def over_dp(block):
        rows, width = block.shape
        return lax.all_gather(low(block), "dp", axis=0, tiled=False)

    done_r = over_dp(reduce_all(part_r.reshape(grid + (rows_r, channels)), axes))
    done_h = over_dp(reduce_all(head_part.reshape(grid + (rows_h, classes)), axes))
    done_c = over_dp(reduce_all(part_c, axes))
    done_b = over_dp(reduce_all(part_b, axes))
    done_a = over_dp(reduce_all(part_a, axes))

    def whole(stacked, first, count):
        picked = wide(stacked[:, first : first + count])
        return picked.reshape(dp_count * count, stacked.shape[2])

    rows_reduce = feature_count // blocks
    rows_query = channels // blocks
    reduce_weight_grad = whole(done_r, 0, rows_reduce)
    query_weight_grad = whole(done_r, rows_reduce, rows_query)
    out_weight_grad = whole(done_r, rows_reduce + rows_query, rows_query)
    head_weight_grad = whole(done_h, 0, rows_h)
    conv_a_grad, conv_b_grad, conv_c_grad = (
        whole(done_a, 0, rows_a), whole(done_b, 0, rows_b), whole(done_c, 0, rows_c)
    )

    key_value = lax.psum(jnp.concatenate([key_part, value_part], 0), "dp")
    key_low, value_low = key_value[:keys_here], key_value[keys_here:]
    memory_grad = low(outer_cols(key_low, w_key) + outer_cols(value_low, w_value))
    bank_grad = low(outer_cols(memory_grad, w_bank))
    width = channels // dp_count

    def columns(value):
        return lax.dynamic_slice_in_dim(value, dp_place * width, width, 1)

    bank_parts = [
        low(part).reshape(bank_count, part.shape[0] // bank_count, width)
        for part in (
            inner_rows(bank, columns(memory_grad)),
            inner_rows(memory_low, columns(key_low)),
            inner_rows(memory_low, columns(value_low)),
        )
    ]
    bank_sum = jnp.sum(wide(to_owners(jnp.concatenate(bank_parts, 1))), axis=0)
    bank_done = wide(lax.all_gather(low(bank_sum), "dp", axis=1, tiled=True))
    bank_rows, channel_rows = feature_count // bank_count, channels // bank_count
    bank_weight_grad = bank_done[:bank_rows]
    key_weight_grad = bank_done[bank_rows : bank_rows + channel_rows]
    value_weight_grad = bank_done[bank_rows + channel_rows :]

    vectors = [
        gain_part,
        shift_part,
        jnp.sum(lin_a_grad * pre_a, axis=0),
        jnp.sum(lin_a_grad, axis=0),
        jnp.sum(lin_b_grad * pre_b, axis=0),
        jnp.sum(lin_b_grad, axis=0),
        jnp.sum(lin_c_grad * pre_c, axis=0),
        jnp.sum(lin_c_grad, axis=0),
    ]
    summed = sum_everywhere(jnp.concatenate(vectors).reshape(-1, channels), ("dp", "bank")).reshape(-1)
    pieces, start = [], 0
    for vector in vectors:
        count = vector.shape[0] // bank_count
        pieces.append(lax.dynamic_slice_in_dim(summed, start + bank_place * count, count, 0))
        start += vector.shape[0]
    gain_grad, shift_grad = pieces[:2]
    scale_a_grad, shift_a_grad, scale_b_grad, shift_b_grad, scale_c_grad, shift_c_grad = pieces[2:]
    return (
        logits_out,
        map_grad,
        bank_grad,
        conv_a_grad,
        scale_a_grad,
        shift_a_grad,
        conv_b_grad,
        scale_b_grad,
        shift_b_grad,
        conv_c_grad,
        scale_c_grad,
        shift_c_grad,
        reduce_weight_grad,
        bank_weight_grad,
        query_weight_grad,
        key_weight_grad,
        value_weight_grad,
        gain_grad,
        shift_grad,
        out_weight_grad,
        head_weight_grad,
    )


def solution(mesh):
    in_specs = (
        P(("dp", "bank"), None),
        P("bank", None),
        P("dp"),
        P(("dp", "bank"), None),
        P(("dp", "bank"), None),
        P("bank", None),
        P(),
        P(),
        P("bank", None),
        P(),
        P(),
        P("bank", None),
        P(),
        P(),
        P(),
        P(),
        P(),
        P(),
        P(),
        P(),
        P(),
        P(),
        P(),
        P("dp", None),
    )
    out_specs = (
        P(("dp", "bank"), None),
        P(("dp", "bank"), None),
        P("bank", None),
        P("bank", None),
        P("bank"),
        P("bank"),
        P("bank", None),
        P("bank"),
        P("bank"),
        P("bank", None),
        P("bank"),
        P("bank"),
        P("bank", None),
        P("bank", None),
        P("bank", None),
        P("bank", None),
        P("bank", None),
        P("bank"),
        P("bank"),
        P("bank", None),
        P("bank", None),
    )
    return jax.shard_map(body, mesh=mesh, in_specs=in_specs, out_specs=out_specs, check_vma=False)
```

```python
import functools

import jax
import jax.numpy as jnp
from jax import lax
from jax.experimental import pallas as pl
from jax.experimental.pallas import tpu as pltpu
from jax.sharding import PartitionSpec as P

FRAMES = 4
SIDE = 8
LANE_ROWS = 16
TILE = 128
ROOT = 0.7978845608028654
CUBIC = 0.044715

epsilon = 1e-05
masked_score = -1e30
places = [(-1, -1), (-1, 0), (-1, 1), (0, -1), (0, 0), (0, 1), (1, -1), (1, 0), (1, 1)]


def product(left, right):
    return jnp.dot(left, right, preferred_element_type=jnp.float32)


def low(value):
    return value.astype(jnp.bfloat16)


def wide(value):
    return value.astype(jnp.float32)


class SubAxis:
    def __init__(self, name, size, stride):
        self.name, self.size, self.stride = name, size, stride

    def place(self):
        return lax.rem(lax.axis_index(self.name) // self.stride, self.size)

    def swap(self, value, step):
        count = lax.axis_size(self.name)
        pairs = [(i, i ^ (step * self.stride)) for i in range(count)]
        return lax.ppermute(value, self.name, pairs)


def block_axes(split, dp_count, bank_count):
    if split:
        return (
            SubAxis("bank", bank_count // 2, 2),
            SubAxis("bank", 2, 1),
            SubAxis("dp", dp_count // 2, 2),
            SubAxis("dp", 2, 1),
        )
    return (
        SubAxis("bank", bank_count // 8, 8),
        SubAxis("bank", 2, 4),
        SubAxis("bank", 2, 2),
        SubAxis("bank", 2, 1),
    )


def block_at(value, place, dim):
    return lax.dynamic_index_in_dim(value, place, dim, keepdims=False)


def reduce_over(value, axis, dim):
    me = axis.place()
    parts = [axis.swap(block_at(value, me ^ step, dim), step) for step in range(1, axis.size)]
    total = wide(block_at(value, me, dim))
    for part in parts:
        total = total + wide(part)
    return total


def reduce_halves(send, keep, axes):
    outer, inner, across, last = axes
    value = low(wide(keep) + wide(last.swap(send, 1)))
    half = outer.size // 2
    first = low(reduce_over(value[:half], across, 2))
    second = low(reduce_over(value[half:], inner, 1))
    first = low(reduce_over(first, inner, 1))
    second = low(reduce_over(second, across, 1))
    return reduce_over(jnp.concatenate([first, second], 0), outer, 0)


def sum_everywhere(value, names):
    for name in names:
        step = 1
        while step < lax.axis_size(name):
            pairs = [(i, i ^ step) for i in range(lax.axis_size(name))]
            value = value + lax.ppermute(value, name, pairs)
            step *= 2
    return value


def to_owners(value):
    return lax.all_to_all(value, "bank", split_axis=0, concat_axis=0, tiled=True)


def to_group(value):
    count = lax.axis_size("bank")
    return to_owners(jnp.broadcast_to(value[None], (count,) + value.shape))


def whole_vmem(count):
    return [pl.BlockSpec(memory_space=pltpu.VMEM)] * count


def params(mib):
    return pltpu.CompilerParams(vmem_limit_bytes=mib * 1024 * 1024)


def gelu_of(x):
    return 0.5 * x * (1.0 + jnp.tanh(ROOT * (x + CUBIC * x * x * x)))


def gelu_slope(x):
    square = x * x
    bent = jnp.tanh(ROOT * x * (1.0 + CUBIC * square))
    return 0.5 * (1.0 + bent) + 0.5 * ROOT * x * (1.0 - bent * bent) * (1.0 + 3.0 * CUBIC * square)


def by_rows(count, step, work):
    def one(number, carry):
        work(pl.ds(pl.multiple_of(number * step, step), step))
        return carry

    lax.fori_loop(0, count // step, one, 0)


def dot_tn(left, right):
    return lax.dot_general(
        left, right, (((0,), (0,)), ((), ())), preferred_element_type=jnp.float32
    )


def dot_nt(left, right):
    return lax.dot_general(
        left, right, (((1,), (1,)), ((), ())), preferred_element_type=jnp.float32
    )


def in_rows(value, step):
    if step == 0:
        return value
    sites, width = value.shape
    tall = value.reshape(sites // (SIDE * SIDE), SIDE, SIDE, width)
    edge = jnp.zeros_like(tall[:, :1])
    if step > 0:
        tall = jnp.concatenate([tall[:, 1:], edge], axis=1)
    else:
        tall = jnp.concatenate([edge, tall[:, :-1]], axis=1)
    return tall.reshape(sites, width)


def in_columns(value, step):
    if step == 0:
        return value
    sites = value.shape[0]
    turned = pltpu.roll(value, (-step) % sites, 0)
    column = lax.broadcasted_iota(jnp.int32, value.shape, 0) % SIDE
    keep = column != (SIDE - 1 if step > 0 else 0)
    return jnp.where(keep, turned, 0.0)


def fetch(source, target, sems, first, groups):
    copies = []
    for block in range(source.shape[0]):
        copies.append(
            pltpu.make_async_copy(
                source.at[block, pl.ds(first, groups)],
                target.at[pl.ds(block * groups, groups)],
                sems.at[block],
            )
        )
    return copies


def fetch_columns(source, target, sems, first, groups):
    return [
        pltpu.make_async_copy(
            source.at[block, pl.ds(first, groups)], target.at[:, block], sems.at[block]
        )
        for block in range(source.shape[0])
    ]


def first_conv(fm_ref, packed_ref, scale_ref, shift_ref, pre_ref, act_ref, weight, sems):
    sites, features = fm_ref.shape
    channels = pre_ref.shape[1]
    groups = weight.shape[0] // packed_ref.shape[0]
    copies = fetch(packed_ref, weight, sems, 0, groups)
    for copy in copies:
        copy.start()
    block_rows = groups * LANE_ROWS
    clip = FRAMES * SIDE * SIDE
    frame = SIDE * SIDE
    waited = 0

    def tap(number):
        nonlocal waited
        end = (number + 1) * features
        while waited < len(copies) and waited * block_rows < end:
            copies[waited].wait()
            waited += 1
        begin = number * features // LANE_ROWS
        return weight[begin : begin + features // LANE_ROWS].reshape(features, channels)

    before = tap(0)
    for start in range(0, sites, clip):
        pre_ref[start : start + frame] = jnp.zeros((frame, channels), jnp.float32)
        pre_ref[start + frame : start + clip] = product(fm_ref[start : start + clip - frame], before)
    pre_ref[...] += product(fm_ref[...], tap(1))
    after = tap(2)
    for start in range(0, sites, clip):
        pre_ref[start : start + clip - frame] += product(fm_ref[start + frame : start + clip], after)

    def finish(rows):
        act_ref[rows] = low(gelu_of(pre_ref[rows] * scale_ref[...] + shift_ref[...]))

    by_rows(sites, 64, finish)


def later_convs(
    act_a_ref, fm_ref, packed_ref, scale_b_ref, shift_b_ref, scale_c_ref, shift_c_ref, pool_ref, w_reduce_ref, w_query_ref,
    pre_b_ref, act_b_ref, pre_c_ref, regions_ref, reduced_ref, queries_ref,
    weight_b, weight_c, out_low, sems_b, sems_c,
):
    sites, channels = act_a_ref.shape
    blocks = packed_ref.shape[0]
    groups_b = weight_b.shape[0] // blocks
    groups_c = weight_c.shape[0]
    groups_a = packed_ref.shape[1] - groups_b - groups_c
    copies_b = fetch(packed_ref, weight_b, sems_b, groups_a, groups_b)
    copies_c = fetch_columns(packed_ref, weight_c, sems_c, groups_a + groups_b, groups_c)
    for copy in copies_b + copies_c:
        copy.start()
    act_a = act_a_ref[...]
    block_rows = groups_b * LANE_ROWS
    sums = {-1: None, 0: None, 1: None}
    waited = 0
    for number, (rise, slide) in enumerate(places):
        while waited < len(copies_b) and waited * block_rows < (number + 1) * channels:
            copies_b[waited].wait()
            waited += 1
        begin = number * channels // LANE_ROWS
        tap = weight_b[begin : begin + channels // LANE_ROWS].reshape(channels, channels)
        part = in_rows(product(act_a, tap), rise)
        sums[slide] = part if sums[slide] is None else sums[slide] + part
    pre_b_ref[...] = sums[0] + in_columns(sums[1], 1) + in_columns(sums[-1], -1)

    def finish(rows):
        act_b_ref[rows] = low(gelu_of(pre_b_ref[rows] * scale_b_ref[...] + shift_b_ref[...]))

    by_rows(sites, 64, finish)
    for copy in copies_c:
        copy.wait()
    reduced_ref[...] = jnp.zeros_like(reduced_ref)

    def chunk(number, carry):
        columns = pl.ds(pl.multiple_of(number * channels, channels), channels)
        pre_c_ref[:, columns] = product(act_b_ref[...], weight_c[number].reshape(channels, channels))

        def finish_c(rows):
            linear = wide(fm_ref[rows, columns]) + pre_c_ref[rows, columns] * scale_c_ref[:, columns] + shift_c_ref[:, columns]
            out_low[rows] = low(gelu_of(linear))

        by_rows(sites, 64, finish_c)
        part = low(product(pool_ref[...], out_low[...]))
        regions_ref[:, columns] = part
        reduced_ref[...] += product(part, w_reduce_ref[columns])
        return carry

    lax.fori_loop(0, groups_c, chunk, 0)
    queries_ref[...] = low(product(low(reduced_ref[...]), w_query_ref[...]))


def column_tile(columns, shape):
    lane = lax.broadcasted_iota(jnp.int32, shape, len(shape) - 1)
    tile = jnp.zeros(shape, jnp.float32)
    for number, column in enumerate(columns):
        rest = column
        for third in range(3):
            piece = wide(low(rest))
            tile = jnp.where(lane == 3 * number + third, piece, tile)
            rest = rest - piece
    return low(tile)


def from_tile(tile, number):
    lane = lax.broadcasted_iota(jnp.int32, tile.shape, tile.ndim - 1)
    picked = jnp.where((lane >= 3 * number) & (lane < 3 * number + 3), wide(tile), 0.0)
    return jnp.sum(picked, axis=-1, keepdims=True)


def attend(half_span, start_ref, queries_ref, keys_ref, values_ref, time_ref, message_ref, scores_ref):
    channels = queries_ref.shape[1]
    positions = start_ref[0] + lax.broadcasted_iota(jnp.int32, scores_ref.shape, 1)
    visible = jnp.abs(time_ref[...] - positions) <= half_span
    scores = dot_nt(queries_ref[...], keys_ref[...]) * (channels ** (-0.5))
    scores = jnp.where(visible, scores, masked_score)
    scores_ref[...] = scores
    top = jnp.max(scores, axis=1, keepdims=True)
    weights = jnp.exp(scores - top)
    total = jnp.sum(weights, axis=1, keepdims=True)
    message_ref[:, :channels] = low(product(low(weights), values_ref[...]))
    message_ref[:, channels:] = column_tile([top, total], (scores.shape[0], TILE))


def merge_rows(arrived_ref, hidden_grad_ref, gain_ref, shift_ref, message_ref, hidden_ref, gain_out_ref, shift_out_ref):
    count, own, packed = arrived_ref.shape
    channels = hidden_grad_ref.shape[1]
    tops = from_tile(arrived_ref[:, :, channels:], 0)
    totals = from_tile(arrived_ref[:, :, channels:], 1)
    top = jnp.max(tops, axis=0)
    factors = jnp.exp(tops - top[None])
    total = jnp.sum(factors * totals, axis=0)
    numer = jnp.sum(factors * wide(arrived_ref[:, :, :channels]), axis=0)
    attended = numer / total
    centred = attended - jnp.mean(attended, axis=1, keepdims=True)
    spread = lax.rsqrt(jnp.mean(centred * centred, axis=1, keepdims=True) + epsilon)
    unit = centred * spread
    normed = unit * gain_ref[...] + shift_ref[...]
    hidden_ref[...] = low(gelu_of(normed))
    normed_grad = hidden_grad_ref[...] * gelu_slope(normed)
    gain_out_ref[...] = jnp.sum(normed_grad * unit, axis=0, keepdims=True)
    shift_out_ref[...] = jnp.sum(normed_grad, axis=0, keepdims=True)
    unit_grad = normed_grad * gain_ref[...]
    attended_grad = spread * (
        unit_grad
        - jnp.mean(unit_grad, axis=1, keepdims=True)
        - unit * jnp.mean(unit_grad * unit, axis=1, keepdims=True)
    )
    centre = jnp.sum(attended_grad * attended, axis=1, keepdims=True) / total
    numer_grad = low(attended_grad / total)
    tile = column_tile([top, centre], (own, TILE))
    for place in range(count):
        message_ref[place, :, :channels] = numer_grad
        message_ref[place, :, channels:] = tile


def attend_back(arrived_ref, scores_ref, keys_ref, values_ref, part_ref, score_grad_ref, weights_ref):
    channels = keys_ref.shape[1]
    top = from_tile(arrived_ref[:, channels:], 0)
    centre = from_tile(arrived_ref[:, channels:], 1)
    weights = jnp.exp(scores_ref[...] - top)
    weights_ref[...] = low(weights)
    prob_grad = dot_nt(arrived_ref[:, :channels], values_ref[...])
    score_grad = low(weights * (prob_grad - centre) * (channels ** (-0.5)))
    score_grad_ref[...] = score_grad
    part_ref[...] = low(product(score_grad, keys_ref[...]))


def half_of(place_ref, bit):
    return jnp.where(place_ref[0] == bit, 1, 0)


def hand_out(buffer, send_ref, keep_ref, sems):
    copies = [
        pltpu.make_async_copy(buffer.at[number], target, sems.at[number])
        for number, target in enumerate((send_ref, keep_ref))
    ]
    for copy in copies:
        copy.start()
    for copy in copies:
        copy.wait()


def store_rows(buffer, place_ref, value, first):
    rows = buffer.shape[2]
    at, end = first, first + value.shape[0]
    while at < end:
        block, offset = divmod(at, rows)
        count = min(rows - offset, end - at)
        buffer[half_of(place_ref, block % 2), block // 2, offset : offset + count] = value[at - first : at - first + count]
        at += count


def fold(value):
    return jnp.sum(value.reshape(value.shape[0] // 8, 8, value.shape[1]), axis=0)


def third_back(
    place_ref, arrived_ref, joined_grad_ref, w_query_ref, w_reduce_ref, pool_ref, pre_c_ref, fm_ref, scale_ref, shift_ref,
    act_b_ref, packed_ref,
    send_ref, keep_ref, lin_c_grad_ref, act_b_grad_ref, scale_out_ref, shift_out_ref, query_grad_ref, reduced_grad_ref,
    weight_c, buffer, out_grad, pre_grad, regions_grad, turned, sems, out_sems,
):
    sites, features = fm_ref.shape
    channels = act_b_ref.shape[1]
    groups_c = weight_c.shape[0]
    blocks = weight_c.shape[1]
    first = packed_ref.shape[1] - groups_c
    copies = fetch_columns(packed_ref, weight_c, sems, first, groups_c)
    for copy in copies:
        copy.start()
    query_grad = low(jnp.sum(wide(arrived_ref[...]), axis=0))
    query_grad_ref[...] = query_grad
    reduced_grad = low(joined_grad_ref[:, features:] + dot_nt(query_grad, w_query_ref[...]))
    reduced_grad_ref[...] = reduced_grad
    regions_grad[...] = low(joined_grad_ref[:, :features] + dot_nt(reduced_grad, w_reduce_ref[...]))
    turned[...] = act_b_ref[...].T
    act_b_grad_ref[...] = jnp.zeros_like(act_b_grad_ref)
    for copy in copies:
        copy.wait()

    def chunk(number, carry):
        columns = pl.ds(pl.multiple_of(number * channels, channels), channels)
        out_grad[...] = dot_tn(pool_ref[...], regions_grad[:, columns])

        def one(step, sums):
            rows = pl.ds(pl.multiple_of(step * 64, 64), 64)
            pre = pre_c_ref[rows, columns]
            scale = scale_ref[:, columns]
            linear = wide(fm_ref[rows, columns]) + pre * scale + shift_ref[:, columns]
            grad = out_grad[rows] * gelu_slope(linear)
            lin_c_grad_ref[rows, columns] = grad
            pre_grad[rows] = low(grad * scale)
            return sums[0] + fold(grad * pre), sums[1] + fold(grad)

        zero = jnp.zeros((8, channels), jnp.float32)
        scale_sum, shift_sum = lax.fori_loop(0, sites // 64, one, (zero, zero))
        scale_out_ref[:, columns] = jnp.sum(scale_sum, axis=0, keepdims=True)
        shift_out_ref[:, columns] = jnp.sum(shift_sum, axis=0, keepdims=True)
        part = low(product(turned[...], pre_grad[...])).reshape(blocks // 2, 2, LANE_ROWS, channels)
        rows = pl.ds(pl.multiple_of(number * LANE_ROWS, LANE_ROWS), LANE_ROWS)
        for bit in range(2):
            buffer[half_of(place_ref, bit), :, rows] = part[:, bit]
        act_b_grad_ref[...] += dot_nt(pre_grad[...], weight_c[number].reshape(channels, channels))
        return carry

    lax.fori_loop(0, groups_c, chunk, 0)
    hand_out(buffer, send_ref, keep_ref, out_sems)


def slope_back(upstream_ref, pre_ref, scale_ref, shift_ref, out_ref, scale_out_ref, shift_out_ref):
    sites, channels = pre_ref.shape

    def one(step, sums):
        rows = pl.ds(pl.multiple_of(step * 64, 64), 64)
        pre = pre_ref[rows]
        grad = upstream_ref[rows] * gelu_slope(pre * scale_ref[...] + shift_ref[...])
        out_ref[rows] = low(grad * scale_ref[...]).astype(out_ref.dtype)
        return sums[0] + fold(grad * pre), sums[1] + fold(grad)

    zero = jnp.zeros((8, channels), jnp.float32)
    scale_sum, shift_sum = lax.fori_loop(0, sites // 64, one, (zero, zero))
    scale_out_ref[...] = jnp.sum(scale_sum, axis=0, keepdims=True)
    shift_out_ref[...] = jnp.sum(shift_sum, axis=0, keepdims=True)


def second_back(
    first, place_ref, act_b_grad_ref, pre_b_ref, scale_b_ref, shift_b_ref, act_a_ref, pre_a_ref, scale_a_ref, shift_a_ref, packed_ref,
    send_ref, keep_ref, pre_a_grad_ref, scale_b_out_ref, shift_b_out_ref, scale_a_out_ref, shift_a_out_ref,
    weight_b, buffer, pre_grad, act_grad, turned, sems, out_sems,
):
    channels = act_a_ref.shape[1]
    blocks = packed_ref.shape[0]
    groups_b = weight_b.shape[0] // blocks
    copies = fetch(packed_ref, weight_b, sems, first, groups_b)
    for copy in copies:
        copy.start()
    slope_back(act_b_grad_ref, pre_b_ref, scale_b_ref, shift_b_ref, pre_grad, scale_b_out_ref, shift_b_out_ref)
    turned[...] = act_a_ref[...].T
    for copy in copies:
        copy.wait()
    for slide in (-1, 0, 1):
        slid = in_columns(pre_grad[...], -slide)
        for number, place in enumerate(places):
            if place[1] != slide:
                continue
            moved = low(in_rows(slid, -place[0]))
            store_rows(buffer, place_ref, low(product(turned[...], moved)), number * channels)
            begin = number * channels // LANE_ROWS
            tap = weight_b[begin : begin + channels // LANE_ROWS].reshape(channels, channels)
            part = dot_nt(moved, tap)
            if slide == -1 and place[0] == -1:
                act_grad[...] = part
            else:
                act_grad[...] += part
    slope_back(act_grad, pre_a_ref, scale_a_ref, shift_a_ref, pre_a_grad_ref, scale_a_out_ref, shift_a_out_ref)
    hand_out(buffer, send_ref, keep_ref, out_sems)


def by_frames(grad, offset):
    if offset == 0:
        return grad
    sites, width = grad.shape
    tall = grad.reshape(sites // (FRAMES * SIDE * SIDE), FRAMES, SIDE * SIDE, width)
    edge = jnp.zeros_like(tall[:, :1])
    if offset > 0:
        tall = jnp.concatenate([edge, tall[:, :-1]], axis=1)
    else:
        tall = jnp.concatenate([tall[:, 1:], edge], axis=1)
    return tall.reshape(sites, width)


def first_back(place_ref, grad_ref, turned_ref, send_ref, keep_ref, buffer, out_sems):
    features = turned_ref.shape[0]
    channels = grad_ref.shape[1]
    for tap in range(3):
        moved = by_frames(grad_ref[...], tap - 1)
        for start in range(0, features, channels):
            part = low(product(turned_ref[start : start + channels], moved))
            store_rows(buffer, place_ref, part, tap * features + start)
    hand_out(buffer, send_ref, keep_ref, out_sems)


def map_back(grad_ref, lin_c_grad_ref, packed_ref, out_ref, weight, moved, sems):
    sites, features = out_ref.shape
    channels = grad_ref.shape[1]
    blocks = packed_ref.shape[0]
    copies = fetch(packed_ref, weight, sems, 0, weight.shape[0] // blocks)
    for copy in copies:
        copy.start()
    for tap in range(3):
        moved[tap] = by_frames(grad_ref[...], tap - 1)
    for copy in copies:
        copy.wait()
    groups = channels // LANE_ROWS

    def chunk(number, carry):
        columns = pl.ds(pl.multiple_of(number * channels, channels), channels)
        total = lin_c_grad_ref[:, columns]
        for tap in range(3):
            rows = pl.ds(tap * (features // LANE_ROWS) + number * groups, groups)
            total = total + dot_nt(moved[tap], weight[rows].reshape(channels, channels))
        out_ref[:, columns] = low(total)
        return carry

    lax.fori_loop(0, features // channels, chunk, 0)

ANY = pl.BlockSpec(memory_space=pl.ANY)
SCALAR = pl.BlockSpec(memory_space=pltpu.SMEM)


def shape_of(dims, kind):
    return jax.ShapeDtypeStruct(dims, kind)


F32 = jnp.float32
BF16 = jnp.bfloat16


def run_first_conv(feature_map, packed, scale, shift, groups):
    sites, channels = feature_map.shape[0], packed.shape[3]
    blocks = packed.shape[0]
    return pl.pallas_call(
        first_conv,
        out_shape=[
            jax.ShapeDtypeStruct((sites, channels), jnp.float32),
            jax.ShapeDtypeStruct((sites, channels), jnp.bfloat16),
        ],
        in_specs=[pl.BlockSpec(memory_space=pltpu.VMEM), pl.BlockSpec(memory_space=pl.ANY)] + whole_vmem(2),
        out_specs=whole_vmem(2),
        scratch_shapes=[
            pltpu.VMEM((blocks * groups, LANE_ROWS, channels), jnp.bfloat16),
            pltpu.SemaphoreType.DMA((blocks,)),
        ],
        compiler_params=params(40),
        name="first_conv",
    )(feature_map, packed, scale.reshape(1, -1), shift.reshape(1, -1))


def run_later_convs(
    act_a, feature_map, packed, scale_b, shift_b, scale_c, shift_c, pooling, w_reduce, w_query, groups_b, groups_c
):
    sites, channels = act_a.shape
    features = feature_map.shape[1]
    blocks = packed.shape[0]
    own = pooling.shape[0]
    return pl.pallas_call(
        later_convs,
        out_shape=[
            jax.ShapeDtypeStruct((sites, channels), jnp.float32),
            jax.ShapeDtypeStruct((sites, channels), jnp.bfloat16),
            jax.ShapeDtypeStruct((sites, features), jnp.float32),
            jax.ShapeDtypeStruct((own, features), jnp.bfloat16),
            jax.ShapeDtypeStruct((own, channels), jnp.float32),
            jax.ShapeDtypeStruct((own, channels), jnp.bfloat16),
        ],
        in_specs=whole_vmem(2) + [pl.BlockSpec(memory_space=pl.ANY)] + whole_vmem(7),
        out_specs=whole_vmem(6),
        scratch_shapes=[
            pltpu.VMEM((blocks * groups_b, LANE_ROWS, channels), jnp.bfloat16),
            pltpu.VMEM((groups_c, blocks, LANE_ROWS, channels), jnp.bfloat16),
            pltpu.VMEM((sites, channels), jnp.bfloat16),
            pltpu.SemaphoreType.DMA((blocks,)),
            pltpu.SemaphoreType.DMA((blocks,)),
        ],
        compiler_params=params(52),
        name="later_convs",
    )(
        act_a, feature_map, packed, scale_b.reshape(1, -1), shift_b.reshape(1, -1), scale_c.reshape(1, -1),
        shift_c.reshape(1, -1), pooling, w_reduce, w_query,
    )


def run_attend(half_span, start, queries, keys, values, times):
    rows, channels = queries.shape
    return pl.pallas_call(
        functools.partial(attend, half_span),
        out_shape=[shape_of((rows, channels + TILE), BF16), shape_of((rows, keys.shape[0]), F32)],
        in_specs=[SCALAR] + whole_vmem(4),
        out_specs=whole_vmem(2),
        compiler_params=params(32),
        name="attend",
    )(start.reshape(1), queries, keys, values, times.reshape(-1, 1))


def run_merge_rows(arrived, hidden_grad, gain, shift):
    own, channels = hidden_grad.shape
    return pl.pallas_call(
        merge_rows,
        out_shape=[
            shape_of(arrived.shape, BF16),
            shape_of((own, channels), BF16),
            shape_of((1, channels), F32),
            shape_of((1, channels), F32),
        ],
        in_specs=whole_vmem(4),
        out_specs=whole_vmem(4),
        compiler_params=params(24),
        name="merge_rows",
    )(arrived, hidden_grad, gain.reshape(1, -1), shift.reshape(1, -1))


def run_attend_back(arrived, scores, keys, values):
    rows, count = scores.shape
    channels = keys.shape[1]
    return pl.pallas_call(
        attend_back,
        out_shape=[shape_of((rows, channels), BF16), shape_of((rows, count), BF16), shape_of((rows, count), BF16)],
        in_specs=whole_vmem(4),
        out_specs=whole_vmem(3),
        compiler_params=params(32),
        name="attend_back",
    )(arrived, scores, keys, values)


def run_third_back(
    place, arrived, joined_grad, w_query, w_reduce, pooling, pre_c, feature_map, scale, shift, act_b, packed, groups_c
):
    sites, features = feature_map.shape
    channels = act_b.shape[1]
    blocks, own = packed.shape[0], pooling.shape[0]
    rows_c = groups_c * LANE_ROWS
    return pl.pallas_call(
        third_back,
        out_shape=[shape_of((blocks // 2, rows_c, channels), BF16)] * 2
        + [
            shape_of((sites, features), F32),
            shape_of((sites, channels), F32),
            shape_of((1, features), F32),
            shape_of((1, features), F32),
            shape_of((own, channels), BF16),
            shape_of((own, channels), BF16),
        ],
        in_specs=[SCALAR] + whole_vmem(10) + [ANY],
        out_specs=[ANY] * 2 + whole_vmem(6),
        scratch_shapes=[
            pltpu.VMEM((groups_c, blocks, LANE_ROWS, channels), BF16),
            pltpu.VMEM((2, blocks // 2, rows_c, channels), BF16),
            pltpu.VMEM((sites, channels), F32),
            pltpu.VMEM((sites, channels), BF16),
            pltpu.VMEM((own, features), BF16),
            pltpu.VMEM((channels, sites), BF16),
            pltpu.SemaphoreType.DMA((blocks,)),
            pltpu.SemaphoreType.DMA((2,)),
        ],
        compiler_params=params(52),
        name="third_back",
    )(
        place.reshape(1), arrived, joined_grad, w_query, w_reduce, pooling, pre_c, feature_map, scale.reshape(1, -1),
        shift.reshape(1, -1), act_b, packed,
    )


def run_second_back(
    place, act_b_grad, pre_b, scale_b, shift_b, act_a, pre_a, scale_a, shift_a, packed, groups_a, groups_b
):
    sites, channels = act_a.shape
    blocks = packed.shape[0]
    rows_b = groups_b * LANE_ROWS
    row = shape_of((1, channels), F32)
    return pl.pallas_call(
        functools.partial(second_back, groups_a),
        out_shape=[shape_of((blocks // 2, rows_b, channels), BF16)] * 2
        + [shape_of((sites, channels), BF16), row, row, row, row],
        in_specs=[SCALAR] + whole_vmem(8) + [ANY],
        out_specs=[ANY] * 2 + whole_vmem(5),
        scratch_shapes=[
            pltpu.VMEM((blocks * groups_b, LANE_ROWS, channels), BF16),
            pltpu.VMEM((2, blocks // 2, rows_b, channels), BF16),
            pltpu.VMEM((sites, channels), F32),
            pltpu.VMEM((sites, channels), F32),
            pltpu.VMEM((channels, sites), BF16),
            pltpu.SemaphoreType.DMA((blocks,)),
            pltpu.SemaphoreType.DMA((2,)),
        ],
        compiler_params=params(52),
        name="second_back",
    )(
        place.reshape(1), act_b_grad, pre_b, scale_b.reshape(1, -1), shift_b.reshape(1, -1), act_a, pre_a,
        scale_a.reshape(1, -1), shift_a.reshape(1, -1), packed,
    )


def run_first_back(place, pre_a_grad, turned_map, blocks, rows_a):
    channels = pre_a_grad.shape[1]
    return pl.pallas_call(
        first_back,
        out_shape=[shape_of((blocks // 2, rows_a, channels), BF16)] * 2,
        in_specs=[SCALAR] + whole_vmem(2),
        out_specs=[ANY] * 2,
        scratch_shapes=[
            pltpu.VMEM((2, blocks // 2, rows_a, channels), BF16),
            pltpu.SemaphoreType.DMA((2,)),
        ],
        compiler_params=params(40),
        name="first_back",
    )(place.reshape(1), pre_a_grad, turned_map)


def run_map_back(pre_a_grad, lin_c_grad, packed, groups_a):
    sites, channels = pre_a_grad.shape
    blocks = packed.shape[0]
    return pl.pallas_call(
        map_back,
        out_shape=shape_of(lin_c_grad.shape, BF16),
        in_specs=whole_vmem(2) + [ANY],
        out_specs=pl.BlockSpec(memory_space=pltpu.VMEM),
        scratch_shapes=[
            pltpu.VMEM((blocks * groups_a, LANE_ROWS, channels), BF16),
            pltpu.VMEM((3, sites, channels), BF16),
            pltpu.SemaphoreType.DMA((blocks,)),
        ],
        compiler_params=params(40),
        name="map_back",
    )(pre_a_grad, lin_c_grad, packed)


def body(
    feature_map,
    bank,
    region_time,
    roi_index,
    roi_weight,
    conv_a,
    scale_a,
    shift_a,
    conv_b,
    scale_b,
    shift_b,
    conv_c,
    scale_c,
    shift_c,
    w_reduce,
    w_bank,
    w_query,
    w_key,
    w_value,
    ln_gain,
    ln_shift,
    w_out,
    w_head,
    logit_grad,
):
    site_count = feature_map.shape[0]
    feature_count = feature_map.shape[1]
    channels = w_query.shape[0]
    keys_here = bank.shape[0]
    own_count = roi_index.shape[0]
    bank_count = lax.axis_size("bank")
    bank_place = lax.axis_index("bank")
    dp_count = lax.axis_size("dp")
    dp_place = lax.axis_index("dp")
    first_row = bank_place * own_count
    half_span = keys_here * bank_count // 2
    group_rows = bank_count * own_count
    chunks = feature_count // channels
    shards = (conv_a, conv_b, conv_c)
    split = all(shard.shape[0] % (LANE_ROWS * dp_count) == 0 for shard in shards)
    axes = block_axes(split, dp_count, bank_count)
    blocks = bank_count * dp_count if split else bank_count
    halves = tuple(axis.size for axis in axes[:3])
    last_place = axes[3].place()

    def own_part(shard):
        if not split:
            return shard
        rows = shard.shape[0] // dp_count
        return lax.dynamic_slice_in_dim(shard, dp_place * rows, rows, 0)

    part_a, part_b, part_c = [own_part(shard) for shard in shards]
    rows_a, rows_b, rows_c = part_a.shape[0], part_b.shape[0], part_c.shape[0]
    groups_a, groups_b, groups_c = rows_a // LANE_ROWS, rows_b // LANE_ROWS, chunks
    pieces_c = [part_c[:, chunk * channels : (chunk + 1) * channels] for chunk in range(chunks)]
    own_packed = jnp.concatenate([part_a, part_b] + pieces_c, 0).reshape(-1, LANE_ROWS, channels)
    packed = lax.all_gather(own_packed, ("bank", "dp") if split else "bank", axis=0, tiled=False)
    packed = packed.reshape((blocks,) + own_packed.shape)

    memory = product(bank, w_bank)
    memory_low = low(memory)
    keys = low(product(memory_low, w_key))
    values = low(product(memory_low, w_value))
    turned_map = feature_map.T
    matches = roi_index[:, :, None] == jnp.arange(site_count, dtype=jnp.int32)[None, None, :]
    pooling = low(jnp.sum(jnp.where(matches, wide(roi_weight)[:, :, None], 0.0), axis=1))
    own_logit_grad = lax.dynamic_slice_in_dim(logit_grad, first_row, own_count, 0)
    joined_grad = dot_nt(own_logit_grad, w_head)
    branch_grad = low(joined_grad[:, feature_count:])
    hidden_grad = dot_nt(branch_grad, w_out)

    pre_a, act_a = run_first_conv(feature_map, packed, scale_a, shift_a, groups_a)
    pre_b, act_b, pre_c, regions, reduced, own_queries = run_later_convs(
        act_a, feature_map, packed, scale_b, shift_b, scale_c, shift_c, pooling, w_reduce, w_query, groups_b, groups_c
    )
    reduced_low = low(reduced)
    queries = to_group(own_queries).reshape(group_rows, channels)
    message, scores = run_attend(half_span, bank_place * keys_here, queries, keys, values, region_time)
    arrived = to_owners(message.reshape(bank_count, own_count, channels + TILE))
    message, hidden_low, gain_part, shift_part = run_merge_rows(arrived, hidden_grad, ln_gain, ln_shift)
    arrived = to_owners(message).reshape(group_rows, channels + TILE)
    query_part, score_grad, weights_low = run_attend_back(arrived, scores, keys, values)
    numer_grad = arrived[:, :channels]
    arrived = to_owners(query_part.reshape(bank_count, own_count, channels))
    key_part = low(dot_tn(score_grad, queries))
    value_part = low(dot_tn(weights_low, numer_grad))
    (
        send_c, keep_c, lin_c_grad, act_b_grad, scale_c_part, shift_c_part, query_grad, reduced_grad
    ) = run_third_back(
        last_place, arrived, joined_grad, w_query, w_reduce, pooling, pre_c, feature_map, scale_c, shift_c, act_b,
        packed, groups_c,
    )
    send_b, keep_b, pre_a_grad, scale_b_part, shift_b_part, scale_a_part, shift_a_part = run_second_back(
        last_place, act_b_grad, pre_b, scale_b, shift_b, act_a, pre_a, scale_a, shift_a, packed, groups_a, groups_b
    )
    send_a, keep_a = run_first_back(last_place, pre_a_grad, turned_map, blocks, rows_a)
    map_grad = run_map_back(pre_a_grad, lin_c_grad, packed, groups_a)

    merged = reduced + product(hidden_low, w_out)
    joined = jnp.concatenate([regions, low(merged)], axis=1)
    logits_out = low(product(joined, w_head))

    region_parts = [
        low(part).reshape(blocks, part.shape[0] // blocks, part.shape[1])
        for part in (
            dot_tn(regions, reduced_grad),
            dot_tn(reduced_low, query_grad),
            dot_tn(hidden_low, branch_grad),
            dot_tn(joined, own_logit_grad),
        )
    ]

    def over_dp(block):
        if split:
            return lax.all_gather(low(block), "dp", axis=0, tiled=False)
        return lax.psum(low(block), "dp")[None]

    def reduced_part(send, keep):
        rows, width = send.shape[-2:]
        dims = halves + (rows, width)
        return over_dp(reduce_halves(send.reshape(dims), keep.reshape(dims), axes))

    def halved(part):
        pairs = part.reshape((blocks // 2, 2) + part.shape[1:])
        return reduced_part(block_at(pairs, 1 - last_place, 1), block_at(pairs, last_place, 1))

    done_r = halved(jnp.concatenate(region_parts[:3], axis=1))
    done_h = halved(region_parts[3])
    done_c = reduced_part(send_c, keep_c)
    done_b = reduced_part(send_b, keep_b)
    done_a = reduced_part(send_a, keep_a)

    def whole(stacked, first, count):
        picked = wide(stacked[:, first : first + count])
        return picked.reshape(stacked.shape[0] * count, stacked.shape[2])

    rows_reduce = feature_count // blocks
    rows_query = channels // blocks
    reduce_weight_grad = whole(done_r, 0, rows_reduce)
    query_weight_grad = whole(done_r, rows_reduce, rows_query)
    out_weight_grad = whole(done_r, rows_reduce + rows_query, rows_query)
    head_weight_grad = whole(done_h, 0, done_h.shape[1])
    conv_a_grad = whole(done_a, 0, rows_a)
    conv_b_grad = whole(done_b, 0, rows_b)
    done_c = wide(done_c).reshape(-1, chunks, LANE_ROWS, channels).transpose(0, 2, 1, 3)
    conv_c_grad = done_c.reshape(-1, feature_count)

    key_value = lax.psum(jnp.concatenate([key_part, value_part], 0), "dp")
    key_low, value_low = key_value[:keys_here], key_value[keys_here:]
    memory_grad = low(dot_nt(key_low, w_key) + dot_nt(value_low, w_value))
    bank_grad = low(dot_nt(memory_grad, w_bank))
    width = channels // dp_count

    def columns(value):
        return lax.dynamic_slice_in_dim(value, dp_place * width, width, 1)

    bank_parts = [
        low(part).reshape(bank_count, part.shape[0] // bank_count, width)
        for part in (
            dot_tn(bank, columns(memory_grad)),
            dot_tn(memory_low, columns(key_low)),
            dot_tn(memory_low, columns(value_low)),
        )
    ]
    bank_sum = jnp.sum(wide(to_owners(jnp.concatenate(bank_parts, 1))), axis=0)
    bank_done = wide(lax.all_gather(low(bank_sum), "dp", axis=1, tiled=True))
    bank_rows, channel_rows = feature_count // bank_count, channels // bank_count
    bank_weight_grad = bank_done[:bank_rows]
    key_weight_grad = bank_done[bank_rows : bank_rows + channel_rows]
    value_weight_grad = bank_done[bank_rows + channel_rows :]

    vectors = [
        part.reshape(-1)
        for part in (
            gain_part, shift_part, scale_a_part, shift_a_part, scale_b_part, shift_b_part, scale_c_part, shift_c_part
        )
    ]
    summed = sum_everywhere(jnp.concatenate(vectors).reshape(-1, channels), ("dp", "bank")).reshape(-1)
    pieces, start = [], 0
    for vector in vectors:
        count = vector.shape[0] // bank_count
        pieces.append(lax.dynamic_slice_in_dim(summed, start + bank_place * count, count, 0))
        start += vector.shape[0]
    gain_grad, shift_grad = pieces[:2]
    scale_a_grad, shift_a_grad, scale_b_grad, shift_b_grad, scale_c_grad, shift_c_grad = pieces[2:]
    return (
        logits_out,
        map_grad,
        bank_grad,
        conv_a_grad,
        scale_a_grad,
        shift_a_grad,
        conv_b_grad,
        scale_b_grad,
        shift_b_grad,
        conv_c_grad,
        scale_c_grad,
        shift_c_grad,
        reduce_weight_grad,
        bank_weight_grad,
        query_weight_grad,
        key_weight_grad,
        value_weight_grad,
        gain_grad,
        shift_grad,
        out_weight_grad,
        head_weight_grad,
    )


def solution(mesh):
    in_specs = (
        P(("dp", "bank"), None),
        P("bank", None),
        P("dp"),
        P(("dp", "bank"), None),
        P(("dp", "bank"), None),
        P("bank", None),
        P(),
        P(),
        P("bank", None),
        P(),
        P(),
        P("bank", None),
        P(),
        P(),
        P(),
        P(),
        P(),
        P(),
        P(),
        P(),
        P(),
        P(),
        P(),
        P("dp", None),
    )
    out_specs = (
        P(("dp", "bank"), None),
        P(("dp", "bank"), None),
        P("bank", None),
        P("bank", None),
        P("bank"),
        P("bank"),
        P("bank", None),
        P("bank"),
        P("bank"),
        P("bank", None),
        P("bank"),
        P("bank"),
        P("bank", None),
        P("bank", None),
        P("bank", None),
        P("bank", None),
        P("bank", None),
        P("bank"),
        P("bank"),
        P("bank", None),
        P("bank", None),
    )
    return jax.shard_map(body, mesh=mesh, in_specs=in_specs, out_specs=out_specs, check_vma=False)
```

```python
import functools

import jax
import jax.numpy as jnp
from jax import lax
from jax.experimental import pallas as pl
from jax.experimental.pallas import tpu as pltpu
from jax.sharding import PartitionSpec as P

FRAMES = 4
SIDE = 8
LANE_ROWS = 16
TILE = 128
ROOT = 0.7978845608028654
CUBIC = 0.044715

epsilon = 1e-05
masked_score = -1e30
places = [(-1, -1), (-1, 0), (-1, 1), (0, -1), (0, 0), (0, 1), (1, -1), (1, 0), (1, 1)]


def product(left, right):
    return jnp.dot(left, right, preferred_element_type=jnp.float32)


def low(value):
    return value.astype(jnp.bfloat16)


def wide(value):
    return value.astype(jnp.float32)


class SubAxis:
    def __init__(self, name, size, stride):
        self.name, self.size, self.stride = name, size, stride

    def place(self):
        return lax.rem(lax.axis_index(self.name) // self.stride, self.size)

    def swap(self, value, step):
        count = lax.axis_size(self.name)
        pairs = [(i, i ^ (step * self.stride)) for i in range(count)]
        return lax.ppermute(value, self.name, pairs)


def block_axes(split, dp_count, bank_count):
    if split:
        return (
            SubAxis("bank", bank_count // 2, 2),
            SubAxis("bank", 2, 1),
            SubAxis("dp", dp_count // 2, 2),
            SubAxis("dp", 2, 1),
        )
    return (
        SubAxis("bank", bank_count // 8, 8),
        SubAxis("bank", 2, 4),
        SubAxis("bank", 2, 2),
        SubAxis("bank", 2, 1),
    )


def to_owners(value):
    return lax.all_to_all(value, "bank", split_axis=0, concat_axis=0, tiled=True)


def to_group(value):
    count = lax.axis_size("bank")
    return to_owners(jnp.broadcast_to(value[None], (count,) + value.shape))


def params(mib):
    return pltpu.CompilerParams(vmem_limit_bytes=mib * 1024 * 1024)


def gelu_of(x):
    return 0.5 * x * (1.0 + jnp.tanh(ROOT * (x + CUBIC * x * x * x)))


def gelu_slope(x):
    square = x * x
    bent = jnp.tanh(ROOT * x * (1.0 + CUBIC * square))
    return 0.5 * (1.0 + bent) + 0.5 * ROOT * x * (1.0 - bent * bent) * (1.0 + 3.0 * CUBIC * square)


def by_rows(count, step, work):
    def one(number, carry):
        work(pl.ds(pl.multiple_of(number * step, step), step))
        return carry

    lax.fori_loop(0, count // step, one, 0)


def dot_tn(left, right):
    return lax.dot_general(
        left, right, (((0,), (0,)), ((), ())), preferred_element_type=jnp.float32
    )


def dot_nt(left, right):
    return lax.dot_general(
        left, right, (((1,), (1,)), ((), ())), preferred_element_type=jnp.float32
    )


def in_rows(value, step):
    if step == 0:
        return value
    sites, width = value.shape
    tall = value.reshape(sites // (SIDE * SIDE), SIDE, SIDE, width)
    edge = jnp.zeros_like(tall[:, :1])
    if step > 0:
        tall = jnp.concatenate([tall[:, 1:], edge], axis=1)
    else:
        tall = jnp.concatenate([edge, tall[:, :-1]], axis=1)
    return tall.reshape(sites, width)


def in_columns(value, step):
    if step == 0:
        return value
    sites = value.shape[0]
    turned = pltpu.roll(value, (-step) % sites, 0)
    column = lax.broadcasted_iota(jnp.int32, value.shape, 0) % SIDE
    keep = column != (SIDE - 1 if step > 0 else 0)
    return jnp.where(keep, turned, 0.0)


def fetch(source, target, sems, first, groups):
    copies = []
    for block in range(source.shape[0]):
        copies.append(
            pltpu.make_async_copy(
                source.at[block, pl.ds(first, groups)],
                target.at[pl.ds(block * groups, groups)],
                sems.at[block],
            )
        )
    return copies


def fetch_columns(source, target, sems, first, groups):
    return [
        pltpu.make_async_copy(
            source.at[block, pl.ds(first, groups)], target.at[:, block], sems.at[block]
        )
        for block in range(source.shape[0])
    ]


def start_all(copies):
    for copy in copies:
        copy.start()
    return copies


def wait_all(copies):
    for copy in copies:
        copy.wait()


def first_conv(fm_ref, packed_ref, scale_ref, shift_ref, pre_out_ref, act_ref, weight_out_ref, weight, pre_ref, sems, out_sems):
    sites, features = fm_ref.shape
    channels = pre_ref.shape[1]
    groups = weight.shape[0] // packed_ref.shape[0]
    copies = fetch(packed_ref, weight, sems, 0, groups)
    for copy in copies:
        copy.start()
    block_rows = groups * LANE_ROWS
    clip = FRAMES * SIDE * SIDE
    frame = SIDE * SIDE
    waited = 0

    def tap(number):
        nonlocal waited
        end = (number + 1) * features
        while waited < len(copies) and waited * block_rows < end:
            copies[waited].wait()
            waited += 1
        begin = number * features // LANE_ROWS
        return weight[begin : begin + features // LANE_ROWS].reshape(features, channels)

    before = tap(0)
    for start in range(0, sites, clip):
        pre_ref[start : start + frame] = jnp.zeros((frame, channels), jnp.float32)
        pre_ref[start + frame : start + clip] = product(fm_ref[start : start + clip - frame], before)
    pre_ref[...] += product(fm_ref[...], tap(1))
    after = tap(2)
    out = start_all([pltpu.make_async_copy(weight, weight_out_ref, out_sems.at[1])])
    for start in range(0, sites, clip):
        pre_ref[start : start + clip - frame] += product(fm_ref[start + frame : start + clip], after)

    def finish(rows):
        act_ref[rows] = low(gelu_of(pre_ref[rows] * scale_ref[...] + shift_ref[...]))

    out += start_all([pltpu.make_async_copy(pre_ref, pre_out_ref, out_sems.at[0])])
    by_rows(sites, 64, finish)
    wait_all(out)


def later_convs(
    act_a_ref, fm_ref, packed_ref, scale_b_ref, shift_b_ref, scale_c_ref, shift_c_ref, pool_ref, w_reduce_ref, w_query_ref,
    pre_b_out_ref, act_b_out_ref, pre_c_ref, regions_ref, reduced_ref, queries_ref,
    weight_b, weight_c, out_low, held_map, held_pre, held_reduce, pre_b_ref, act_b_ref, sems_b, sems_c, sems,
):
    sites, channels = act_a_ref.shape
    blocks = packed_ref.shape[0]
    groups_b = weight_b.shape[0] // blocks
    groups_c = weight_c.shape[0]
    groups_a = packed_ref.shape[1] - groups_b - groups_c
    copies_b = start_all(fetch(packed_ref, weight_b, sems_b, groups_a, groups_b))
    copies_c = start_all(fetch_columns(packed_ref, weight_c, sems_c, groups_a + groups_b, groups_c))
    others = start_all(
        [
            pltpu.make_async_copy(fm_ref, held_map, sems.at[0]),
            pltpu.make_async_copy(w_reduce_ref, held_reduce, sems.at[1]),
        ]
    )
    act_a = act_a_ref[...]
    block_rows = groups_b * LANE_ROWS
    sums = {-1: None, 0: None, 1: None}
    waited = 0
    for number, (rise, slide) in enumerate(places):
        while waited < len(copies_b) and waited * block_rows < (number + 1) * channels:
            copies_b[waited].wait()
            waited += 1
        begin = number * channels // LANE_ROWS
        tap = weight_b[begin : begin + channels // LANE_ROWS].reshape(channels, channels)
        part = in_rows(product(act_a, tap), rise)
        sums[slide] = part if sums[slide] is None else sums[slide] + part
    pre_b_ref[...] = sums[0] + in_columns(sums[1], 1) + in_columns(sums[-1], -1)

    outs = start_all([pltpu.make_async_copy(pre_b_ref, pre_b_out_ref, sems.at[2 + groups_c])])

    def finish(rows):
        act_b_ref[rows] = low(gelu_of(pre_b_ref[rows] * scale_b_ref[...] + shift_b_ref[...]))

    by_rows(sites, 64, finish)
    outs += start_all([pltpu.make_async_copy(act_b_ref, act_b_out_ref, sems.at[3 + groups_c])])
    wait_all(copies_c + others)
    reduced_ref[...] = jnp.zeros_like(reduced_ref)

    def chunk(number, carry):
        columns = pl.ds(pl.multiple_of(number * channels, channels), channels)
        held_pre[:, columns] = product(act_b_ref[...], weight_c[number].reshape(channels, channels))
        pltpu.make_async_copy(held_pre.at[:, columns], pre_c_ref.at[:, columns], sems.at[2 + number]).start()

        def finish_c(rows):
            linear = wide(held_map[rows, columns]) + held_pre[rows, columns] * scale_c_ref[:, columns] + shift_c_ref[:, columns]
            out_low[rows] = low(gelu_of(linear))

        by_rows(sites, 64, finish_c)
        part = low(product(pool_ref[...], out_low[...]))
        regions_ref[:, columns] = part
        reduced_ref[...] += product(part, held_reduce[columns])
        return carry

    lax.fori_loop(0, groups_c, chunk, 0)
    queries = low(product(low(reduced_ref[...]), w_query_ref[...]))
    for place in range(queries_ref.shape[0]):
        queries_ref[place] = queries
    for number in range(groups_c):
        columns = pl.ds(number * channels, channels)
        outs.append(pltpu.make_async_copy(held_pre.at[:, columns], pre_c_ref.at[:, columns], sems.at[2 + number]))
    wait_all(outs)


def column_tile(columns, shape):
    lane = lax.broadcasted_iota(jnp.int32, shape, len(shape) - 1)
    tile = jnp.zeros(shape, jnp.float32)
    for number, column in enumerate(columns):
        rest = column
        for third in range(3):
            piece = wide(low(rest))
            tile = jnp.where(lane == 3 * number + third, piece, tile)
            rest = rest - piece
    return low(tile)


def from_tile(tile, number):
    lane = lax.broadcasted_iota(jnp.int32, tile.shape, tile.ndim - 1)
    picked = jnp.where((lane >= 3 * number) & (lane < 3 * number + 3), wide(tile), 0.0)
    return jnp.sum(picked, axis=-1, keepdims=True)


def attend(half_span, places_ref, queries_ref, keys_ref, values_ref, time_ref, message_ref, scores_ref):
    channels = queries_ref.shape[1]
    positions = places_ref[5] + lax.broadcasted_iota(jnp.int32, scores_ref.shape, 1)
    visible = jnp.abs(time_ref[...] - positions) <= half_span
    scores = dot_nt(queries_ref[...], keys_ref[...]) * (channels ** (-0.5))
    scores = jnp.where(visible, scores, masked_score)
    scores_ref[...] = scores
    top = jnp.max(scores, axis=1, keepdims=True)
    weights = jnp.exp(scores - top)
    total = jnp.sum(weights, axis=1, keepdims=True)
    message_ref[:, :channels] = low(product(low(weights), values_ref[...]))
    message_ref[:, channels:] = column_tile([top, total], (scores.shape[0], TILE))


def merge_rows(places_ref, arrived_ref, hidden_grad_ref, gain_ref, shift_ref, message_ref, hidden_ref, gain_out_ref, shift_out_ref):
    count, own, packed = arrived_ref.shape
    channels = hidden_grad_ref.shape[1]
    tops = from_tile(arrived_ref[:, :, channels:], 0)
    totals = from_tile(arrived_ref[:, :, channels:], 1)
    top = jnp.max(tops, axis=0)
    factors = jnp.exp(tops - top[None])
    total = jnp.sum(factors * totals, axis=0)
    numer = jnp.sum(factors * wide(arrived_ref[:, :, :channels]), axis=0)
    attended = numer / total
    centred = attended - jnp.mean(attended, axis=1, keepdims=True)
    spread = lax.rsqrt(jnp.mean(centred * centred, axis=1, keepdims=True) + epsilon)
    unit = centred * spread
    normed = unit * gain_ref[...] + shift_ref[...]
    hidden_ref[...] = low(gelu_of(normed))
    normed_grad = hidden_grad_ref[...] * gelu_slope(normed)
    gain_out_ref[...] = jnp.sum(normed_grad * unit, axis=0, keepdims=True)
    shift_out_ref[...] = jnp.sum(normed_grad, axis=0, keepdims=True)
    unit_grad = normed_grad * gain_ref[...]
    attended_grad = spread * (
        unit_grad
        - jnp.mean(unit_grad, axis=1, keepdims=True)
        - unit * jnp.mean(unit_grad * unit, axis=1, keepdims=True)
    )
    centre = jnp.sum(attended_grad * attended, axis=1, keepdims=True) / total
    numer_grad = low(attended_grad / total)
    tile = column_tile([top, centre], (own, TILE))
    for place in range(count):
        message_ref[place, :, :channels] = numer_grad
        message_ref[place, :, channels:] = tile


def attend_back(places_ref, arrived_ref, scores_ref, keys_ref, values_ref, part_ref, score_grad_ref, weights_ref):
    channels = keys_ref.shape[1]
    top = from_tile(arrived_ref[:, channels:], 0)
    centre = from_tile(arrived_ref[:, channels:], 1)
    weights = jnp.exp(scores_ref[...] - top)
    weights_ref[...] = low(weights)
    prob_grad = dot_nt(arrived_ref[:, :channels], values_ref[...])
    score_grad = low(weights * (prob_grad - centre) * (channels ** (-0.5)))
    score_grad_ref[...] = score_grad
    part_ref[...] = low(product(score_grad, keys_ref[...]))


def half_of(place_ref, bit):
    return jnp.where(place_ref[3] == bit, 1, 0)


def fold(value):
    return jnp.sum(value.reshape(value.shape[0] // 8, 8, value.shape[1]), axis=0)


def region_back(
    places_ref, arrived_ref, joined_grad_ref, w_query_ref, w_reduce_ref, query_grad_ref, reduced_grad_ref, regions_grad_ref
):
    features = regions_grad_ref.shape[1]
    query_grad = low(jnp.sum(wide(arrived_ref[...]), axis=0))
    query_grad_ref[...] = query_grad
    reduced_grad = low(joined_grad_ref[:, features:] + dot_nt(query_grad, w_query_ref[...]))
    reduced_grad_ref[...] = reduced_grad
    regions_grad_ref[...] = low(joined_grad_ref[:, :features] + dot_nt(reduced_grad, w_reduce_ref[...]))


def hand_out(buffer, send_ref, keep_ref, sems):
    copies = [
        pltpu.make_async_copy(buffer.at[number], target, sems.at[number])
        for number, target in enumerate((send_ref, keep_ref))
    ]
    for copy in copies:
        copy.start()
    for copy in copies:
        copy.wait()


def store_rows(buffer, place_ref, value, first, rows):
    at, end = first, first + value.shape[0]
    while at < end:
        block, offset = divmod(at, rows)
        count = min(rows - offset, end - at)
        buffer[half_of(place_ref, block % 2), block // 2, offset : offset + count] = value[at - first : at - first + count]
        at += count


def slope_back(upstream_ref, pre_ref, scale_ref, shift_ref, out_ref, scale_out_ref, shift_out_ref):
    sites, channels = pre_ref.shape

    def one(step, sums):
        rows = pl.ds(pl.multiple_of(step * 64, 64), 64)
        pre = pre_ref[rows]
        grad = upstream_ref[rows] * gelu_slope(pre * scale_ref[...] + shift_ref[...])
        out_ref[rows] = low(grad * scale_ref[...]).astype(out_ref.dtype)
        return sums[0] + fold(grad * pre), sums[1] + fold(grad)

    zero = jnp.zeros((8, channels), jnp.float32)
    scale_sum, shift_sum = lax.fori_loop(0, sites // 64, one, (zero, zero))
    scale_out_ref[...] = jnp.sum(scale_sum, axis=0, keepdims=True)
    shift_out_ref[...] = jnp.sum(shift_sum, axis=0, keepdims=True)


def later_back(
    groups_a, groups_b, place_ref, regions_grad_ref, pool_ref, scale_ref, shift_ref, scales_ref, pre_c_ref, fm_ref, act_b_ref,
    pre_b_ref, act_a_ref, pre_a_ref, packed_ref,
    send_ref, keep_ref, lin_c_grad_ref, pre_a_grad_ref, scale_c_out_ref, shift_c_out_ref, scale_b_out_ref, shift_b_out_ref,
    scale_a_out_ref, shift_a_out_ref,
    weight_b, weight_c, buffer, out_grad, pre_grad, turned, act_grad, wide_grad,
    held_pre_c, held_map, held_act_b, held_pre_b, held_act_a, held_pre_a, held_lin, sems_b, sems_c, out_sems, sems,
):
    sites, features = held_map.shape
    channels = held_act_b.shape[1]
    chunks, blocks = weight_c.shape[0], weight_c.shape[1]
    rows_b = groups_b * LANE_ROWS

    def part_of(source, target, number, sem):
        columns = pl.ds(pl.multiple_of(number * channels, channels), channels)
        return pltpu.make_async_copy(source.at[:, columns], target.at[:, columns], sems.at[sem + number])

    early = start_all([pltpu.make_async_copy(act_b_ref, held_act_b, sems.at[0])])
    copies_c = start_all(fetch_columns(packed_ref, weight_c, sems_c, groups_a + groups_b, chunks))
    for number in range(chunks):
        part_of(pre_c_ref, held_pre_c, number, 4).start()
        part_of(fm_ref, held_map, number, 4 + chunks).start()
    late = start_all(
        [
            pltpu.make_async_copy(pre_b_ref, held_pre_b, sems.at[1]),
            pltpu.make_async_copy(act_a_ref, held_act_a, sems.at[2]),
            pltpu.make_async_copy(pre_a_ref, held_pre_a, sems.at[3]),
        ]
    )
    copies_b = start_all(fetch(packed_ref, weight_b, sems_b, groups_a, groups_b))
    scale_b_ref, shift_b_ref, scale_a_ref, shift_a_ref = [scales_ref.at[pl.ds(number, 1)] for number in range(4)]
    act_grad[...] = jnp.zeros_like(act_grad)
    wait_all(early)
    turned[...] = held_act_b[...].T
    wait_all(copies_c)

    def chunk(number, carry):
        columns = pl.ds(pl.multiple_of(number * channels, channels), channels)
        out_grad[...] = dot_tn(pool_ref[...], regions_grad_ref[:, columns])
        part_of(pre_c_ref, held_pre_c, number, 4).wait()
        part_of(fm_ref, held_map, number, 4 + chunks).wait()

        def one(step, sums):
            rows = pl.ds(pl.multiple_of(step * 64, 64), 64)
            pre = held_pre_c[rows, columns]
            scale = scale_ref[:, columns]
            linear = wide(held_map[rows, columns]) + pre * scale + shift_ref[:, columns]
            grad = out_grad[rows] * gelu_slope(linear)
            held_lin[rows, columns] = low(grad)
            pre_grad[rows] = low(grad * scale)
            return sums[0] + fold(grad * pre), sums[1] + fold(grad)

        zero = jnp.zeros((8, channels), jnp.float32)
        scale_sum, shift_sum = lax.fori_loop(0, sites // 64, one, (zero, zero))
        part_of(held_lin, lin_c_grad_ref, number, 4 + 2 * chunks).start()
        scale_c_out_ref[:, columns] = jnp.sum(scale_sum, axis=0, keepdims=True)
        shift_c_out_ref[:, columns] = jnp.sum(shift_sum, axis=0, keepdims=True)
        part = low(product(turned[...], pre_grad[...])).reshape(blocks // 2, 2, LANE_ROWS, channels)
        rows = pl.ds(pl.multiple_of(rows_b + number * LANE_ROWS, LANE_ROWS), LANE_ROWS)
        for bit in range(2):
            buffer[half_of(place_ref, bit), :, rows] = part[:, bit]
        act_grad[...] += dot_nt(pre_grad[...], weight_c[number].reshape(channels, channels))
        return carry

    lax.fori_loop(0, chunks, chunk, 0)
    wait_all(late)
    slope_back(act_grad, held_pre_b, scale_b_ref, shift_b_ref, wide_grad, scale_b_out_ref, shift_b_out_ref)
    turned[...] = held_act_a[...].T
    wait_all(copies_b)
    for slide in (-1, 0, 1):
        slid = in_columns(wide_grad[...], -slide)
        for number, place in enumerate(places):
            if place[1] != slide:
                continue
            moved = low(in_rows(slid, -place[0]))
            store_rows(buffer, place_ref, low(product(turned[...], moved)), number * channels, rows_b)
            begin = number * channels // LANE_ROWS
            tap = weight_b[begin : begin + channels // LANE_ROWS].reshape(channels, channels)
            part = dot_nt(moved, tap)
            if slide == -1 and place[0] == -1:
                act_grad[...] = part
            else:
                act_grad[...] += part
    slope_back(act_grad, held_pre_a, scale_a_ref, shift_a_ref, pre_a_grad_ref, scale_a_out_ref, shift_a_out_ref)
    hand_out(buffer, send_ref, keep_ref, out_sems)
    for number in range(chunks):
        part_of(held_lin, lin_c_grad_ref, number, 4 + 2 * chunks).wait()


def by_frames(grad, offset):
    if offset == 0:
        return grad
    sites, width = grad.shape
    tall = grad.reshape(sites // (FRAMES * SIDE * SIDE), FRAMES, SIDE * SIDE, width)
    edge = jnp.zeros_like(tall[:, :1])
    if offset > 0:
        tall = jnp.concatenate([edge, tall[:, :-1]], axis=1)
    else:
        tall = jnp.concatenate([tall[:, 1:], edge], axis=1)
    return tall.reshape(sites, width)


def first_back(place_ref, grad_ref, own_ref, got_ref, turned_ref, send_ref, keep_ref, sum_ref, buffer, held, sems, out_sems):
    features, sites = held.shape
    channels = grad_ref.shape[1]
    copies = [
        pltpu.make_async_copy(turned_ref.at[pl.ds(start, channels)], held.at[pl.ds(start, channels)], sems.at[start // channels])
        for start in range(0, features, channels)
    ]
    start_all(copies)
    sum_ref[...] = add_low(own_ref[...], got_ref[...])
    for tap in range(3):
        moved = by_frames(grad_ref[...], tap - 1)
        for start in range(0, features, channels):
            if tap == 0:
                copies[start // channels].wait()
            part = low(product(held[start : start + channels], moved))
            store_rows(buffer, place_ref, part, tap * features + start, buffer.shape[2])
    hand_out(buffer, send_ref, keep_ref, out_sems)


def map_back(places_ref, grad_ref, weight_ref, lin_c_grad_ref, out_ref, moved, held_lin, held_out, sems):
    sites, features = held_out.shape
    channels = grad_ref.shape[1]
    copies = start_all([pltpu.make_async_copy(lin_c_grad_ref, held_lin, sems.at[0])])
    for tap in range(3):
        moved[tap] = by_frames(grad_ref[...], tap - 1)
    wait_all(copies)
    groups = channels // LANE_ROWS

    def chunk(number, carry):
        columns = pl.ds(pl.multiple_of(number * channels, channels), channels)
        total = wide(held_lin[:, columns])
        for tap in range(3):
            rows = pl.ds(tap * (features // LANE_ROWS) + number * groups, groups)
            total = total + dot_nt(moved[tap], weight_ref[rows].reshape(channels, channels))
        held_out[:, columns] = low(total)
        pltpu.make_async_copy(held_out.at[:, columns], out_ref.at[:, columns], sems.at[1 + number]).start()
        return carry

    lax.fori_loop(0, features // channels, chunk, 0)
    copies = []
    for number in range(features // channels):
        columns = pl.ds(number * channels, channels)
        copies.append(pltpu.make_async_copy(held_out.at[:, columns], out_ref.at[:, columns], sems.at[1 + number]))
    wait_all(copies)


COST = 6e9
WINDOW = 0.1
F32 = jnp.float32
BF16 = jnp.bfloat16
ANY = pl.BlockSpec(memory_space=pl.ANY)
SCALAR = pl.BlockSpec(memory_space=pltpu.SMEM)
HELD = pl.BlockSpec(memory_space=pltpu.VMEM)


def shape_of(dims, kind):
    return jax.ShapeDtypeStruct(dims, kind)


def add_low(left, right):
    return low(wide(left) + wide(right))


class Blocks:
    def __init__(self, ref, first, dims, rows):
        self.ref, self.first, self.dims, self.rows = ref, first, dims, rows

    def span(self, index):
        index = index if isinstance(index, tuple) else (index,)
        flat = 0
        for place, size in zip(index, self.dims):
            flat = flat * size + place
        return pl.ds(pl.multiple_of(self.first + flat * self.rows, LANE_ROWS), self.rows)

    def __getitem__(self, index):
        return self.ref[self.span(index)]

    def __setitem__(self, index, value):
        self.ref[self.span(index)] = value


def after_last(places_ref, keep_ref, got_ref, keep_one, send_one, keep_two, send_two):
    half = keep_ref.shape[0] // 2
    across, inner = places_ref[0], places_ref[1]

    def one(number, carry):
        for place in range(2):
            keep_one[number, place] = add_low(keep_ref[number, place, across], got_ref[number, place, across])
            send_one[number, place] = add_low(keep_ref[number, place, 1 - across], got_ref[number, place, 1 - across])
            later = number + half
            keep_two[number, place] = add_low(keep_ref[later, inner, place], got_ref[later, inner, place])
            send_two[number, place] = add_low(keep_ref[later, 1 - inner, place], got_ref[later, 1 - inner, place])
        return carry

    lax.fori_loop(0, half, one, 0)


def after_cross(places_ref, keep_one, got_one, keep_two, got_two, kept_one, send_one, kept_two, send_two):
    across, inner = places_ref[0], places_ref[1]

    def one(number, carry):
        kept_one[number] = add_low(keep_one[number, inner], got_one[number, inner])
        send_one[number] = add_low(keep_one[number, 1 - inner], got_one[number, 1 - inner])
        kept_two[number] = add_low(keep_two[number, across], got_two[number, across])
        send_two[number] = add_low(keep_two[number, 1 - across], got_two[number, 1 - across])
        return carry

    lax.fori_loop(0, keep_two.shape[0], one, 0)


def after_plane(places_ref, keep_one, got_one, keep_two, got_two, kept_ref, sends):
    half = keep_one.shape[0]
    outer = places_ref[2]

    def block(place, target):
        @pl.when(place < half)
        def _():
            target[...] = add_low(keep_one[lax.rem(place, half)], got_one[lax.rem(place, half)])

        @pl.when(place >= half)
        def _():
            target[...] = add_low(keep_two[lax.rem(place, half)], got_two[lax.rem(place, half)])

    block(outer, kept_ref)
    for step, target in enumerate(sends):
        block(outer ^ (step + 1), target)


def total_of(refs):
    total = wide(refs[0][...])
    for ref in refs[1:]:
        total = total + wide(ref[...])
    return total


def round_two(
    places_ref, keep_one, got_one, keep_two, got_two, keep_a, got_a,
    kept_one, kept_two, keep_a_one, keep_a_two, across_ref, inner_ref,
):
    half, rows = kept_one.shape[:2]
    rows_a = keep_a_one.shape[2]
    below = 2 * half * rows_a
    after_last(
        places_ref, keep_a, got_a, keep_a_one, Blocks(across_ref, 0, (half, 2), rows_a), keep_a_two,
        Blocks(inner_ref, 0, (half, 2), rows_a),
    )
    after_cross(
        places_ref, keep_one, got_one, keep_two, got_two, kept_one, Blocks(inner_ref, below, (half,), rows), kept_two,
        Blocks(across_ref, below, (half,), rows),
    )


def bank_spans(lines, width, channels):
    groups = channels // width
    step = -(-lines // (groups * LANE_ROWS)) * LANE_ROWS
    return [(first, min(first + step, lines)) for first in range(0, lines, step)], step


def store_narrow(target, first, value, channels):
    lines, width = value.shape
    spans, step = bank_spans(lines, width, channels)
    target[first : first + step] = jnp.zeros((step, channels), BF16)
    for number, (begin, end) in enumerate(spans):
        target[first : first + end - begin, number * width : (number + 1) * width] = value[begin:end]


def load_narrow(value, first, lines, width):
    spans, _ = bank_spans(lines, width, value.shape[1])
    pieces = [
        value[first : first + end - begin, number * width : (number + 1) * width]
        for number, (begin, end) in enumerate(spans)
    ]
    return jnp.concatenate(pieces, axis=0)


def round_three(count, split, places_ref, kept_one, kept_two, keep_a_one, keep_a_two, got_across, got_inner, *refs):
    bank_refs, refs = (refs[:count], refs[count:]) if split else (refs[:1], refs[1:])
    kept_ref, sends, refs = refs[0], refs[1 : count], refs[count:]
    kept_a_one, kept_a_two, bank_keep_ref, across_ref, inner_ref = refs
    half, rows, channels = kept_one.shape
    rows_a = keep_a_one.shape[2]
    below = 2 * half * rows_a
    after_plane(
        places_ref, kept_one, Blocks(got_inner, below, (half,), rows), kept_two, Blocks(got_across, below, (half,), rows),
        kept_ref, sends,
    )
    after_cross(
        places_ref, keep_a_one, Blocks(got_across, 0, (half, 2), rows_a), keep_a_two,
        Blocks(got_inner, 0, (half, 2), rows_a), kept_a_one, Blocks(inner_ref, 0, (half,), rows_a), kept_a_two,
        Blocks(across_ref, 0, (half,), rows_a),
    )
    inner = places_ref[7] if split else 0
    keep = total_of([ref.at[inner] for ref in bank_refs])
    store_narrow(bank_keep_ref, 0, low(keep), channels)
    if split:
        send = total_of([ref.at[1 - inner] for ref in bank_refs])
        store_narrow(inner_ref, half * rows_a, low(send), channels)
    else:
        inner_ref[half * rows_a :] = bank_keep_ref[...]


def round_four(count, split, places_ref, *refs):
    plane_refs, refs = refs[:count], refs[count:]
    kept_a_one, kept_a_two, bank_keep_ref, got_across, got_inner = refs[:5]
    region_refs, refs = (refs[5:7], refs[7:]) if split else (refs[5:6], refs[6:])
    done_ref, region_ref, kept_a_ref, *sends = refs
    half, rows_a, channels = kept_a_one.shape
    rows = plane_refs[0].shape[0]
    below = half * rows_a
    after_plane(
        places_ref, kept_a_one, Blocks(got_inner, 0, (half,), rows_a), kept_a_two,
        Blocks(got_across, 0, (half,), rows_a), kept_a_ref, sends,
    )
    done_ref[:rows] = low(total_of(plane_refs))
    done_ref[rows:] = add_low(bank_keep_ref[...], got_inner[below:]) if split else bank_keep_ref[...]
    region_ref[...] = low(total_of(region_refs))


def round_last(count, split, widths, places_ref, *refs):
    outer_refs, refs = refs[:count], refs[count:]
    region_refs, refs = (refs[:2], refs[2:]) if split else (refs[:1], refs[1:])
    done_refs, refs = (refs[:2], refs[2:]) if split else ((), refs)
    part_ref, reduce_ref, query_ref, out_ref, head_ref, *both = refs
    part_ref[...] = low(total_of(outer_refs))
    region = total_of(region_refs)
    _, _, feature_rows, channel_rows, _, joined_rows = widths
    reduce_ref[...] = region[:feature_rows]
    query_ref[...] = region[feature_rows : feature_rows + channel_rows]
    out_ref[...] = region[feature_rows + channel_rows : feature_rows + 2 * channel_rows]
    head = load_narrow(region, feature_rows + 2 * channel_rows, joined_rows, TILE)
    head_ref[...] = head[:, : head_ref.shape[1]]
    for number, ref in enumerate(done_refs):
        both[0][number] = ref[...]


def sum_swap(places_ref, *refs):
    refs[-1][...] = low(total_of(refs[:-1]))


def region_pack(
    places_ref, regions_ref, reduced_ref, hidden_ref, query_grad_ref, reduced_grad_ref, w_out_ref, w_head_ref,
    logits_ref, message_ref,
):
    count = message_ref.shape[0]
    channels = reduced_ref.shape[1]
    reduced = reduced_ref[...]
    merged = low(reduced + product(hidden_ref[...], w_out_ref[...]))
    joined = jnp.concatenate([regions_ref[...], merged], axis=1)
    logits_ref[...] = low(product(joined, w_head_ref[...]))[:, : logits_ref.shape[1]]
    reduced_low = low(reduced)
    parts = [regions_ref[...], reduced_low, hidden_ref[...], joined]
    shared = [reduced_grad_ref[...], query_grad_ref[...]]
    for place in range(count):
        pieces = list(shared)
        for part in parts:
            width = part.shape[1] // count
            pieces.append(part[:, place * width : (place + 1) * width])
        spare = message_ref.shape[2] - sum(piece.shape[1] for piece in pieces)
        if spare:
            pieces.append(jnp.zeros((reduced.shape[0], spare), BF16))
        message_ref[place] = jnp.concatenate(pieces, axis=1)


def key_value_parts(places_ref, score_grad_ref, queries_ref, weights_ref, arrived_ref, out_ref):
    keys_here = score_grad_ref.shape[1]
    out_ref[:keys_here] = low(dot_tn(score_grad_ref[...], queries_ref[...]))
    out_ref[keys_here:] = low(dot_tn(weights_ref[...], arrived_ref[:, : queries_ref.shape[1]]))


def region_sums(widths, places_ref, group_ref, branch_grad_ref, logit_grad_ref, out_ref):
    ends, start = [], 0
    for width in widths:
        ends.append((start, start + width))
        start += width
    reduced_grad, query_grad, regions, reduced, hidden, joined = [group_ref[:, begin:end] for begin, end in ends]
    first, second = widths[2], widths[2] + widths[3]
    third = second + widths[4]
    channels = reduced_grad.shape[1]
    out_ref[:first] = low(dot_tn(regions, reduced_grad))
    out_ref[first:second] = low(dot_tn(reduced, query_grad))
    out_ref[second:third] = low(dot_tn(hidden, branch_grad_ref[...]))
    head = low(dot_tn(joined, logit_grad_ref[...]))
    store_narrow(out_ref, third, head, channels)


def bank_back(
    places_ref, sums_ref, w_key_ref, w_value_ref, w_bank_ref, turned_bank_ref, turned_memory_ref, *refs
):
    vectors, bank_grad_ref, outs, (message_ref, grads) = refs[:8], refs[8], refs[9:-2], refs[-2:]
    keys_here, features = bank_grad_ref.shape
    channels = sums_ref.shape[1]
    count, _, width = message_ref.shape
    key_low, value_low = sums_ref[:keys_here], sums_ref[keys_here:]
    memory_grad = low(dot_nt(key_low, w_key_ref[...]) + dot_nt(value_low, w_value_ref[...]))
    for start in range(0, features, channels):
        bank_grad_ref[:, start : start + channels] = low(dot_nt(memory_grad, w_bank_ref[start : start + channels]))
    grads[:keys_here] = memory_grad
    grads[keys_here : 2 * keys_here] = key_low
    grads[2 * keys_here :] = value_low

    def columns(rows):
        if width % TILE == 0:
            return grads[rows, pl.ds(pl.multiple_of(places_ref[4] * width, width), width)]
        picked = grads[rows, :width]
        for number in range(1, channels // width):
            picked = jnp.where(places_ref[4] == number, grads[rows, number * width : (number + 1) * width], picked)
        return picked

    feature_rows, channel_rows = features // count, channels // count
    part = low(product(turned_bank_ref[...], columns(pl.ds(0, keys_here))))
    message_ref[:, :feature_rows] = part.reshape(count, feature_rows, width)
    at = feature_rows
    for number in (1, 2):
        part = low(product(turned_memory_ref[...], columns(pl.ds(number * keys_here, keys_here))))
        message_ref[:, at : at + channel_rows] = part.reshape(count, channel_rows, width)
        at += channel_rows
    spare = message_ref.shape[1] - at
    for place in range(count):
        row = []
        for vector_ref in vectors:
            share = vector_ref.shape[1] // count
            row.append(vector_ref[:, place * share : (place + 1) * share])
        total = sum(piece.shape[1] for piece in row)
        lines = -(-total // width)
        if lines * width > total:
            row.append(jnp.zeros((1, lines * width - total), F32))
        row = jnp.concatenate(row, axis=1)
        tile = [row[:, line * width : (line + 1) * width] for line in range(lines)]
        tile.append(jnp.zeros((spare - lines, width), F32))
        message_ref[place, at:] = low(jnp.concatenate(tile, axis=0))
    inner = outs[0].shape[0]
    for step, out_ref in enumerate(outs):
        out_ref[...] = message_ref[pl.ds((places_ref[6] ^ step) * inner, inner)]


def finish(shape_info, places_ref, part_ref, *refs):
    rows_b, rows_c, feature_rows, channel_rows, lines, split = shape_info
    if split:
        own_ref, got_ref, refs = refs[0], refs[1], refs[2:]
        weight_refs = [own_ref.at[0], got_ref.at[0], own_ref.at[1], got_ref.at[1]]
        bank_refs, first = weight_refs, rows_b + rows_c
    else:
        weight_refs, bank_refs, refs, first = refs[:1], refs[1:-14], refs[-14:], 0
    conv_a_ref, conv_b_ref, conv_c_ref, bank_out_ref, key_ref, value_ref = refs[:6]
    vectors = refs[6:]
    conv_a_ref[...] = wide(part_ref[...]).reshape(conv_a_ref.shape)
    channels = weight_refs[0].shape[1]
    width = channels // len(bank_refs)

    def spot(number, size):
        if not split:
            return pl.ds(number * size, size)
        return pl.ds(pl.multiple_of((places_ref[4] ^ number) * size, size), size)

    for number, ref in enumerate(weight_refs):
        conv_b_ref[spot(number, rows_b)] = wide(ref[:rows_b])
        for chunk in range(rows_c // LANE_ROWS):
            begin = rows_b + chunk * LANE_ROWS
            conv_c_ref[spot(number, LANE_ROWS), chunk * channels : (chunk + 1) * channels] = wide(
                ref[begin : begin + LANE_ROWS]
            )
    tile = None
    at = feature_rows + 2 * channel_rows
    for number, ref in enumerate(bank_refs):
        bank = wide(load_narrow(ref, first, lines, width))
        columns = spot(number, width)
        bank_out_ref[:, columns] = bank[:feature_rows]
        key_ref[:, columns] = bank[feature_rows : feature_rows + channel_rows]
        value_ref[:, columns] = bank[feature_rows + channel_rows : at]
        tile = bank[at:] if tile is None else tile + bank[at:]
    total = sum(ref.shape[1] for ref in vectors)
    row = jnp.concatenate([tile[line : line + 1] for line in range(-(-total // width))], axis=1)
    at = 0
    for ref in vectors:
        ref[...] = row[:, at : at + ref.shape[1]]
        at += ref.shape[1]


def run_kernel(
    kernel, places, arrays, shapes, name, micros, scratch=(), raw_in=(), raw_out=(), fetched=(), limit=8
):
    count_in, count_out, fetched = len(arrays), len(shapes), list(fetched)

    def wrapped(*refs):
        places_ref, ins = refs[0], list(refs[1 : 1 + count_in])
        out_places, outs = refs[1 + count_in], list(refs[2 + count_in : 2 + count_in + count_out])
        extra = refs[2 + count_in + count_out :]
        if fetched:
            held, sems, extra = extra[: len(fetched)], extra[len(fetched)], extra[len(fetched) + 1 :]
            copies = start_all(
                [
                    pltpu.make_async_copy(ins[number], held[slot], sems.at[slot])
                    for slot, number in enumerate(fetched)
                ]
            )
        for number in range(places.shape[0]):
            out_places[number] = places_ref[number]
        if fetched:
            wait_all(copies)
            for slot, number in enumerate(fetched):
                ins[number] = held[slot]
        kernel(places_ref, *ins, *outs, *extra)

    outside = [*raw_in, *fetched]
    buffers = [pltpu.VMEM(arrays[number].shape, arrays[number].dtype) for number in fetched]
    if fetched:
        buffers.append(pltpu.SemaphoreType.DMA((len(fetched),)))
    return pl.pallas_call(
        wrapped,
        out_shape=[shape_of(places.shape, jnp.int32)] + list(shapes),
        in_specs=[SCALAR] + [ANY if number in outside else HELD for number in range(count_in)],
        out_specs=[SCALAR] + [ANY if number in raw_out else HELD for number in range(count_out)],
        scratch_shapes=buffers + list(scratch),
        compiler_params=params(limit),
        cost_estimate=pl.CostEstimate(
            flops=int(micros * COST), bytes_accessed=int(micros * COST / 1000), transcendentals=0
        ),
        name=name,
    )(places, *arrays)


def run_first_conv(feature_map, packed, scale, shift, groups):
    sites, channels = feature_map.shape[0], packed.shape[3]
    blocks = packed.shape[0]
    return pl.pallas_call(
        first_conv,
        out_shape=[
            jax.ShapeDtypeStruct((sites, channels), jnp.float32),
            jax.ShapeDtypeStruct((sites, channels), jnp.bfloat16),
            jax.ShapeDtypeStruct((blocks * groups, LANE_ROWS, channels), jnp.bfloat16),
        ],
        in_specs=[pl.BlockSpec(memory_space=pltpu.VMEM), pl.BlockSpec(memory_space=pl.ANY)] + [HELD] * 2,
        out_specs=[ANY, HELD, ANY],
        scratch_shapes=[
            pltpu.VMEM((blocks * groups, LANE_ROWS, channels), jnp.bfloat16),
            pltpu.VMEM((sites, channels), jnp.float32),
            pltpu.SemaphoreType.DMA((blocks,)),
            pltpu.SemaphoreType.DMA((2,)),
        ],
        compiler_params=params(52),
        cost_estimate=pl.CostEstimate(flops=int(6 * COST), bytes_accessed=int(6 * COST / 1000), transcendentals=0),
        name="first_conv",
    )(feature_map, packed, scale.reshape(1, -1), shift.reshape(1, -1))


def run_later_convs(
    act_a, feature_map, packed, scale_b, shift_b, scale_c, shift_c, pooling, w_reduce, w_query, groups_b, groups_c
):
    sites, channels = act_a.shape
    features = feature_map.shape[1]
    blocks = packed.shape[0]
    own = pooling.shape[0]
    group = lax.axis_size("bank")
    return pl.pallas_call(
        later_convs,
        out_shape=[
            jax.ShapeDtypeStruct((sites, channels), jnp.float32),
            jax.ShapeDtypeStruct((sites, channels), jnp.bfloat16),
            jax.ShapeDtypeStruct((sites, features), jnp.float32),
            jax.ShapeDtypeStruct((own, features), jnp.bfloat16),
            jax.ShapeDtypeStruct((own, channels), jnp.float32),
            jax.ShapeDtypeStruct((group, own, channels), jnp.bfloat16),
        ],
        in_specs=[HELD] + [ANY] * 2 + [HELD] * 5 + [ANY, HELD],
        out_specs=[ANY] * 3 + [HELD] * 3,
        scratch_shapes=[
            pltpu.VMEM((blocks * groups_b, LANE_ROWS, channels), jnp.bfloat16),
            pltpu.VMEM((groups_c, blocks, LANE_ROWS, channels), jnp.bfloat16),
            pltpu.VMEM((sites, channels), jnp.bfloat16),
            pltpu.VMEM((sites, features), jnp.bfloat16),
            pltpu.VMEM((sites, features), jnp.float32),
            pltpu.VMEM(w_reduce.shape, jnp.bfloat16),
            pltpu.VMEM((sites, channels), jnp.float32),
            pltpu.VMEM((sites, channels), jnp.bfloat16),
            pltpu.SemaphoreType.DMA((blocks,)),
            pltpu.SemaphoreType.DMA((blocks,)),
            pltpu.SemaphoreType.DMA((4 + groups_c,)),
        ],
        compiler_params=params(52),
        cost_estimate=pl.CostEstimate(flops=int(15 * COST), bytes_accessed=int(15 * COST / 1000), transcendentals=0),
        name="later_convs",
    )(
        act_a, feature_map, packed, scale_b.reshape(1, -1), shift_b.reshape(1, -1), scale_c.reshape(1, -1),
        shift_c.reshape(1, -1), pooling, w_reduce, w_query,
    )


def body(
    feature_map,
    bank,
    region_time,
    roi_index,
    roi_weight,
    conv_a,
    scale_a,
    shift_a,
    conv_b,
    scale_b,
    shift_b,
    conv_c,
    scale_c,
    shift_c,
    w_reduce,
    w_bank,
    w_query,
    w_key,
    w_value,
    ln_gain,
    ln_shift,
    w_out,
    w_head,
    logit_grad,
):
    site_count = feature_map.shape[0]
    feature_count = feature_map.shape[1]
    channels = w_query.shape[0]
    classes = w_head.shape[1]
    keys_here = bank.shape[0]
    own_count = roi_index.shape[0]
    bank_count = lax.axis_size("bank")
    bank_place = lax.axis_index("bank")
    dp_count = lax.axis_size("dp")
    dp_place = lax.axis_index("dp")
    first_row = bank_place * own_count
    half_span = keys_here * bank_count // 2
    group_rows = bank_count * own_count
    chunks = feature_count // channels
    shards = (conv_a, conv_b, conv_c)
    split = dp_count // 2 == 2 and all(shard.shape[0] % (LANE_ROWS * dp_count) == 0 for shard in shards)
    axes = block_axes(split, dp_count, bank_count)
    outer, inner, across, last = axes
    outer_count = outer.size if split else 1
    blocks = bank_count * dp_count if split else bank_count
    halves = tuple(axis.size for axis in axes[:3])
    places_here = jnp.stack([across.place(), inner.place(), outer.place(), last.place(), dp_place, bank_place * keys_here, outer.place() if split else 0 * bank_place, inner.place()])

    def own_part(shard):
        if not split:
            return shard
        rows = shard.shape[0] // dp_count
        return lax.dynamic_slice_in_dim(shard, dp_place * rows, rows, 0)

    part_a, part_b, part_c = [own_part(shard) for shard in shards]
    rows_a, rows_b, rows_c = part_a.shape[0], part_b.shape[0], part_c.shape[0]
    groups_a, groups_b, groups_c = rows_a // LANE_ROWS, rows_b // LANE_ROWS, chunks
    pieces_c = [part_c[:, chunk * channels : (chunk + 1) * channels] for chunk in range(chunks)]
    own_packed = jnp.concatenate([part_a, part_b] + pieces_c, 0).reshape(-1, LANE_ROWS, channels)
    packed = lax.all_gather(own_packed, ("bank", "dp") if split else "bank", axis=0, tiled=False)
    packed = packed.reshape((blocks,) + own_packed.shape)

    memory = product(bank, w_bank)
    memory_low = low(memory)
    keys = low(product(memory_low, w_key))
    values = low(product(memory_low, w_value))
    turned_map, turned_bank, turned_memory = feature_map.T, bank.T, memory_low.T
    matches = roi_index[:, :, None] == jnp.arange(site_count, dtype=jnp.int32)[None, None, :]
    pooling = low(jnp.sum(jnp.where(matches, wide(roi_weight)[:, :, None], 0.0), axis=1))
    own_logit_grad = lax.dynamic_slice_in_dim(logit_grad, first_row, own_count, 0)
    joined_grad = dot_nt(own_logit_grad, w_head)
    branch_grad = low(joined_grad[:, feature_count:])
    hidden_grad = dot_nt(branch_grad, w_out)
    group_branch_grad = low(dot_nt(logit_grad, w_head[feature_count:]))
    spare = ((0, 0), (0, TILE - classes))
    wide_head, wide_logit_grad = jnp.pad(w_head, spare), jnp.pad(logit_grad, spare)
    time_column = region_time.reshape(-1, 1)
    scales = jnp.stack([scale_b, shift_b, scale_a, shift_a])
    (
        packed, turned_bank, turned_memory, keys, values, turned_map, pooling, joined_grad, hidden_grad,
        group_branch_grad, wide_head, wide_logit_grad, time_column, scales, places_here,
    ) = lax.optimization_barrier(
        (
            packed, turned_bank, turned_memory, keys, values, turned_map, pooling, joined_grad, hidden_grad,
            group_branch_grad, wide_head, wide_logit_grad, time_column, scales, places_here,
        )
    )

    pre_a, act_a, weight_a = run_first_conv(feature_map, packed, scale_a, shift_a, groups_a)
    pre_b, act_b, pre_c, regions, reduced, own_queries = run_later_convs(
        act_a, feature_map, packed, scale_b, shift_b, scale_c, shift_c, pooling, w_reduce, w_query, groups_b, groups_c
    )
    queries = to_owners(own_queries).reshape(group_rows, channels)
    places, message, scores = run_kernel(
        functools.partial(attend, half_span),
        places_here,
        [queries, keys, values, time_column],
        [shape_of((group_rows, channels + TILE), BF16), shape_of((group_rows, keys_here), F32)],
        "attend",
        2,
    )
    arrived = to_owners(message.reshape(bank_count, own_count, channels + TILE))
    row = shape_of((1, channels), F32)
    places, message, hidden_low, gain_part, shift_part = run_kernel(
        merge_rows,
        places,
        [arrived, hidden_grad, ln_gain.reshape(1, -1), ln_shift.reshape(1, -1)],
        [shape_of(arrived.shape, BF16), shape_of((own_count, channels), BF16), row, row],
        "merge_rows",
        2,
    )
    arrived = to_owners(message).reshape(group_rows, channels + TILE)
    group_shape = shape_of((group_rows, channels), BF16)
    weight_shape = shape_of((group_rows, keys_here), BF16)
    places, query_part, score_grad, weights_low = run_kernel(
        attend_back,
        places,
        [arrived, scores, keys, values],
        [group_shape, weight_shape, weight_shape],
        "attend_back",
        2,
    )
    query_parts = to_owners(query_part.reshape(bank_count, own_count, channels))
    places, key_value = run_kernel(
        key_value_parts,
        places,
        [score_grad, queries, weights_low, arrived],
        [shape_of((2 * keys_here, channels), BF16)],
        "key_value_parts",
        3,
    )

    def dp_swap(value, step):
        return lax.ppermute(value, "dp", [(i, i ^ step) for i in range(dp_count)])

    key_value_got = dp_swap(key_value, 1)

    def summed_swap(places, own, got):
        places, own = run_kernel(
            sum_swap, places, [own, got], [shape_of(own.shape, BF16)], "sum_swap", 2
        )
        return places, own

    places, key_value = summed_swap(places, key_value, key_value_got)
    step = 2
    while step * 2 < dp_count:
        places, key_value = summed_swap(places, key_value, dp_swap(key_value, step))
        step *= 2
    key_value_got = dp_swap(key_value, step)
    own_shape = shape_of((own_count, channels), BF16)
    places, query_grad, reduced_grad, regions_grad = run_kernel(
        region_back,
        places,
        [query_parts, joined_grad, w_query, w_reduce],
        [own_shape, own_shape, shape_of((own_count, feature_count), BF16)],
        "region_back",
        3,
    )
    half_blocks = blocks // 2
    rows_bc = rows_b + groups_c * LANE_ROWS
    wide_row = shape_of((1, feature_count), F32)
    maps = (site_count, feature_count)
    inside = (site_count, channels)
    (
        places, send_bc, keep_bc, lin_c_grad, pre_a_grad,
        scale_c_part, shift_c_part, scale_b_part, shift_b_part, scale_a_part, shift_a_part,
    ) = run_kernel(
        functools.partial(later_back, groups_a, groups_b),
        places,
        [
            regions_grad, pooling, scale_c.reshape(1, -1), shift_c.reshape(1, -1),
            scales, pre_c, feature_map, act_b, pre_b, act_a, pre_a, packed,
        ],
        [shape_of((half_blocks, rows_bc, channels), BF16)] * 2
        + [shape_of(maps, BF16), shape_of(inside, BF16), wide_row, wide_row]
        + [row] * 4,
        "later_back",
        28,
        scratch=[
            pltpu.VMEM((blocks * groups_b, LANE_ROWS, channels), BF16),
            pltpu.VMEM((groups_c, blocks, LANE_ROWS, channels), BF16),
            pltpu.VMEM((2, half_blocks, rows_bc, channels), BF16),
            pltpu.VMEM(inside, F32),
            pltpu.VMEM(inside, BF16),
            pltpu.VMEM((channels, site_count), BF16),
            pltpu.VMEM(inside, F32),
            pltpu.VMEM(inside, F32),
            pltpu.VMEM(maps, F32),
            pltpu.VMEM(maps, BF16),
            pltpu.VMEM(inside, BF16),
            pltpu.VMEM(inside, F32),
            pltpu.VMEM(inside, BF16),
            pltpu.VMEM(inside, F32),
            pltpu.VMEM(maps, BF16),
            pltpu.SemaphoreType.DMA((blocks,)),
            pltpu.SemaphoreType.DMA((blocks,)),
            pltpu.SemaphoreType.DMA((2,)),
            pltpu.SemaphoreType.DMA((4 + 3 * chunks,)),
        ],
        raw_in=range(5, 12),
        raw_out=(0, 1, 2),
        limit=40,
    )
    got_bc = last.swap(send_bc, 1)

    def parted(value):
        return value.reshape(halves + value.shape[1:])

    places, send_a, keep_a, key_value = run_kernel(
        first_back,
        places,
        [pre_a_grad, key_value, key_value_got, turned_map],
        [shape_of((half_blocks, rows_a, channels), BF16)] * 2 + [shape_of(key_value.shape, BF16)],
        "first_back",
        6,
        scratch=[
            pltpu.VMEM((2, half_blocks, rows_a, channels), BF16),
            pltpu.VMEM(turned_map.shape, BF16),
            pltpu.SemaphoreType.DMA((chunks,)),
            pltpu.SemaphoreType.DMA((2,)),
        ],
        raw_in=(3,),
        raw_out=(0, 1),
        limit=20,
    )
    got_a = last.swap(send_a, 1)
    half = outer.size // 2
    plane_shape = (half, 2, rows_bc, channels)
    places, keep_one, send_one, keep_two, send_two = run_kernel(
        after_last, places, [parted(keep_bc), parted(got_bc)], [shape_of(plane_shape, BF16)] * 4, "round_one", 4
    )
    got_one, got_two = across.swap(send_one, 1), inner.swap(send_two, 1)
    places, map_grad = run_kernel(
        map_back,
        places,
        [pre_a_grad, weight_a, lin_c_grad],
        [shape_of(maps, BF16)],
        "map_back",
        WINDOW,
        scratch=[
            pltpu.VMEM((3,) + inside, BF16),
            pltpu.VMEM(maps, BF16),
            pltpu.VMEM(maps, BF16),
            pltpu.SemaphoreType.DMA((1 + chunks,)),
        ],
        raw_in=(2,),
        raw_out=(0,),
        limit=12,
    )
    block_bc, block_a = shape_of((half, rows_bc, channels), BF16), shape_of((half, 2, rows_a, channels), BF16)
    both = shape_of((half * (2 * rows_a + rows_bc), channels), BF16)
    places, kept_one, kept_two, keep_a_one, keep_a_two, send_across, send_inner = run_kernel(
        round_two,
        places,
        [keep_one, got_one, keep_two, got_two, parted(keep_a), parted(got_a)],
        [block_bc, block_bc, block_a, block_a, both, both],
        "round_two",
        5,
    )
    got_across, got_inner = across.swap(send_across, 1), inner.swap(send_inner, 1)
    feature_rows, channel_rows = feature_count // bank_count, channels // bank_count
    joined_rows = (feature_count + channels) // bank_count
    widths = (channels, channels, feature_rows, channel_rows, channel_rows, joined_rows)
    message_width = -(-sum(widths) // TILE) * TILE
    places, logits_out, message = run_kernel(
        region_pack,
        places,
        [regions, reduced, hidden_low, query_grad, reduced_grad, w_out, wide_head],
        [shape_of((own_count, classes), BF16), shape_of((bank_count, own_count, message_width), BF16)],
        "region_pack",
        WINDOW,
    )
    group = to_owners(message).reshape(group_rows, message_width)

    vectors = [
        gain_part, shift_part, scale_a_part, shift_a_part, scale_b_part, shift_b_part, scale_c_part, shift_c_part
    ]
    width = channels // dp_count
    lines = -(-sum(vector.shape[1] for vector in vectors) // (bank_count * width))
    lines = -(-lines // LANE_ROWS) * LANE_ROWS
    bank_lines = feature_rows + 2 * channel_rows + lines
    bank_step = bank_spans(bank_lines, width, channels)[1]
    region_lines = feature_rows + 2 * channel_rows + bank_spans(joined_rows, TILE, channels)[1]
    places, bank_grad, *bank_pieces = run_kernel(
        bank_back,
        places,
        [key_value, w_key, w_value, w_bank, turned_bank, turned_memory] + vectors,
        [shape_of(bank.shape, BF16)]
        + [shape_of((bank_count // outer_count, bank_lines, width), BF16)] * outer_count,
        "bank_back",
        WINDOW,
        scratch=[
            pltpu.VMEM((bank_count, bank_lines, width), BF16),
            pltpu.VMEM((3 * keys_here, channels), BF16),
        ],
        limit=8,
    )
    if split:
        bank_parts = [bank_pieces[0]] + [outer.swap(piece, step + 1) for step, piece in enumerate(bank_pieces[1:])]
    else:
        bank_parts = [low(jnp.sum(wide(to_owners(bank_pieces[0])), axis=0, keepdims=True))]
    one_bc, half_a = shape_of((rows_bc, channels), BF16), shape_of((half, rows_a, channels), BF16)
    results = run_kernel(
        functools.partial(round_three, outer.size, split),
        places,
        [kept_one, kept_two, keep_a_one, keep_a_two, got_across, got_inner] + bank_parts,
        [one_bc] * outer.size
        + [half_a, half_a, shape_of((bank_step, channels), BF16)]
        + [
            shape_of((half * rows_a, channels), BF16),
            shape_of((half * rows_a + bank_step, channels), BF16),
        ],
        "round_three",
        5,
    )
    places, pieces_bc = results[0], results[1 : 1 + outer.size]
    kept_a_one, kept_a_two, bank_keep, send_across, send_inner = results[1 + outer.size :]
    got_across, got_inner = across.swap(send_across, 1), inner.swap(send_inner, 1)
    got_bc = [outer.swap(piece, step + 1) for step, piece in enumerate(pieces_bc[1:])]
    places, region_parts = run_kernel(
        functools.partial(region_sums, widths),
        places,
        [group, group_branch_grad, wide_logit_grad],
        [shape_of((region_lines, channels), BF16)],
        "region_sums",
        WINDOW,
    )
    region_both = [region_parts, dp_swap(region_parts, 1)] if split else [lax.psum(region_parts, "dp")]
    results = run_kernel(
        functools.partial(round_four, outer.size, split),
        places,
        [pieces_bc[0], *got_bc, kept_a_one, kept_a_two, bank_keep, got_across, got_inner, *region_both],
        [shape_of((rows_bc + bank_step, channels), BF16), shape_of(region_parts.shape, BF16)]
        + [shape_of((rows_a, channels), BF16)] * outer.size,
        "round_four",
        4,
    )
    places, done, region_parts, kept_a, *pieces_a = results
    got_a = [outer.swap(piece, step + 1) for step, piece in enumerate(pieces_a)]
    region_both = [region_parts, across.swap(region_parts, 1)] if split else [region_parts]
    done_both = [done, across.swap(done, 1)] if split else []
    row_block = shape_of((channel_rows, channels), F32)
    results = run_kernel(
        functools.partial(round_last, outer.size, split, widths),
        places,
        [kept_a, *got_a, *region_both, *done_both],
        [shape_of((rows_a, channels), BF16), shape_of((feature_rows, channels), F32), row_block, row_block]
        + [shape_of((joined_rows, classes), F32)]
        + [shape_of((2,) + done.shape, BF16)] * len(done_both[1:]),
        "round_last",
        2,
    )
    places, part_a, reduce_weight_grad, query_weight_grad, out_weight_grad, head_weight_grad = results[:6]
    if split:
        done_a = lax.all_gather(part_a, "dp", axis=0, tiled=False)
        done_all = [results[6], last.swap(results[6], 1)]
    else:
        done_a = lax.psum(part_a, "dp")
        bank_all = lax.all_gather(done[rows_bc:], "dp", axis=0, tiled=False)
        done_all = [lax.psum(done[:rows_bc], "dp")] + [bank_all[place] for place in range(dp_count)]
    info = (rows_b, groups_c * LANE_ROWS, feature_rows, channel_rows, bank_lines, split)
    results = run_kernel(
        functools.partial(finish, info),
        places,
        [done_a, *done_all],
        [shape_of(conv_a.shape, F32), shape_of(conv_b.shape, F32), shape_of(conv_c.shape, F32)]
        + [shape_of((feature_rows, channels), F32), row_block, row_block]
        + [shape_of((1, vector.shape[1] // bank_count), F32) for vector in vectors],
        "finish",
        3,
    )
    places, conv_a_grad, conv_b_grad, conv_c_grad, bank_weight_grad, key_weight_grad, value_weight_grad = results[:7]
    small = [value.reshape(-1) for value in results[7:]]
    gain_grad, shift_grad = small[:2]
    scale_a_grad, shift_a_grad, scale_b_grad, shift_b_grad, scale_c_grad, shift_c_grad = small[2:]
    return (
        logits_out,
        map_grad,
        bank_grad,
        conv_a_grad,
        scale_a_grad,
        shift_a_grad,
        conv_b_grad,
        scale_b_grad,
        shift_b_grad,
        conv_c_grad,
        scale_c_grad,
        shift_c_grad,
        reduce_weight_grad,
        bank_weight_grad,
        query_weight_grad,
        key_weight_grad,
        value_weight_grad,
        gain_grad,
        shift_grad,
        out_weight_grad,
        head_weight_grad,
    )


def solution(mesh):
    in_specs = (
        P(("dp", "bank"), None),
        P("bank", None),
        P("dp"),
        P(("dp", "bank"), None),
        P(("dp", "bank"), None),
        P("bank", None),
        P(),
        P(),
        P("bank", None),
        P(),
        P(),
        P("bank", None),
        P(),
        P(),
        P(),
        P(),
        P(),
        P(),
        P(),
        P(),
        P(),
        P(),
        P(),
        P("dp", None),
    )
    out_specs = (
        P(("dp", "bank"), None),
        P(("dp", "bank"), None),
        P("bank", None),
        P("bank", None),
        P("bank"),
        P("bank"),
        P("bank", None),
        P("bank"),
        P("bank"),
        P("bank", None),
        P("bank"),
        P("bank"),
        P("bank", None),
        P("bank", None),
        P("bank", None),
        P("bank", None),
        P("bank", None),
        P("bank"),
        P("bank"),
        P("bank", None),
        P("bank", None),
    )
    return jax.shard_map(body, mesh=mesh, in_specs=in_specs, out_specs=out_specs, check_vma=False)
```

```python
import functools

import jax
import jax.numpy as jnp
from jax import lax
from jax.experimental import pallas as pl
from jax.experimental.pallas import tpu as pltpu
from jax.sharding import PartitionSpec as P

FRAMES = 4
SIDE = 8
LANE_ROWS = 16
TILE = 128
ROOT = 0.7978845608028654
CUBIC = 0.044715

epsilon = 1e-05
masked_score = -1e30
places = [(-1, -1), (-1, 0), (-1, 1), (0, -1), (0, 0), (0, 1), (1, -1), (1, 0), (1, 1)]


def product(left, right):
    return jnp.dot(left, right, preferred_element_type=jnp.float32)


def low(value):
    return value.astype(jnp.bfloat16)


def wide(value):
    return value.astype(jnp.float32)


class SubAxis:
    def __init__(self, name, size, stride):
        self.name, self.size, self.stride = name, size, stride

    def place(self):
        return lax.rem(lax.axis_index(self.name) // self.stride, self.size)

    def swap(self, value, step):
        count = lax.axis_size(self.name)
        pairs = [(i, i ^ (step * self.stride)) for i in range(count)]
        return lax.ppermute(value, self.name, pairs)


def block_axes(split, dp_count, bank_count):
    if split:
        return (
            SubAxis("bank", bank_count // 2, 2),
            SubAxis("bank", 2, 1),
            SubAxis("dp", dp_count // 2, 2),
            SubAxis("dp", 2, 1),
        )
    return (
        SubAxis("bank", bank_count // 8, 8),
        SubAxis("bank", 2, 4),
        SubAxis("bank", 2, 2),
        SubAxis("bank", 2, 1),
    )


def gather_blocks(own, axes, places, steps):
    outer, inner, across, last = axes
    blocks = [own] + [outer.swap(own, step) for step in range(1, outer.size)]
    places = steps[0](places)
    *blocks, places = lax.optimization_barrier((*blocks, places))
    blocks = jnp.stack(blocks)
    half = outer.size // 2
    first, second = blocks[:half], blocks[half:]
    got_first, got_second = across.swap(first, 1), inner.swap(second, 1)
    places = steps[1](places)
    first, got_first, second, got_second, places = lax.optimization_barrier((first, got_first, second, got_second, places))
    first, second = jnp.concatenate([first, got_first]), jnp.concatenate([second, got_second])
    got_first, got_second = inner.swap(first, 1), across.swap(second, 1)
    places = steps[2](places)
    first, got_first, second, got_second, places = lax.optimization_barrier((first, got_first, second, got_second, places))
    near = jnp.concatenate([first, got_first, second, got_second])
    return places, [near, last.swap(near, 1)]


def to_owners(value):
    return lax.all_to_all(value, "bank", split_axis=0, concat_axis=0, tiled=True)


def to_group(value):
    count = lax.axis_size("bank")
    return to_owners(jnp.broadcast_to(value[None], (count,) + value.shape))


def params(mib):
    return pltpu.CompilerParams(vmem_limit_bytes=mib * 1024 * 1024)


def gelu_of(x):
    return 0.5 * x * (1.0 + jnp.tanh(ROOT * (x + CUBIC * x * x * x)))


def gelu_slope(x):
    square = x * x
    bent = jnp.tanh(ROOT * x * (1.0 + CUBIC * square))
    return 0.5 * (1.0 + bent) + 0.5 * ROOT * x * (1.0 - bent * bent) * (1.0 + 3.0 * CUBIC * square)


def by_rows(count, step, work):
    def one(number, carry):
        work(pl.ds(pl.multiple_of(number * step, step), step))
        return carry

    lax.fori_loop(0, count // step, one, 0)


def dot_tn(left, right):
    return lax.dot_general(
        left, right, (((0,), (0,)), ((), ())), preferred_element_type=jnp.float32
    )


def dot_nt(left, right):
    return lax.dot_general(
        left, right, (((1,), (1,)), ((), ())), preferred_element_type=jnp.float32
    )


def in_rows(value, step):
    if step == 0:
        return value
    sites, width = value.shape
    tall = value.reshape(sites // (SIDE * SIDE), SIDE, SIDE, width)
    edge = jnp.zeros_like(tall[:, :1])
    if step > 0:
        tall = jnp.concatenate([tall[:, 1:], edge], axis=1)
    else:
        tall = jnp.concatenate([edge, tall[:, :-1]], axis=1)
    return tall.reshape(sites, width)


def in_columns(value, step):
    if step == 0:
        return value
    sites = value.shape[0]
    turned = pltpu.roll(value, (-step) % sites, 0)
    column = lax.broadcasted_iota(jnp.int32, value.shape, 0) % SIDE
    keep = column != (SIDE - 1 if step > 0 else 0)
    return jnp.where(keep, turned, 0.0)


def fetch(source, target, sems, first, groups):
    copies = []
    for block in range(source.shape[0]):
        copies.append(
            pltpu.make_async_copy(
                source.at[block, pl.ds(first, groups)],
                target.at[pl.ds(block * groups, groups)],
                sems.at[block],
            )
        )
    return copies


def fetch_columns(source, target, sems, first, groups):
    return [
        pltpu.make_async_copy(
            source.at[block, pl.ds(first, groups)], target.at[:, block], sems.at[block]
        )
        for block in range(source.shape[0])
    ]


def start_all(copies):
    for copy in copies:
        copy.start()
    return copies


def wait_all(copies):
    for copy in copies:
        copy.wait()


def gathered_spot(places_ref, number, far):
    second, rest = divmod(number, 8)
    high, low_bits = divmod(rest, 4)
    middle, step = divmod(low_bits, 2)
    across, inner = (high, middle) if second else (middle, high)
    outer = (places_ref[2] ^ (2 * second + step)) * 2 + (places_ref[1] ^ inner)
    return (outer * 2 + (places_ref[0] ^ across)) * 2 + (places_ref[3] ^ far)


def first_conv(places_ref, fm_ref, *refs):
    sources, refs = refs[:-9], refs[-9:]
    scale_ref, shift_ref, pre_out_ref, act_ref, weight_out_ref, weight, pre_ref, sems, out_sems = refs
    sites, features = fm_ref.shape
    channels = act_ref.shape[1]
    groups = sources[0].shape[1]
    copies = []
    for far, source in enumerate(sources):
        for number in range(source.shape[0]):
            block = gathered_spot(places_ref, number, far) if len(sources) > 1 else number
            target = weight.at[pl.ds(block * groups, groups)]
            copies.append(pltpu.make_async_copy(source.at[number], target, sems.at[len(copies)]))
    start_all(copies)
    clip = FRAMES * SIDE * SIDE
    frame = SIDE * SIDE
    wait_all(copies)
    out = start_all([pltpu.make_async_copy(weight, weight_out_ref, out_sems.at[1])])

    def tap(number):
        begin = number * features // LANE_ROWS
        return weight[begin : begin + features // LANE_ROWS].reshape(features, channels)

    before = tap(0)
    for start in range(0, sites, clip):
        pre_ref[start : start + frame] = jnp.zeros((frame, channels), jnp.float32)
        pre_ref[start + frame : start + clip] = product(fm_ref[start : start + clip - frame], before)
    pre_ref[...] += product(fm_ref[...], tap(1))
    after = tap(2)
    for start in range(0, sites, clip):
        pre_ref[start : start + clip - frame] += product(fm_ref[start + frame : start + clip], after)

    def finish(rows):
        act_ref[rows] = low(gelu_of(pre_ref[rows] * scale_ref[...] + shift_ref[...]))

    out += start_all([pltpu.make_async_copy(pre_ref, pre_out_ref, out_sems.at[0])])
    by_rows(sites, 128, finish)
    wait_all(out)


def later_convs(
    act_a_ref, fm_ref, packed_ref, scale_b_ref, shift_b_ref, scale_c_ref, shift_c_ref, pool_ref, w_reduce_ref, w_query_ref,
    pre_b_out_ref, act_b_out_ref, pre_c_ref, regions_out_ref, reduced_out_ref, queries_ref,
    weight_b, weight_c, out_low, held_map, held_pre, held_reduce, pre_b_ref, act_b_ref, regions_ref, reduced_ref, sems_b, sems_c, sems,
):
    sites, channels = act_a_ref.shape
    blocks = packed_ref.shape[0]
    groups_b = weight_b.shape[0] // blocks
    groups_c = weight_c.shape[0]
    groups_a = packed_ref.shape[1] - groups_b - groups_c
    copies_b = start_all(fetch(packed_ref, weight_b, sems_b, groups_a, groups_b))
    copies_c = start_all(fetch_columns(packed_ref, weight_c, sems_c, groups_a + groups_b, groups_c))
    others = start_all(
        [
            pltpu.make_async_copy(fm_ref, held_map, sems.at[0]),
            pltpu.make_async_copy(w_reduce_ref, held_reduce, sems.at[1]),
        ]
    )
    act_a = act_a_ref[...]
    block_rows = groups_b * LANE_ROWS
    sums = {-1: None, 0: None, 1: None}
    waited = 0
    for number, (rise, slide) in enumerate(places):
        while waited < len(copies_b) and waited * block_rows < (number + 1) * channels:
            copies_b[waited].wait()
            waited += 1
        begin = number * channels // LANE_ROWS
        tap = weight_b[begin : begin + channels // LANE_ROWS].reshape(channels, channels)
        part = in_rows(product(act_a, tap), rise)
        sums[slide] = part if sums[slide] is None else sums[slide] + part
    pre_b_ref[...] = sums[0] + in_columns(sums[1], 1) + in_columns(sums[-1], -1)

    outs = start_all([pltpu.make_async_copy(pre_b_ref, pre_b_out_ref, sems.at[2 + groups_c])])

    def finish(rows):
        act_b_ref[rows] = low(gelu_of(pre_b_ref[rows] * scale_b_ref[...] + shift_b_ref[...]))

    by_rows(sites, 128, finish)
    outs += start_all([pltpu.make_async_copy(act_b_ref, act_b_out_ref, sems.at[3 + groups_c])])
    wait_all(copies_c + others)
    reduced_ref[...] = jnp.zeros_like(reduced_ref)

    def chunk(number, carry):
        columns = pl.ds(pl.multiple_of(number * channels, channels), channels)
        held_pre[:, columns] = product(act_b_ref[...], weight_c[number].reshape(channels, channels))
        pltpu.make_async_copy(held_pre.at[:, columns], pre_c_ref.at[:, columns], sems.at[2 + number]).start()

        def finish_c(rows):
            linear = wide(held_map[rows, columns]) + held_pre[rows, columns] * scale_c_ref[:, columns] + shift_c_ref[:, columns]
            out_low[rows] = low(gelu_of(linear))

        by_rows(sites, 128, finish_c)
        part = low(product(pool_ref[...], out_low[...]))
        regions_ref[:, columns] = part
        reduced_ref[...] += product(part, held_reduce[columns])
        return carry

    lax.fori_loop(0, groups_c, chunk, 0)
    outs += start_all(
        [
            pltpu.make_async_copy(regions_ref, regions_out_ref, sems.at[4 + groups_c]),
            pltpu.make_async_copy(reduced_ref, reduced_out_ref, sems.at[5 + groups_c]),
        ]
    )
    queries = low(product(low(reduced_ref[...]), w_query_ref[...]))
    for place in range(queries_ref.shape[0]):
        queries_ref[place] = queries
    for number in range(groups_c):
        columns = pl.ds(number * channels, channels)
        outs.append(pltpu.make_async_copy(held_pre.at[:, columns], pre_c_ref.at[:, columns], sems.at[2 + number]))
    wait_all(outs)


def column_tile(columns, shape):
    lane = lax.broadcasted_iota(jnp.int32, shape, len(shape) - 1)
    tile = jnp.zeros(shape, jnp.float32)
    for number, column in enumerate(columns):
        rest = column
        for third in range(3):
            piece = wide(low(rest))
            tile = jnp.where(lane == 3 * number + third, piece, tile)
            rest = rest - piece
    return low(tile)


def from_tile(tile, number):
    lane = lax.broadcasted_iota(jnp.int32, tile.shape, tile.ndim - 1)
    picked = jnp.where((lane >= 3 * number) & (lane < 3 * number + 3), wide(tile), 0.0)
    return jnp.sum(picked, axis=-1, keepdims=True)


def attend(half_span, places_ref, queries_ref, keys_ref, values_ref, time_ref, message_ref, scores_ref):
    channels = queries_ref.shape[1]
    positions = places_ref[5] + lax.broadcasted_iota(jnp.int32, scores_ref.shape, 1)
    visible = jnp.abs(time_ref[...] - positions) <= half_span
    scores = dot_nt(queries_ref[...], keys_ref[...]) * (channels ** (-0.5))
    scores = jnp.where(visible, scores, masked_score)
    scores_ref[...] = scores
    top = jnp.max(scores, axis=1, keepdims=True)
    weights = jnp.exp(scores - top)
    total = jnp.sum(weights, axis=1, keepdims=True)
    message_ref[:, :channels] = low(product(low(weights), values_ref[...]))
    message_ref[:, channels:] = column_tile([top, total], (scores.shape[0], TILE))


def merge_rows(places_ref, arrived_ref, hidden_grad_ref, gain_ref, shift_ref, message_ref, hidden_ref, gain_out_ref, shift_out_ref):
    count, own, packed = arrived_ref.shape
    channels = hidden_grad_ref.shape[1]
    tops = from_tile(arrived_ref[:, :, channels:], 0)
    totals = from_tile(arrived_ref[:, :, channels:], 1)
    top = jnp.max(tops, axis=0)
    factors = jnp.exp(tops - top[None])
    total = jnp.sum(factors * totals, axis=0)
    numer = jnp.sum(factors * wide(arrived_ref[:, :, :channels]), axis=0)
    attended = numer / total
    centred = attended - jnp.mean(attended, axis=1, keepdims=True)
    spread = lax.rsqrt(jnp.mean(centred * centred, axis=1, keepdims=True) + epsilon)
    unit = centred * spread
    normed = unit * gain_ref[...] + shift_ref[...]
    hidden_ref[...] = low(gelu_of(normed))
    normed_grad = hidden_grad_ref[...] * gelu_slope(normed)
    gain_out_ref[...] = jnp.sum(normed_grad * unit, axis=0, keepdims=True)
    shift_out_ref[...] = jnp.sum(normed_grad, axis=0, keepdims=True)
    unit_grad = normed_grad * gain_ref[...]
    attended_grad = spread * (
        unit_grad
        - jnp.mean(unit_grad, axis=1, keepdims=True)
        - unit * jnp.mean(unit_grad * unit, axis=1, keepdims=True)
    )
    centre = jnp.sum(attended_grad * attended, axis=1, keepdims=True) / total
    numer_grad = low(attended_grad / total)
    tile = column_tile([top, centre], (own, TILE))
    for place in range(count):
        message_ref[place, :, :channels] = numer_grad
        message_ref[place, :, channels:] = tile


def attend_back(places_ref, arrived_ref, scores_ref, keys_ref, values_ref, part_ref, score_grad_ref, weights_ref):
    channels = keys_ref.shape[1]
    top = from_tile(arrived_ref[:, channels:], 0)
    centre = from_tile(arrived_ref[:, channels:], 1)
    weights = jnp.exp(scores_ref[...] - top)
    weights_ref[...] = low(weights)
    prob_grad = dot_nt(arrived_ref[:, :channels], values_ref[...])
    score_grad = low(weights * (prob_grad - centre) * (channels ** (-0.5)))
    score_grad_ref[...] = score_grad
    part_ref[...] = low(product(score_grad, keys_ref[...]))


def half_of(place_ref, bit):
    return jnp.where(place_ref[3] == bit, 1, 0)


def fold(value):
    return jnp.sum(value.reshape(value.shape[0] // 8, 8, value.shape[1]), axis=0)


def region_back(
    places_ref, arrived_ref, joined_grad_ref, w_query_ref, w_reduce_ref, query_grad_ref, reduced_grad_ref, regions_grad_ref
):
    features = regions_grad_ref.shape[1]
    query_grad = low(jnp.sum(wide(arrived_ref[...]), axis=0))
    query_grad_ref[...] = query_grad
    reduced_grad = low(joined_grad_ref[:, features:] + dot_nt(query_grad, w_query_ref[...]))
    reduced_grad_ref[...] = reduced_grad
    regions_grad_ref[...] = low(joined_grad_ref[:, :features] + dot_nt(reduced_grad, w_reduce_ref[...]))


def hand_out(buffer, send_ref, keep_ref, sems):
    copies = [
        pltpu.make_async_copy(buffer.at[number], target, sems.at[number])
        for number, target in enumerate((send_ref, keep_ref))
    ]
    for copy in copies:
        copy.start()
    for copy in copies:
        copy.wait()


def store_rows(buffer, place_ref, value, first, rows):
    at, end = first, first + value.shape[0]
    while at < end:
        block, offset = divmod(at, rows)
        count = min(rows - offset, end - at)
        buffer[half_of(place_ref, block % 2), block // 2, offset : offset + count] = value[at - first : at - first + count]
        at += count


def slope_back(upstream_ref, pre_ref, scale_ref, shift_ref, out_ref, scale_out_ref, shift_out_ref):
    sites, channels = pre_ref.shape

    def one(step, sums):
        rows = pl.ds(pl.multiple_of(step * 128, 128), 128)
        pre = pre_ref[rows]
        grad = upstream_ref[rows] * gelu_slope(pre * scale_ref[...] + shift_ref[...])
        out_ref[rows] = low(grad * scale_ref[...]).astype(out_ref.dtype)
        return sums[0] + fold(grad * pre), sums[1] + fold(grad)

    zero = jnp.zeros((8, channels), jnp.float32)
    scale_sum, shift_sum = lax.fori_loop(0, sites // 128, one, (zero, zero))
    scale_out_ref[...] = jnp.sum(scale_sum, axis=0, keepdims=True)
    shift_out_ref[...] = jnp.sum(shift_sum, axis=0, keepdims=True)


def later_back(
    groups_a, groups_b, place_ref, regions_grad_ref, pool_ref, scale_ref, shift_ref, scales_ref, pre_c_ref, fm_ref, act_b_ref,
    pre_b_ref, act_a_ref, pre_a_ref, packed_ref,
    send_ref, keep_ref, lin_c_grad_ref, pre_a_grad_ref, scale_c_out_ref, shift_c_out_ref, scale_b_out_ref, shift_b_out_ref,
    scale_a_out_ref, shift_a_out_ref,
    weight_b, weight_c, buffer, out_grad, pre_grad, turned, act_grad, wide_grad,
    held_pre_c, held_map, held_act_b, held_pre_b, held_act_a, held_pre_a, held_lin, sems_b, sems_c, out_sems, sems,
):
    sites, features = held_map.shape
    channels = held_act_b.shape[1]
    chunks, blocks = weight_c.shape[0], weight_c.shape[1]
    rows_b = groups_b * LANE_ROWS

    def part_of(source, target, number, sem):
        columns = pl.ds(pl.multiple_of(number * channels, channels), channels)
        return pltpu.make_async_copy(source.at[:, columns], target.at[:, columns], sems.at[sem + number])

    early = start_all([pltpu.make_async_copy(act_b_ref, held_act_b, sems.at[0])])
    copies_c = start_all(fetch_columns(packed_ref, weight_c, sems_c, groups_a + groups_b, chunks))
    for number in range(chunks):
        part_of(pre_c_ref, held_pre_c, number, 4).start()
        part_of(fm_ref, held_map, number, 4 + chunks).start()
    late = start_all(
        [
            pltpu.make_async_copy(pre_b_ref, held_pre_b, sems.at[1]),
            pltpu.make_async_copy(act_a_ref, held_act_a, sems.at[2]),
            pltpu.make_async_copy(pre_a_ref, held_pre_a, sems.at[3]),
        ]
    )
    copies_b = start_all(fetch(packed_ref, weight_b, sems_b, groups_a, groups_b))
    scale_b_ref, shift_b_ref, scale_a_ref, shift_a_ref = [scales_ref.at[pl.ds(number, 1)] for number in range(4)]
    act_grad[...] = jnp.zeros_like(act_grad)
    wait_all(early)
    turned[...] = held_act_b[...].T
    wait_all(copies_c)

    def chunk(number, carry):
        columns = pl.ds(pl.multiple_of(number * channels, channels), channels)
        out_grad[...] = dot_tn(pool_ref[...], regions_grad_ref[:, columns])
        part_of(pre_c_ref, held_pre_c, number, 4).wait()
        part_of(fm_ref, held_map, number, 4 + chunks).wait()

        def one(step, sums):
            rows = pl.ds(pl.multiple_of(step * 128, 128), 128)
            pre = held_pre_c[rows, columns]
            scale = scale_ref[:, columns]
            linear = wide(held_map[rows, columns]) + pre * scale + shift_ref[:, columns]
            grad = out_grad[rows] * gelu_slope(linear)
            held_lin[rows, columns] = low(grad)
            pre_grad[rows] = low(grad * scale)
            return sums[0] + fold(grad * pre), sums[1] + fold(grad)

        zero = jnp.zeros((8, channels), jnp.float32)
        scale_sum, shift_sum = lax.fori_loop(0, sites // 128, one, (zero, zero))
        part_of(held_lin, lin_c_grad_ref, number, 4 + 2 * chunks).start()
        scale_c_out_ref[:, columns] = jnp.sum(scale_sum, axis=0, keepdims=True)
        shift_c_out_ref[:, columns] = jnp.sum(shift_sum, axis=0, keepdims=True)
        part = low(product(turned[...], pre_grad[...])).reshape(blocks // 2, 2, LANE_ROWS, channels)
        rows = pl.ds(pl.multiple_of(rows_b + number * LANE_ROWS, LANE_ROWS), LANE_ROWS)
        for bit in range(2):
            buffer[half_of(place_ref, bit), :, rows] = part[:, bit]
        act_grad[...] += dot_nt(pre_grad[...], weight_c[number].reshape(channels, channels))
        return carry

    lax.fori_loop(0, chunks, chunk, 0)
    wait_all(late)
    slope_back(act_grad, held_pre_b, scale_b_ref, shift_b_ref, wide_grad, scale_b_out_ref, shift_b_out_ref)
    turned[...] = held_act_a[...].T
    wait_all(copies_b)
    for slide in (-1, 0, 1):
        slid = in_columns(wide_grad[...], -slide)
        for number, place in enumerate(places):
            if place[1] != slide:
                continue
            moved = low(in_rows(slid, -place[0]))
            store_rows(buffer, place_ref, low(product(turned[...], moved)), number * channels, rows_b)
            begin = number * channels // LANE_ROWS
            tap = weight_b[begin : begin + channels // LANE_ROWS].reshape(channels, channels)
            part = dot_nt(moved, tap)
            if slide == -1 and place[0] == -1:
                act_grad[...] = part
            else:
                act_grad[...] += part
    slope_back(act_grad, held_pre_a, scale_a_ref, shift_a_ref, pre_a_grad_ref, scale_a_out_ref, shift_a_out_ref)
    hand_out(buffer, send_ref, keep_ref, out_sems)
    for number in range(chunks):
        part_of(held_lin, lin_c_grad_ref, number, 4 + 2 * chunks).wait()


def by_frames(grad, offset):
    if offset == 0:
        return grad
    sites, width = grad.shape
    tall = grad.reshape(sites // (FRAMES * SIDE * SIDE), FRAMES, SIDE * SIDE, width)
    edge = jnp.zeros_like(tall[:, :1])
    if offset > 0:
        tall = jnp.concatenate([edge, tall[:, :-1]], axis=1)
    else:
        tall = jnp.concatenate([tall[:, 1:], edge], axis=1)
    return tall.reshape(sites, width)


def first_back(place_ref, grad_ref, own_ref, got_ref, turned_ref, send_ref, keep_ref, sum_ref, buffer, held, sems, out_sems):
    features, sites = held.shape
    channels = grad_ref.shape[1]
    copies = [
        pltpu.make_async_copy(turned_ref.at[pl.ds(start, channels)], held.at[pl.ds(start, channels)], sems.at[start // channels])
        for start in range(0, features, channels)
    ]
    start_all(copies)
    sum_ref[...] = add_low(own_ref[...], got_ref[...])
    for tap in range(3):
        moved = by_frames(grad_ref[...], tap - 1)
        for start in range(0, features, channels):
            if tap == 0:
                copies[start // channels].wait()
            part = low(product(held[start : start + channels], moved))
            store_rows(buffer, place_ref, part, tap * features + start, buffer.shape[2])
    hand_out(buffer, send_ref, keep_ref, out_sems)


def map_back(places_ref, grad_ref, weight_ref, lin_c_grad_ref, out_ref, moved, held_lin, held_out, sems):
    sites, features = held_out.shape
    channels = grad_ref.shape[1]
    copies = start_all([pltpu.make_async_copy(lin_c_grad_ref, held_lin, sems.at[0])])
    for tap in range(3):
        moved[tap] = by_frames(grad_ref[...], tap - 1)
    wait_all(copies)
    groups = channels // LANE_ROWS

    def chunk(number, carry):
        columns = pl.ds(pl.multiple_of(number * channels, channels), channels)
        total = wide(held_lin[:, columns])
        for tap in range(3):
            rows = pl.ds(tap * (features // LANE_ROWS) + number * groups, groups)
            total = total + dot_nt(moved[tap], weight_ref[rows].reshape(channels, channels))
        held_out[:, columns] = low(total)
        pltpu.make_async_copy(held_out.at[:, columns], out_ref.at[:, columns], sems.at[1 + number]).start()
        return carry

    lax.fori_loop(0, features // channels, chunk, 0)
    copies = []
    for number in range(features // channels):
        columns = pl.ds(number * channels, channels)
        copies.append(pltpu.make_async_copy(held_out.at[:, columns], out_ref.at[:, columns], sems.at[1 + number]))
    wait_all(copies)


COST = 6e9
WINDOW = 0.1
FIRST_LIMIT = 52
F32 = jnp.float32
BF16 = jnp.bfloat16
ANY = pl.BlockSpec(memory_space=pl.ANY)
SCALAR = pl.BlockSpec(memory_space=pltpu.SMEM)
HELD = pl.BlockSpec(memory_space=pltpu.VMEM)


def shape_of(dims, kind):
    return jax.ShapeDtypeStruct(dims, kind)


def add_low(left, right):
    return left + right


class Blocks:
    def __init__(self, ref, first, dims, rows):
        self.ref, self.first, self.dims, self.rows = ref, first, dims, rows

    def span(self, index):
        index = index if isinstance(index, tuple) else (index,)
        flat = 0
        for place, size in zip(index, self.dims):
            flat = flat * size + place
        return pl.ds(pl.multiple_of(self.first + flat * self.rows, LANE_ROWS), self.rows)

    def __getitem__(self, index):
        return self.ref[self.span(index)]

    def __setitem__(self, index, value):
        self.ref[self.span(index)] = value


def after_last(places_ref, keep_ref, got_ref, keep_one, send_one, keep_two, send_two):
    half = keep_ref.shape[0] // 2
    across, inner = places_ref[0], places_ref[1]

    def one(number, carry):
        for place in range(2):
            keep_one[number, place] = add_low(keep_ref[number, place, across], got_ref[number, place, across])
            send_one[number, place] = add_low(keep_ref[number, place, 1 - across], got_ref[number, place, 1 - across])
            later = number + half
            keep_two[number, place] = add_low(keep_ref[later, inner, place], got_ref[later, inner, place])
            send_two[number, place] = add_low(keep_ref[later, 1 - inner, place], got_ref[later, 1 - inner, place])
        return carry

    lax.fori_loop(0, half, one, 0)


def after_cross(places_ref, keep_one, got_one, keep_two, got_two, kept_one, send_one, kept_two, send_two):
    across, inner = places_ref[0], places_ref[1]

    def one(number, carry):
        kept_one[number] = add_low(keep_one[number, inner], got_one[number, inner])
        send_one[number] = add_low(keep_one[number, 1 - inner], got_one[number, 1 - inner])
        kept_two[number] = add_low(keep_two[number, across], got_two[number, across])
        send_two[number] = add_low(keep_two[number, 1 - across], got_two[number, 1 - across])
        return carry

    lax.fori_loop(0, keep_two.shape[0], one, 0)


def after_plane(places_ref, keep_one, got_one, keep_two, got_two, kept_ref, sends):
    half = keep_one.shape[0]
    outer = places_ref[2]

    def block(place, target):
        @pl.when(place < half)
        def _():
            target[...] = add_low(keep_one[lax.rem(place, half)], got_one[lax.rem(place, half)])

        @pl.when(place >= half)
        def _():
            target[...] = add_low(keep_two[lax.rem(place, half)], got_two[lax.rem(place, half)])

    block(outer, kept_ref)
    for step, target in enumerate(sends):
        block(outer ^ (step + 1), target)


def total_of(refs):
    total = wide(refs[0][...])
    for ref in refs[1:]:
        total = total + wide(ref[...])
    return total


def round_two(
    places_ref, keep_one, got_one, keep_two, got_two, keep_a, got_a,
    kept_one, kept_two, keep_a_one, keep_a_two, across_ref, inner_ref,
):
    half, rows = kept_one.shape[:2]
    rows_a = keep_a_one.shape[2]
    below = 2 * half * rows_a
    after_last(
        places_ref, keep_a, got_a, keep_a_one, Blocks(across_ref, 0, (half, 2), rows_a), keep_a_two,
        Blocks(inner_ref, 0, (half, 2), rows_a),
    )
    after_cross(
        places_ref, keep_one, got_one, keep_two, got_two, kept_one, Blocks(inner_ref, below, (half,), rows), kept_two,
        Blocks(across_ref, below, (half,), rows),
    )


def bank_spans(lines, width, channels):
    groups = channels // width
    step = -(-lines // (groups * LANE_ROWS)) * LANE_ROWS
    return [(first, min(first + step, lines)) for first in range(0, lines, step)], step


def store_narrow(target, first, value, channels):
    lines, width = value.shape
    spans, step = bank_spans(lines, width, channels)
    target[first : first + step] = jnp.zeros((step, channels), BF16)
    for number, (begin, end) in enumerate(spans):
        target[first : first + end - begin, number * width : (number + 1) * width] = value[begin:end]


def load_narrow(value, first, lines, width):
    spans, _ = bank_spans(lines, width, value.shape[1])
    pieces = [
        value[first : first + end - begin, number * width : (number + 1) * width]
        for number, (begin, end) in enumerate(spans)
    ]
    return jnp.concatenate(pieces, axis=0)


def round_three(count, split, places_ref, kept_one, kept_two, keep_a_one, keep_a_two, got_across, got_inner, *refs):
    region_refs, refs = (refs[:2], refs[2:]) if split else (refs[:1], refs[1:])
    bank_refs, refs = (refs[:count], refs[count:]) if split else (refs[:1], refs[1:])
    kept_ref, sends, refs = refs[0], refs[1 : count], refs[count:]
    kept_a_one, kept_a_two, bank_keep_ref, across_ref, inner_ref = refs
    half, rows, channels = kept_one.shape
    rows_a = keep_a_one.shape[2]
    below = 2 * half * rows_a
    after_plane(
        places_ref, kept_one, Blocks(got_inner, below, (half,), rows), kept_two, Blocks(got_across, below, (half,), rows),
        kept_ref, sends,
    )
    after_cross(
        places_ref, keep_a_one, Blocks(got_across, 0, (half, 2), rows_a), keep_a_two,
        Blocks(got_inner, 0, (half, 2), rows_a), kept_a_one, Blocks(inner_ref, 0, (half,), rows_a), kept_a_two,
        Blocks(across_ref, 0, (half,), rows_a),
    )
    across_ref[half * rows_a :] = low(total_of(region_refs))
    inner = places_ref[7] if split else 0
    keep = total_of([ref.at[inner] for ref in bank_refs])
    store_narrow(bank_keep_ref, 0, low(keep), channels)
    if split:
        send = total_of([ref.at[1 - inner] for ref in bank_refs])
        store_narrow(inner_ref, half * rows_a, low(send), channels)
    else:
        inner_ref[half * rows_a :] = bank_keep_ref[...]


def round_four(count, split, widths, places_ref, *refs):
    plane_refs, refs = refs[:count], refs[count:]
    kept_a_one, kept_a_two, bank_keep_ref, across_ref, got_across, got_inner, done_ref, kept_a_ref = refs[:8]
    sends, (reduce_ref, query_ref, out_ref, head_ref) = refs[8 : 7 + count], refs[7 + count :]
    half, rows_a, channels = kept_a_one.shape
    rows = plane_refs[0].shape[0]
    below = half * rows_a
    after_plane(
        places_ref, kept_a_one, Blocks(got_inner, 0, (half,), rows_a), kept_a_two,
        Blocks(got_across, 0, (half,), rows_a), kept_a_ref, sends,
    )
    done_ref[:rows] = low(total_of(plane_refs))
    done_ref[rows:] = add_low(bank_keep_ref[...], got_inner[below:]) if split else bank_keep_ref[...]
    region = wide(across_ref[below:]) + wide(got_across[below:]) if split else wide(across_ref[below:])
    _, _, feature_rows, channel_rows, _, joined_rows = widths
    reduce_ref[...] = region[:feature_rows]
    query_ref[...] = region[feature_rows : feature_rows + channel_rows]
    out_ref[...] = region[feature_rows + channel_rows : feature_rows + 2 * channel_rows]
    head = load_narrow(region, feature_rows + 2 * channel_rows, joined_rows, TILE)
    head_ref[...] = head[:, : head_ref.shape[1]]


def round_last(count, places_ref, *refs):
    part_ref, both = refs[-1 if len(refs) == count + 1 else -2], refs[-1]
    part_ref[...] = low(total_of(refs[:count]))
    if len(refs) > count + 1:
        for number, ref in enumerate(refs[count : count + 2]):
            both[number] = ref[...]


def sum_swap(places_ref, *refs):
    refs[-1][...] = low(total_of(refs[:-1]))


def front_pack(groups_a, groups_b, places_ref, conv_a_ref, conv_b_ref, conv_c_ref, own_a_ref, own_ref, sems):
    place = places_ref[9]
    chunks = own_ref.shape[0] - groups_b
    channels = own_ref.shape[2]
    copies = [
        pltpu.make_async_copy(conv_b_ref.at[pl.ds(place * groups_b, groups_b)], own_ref.at[pl.ds(0, groups_b)], sems.at[0]),
        pltpu.make_async_copy(conv_a_ref.at[pl.ds(place * groups_a, groups_a)], own_a_ref, sems.at[1]),
    ]
    for chunk in range(chunks):
        copies.append(
            pltpu.make_async_copy(
                conv_c_ref.at[place, :, pl.ds(chunk * channels, channels)], own_ref.at[groups_b + chunk], sems.at[2 + chunk]
            )
        )
    wait_all(start_all(copies))


def front_turn(places_ref, map_ref, bank_ref, turned_map_ref, turned_bank_ref):
    sites, features = map_ref.shape
    for start in range(0, features, sites):
        turned_map_ref[start : start + sites] = map_ref[:, start : start + sites].T
        turned_bank_ref[start : start + sites] = bank_ref[:, start : start + sites].T


def front_bank(places_ref, bank_ref, w_bank_ref, w_key_ref, w_value_ref, keys_ref, values_ref, turned_memory_ref):
    memory = low(product(bank_ref[...], w_bank_ref[...]))
    keys_ref[...] = low(product(memory, w_key_ref[...]))
    values_ref[...] = low(product(memory, w_value_ref[...]))
    turned_memory_ref[...] = memory.T


def front_head(
    places_ref, index_ref, weight_ref, logit_grad_ref, w_head_ref, w_out_ref,
    pool_ref, joined_grad_ref, hidden_grad_ref, branch_grad_ref,
):
    own, taps = index_ref.shape
    sites = pool_ref.shape[1]
    channels = hidden_grad_ref.shape[1]
    features = w_head_ref.shape[0] - channels
    column = lax.broadcasted_iota(jnp.int32, (own, sites), 1)
    pool = jnp.zeros((own, sites), F32)
    for tap in range(taps):
        weight = wide(weight_ref[:, tap : tap + 1])
        pool = pool + jnp.where(column == index_ref[:, tap : tap + 1], weight, 0.0)
    pool_ref[...] = low(pool)
    logit_grad = logit_grad_ref[pl.ds(pl.multiple_of(places_ref[8], LANE_ROWS), own)]
    joined_grad = dot_nt(logit_grad, w_head_ref[...])
    joined_grad_ref[...] = joined_grad
    hidden_grad_ref[...] = dot_nt(low(joined_grad[:, features:]), w_out_ref[...])
    branch_grad_ref[...] = low(dot_nt(logit_grad_ref[...], w_head_ref[features:]))


def region_pack(
    places_ref, regions_ref, reduced_ref, hidden_ref, query_grad_ref, reduced_grad_ref, w_out_ref, w_head_ref,
    logits_ref, message_ref,
):
    count = message_ref.shape[0]
    channels = reduced_ref.shape[1]
    reduced = reduced_ref[...]
    merged = low(reduced + product(hidden_ref[...], w_out_ref[...]))
    joined = jnp.concatenate([regions_ref[...], merged], axis=1)
    logits_ref[...] = low(product(joined, w_head_ref[...]))[:, : logits_ref.shape[1]]
    reduced_low = low(reduced)
    parts = [regions_ref[...], reduced_low, hidden_ref[...], joined]
    shared = [reduced_grad_ref[...], query_grad_ref[...]]
    for place in range(count):
        pieces = list(shared)
        for part in parts:
            width = part.shape[1] // count
            pieces.append(part[:, place * width : (place + 1) * width])
        spare = message_ref.shape[2] - sum(piece.shape[1] for piece in pieces)
        if spare:
            pieces.append(jnp.zeros((reduced.shape[0], spare), BF16))
        message_ref[place] = jnp.concatenate(pieces, axis=1)


def key_value_parts(places_ref, score_grad_ref, queries_ref, weights_ref, arrived_ref, out_ref):
    keys_here = score_grad_ref.shape[1]
    out_ref[:keys_here] = low(dot_tn(score_grad_ref[...], queries_ref[...]))
    out_ref[keys_here:] = low(dot_tn(weights_ref[...], arrived_ref[:, : queries_ref.shape[1]]))


def region_sums(widths, places_ref, group_ref, branch_grad_ref, logit_grad_ref, out_ref):
    ends, start = [], 0
    for width in widths:
        ends.append((start, start + width))
        start += width
    reduced_grad, query_grad, regions, reduced, hidden, joined = [group_ref[:, begin:end] for begin, end in ends]
    first, second = widths[2], widths[2] + widths[3]
    third = second + widths[4]
    channels = reduced_grad.shape[1]
    out_ref[:first] = low(dot_tn(regions, reduced_grad))
    out_ref[first:second] = low(dot_tn(reduced, query_grad))
    out_ref[second:third] = low(dot_tn(hidden, branch_grad_ref[...]))
    head = low(dot_tn(joined, logit_grad_ref[...]))
    store_narrow(out_ref, third, head, channels)


def bank_back(
    places_ref, sums_ref, w_key_ref, w_value_ref, w_bank_ref, turned_bank_ref, turned_memory_ref, *refs
):
    vectors, bank_grad_ref, outs, (message_ref, grads) = refs[:8], refs[8], refs[9:-2], refs[-2:]
    keys_here, features = bank_grad_ref.shape
    channels = sums_ref.shape[1]
    count, _, width = message_ref.shape
    key_low, value_low = sums_ref[:keys_here], sums_ref[keys_here:]
    memory_grad = low(dot_nt(key_low, w_key_ref[...]) + dot_nt(value_low, w_value_ref[...]))
    for start in range(0, features, channels):
        bank_grad_ref[:, start : start + channels] = low(dot_nt(memory_grad, w_bank_ref[start : start + channels]))
    grads[:keys_here] = memory_grad
    grads[keys_here : 2 * keys_here] = key_low
    grads[2 * keys_here :] = value_low

    def columns(rows):
        if width % TILE == 0:
            return grads[rows, pl.ds(pl.multiple_of(places_ref[4] * width, width), width)]
        picked = grads[rows, :width]
        for number in range(1, channels // width):
            picked = jnp.where(places_ref[4] == number, grads[rows, number * width : (number + 1) * width], picked)
        return picked

    feature_rows, channel_rows = features // count, channels // count
    part = low(product(turned_bank_ref[...], columns(pl.ds(0, keys_here))))
    message_ref[:, :feature_rows] = part.reshape(count, feature_rows, width)
    at = feature_rows
    for number in (1, 2):
        part = low(product(turned_memory_ref[...], columns(pl.ds(number * keys_here, keys_here))))
        message_ref[:, at : at + channel_rows] = part.reshape(count, channel_rows, width)
        at += channel_rows
    spare = message_ref.shape[1] - at
    for place in range(count):
        row = []
        for vector_ref in vectors:
            share = vector_ref.shape[1] // count
            row.append(vector_ref[:, place * share : (place + 1) * share])
        total = sum(piece.shape[1] for piece in row)
        lines = -(-total // width)
        if lines * width > total:
            row.append(jnp.zeros((1, lines * width - total), F32))
        row = jnp.concatenate(row, axis=1)
        tile = [row[:, line * width : (line + 1) * width] for line in range(lines)]
        tile.append(jnp.zeros((spare - lines, width), F32))
        message_ref[place, at:] = low(jnp.concatenate(tile, axis=0))
    inner = outs[0].shape[0]
    for step, out_ref in enumerate(outs):
        out_ref[...] = message_ref[pl.ds((places_ref[6] ^ step) * inner, inner)]


def finish(shape_info, places_ref, part_ref, *refs):
    rows_b, rows_c, feature_rows, channel_rows, lines, split = shape_info
    if split:
        own_ref, got_ref, refs = refs[0], refs[1], refs[2:]
        weight_refs = [own_ref.at[0], got_ref.at[0], own_ref.at[1], got_ref.at[1]]
        bank_refs, first = weight_refs, rows_b + rows_c
    else:
        weight_refs, bank_refs, refs, first = refs[:1], refs[1:-14], refs[-14:], 0
    conv_a_ref, conv_b_ref, conv_c_ref, bank_out_ref, key_ref, value_ref = refs[:6]
    vectors = refs[6:]
    conv_a_ref[...] = wide(part_ref[...]).reshape(conv_a_ref.shape)
    channels = weight_refs[0].shape[1]
    width = channels // len(bank_refs)

    def spot(number, size):
        if not split:
            return pl.ds(number * size, size)
        return pl.ds(pl.multiple_of((places_ref[4] ^ number) * size, size), size)

    for number, ref in enumerate(weight_refs):
        conv_b_ref[spot(number, rows_b)] = wide(ref[:rows_b])
        for chunk in range(rows_c // LANE_ROWS):
            begin = rows_b + chunk * LANE_ROWS
            conv_c_ref[spot(number, LANE_ROWS), chunk * channels : (chunk + 1) * channels] = wide(
                ref[begin : begin + LANE_ROWS]
            )
    tile = None
    at = feature_rows + 2 * channel_rows
    for number, ref in enumerate(bank_refs):
        bank = wide(load_narrow(ref, first, lines, width))
        columns = spot(number, width)
        bank_out_ref[:, columns] = bank[:feature_rows]
        key_ref[:, columns] = bank[feature_rows : feature_rows + channel_rows]
        value_ref[:, columns] = bank[feature_rows + channel_rows : at]
        tile = bank[at:] if tile is None else tile + bank[at:]
    total = sum(ref.shape[1] for ref in vectors)
    row = jnp.concatenate([tile[line : line + 1] for line in range(-(-total // width))], axis=1)
    at = 0
    for ref in vectors:
        ref[...] = row[:, at : at + ref.shape[1]]
        at += ref.shape[1]


def run_kernel(
    kernel, places, arrays, shapes, name, micros, scratch=(), raw_in=(), raw_out=(), fetched=(), limit=8
):
    count_in, count_out, fetched = len(arrays), len(shapes), list(fetched)

    def wrapped(*refs):
        places_ref, ins = refs[0], list(refs[1 : 1 + count_in])
        out_places, outs = refs[1 + count_in], refs[2 + count_in : 2 + count_in + count_out]
        extra = refs[2 + count_in + count_out :]
        if fetched:
            held, sems, extra = extra[: len(fetched)], extra[len(fetched)], extra[len(fetched) + 1 :]
            copies = start_all(
                [pltpu.make_async_copy(ins[number], held[slot], sems.at[slot]) for slot, number in enumerate(fetched)]
            )
        for number in range(places.shape[0]):
            out_places[number] = places_ref[number]
        if fetched:
            wait_all(copies)
            for slot, number in enumerate(fetched):
                ins[number] = held[slot]
        kernel(places_ref, *ins, *outs, *extra)

    outside = [*raw_in, *fetched]
    buffers = [pltpu.VMEM(arrays[number].shape, arrays[number].dtype) for number in fetched]
    if fetched:
        buffers.append(pltpu.SemaphoreType.DMA((len(fetched),)))
    return pl.pallas_call(
        wrapped,
        out_shape=[shape_of(places.shape, jnp.int32)] + list(shapes),
        in_specs=[SCALAR] + [ANY if number in outside else HELD for number in range(count_in)],
        out_specs=[SCALAR] + [ANY if number in raw_out else HELD for number in range(count_out)],
        scratch_shapes=buffers + list(scratch),
        compiler_params=params(limit),
        cost_estimate=pl.CostEstimate(
            flops=int(micros * COST), bytes_accessed=int(micros * COST / 1000), transcendentals=0
        ),
        name=name,
    )(places, *arrays)


def run_first_conv(places, feature_map, sources, scale, shift):
    sites, channels = feature_map.shape[0], sources[0].shape[3]
    groups = sources[0].shape[1]
    blocks = sum(source.shape[0] for source in sources)
    return pl.pallas_call(
        first_conv,
        out_shape=[
            shape_of((sites, channels), F32),
            shape_of((sites, channels), BF16),
            shape_of((blocks * groups, LANE_ROWS, channels), BF16),
        ],
        in_specs=[SCALAR, HELD] + [ANY] * len(sources) + [HELD] * 2,
        out_specs=[ANY, HELD, ANY],
        scratch_shapes=[
            pltpu.VMEM((blocks * groups, LANE_ROWS, channels), BF16),
            pltpu.VMEM((sites, channels), F32),
            pltpu.SemaphoreType.DMA((blocks,)),
            pltpu.SemaphoreType.DMA((2,)),
        ],
        compiler_params=params(FIRST_LIMIT),
        cost_estimate=pl.CostEstimate(flops=int(6 * COST), bytes_accessed=int(6 * COST / 1000), transcendentals=0),
        name="first_conv",
    )(places, feature_map, *sources, scale.reshape(1, -1), shift.reshape(1, -1))


def run_later_convs(
    act_a, feature_map, packed, scale_b, shift_b, scale_c, shift_c, pooling, w_reduce, w_query, groups_b, groups_c
):
    sites, channels = act_a.shape
    features = feature_map.shape[1]
    blocks = packed.shape[0]
    own = pooling.shape[0]
    group = lax.axis_size("bank")
    return pl.pallas_call(
        later_convs,
        out_shape=[
            jax.ShapeDtypeStruct((sites, channels), jnp.float32),
            jax.ShapeDtypeStruct((sites, channels), jnp.bfloat16),
            jax.ShapeDtypeStruct((sites, features), jnp.float32),
            jax.ShapeDtypeStruct((own, features), jnp.bfloat16),
            jax.ShapeDtypeStruct((own, channels), jnp.float32),
            jax.ShapeDtypeStruct((group, own, channels), jnp.bfloat16),
        ],
        in_specs=[HELD] + [ANY] * 2 + [HELD] * 5 + [ANY, HELD],
        out_specs=[ANY] * 5 + [HELD],
        scratch_shapes=[
            pltpu.VMEM((blocks * groups_b, LANE_ROWS, channels), jnp.bfloat16),
            pltpu.VMEM((groups_c, blocks, LANE_ROWS, channels), jnp.bfloat16),
            pltpu.VMEM((sites, channels), jnp.bfloat16),
            pltpu.VMEM((sites, features), jnp.bfloat16),
            pltpu.VMEM((sites, features), jnp.float32),
            pltpu.VMEM(w_reduce.shape, jnp.bfloat16),
            pltpu.VMEM((sites, channels), jnp.float32),
            pltpu.VMEM((sites, channels), jnp.bfloat16),
            pltpu.VMEM((own, features), jnp.bfloat16),
            pltpu.VMEM((own, channels), jnp.float32),
            pltpu.SemaphoreType.DMA((blocks,)),
            pltpu.SemaphoreType.DMA((blocks,)),
            pltpu.SemaphoreType.DMA((6 + groups_c,)),
        ],
        compiler_params=params(52),
        cost_estimate=pl.CostEstimate(flops=int(15 * COST), bytes_accessed=int(15 * COST / 1000), transcendentals=0),
        name="later_convs",
    )(
        act_a, feature_map, packed, scale_b.reshape(1, -1), shift_b.reshape(1, -1), scale_c.reshape(1, -1),
        shift_c.reshape(1, -1), pooling, w_reduce, w_query,
    )


def body(
    feature_map,
    bank,
    region_time,
    roi_index,
    roi_weight,
    conv_a,
    scale_a,
    shift_a,
    conv_b,
    scale_b,
    shift_b,
    conv_c,
    scale_c,
    shift_c,
    w_reduce,
    w_bank,
    w_query,
    w_key,
    w_value,
    ln_gain,
    ln_shift,
    w_out,
    w_head,
    logit_grad,
):
    site_count = feature_map.shape[0]
    feature_count = feature_map.shape[1]
    channels = w_query.shape[0]
    classes = w_head.shape[1]
    keys_here = bank.shape[0]
    own_count = roi_index.shape[0]
    bank_count = lax.axis_size("bank")
    bank_place = lax.axis_index("bank")
    dp_count = lax.axis_size("dp")
    dp_place = lax.axis_index("dp")
    first_row = bank_place * own_count
    half_span = keys_here * bank_count // 2
    group_rows = bank_count * own_count
    chunks = feature_count // channels
    shards = (conv_a, conv_b, conv_c)
    split = dp_count // 2 == 2 and bank_count // 2 == 4 and all(shard.shape[0] % (LANE_ROWS * dp_count) == 0 for shard in shards)
    axes = block_axes(split, dp_count, bank_count)
    outer, inner, across, last = axes
    outer_count = outer.size if split else 1
    blocks = bank_count * dp_count if split else bank_count
    halves = tuple(axis.size for axis in axes[:3])
    places_here = jnp.stack([across.place(), inner.place(), outer.place(), last.place(), dp_place, bank_place * keys_here, outer.place() if split else 0 * bank_place, inner.place(), first_row, dp_place if split else 0 * dp_place])

    parts = dp_count if split else 1
    rows_a, rows_b, rows_c = [shard.shape[0] // parts for shard in shards]
    groups_a, groups_b, groups_c = rows_a // LANE_ROWS, rows_b // LANE_ROWS, chunks
    places, own_a, own_packed = run_kernel(
        functools.partial(front_pack, groups_a, groups_b),
        places_here,
        [shard.reshape(-1, LANE_ROWS, shard.shape[1]) for shard in shards],
        [shape_of((groups_a, LANE_ROWS, channels), BF16), shape_of((groups_b + chunks, LANE_ROWS, channels), BF16)],
        "front_pack",
        1,
        scratch=[pltpu.SemaphoreType.DMA((2 + chunks,))],
        raw_in=(0, 1, 2),
        raw_out=(0, 1),
    )
    packed = lax.all_gather(own_packed, ("bank", "dp") if split else "bank", axis=0, tiled=False)
    packed = packed.reshape((blocks,) + own_packed.shape)
    spare = ((0, 0), (0, TILE - classes))
    wide_head, wide_logit_grad = jnp.pad(w_head, spare), jnp.pad(logit_grad, spare)
    front = {}

    def turn(places):
        places, front["turned_map"], front["turned_bank"] = run_kernel(
            front_turn,
            places,
            [feature_map, bank],
            [shape_of((feature_count, site_count), BF16), shape_of((feature_count, keys_here), BF16)],
            "front_turn",
            6,
            limit=16,
        )
        return places

    def project(places):
        inside = shape_of((keys_here, channels), BF16)
        places, front["keys"], front["values"], front["turned_memory"] = run_kernel(
            front_bank,
            places,
            [bank, w_bank, w_key, w_value],
            [inside, inside, shape_of((channels, keys_here), BF16)],
            "front_bank",
            6,
            limit=16,
        )
        return places

    def head(places):
        places, front["pooling"], front["joined_grad"], front["hidden_grad"], front["group_branch_grad"] = run_kernel(
            front_head,
            places,
            [roi_index, roi_weight, wide_logit_grad, wide_head, w_out],
            [
                shape_of((own_count, site_count), BF16),
                shape_of((own_count, w_head.shape[0]), F32),
                shape_of((own_count, channels), F32),
                shape_of((group_rows, channels), BF16),
            ],
            "front_head",
            4,
            limit=16,
        )
        return places

    if split:
        places, sources = gather_blocks(own_a, axes, places, [turn, project, head])
    else:
        places, sources = head(project(turn(places))), [lax.all_gather(own_a, "bank", axis=0, tiled=False)]
    turned_map, turned_bank, turned_memory = front["turned_map"], front["turned_bank"], front["turned_memory"]
    keys, values, pooling = front["keys"], front["values"], front["pooling"]
    joined_grad, hidden_grad, group_branch_grad = front["joined_grad"], front["hidden_grad"], front["group_branch_grad"]
    time_column = region_time.reshape(-1, 1)
    scales = jnp.stack([scale_b, shift_b, scale_a, shift_a])
    places, time_column, scales, *sources = lax.optimization_barrier((places, time_column, scales, *sources))

    pre_a, act_a, weight_a = run_first_conv(places, feature_map, sources, scale_a, shift_a)
    pre_b, act_b, pre_c, regions, reduced, own_queries = run_later_convs(
        act_a, feature_map, packed, scale_b, shift_b, scale_c, shift_c, pooling, w_reduce, w_query, groups_b, groups_c
    )
    queries = to_owners(own_queries).reshape(group_rows, channels)
    places, message, scores = run_kernel(
        functools.partial(attend, half_span),
        places,
        [queries, keys, values, time_column],
        [shape_of((group_rows, channels + TILE), BF16), shape_of((group_rows, keys_here), F32)],
        "attend",
        2,
    )
    arrived = to_owners(message.reshape(bank_count, own_count, channels + TILE))
    row = shape_of((1, channels), F32)
    places, message, hidden_low, gain_part, shift_part = run_kernel(
        merge_rows,
        places,
        [arrived, hidden_grad, ln_gain.reshape(1, -1), ln_shift.reshape(1, -1)],
        [shape_of(arrived.shape, BF16), shape_of((own_count, channels), BF16), row, row],
        "merge_rows",
        2,
    )
    arrived = to_owners(message).reshape(group_rows, channels + TILE)
    group_shape = shape_of((group_rows, channels), BF16)
    weight_shape = shape_of((group_rows, keys_here), BF16)
    places, query_part, score_grad, weights_low = run_kernel(
        attend_back,
        places,
        [arrived, scores, keys, values],
        [group_shape, weight_shape, weight_shape],
        "attend_back",
        2,
    )
    query_parts = to_owners(query_part.reshape(bank_count, own_count, channels))
    places, key_value = run_kernel(
        key_value_parts,
        places,
        [score_grad, queries, weights_low, arrived],
        [shape_of((2 * keys_here, channels), BF16)],
        "key_value_parts",
        3,
    )

    def dp_swap(value, step):
        return lax.ppermute(value, "dp", [(i, i ^ step) for i in range(dp_count)])

    key_value_got = dp_swap(key_value, 1)

    def summed_swap(places, own, got):
        places, own = run_kernel(
            sum_swap, places, [own, got], [shape_of(own.shape, BF16)], "sum_swap", 2
        )
        return places, own

    places, key_value = summed_swap(places, key_value, key_value_got)
    step = 2
    while step * 2 < dp_count:
        places, key_value = summed_swap(places, key_value, dp_swap(key_value, step))
        step *= 2
    key_value_got = dp_swap(key_value, step)
    own_shape = shape_of((own_count, channels), BF16)
    places, query_grad, reduced_grad, regions_grad = run_kernel(
        region_back,
        places,
        [query_parts, joined_grad, w_query, w_reduce],
        [own_shape, own_shape, shape_of((own_count, feature_count), BF16)],
        "region_back",
        3,
    )
    half_blocks = blocks // 2
    rows_bc = rows_b + groups_c * LANE_ROWS
    wide_row = shape_of((1, feature_count), F32)
    maps = (site_count, feature_count)
    inside = (site_count, channels)
    (
        places, send_bc, keep_bc, lin_c_grad, pre_a_grad,
        scale_c_part, shift_c_part, scale_b_part, shift_b_part, scale_a_part, shift_a_part,
    ) = run_kernel(
        functools.partial(later_back, 0, groups_b),
        places,
        [
            regions_grad, pooling, scale_c.reshape(1, -1), shift_c.reshape(1, -1),
            scales, pre_c, feature_map, act_b, pre_b, act_a, pre_a, packed,
        ],
        [shape_of((half_blocks, rows_bc, channels), BF16)] * 2
        + [shape_of(maps, BF16), shape_of(inside, BF16), wide_row, wide_row]
        + [row] * 4,
        "later_back",
        28,
        scratch=[
            pltpu.VMEM((blocks * groups_b, LANE_ROWS, channels), BF16),
            pltpu.VMEM((groups_c, blocks, LANE_ROWS, channels), BF16),
            pltpu.VMEM((2, half_blocks, rows_bc, channels), BF16),
            pltpu.VMEM(inside, F32),
            pltpu.VMEM(inside, BF16),
            pltpu.VMEM((channels, site_count), BF16),
            pltpu.VMEM(inside, F32),
            pltpu.VMEM(inside, F32),
            pltpu.VMEM(maps, F32),
            pltpu.VMEM(maps, BF16),
            pltpu.VMEM(inside, BF16),
            pltpu.VMEM(inside, F32),
            pltpu.VMEM(inside, BF16),
            pltpu.VMEM(inside, F32),
            pltpu.VMEM(maps, BF16),
            pltpu.SemaphoreType.DMA((blocks,)),
            pltpu.SemaphoreType.DMA((blocks,)),
            pltpu.SemaphoreType.DMA((2,)),
            pltpu.SemaphoreType.DMA((4 + 3 * chunks,)),
        ],
        raw_in=range(5, 12),
        raw_out=(0, 1, 2),
        limit=40,
    )
    got_bc = last.swap(send_bc, 1)

    def parted(value):
        return value.reshape(halves + value.shape[1:])

    places, send_a, keep_a, key_value = run_kernel(
        first_back,
        places,
        [pre_a_grad, key_value, key_value_got, turned_map],
        [shape_of((half_blocks, rows_a, channels), BF16)] * 2 + [shape_of(key_value.shape, BF16)],
        "first_back",
        6,
        scratch=[
            pltpu.VMEM((2, half_blocks, rows_a, channels), BF16),
            pltpu.VMEM(turned_map.shape, BF16),
            pltpu.SemaphoreType.DMA((chunks,)),
            pltpu.SemaphoreType.DMA((2,)),
        ],
        raw_in=(3,),
        raw_out=(0, 1),
        limit=20,
    )
    got_a = last.swap(send_a, 1)
    half = outer.size // 2
    plane_shape = (half, 2, rows_bc, channels)
    places, keep_one, send_one, keep_two, send_two = run_kernel(
        after_last, places, [parted(keep_bc), parted(got_bc)], [shape_of(plane_shape, BF16)] * 4, "round_one", 4
    )
    got_one, got_two = across.swap(send_one, 1), inner.swap(send_two, 1)
    feature_rows, channel_rows = feature_count // bank_count, channels // bank_count
    joined_rows = (feature_count + channels) // bank_count
    widths = (channels, channels, feature_rows, channel_rows, channel_rows, joined_rows)
    message_width = -(-sum(widths) // TILE) * TILE
    places, logits_out, message = run_kernel(
        region_pack,
        places,
        [regions, reduced, hidden_low, query_grad, reduced_grad, w_out, wide_head],
        [shape_of((own_count, classes), BF16), shape_of((bank_count, own_count, message_width), BF16)],
        "region_pack",
        WINDOW,
    )
    group = to_owners(message).reshape(group_rows, message_width)

    places, map_grad = run_kernel(
        map_back,
        places,
        [pre_a_grad, weight_a, lin_c_grad],
        [shape_of(maps, BF16)],
        "map_back",
        WINDOW,
        scratch=[
            pltpu.VMEM((3,) + inside, BF16),
            pltpu.VMEM(maps, BF16),
            pltpu.VMEM(maps, BF16),
            pltpu.SemaphoreType.DMA((1 + chunks,)),
        ],
        raw_in=(2,),
        raw_out=(0,),
        limit=12,
    )
    block_bc, block_a = shape_of((half, rows_bc, channels), BF16), shape_of((half, 2, rows_a, channels), BF16)
    both = shape_of((half * (2 * rows_a + rows_bc), channels), BF16)
    places, kept_one, kept_two, keep_a_one, keep_a_two, send_across, send_inner = run_kernel(
        round_two,
        places,
        [keep_one, got_one, keep_two, got_two, parted(keep_a), parted(got_a)],
        [block_bc, block_bc, block_a, block_a, both, both],
        "round_two",
        5,
    )
    got_across, got_inner = across.swap(send_across, 1), inner.swap(send_inner, 1)
    vectors = [
        gain_part, shift_part, scale_a_part, shift_a_part, scale_b_part, shift_b_part, scale_c_part, shift_c_part
    ]
    width = channels // dp_count
    lines = -(-sum(vector.shape[1] for vector in vectors) // (bank_count * width))
    lines = -(-lines // LANE_ROWS) * LANE_ROWS
    bank_lines = feature_rows + 2 * channel_rows + lines
    bank_step = bank_spans(bank_lines, width, channels)[1]
    region_lines = feature_rows + 2 * channel_rows + bank_spans(joined_rows, TILE, channels)[1]
    places, bank_grad, *bank_pieces = run_kernel(
        bank_back,
        places,
        [key_value, w_key, w_value, w_bank, turned_bank, turned_memory] + vectors,
        [shape_of(bank.shape, BF16)]
        + [shape_of((bank_count // outer_count, bank_lines, width), BF16)] * outer_count,
        "bank_back",
        WINDOW,
        scratch=[
            pltpu.VMEM((bank_count, bank_lines, width), BF16),
            pltpu.VMEM((3 * keys_here, channels), BF16),
        ],
        limit=8,
    )
    places, region_parts = run_kernel(
        functools.partial(region_sums, widths),
        places,
        [group, group_branch_grad, wide_logit_grad],
        [shape_of((region_lines, channels), BF16)],
        "region_sums",
        WINDOW,
    )
    region_both = [region_parts, dp_swap(region_parts, 1)] if split else [lax.psum(region_parts, "dp")]
    if split:
        bank_parts = [bank_pieces[0]] + [outer.swap(piece, step + 1) for step, piece in enumerate(bank_pieces[1:])]
    else:
        bank_parts = [low(jnp.sum(wide(to_owners(bank_pieces[0])), axis=0, keepdims=True))]
    one_bc, half_a = shape_of((rows_bc, channels), BF16), shape_of((half, rows_a, channels), BF16)
    results = run_kernel(
        functools.partial(round_three, outer.size, split),
        places,
        [kept_one, kept_two, keep_a_one, keep_a_two, got_across, got_inner] + region_both + bank_parts,
        [one_bc] * outer.size
        + [half_a, half_a, shape_of((bank_step, channels), BF16)]
        + [
            shape_of((half * rows_a + region_lines, channels), BF16),
            shape_of((half * rows_a + bank_step, channels), BF16),
        ],
        "round_three",
        5,
    )
    places, pieces_bc = results[0], results[1 : 1 + outer.size]
    kept_a_one, kept_a_two, bank_keep, send_across, send_inner = results[1 + outer.size :]
    got_across, got_inner = across.swap(send_across, 1), inner.swap(send_inner, 1)
    got_bc = [outer.swap(piece, step + 1) for step, piece in enumerate(pieces_bc[1:])]
    row_block = shape_of((channel_rows, channels), F32)
    results = run_kernel(
        functools.partial(round_four, outer.size, split, widths),
        places,
        [pieces_bc[0], *got_bc, kept_a_one, kept_a_two, bank_keep, send_across, got_across, got_inner],
        [shape_of((rows_bc + bank_step, channels), BF16)]
        + [shape_of((rows_a, channels), BF16)] * outer.size
        + [shape_of((feature_rows, channels), F32), row_block, row_block, shape_of((joined_rows, classes), F32)],
        "round_four",
        4,
    )
    places, done, kept_a, *pieces_a = results[: 2 + outer.size]
    reduce_weight_grad, query_weight_grad, out_weight_grad, head_weight_grad = results[2 + outer.size :]
    got_a = [outer.swap(piece, step + 1) for step, piece in enumerate(pieces_a)]
    done_both = [done, across.swap(done, 1)] if split else []
    row_block = shape_of((channel_rows, channels), F32)
    places, part_a, *both = run_kernel(
        functools.partial(round_last, outer.size),
        places,
        [kept_a, *got_a, *done_both],
        [shape_of((rows_a, channels), BF16)] + [shape_of((2,) + done.shape, BF16)] * len(done_both[1:]),
        "round_last",
        2,
    )
    if split:
        done_a = lax.all_gather(part_a, "dp", axis=0, tiled=False)
        done_all = [both[0], last.swap(both[0], 1)]
    else:
        done_a = lax.psum(part_a, "dp")
        bank_all = lax.all_gather(done[rows_bc:], "dp", axis=0, tiled=False)
        done_all = [lax.psum(done[:rows_bc], "dp")] + [bank_all[place] for place in range(dp_count)]
    info = (rows_b, groups_c * LANE_ROWS, feature_rows, channel_rows, bank_lines, split)
    results = run_kernel(
        functools.partial(finish, info),
        places,
        [done_a, *done_all],
        [shape_of(conv_a.shape, F32), shape_of(conv_b.shape, F32), shape_of(conv_c.shape, F32)]
        + [shape_of((feature_rows, channels), F32), row_block, row_block]
        + [shape_of((1, vector.shape[1] // bank_count), F32) for vector in vectors],
        "finish",
        3,
    )
    places, conv_a_grad, conv_b_grad, conv_c_grad, bank_weight_grad, key_weight_grad, value_weight_grad = results[:7]
    small = [value.reshape(-1) for value in results[7:]]
    gain_grad, shift_grad = small[:2]
    scale_a_grad, shift_a_grad, scale_b_grad, shift_b_grad, scale_c_grad, shift_c_grad = small[2:]
    return (
        logits_out,
        map_grad,
        bank_grad,
        conv_a_grad,
        scale_a_grad,
        shift_a_grad,
        conv_b_grad,
        scale_b_grad,
        shift_b_grad,
        conv_c_grad,
        scale_c_grad,
        shift_c_grad,
        reduce_weight_grad,
        bank_weight_grad,
        query_weight_grad,
        key_weight_grad,
        value_weight_grad,
        gain_grad,
        shift_grad,
        out_weight_grad,
        head_weight_grad,
    )


def solution(mesh):
    in_specs = (
        P(("dp", "bank"), None),
        P("bank", None),
        P("dp"),
        P(("dp", "bank"), None),
        P(("dp", "bank"), None),
        P("bank", None),
        P(),
        P(),
        P("bank", None),
        P(),
        P(),
        P("bank", None),
        P(),
        P(),
        P(),
        P(),
        P(),
        P(),
        P(),
        P(),
        P(),
        P(),
        P(),
        P("dp", None),
    )
    out_specs = (
        P(("dp", "bank"), None),
        P(("dp", "bank"), None),
        P("bank", None),
        P("bank", None),
        P("bank"),
        P("bank"),
        P("bank", None),
        P("bank"),
        P("bank"),
        P("bank", None),
        P("bank"),
        P("bank"),
        P("bank", None),
        P("bank", None),
        P("bank", None),
        P("bank", None),
        P("bank", None),
        P("bank"),
        P("bank"),
        P("bank", None),
        P("bank", None),
    )
    return jax.shard_map(body, mesh=mesh, in_specs=in_specs, out_specs=out_specs, check_vma=False)
```

```python
import functools

import jax
import jax.numpy as jnp
from jax import lax
from jax.experimental import pallas as pl
from jax.experimental.pallas import tpu as pltpu
from jax.sharding import PartitionSpec as P

FRAMES = 4
SIDE = 8
LANE_ROWS = 16
TILE = 128
ROOT = 0.7978845608028654
CUBIC = 0.044715

epsilon = 1e-05
masked_score = -1e30
places = [(-1, -1), (-1, 0), (-1, 1), (0, -1), (0, 0), (0, 1), (1, -1), (1, 0), (1, 1)]


def product(left, right):
    return jnp.dot(left, right, preferred_element_type=jnp.float32)


def low(value):
    return value.astype(jnp.bfloat16)


def wide(value):
    return value.astype(jnp.float32)


class SubAxis:
    def __init__(self, name, size, stride):
        self.name, self.size, self.stride = name, size, stride

    def place(self):
        return lax.rem(lax.axis_index(self.name) // self.stride, self.size)

    def swap(self, value, step):
        count = lax.axis_size(self.name)
        pairs = [(i, i ^ (step * self.stride)) for i in range(count)]
        return lax.ppermute(value, self.name, pairs)


def block_axes(split, dp_count, bank_count):
    if split:
        return (
            SubAxis("bank", bank_count // 2, 2),
            SubAxis("bank", 2, 1),
            SubAxis("dp", dp_count // 2, 2),
            SubAxis("dp", 2, 1),
        )
    return (
        SubAxis("bank", bank_count // 8, 8),
        SubAxis("bank", 2, 4),
        SubAxis("bank", 2, 2),
        SubAxis("bank", 2, 1),
    )


def gather_blocks(own, axes, places, steps):
    outer, inner, across, last = axes
    blocks = [own] + [outer.swap(own, step) for step in range(1, outer.size)]
    places = steps[0](places)
    *blocks, places = lax.optimization_barrier((*blocks, places))
    blocks = jnp.stack(blocks)
    half = outer.size // 2
    first, second = blocks[:half], blocks[half:]
    got_first, got_second = across.swap(first, 1), inner.swap(second, 1)
    places = steps[1](places)
    first, got_first, second, got_second, places = lax.optimization_barrier((first, got_first, second, got_second, places))
    first, second = jnp.concatenate([first, got_first]), jnp.concatenate([second, got_second])
    got_first, got_second = inner.swap(first, 1), across.swap(second, 1)
    places = steps[2](places)
    first, got_first, second, got_second, places = lax.optimization_barrier((first, got_first, second, got_second, places))
    near = jnp.concatenate([first, got_first, second, got_second])
    return places, [near, last.swap(near, 1)]


def to_owners(value):
    return lax.all_to_all(value, "bank", split_axis=0, concat_axis=0, tiled=True)


def to_group(value):
    count = lax.axis_size("bank")
    return to_owners(jnp.broadcast_to(value[None], (count,) + value.shape))


def params(mib):
    return pltpu.CompilerParams(vmem_limit_bytes=mib * 1024 * 1024)


def gelu_of(x):
    return 0.5 * x * (1.0 + jnp.tanh(ROOT * (x + CUBIC * x * x * x)))


def gelu_slope(x):
    square = x * x
    bent = jnp.tanh(ROOT * x * (1.0 + CUBIC * square))
    return 0.5 * (1.0 + bent) + 0.5 * ROOT * x * (1.0 - bent * bent) * (1.0 + 3.0 * CUBIC * square)


def by_rows(count, step, work):
    def one(number, carry):
        work(pl.ds(pl.multiple_of(number * step, step), step))
        return carry

    lax.fori_loop(0, count // step, one, 0)


def dot_tn(left, right):
    return lax.dot_general(
        left, right, (((0,), (0,)), ((), ())), preferred_element_type=jnp.float32
    )


def dot_nt(left, right):
    return lax.dot_general(
        left, right, (((1,), (1,)), ((), ())), preferred_element_type=jnp.float32
    )


def in_rows(value, step):
    if step == 0:
        return value
    sites, width = value.shape
    tall = value.reshape(sites // (SIDE * SIDE), SIDE, SIDE, width)
    edge = jnp.zeros_like(tall[:, :1])
    if step > 0:
        tall = jnp.concatenate([tall[:, 1:], edge], axis=1)
    else:
        tall = jnp.concatenate([edge, tall[:, :-1]], axis=1)
    return tall.reshape(sites, width)


def in_columns(value, step):
    if step == 0:
        return value
    sites = value.shape[0]
    turned = pltpu.roll(value, (-step) % sites, 0)
    column = lax.broadcasted_iota(jnp.int32, value.shape, 0) % SIDE
    keep = column != (SIDE - 1 if step > 0 else 0)
    return jnp.where(keep, turned, 0.0)


def fetch(source, target, sems, first, groups):
    copies = []
    for block in range(source.shape[0]):
        copies.append(
            pltpu.make_async_copy(
                source.at[block, pl.ds(first, groups)],
                target.at[pl.ds(block * groups, groups)],
                sems.at[block],
            )
        )
    return copies


def fetch_columns(source, target, sems, first, groups):
    return [
        pltpu.make_async_copy(
            source.at[block, pl.ds(first, groups)], target.at[:, block], sems.at[block]
        )
        for block in range(source.shape[0])
    ]


def start_all(copies):
    for copy in copies:
        copy.start()
    return copies


def wait_all(copies):
    for copy in copies:
        copy.wait()


def gathered_spot(places_ref, number, far):
    second, rest = divmod(number, 8)
    high, low_bits = divmod(rest, 4)
    middle, step = divmod(low_bits, 2)
    across, inner = (high, middle) if second else (middle, high)
    outer = (places_ref[2] ^ (2 * second + step)) * 2 + (places_ref[1] ^ inner)
    return (outer * 2 + (places_ref[0] ^ across)) * 2 + (places_ref[3] ^ far)


def first_conv(places_ref, fm_ref, *refs):
    sources, refs = refs[:-9], refs[-9:]
    scale_ref, shift_ref, pre_out_ref, act_ref, weight_out_ref, weight, pre_ref, sems, out_sems = refs
    sites, features = fm_ref.shape
    channels = act_ref.shape[1]
    groups = sources[0].shape[1]
    copies = []
    for far, source in enumerate(sources):
        for number in range(source.shape[0]):
            block = gathered_spot(places_ref, number, far) if len(sources) > 1 else number
            target = weight.at[pl.ds(block * groups, groups)]
            copies.append(pltpu.make_async_copy(source.at[number], target, sems.at[len(copies)]))
    start_all(copies)
    clip = FRAMES * SIDE * SIDE
    frame = SIDE * SIDE
    wait_all(copies)
    out = start_all([pltpu.make_async_copy(weight, weight_out_ref, out_sems.at[1])])

    def tap(number):
        begin = number * features // LANE_ROWS
        return weight[begin : begin + features // LANE_ROWS].reshape(features, channels)

    before = tap(0)
    for start in range(0, sites, clip):
        pre_ref[start : start + frame] = jnp.zeros((frame, channels), jnp.float32)
        pre_ref[start + frame : start + clip] = product(fm_ref[start : start + clip - frame], before)
    pre_ref[...] += product(fm_ref[...], tap(1))
    after = tap(2)
    for start in range(0, sites, clip):
        pre_ref[start : start + clip - frame] += product(fm_ref[start + frame : start + clip], after)

    def finish(rows):
        act_ref[rows] = low(gelu_of(pre_ref[rows] * scale_ref[...] + shift_ref[...]))

    out += start_all([pltpu.make_async_copy(pre_ref, pre_out_ref, out_sems.at[0])])
    by_rows(sites, 128, finish)
    wait_all(out)


def later_convs(
    act_a_ref, fm_ref, packed_ref, scale_b_ref, shift_b_ref, scale_c_ref, shift_c_ref, pool_ref, w_reduce_ref, w_query_ref,
    pre_b_out_ref, act_b_out_ref, pre_c_ref, regions_out_ref, reduced_out_ref, queries_ref,
    weight_b, weight_c, out_low, held_map, held_pre, held_reduce, pre_b_ref, act_b_ref, regions_ref, reduced_ref, sems_b, sems_c, sems,
):
    sites, channels = act_a_ref.shape
    blocks = packed_ref.shape[0]
    groups_b = weight_b.shape[0] // blocks
    groups_c = weight_c.shape[0]
    groups_a = packed_ref.shape[1] - groups_b - groups_c
    copies_b = start_all(fetch(packed_ref, weight_b, sems_b, groups_a, groups_b))
    copies_c = start_all(fetch_columns(packed_ref, weight_c, sems_c, groups_a + groups_b, groups_c))
    others = start_all(
        [
            pltpu.make_async_copy(fm_ref, held_map, sems.at[0]),
            pltpu.make_async_copy(w_reduce_ref, held_reduce, sems.at[1]),
        ]
    )
    act_a = act_a_ref[...]
    block_rows = groups_b * LANE_ROWS
    sums = {-1: None, 0: None, 1: None}
    waited = 0
    for number, (rise, slide) in enumerate(places):
        while waited < len(copies_b) and waited * block_rows < (number + 1) * channels:
            copies_b[waited].wait()
            waited += 1
        begin = number * channels // LANE_ROWS
        tap = weight_b[begin : begin + channels // LANE_ROWS].reshape(channels, channels)
        part = in_rows(product(act_a, tap), rise)
        sums[slide] = part if sums[slide] is None else sums[slide] + part
    pre_b_ref[...] = sums[0] + in_columns(sums[1], 1) + in_columns(sums[-1], -1)

    outs = start_all([pltpu.make_async_copy(pre_b_ref, pre_b_out_ref, sems.at[2 + groups_c])])

    def finish(rows):
        act_b_ref[rows] = low(gelu_of(pre_b_ref[rows] * scale_b_ref[...] + shift_b_ref[...]))

    by_rows(sites, 128, finish)
    outs += start_all([pltpu.make_async_copy(act_b_ref, act_b_out_ref, sems.at[3 + groups_c])])
    wait_all(copies_c + others)
    reduced_ref[...] = jnp.zeros_like(reduced_ref)

    def chunk(number, carry):
        columns = pl.ds(pl.multiple_of(number * channels, channels), channels)
        held_pre[:, columns] = product(act_b_ref[...], weight_c[number].reshape(channels, channels))
        pltpu.make_async_copy(held_pre.at[:, columns], pre_c_ref.at[:, columns], sems.at[2 + number]).start()

        def finish_c(rows):
            linear = wide(held_map[rows, columns]) + held_pre[rows, columns] * scale_c_ref[:, columns] + shift_c_ref[:, columns]
            out_low[rows] = low(gelu_of(linear))

        by_rows(sites, 128, finish_c)
        part = low(product(pool_ref[...], out_low[...]))
        regions_ref[:, columns] = part
        reduced_ref[...] += product(part, held_reduce[columns])
        return carry

    lax.fori_loop(0, groups_c, chunk, 0)
    outs += start_all(
        [
            pltpu.make_async_copy(regions_ref, regions_out_ref, sems.at[4 + groups_c]),
            pltpu.make_async_copy(reduced_ref, reduced_out_ref, sems.at[5 + groups_c]),
        ]
    )
    queries = low(product(low(reduced_ref[...]), w_query_ref[...]))
    for place in range(queries_ref.shape[0]):
        queries_ref[place] = queries
    for number in range(groups_c):
        columns = pl.ds(number * channels, channels)
        outs.append(pltpu.make_async_copy(held_pre.at[:, columns], pre_c_ref.at[:, columns], sems.at[2 + number]))
    wait_all(outs)


def column_tile(columns, shape):
    lane = lax.broadcasted_iota(jnp.int32, shape, len(shape) - 1)
    tile = jnp.zeros(shape, jnp.float32)
    for number, column in enumerate(columns):
        rest = column
        for third in range(3):
            piece = wide(low(rest))
            tile = jnp.where(lane == 3 * number + third, piece, tile)
            rest = rest - piece
    return low(tile)


def from_tile(tile, number):
    lane = lax.broadcasted_iota(jnp.int32, tile.shape, tile.ndim - 1)
    picked = jnp.where((lane >= 3 * number) & (lane < 3 * number + 3), wide(tile), 0.0)
    return jnp.sum(picked, axis=-1, keepdims=True)


def attend(half_span, places_ref, queries_ref, keys_ref, values_ref, time_ref, message_ref, scores_ref):
    channels = queries_ref.shape[1]
    positions = places_ref[5] + lax.broadcasted_iota(jnp.int32, scores_ref.shape, 1)
    visible = jnp.abs(time_ref[...] - positions) <= half_span
    scores = dot_nt(queries_ref[...], keys_ref[...]) * (channels ** (-0.5))
    scores = jnp.where(visible, scores, masked_score)
    scores_ref[...] = scores
    top = jnp.max(scores, axis=1, keepdims=True)
    weights = jnp.exp(scores - top)
    total = jnp.sum(weights, axis=1, keepdims=True)
    message_ref[:, :channels] = low(product(low(weights), values_ref[...]))
    message_ref[:, channels:] = column_tile([top, total], (scores.shape[0], TILE))


def merge_rows(places_ref, arrived_ref, hidden_grad_ref, gain_ref, shift_ref, message_ref, hidden_ref, gain_out_ref, shift_out_ref):
    count, own, packed = arrived_ref.shape
    channels = hidden_grad_ref.shape[1]
    tops = from_tile(arrived_ref[:, :, channels:], 0)
    totals = from_tile(arrived_ref[:, :, channels:], 1)
    top = jnp.max(tops, axis=0)
    factors = jnp.exp(tops - top[None])
    total = jnp.sum(factors * totals, axis=0)
    numer = jnp.sum(factors * wide(arrived_ref[:, :, :channels]), axis=0)
    attended = numer / total
    centred = attended - jnp.mean(attended, axis=1, keepdims=True)
    spread = lax.rsqrt(jnp.mean(centred * centred, axis=1, keepdims=True) + epsilon)
    unit = centred * spread
    normed = unit * gain_ref[...] + shift_ref[...]
    hidden_ref[...] = low(gelu_of(normed))
    normed_grad = hidden_grad_ref[...] * gelu_slope(normed)
    gain_out_ref[...] = jnp.sum(normed_grad * unit, axis=0, keepdims=True)
    shift_out_ref[...] = jnp.sum(normed_grad, axis=0, keepdims=True)
    unit_grad = normed_grad * gain_ref[...]
    attended_grad = spread * (
        unit_grad
        - jnp.mean(unit_grad, axis=1, keepdims=True)
        - unit * jnp.mean(unit_grad * unit, axis=1, keepdims=True)
    )
    centre = jnp.sum(attended_grad * attended, axis=1, keepdims=True) / total
    numer_grad = low(attended_grad / total)
    tile = column_tile([top, centre], (own, TILE))
    for place in range(count):
        message_ref[place, :, :channels] = numer_grad
        message_ref[place, :, channels:] = tile


def attend_back(places_ref, arrived_ref, scores_ref, keys_ref, values_ref, part_ref, score_grad_ref, weights_ref):
    channels = keys_ref.shape[1]
    top = from_tile(arrived_ref[:, channels:], 0)
    centre = from_tile(arrived_ref[:, channels:], 1)
    weights = jnp.exp(scores_ref[...] - top)
    weights_ref[...] = low(weights)
    prob_grad = dot_nt(arrived_ref[:, :channels], values_ref[...])
    score_grad = low(weights * (prob_grad - centre) * (channels ** (-0.5)))
    score_grad_ref[...] = score_grad
    part_ref[...] = low(product(score_grad, keys_ref[...]))


def half_of(place_ref, bit):
    return jnp.where(place_ref[3] == bit, 1, 0)


def fold(value):
    return jnp.sum(value.reshape(value.shape[0] // 8, 8, value.shape[1]), axis=0)


def region_back(
    places_ref, arrived_ref, joined_grad_ref, w_query_ref, w_reduce_ref, query_grad_ref, reduced_grad_ref, regions_grad_ref
):
    features = regions_grad_ref.shape[1]
    query_grad = low(jnp.sum(wide(arrived_ref[...]), axis=0))
    query_grad_ref[...] = query_grad
    reduced_grad = low(joined_grad_ref[:, features:] + dot_nt(query_grad, w_query_ref[...]))
    reduced_grad_ref[...] = reduced_grad
    regions_grad_ref[...] = low(joined_grad_ref[:, :features] + dot_nt(reduced_grad, w_reduce_ref[...]))


def hand_out(buffer, send_ref, keep_ref, sems):
    return start_all(
        [
            pltpu.make_async_copy(buffer.at[number], target, sems.at[number])
            for number, target in enumerate((send_ref, keep_ref))
        ]
    )


def store_rows(buffer, place_ref, value, first, rows):
    at, end = first, first + value.shape[0]
    while at < end:
        block, offset = divmod(at, rows)
        count = min(rows - offset, end - at)
        buffer[half_of(place_ref, block % 2), block // 2, offset : offset + count] = value[at - first : at - first + count]
        at += count


def slopes_outer(places_ref, scale_ref, shift_ref, pre_ref, map_ref, out_ref, held_pre, held_map, held_out, sems):
    sites, features = held_map.shape
    chunks = sems.shape[1]
    width = features // chunks

    def part_of(source, target, number, row):
        columns = pl.ds(pl.multiple_of(number * width, width), width)
        return pltpu.make_async_copy(source.at[:, columns], target.at[:, columns], sems.at[row, number])

    for number in range(chunks):
        start_all([part_of(pre_ref, held_pre, number, 0), part_of(map_ref, held_map, number, 1)])

    def chunk(number, carry):
        columns = pl.ds(pl.multiple_of(number * width, width), width)
        wait_all([part_of(pre_ref, held_pre, number, 0), part_of(map_ref, held_map, number, 1)])

        def one(rows):
            linear = wide(held_map[rows, columns]) + held_pre[rows, columns] * scale_ref[:, columns] + shift_ref[:, columns]
            held_out[rows, columns] = low(gelu_slope(linear))

        by_rows(sites, 128, one)
        part_of(held_out, out_ref, number, 2).start()
        return carry

    lax.fori_loop(0, chunks, chunk, 0)
    wait_all([part_of(held_out, out_ref, number, 2) for number in range(chunks)])


def slope_back(upstream_ref, pre_ref, scale_ref, shift_ref, out_ref, scale_out_ref, shift_out_ref):
    sites, channels = pre_ref.shape

    def one(step, sums):
        rows = pl.ds(pl.multiple_of(step * 128, 128), 128)
        pre = pre_ref[rows]
        grad = upstream_ref[rows] * gelu_slope(pre * scale_ref[...] + shift_ref[...])
        out_ref[rows] = low(grad * scale_ref[...]).astype(out_ref.dtype)
        return sums[0] + fold(grad * pre), sums[1] + fold(grad)

    zero = jnp.zeros((8, channels), jnp.float32)
    scale_sum, shift_sum = lax.fori_loop(0, sites // 128, one, (zero, zero))
    scale_out_ref[...] = jnp.sum(scale_sum, axis=0, keepdims=True)
    shift_out_ref[...] = jnp.sum(shift_sum, axis=0, keepdims=True)


def later_back(
    groups_a, groups_b, place_ref, regions_grad_ref, pool_ref, scale_ref, scales_ref, pre_c_ref, slope_ref, act_b_ref,
    pre_b_ref, act_a_ref, pre_a_ref, packed_ref,
    send_ref, keep_ref, lin_c_grad_ref, pre_a_grad_ref, scale_c_out_ref, shift_c_out_ref, scale_b_out_ref, shift_b_out_ref,
    scale_a_out_ref, shift_a_out_ref,
    weight_b, weight_c, buffer, out_grad, pre_grad, turned, act_grad, wide_grad,
    held_pre_c, held_map, held_act_b, held_pre_b, held_act_a, held_pre_a, held_lin, sems_b, sems_c, out_sems, sems,
):
    sites, features = held_map.shape
    channels = held_act_b.shape[1]
    chunks, blocks = weight_c.shape[0], weight_c.shape[1]
    rows_b = groups_b * LANE_ROWS

    def part_of(source, target, number, sem):
        columns = pl.ds(pl.multiple_of(number * channels, channels), channels)
        return pltpu.make_async_copy(source.at[:, columns], target.at[:, columns], sems.at[sem + number])

    early = start_all([pltpu.make_async_copy(act_b_ref, held_act_b, sems.at[0])])
    copies_c = start_all(fetch_columns(packed_ref, weight_c, sems_c, groups_a + groups_b, chunks))
    for number in range(chunks):
        part_of(pre_c_ref, held_pre_c, number, 4).start()
        part_of(slope_ref, held_map, number, 4 + chunks).start()
    late = start_all(
        [
            pltpu.make_async_copy(pre_b_ref, held_pre_b, sems.at[1]),
            pltpu.make_async_copy(act_a_ref, held_act_a, sems.at[2]),
            pltpu.make_async_copy(pre_a_ref, held_pre_a, sems.at[3]),
        ]
    )
    copies_b = start_all(fetch(packed_ref, weight_b, sems_b, groups_a, groups_b))
    scale_b_ref, shift_b_ref, scale_a_ref, shift_a_ref = [scales_ref.at[pl.ds(number, 1)] for number in range(4)]
    act_grad[...] = jnp.zeros_like(act_grad)
    wait_all(early)
    turned[...] = held_act_b[...].T
    wait_all(copies_c)

    def chunk(number, carry):
        columns = pl.ds(pl.multiple_of(number * channels, channels), channels)
        out_grad[...] = dot_tn(pool_ref[...], regions_grad_ref[:, columns])
        part_of(pre_c_ref, held_pre_c, number, 4).wait()
        part_of(slope_ref, held_map, number, 4 + chunks).wait()

        def one(step, sums):
            rows = pl.ds(pl.multiple_of(step * 128, 128), 128)
            pre = held_pre_c[rows, columns]
            scale = scale_ref[:, columns]
            grad = out_grad[rows] * wide(held_map[rows, columns])
            held_lin[rows, columns] = low(grad)
            pre_grad[rows] = low(grad * scale)
            return sums[0] + fold(grad * pre), sums[1] + fold(grad)

        zero = jnp.zeros((8, channels), jnp.float32)
        scale_sum, shift_sum = lax.fori_loop(0, sites // 128, one, (zero, zero))
        part_of(held_lin, lin_c_grad_ref, number, 4 + 2 * chunks).start()
        scale_c_out_ref[:, columns] = jnp.sum(scale_sum, axis=0, keepdims=True)
        shift_c_out_ref[:, columns] = jnp.sum(shift_sum, axis=0, keepdims=True)
        part = low(product(turned[...], pre_grad[...])).reshape(blocks // 2, 2, LANE_ROWS, channels)
        rows = pl.ds(pl.multiple_of(rows_b + number * LANE_ROWS, LANE_ROWS), LANE_ROWS)
        for bit in range(2):
            buffer[half_of(place_ref, bit), :, rows] = part[:, bit]
        act_grad[...] += dot_nt(pre_grad[...], weight_c[number].reshape(channels, channels))
        return carry

    lax.fori_loop(0, chunks, chunk, 0)
    wait_all(late)
    slope_back(act_grad, held_pre_b, scale_b_ref, shift_b_ref, wide_grad, scale_b_out_ref, shift_b_out_ref)
    turned[...] = held_act_a[...].T
    wait_all(copies_b)
    for slide in (-1, 0, 1):
        slid = in_columns(wide_grad[...], -slide)
        for number, place in enumerate(places):
            if place[1] != slide:
                continue
            moved = low(in_rows(slid, -place[0]))
            store_rows(buffer, place_ref, low(product(turned[...], moved)), number * channels, rows_b)
            begin = number * channels // LANE_ROWS
            tap = weight_b[begin : begin + channels // LANE_ROWS].reshape(channels, channels)
            part = dot_nt(moved, tap)
            if slide == -1 and place[0] == -1:
                act_grad[...] = part
            else:
                act_grad[...] += part
    copies = hand_out(buffer, send_ref, keep_ref, out_sems)
    slope_back(act_grad, held_pre_a, scale_a_ref, shift_a_ref, pre_a_grad_ref, scale_a_out_ref, shift_a_out_ref)
    wait_all(copies)
    for number in range(chunks):
        part_of(held_lin, lin_c_grad_ref, number, 4 + 2 * chunks).wait()


def by_frames(grad, offset):
    if offset == 0:
        return grad
    sites, width = grad.shape
    tall = grad.reshape(sites // (FRAMES * SIDE * SIDE), FRAMES, SIDE * SIDE, width)
    edge = jnp.zeros_like(tall[:, :1])
    if offset > 0:
        tall = jnp.concatenate([edge, tall[:, :-1]], axis=1)
    else:
        tall = jnp.concatenate([tall[:, 1:], edge], axis=1)
    return tall.reshape(sites, width)


def first_back(place_ref, grad_ref, own_ref, got_ref, turned_ref, send_ref, keep_ref, sum_ref, buffer, held, sems, out_sems):
    features, sites = held.shape
    channels = grad_ref.shape[1]
    copies = [
        pltpu.make_async_copy(turned_ref.at[pl.ds(start, channels)], held.at[pl.ds(start, channels)], sems.at[start // channels])
        for start in range(0, features, channels)
    ]
    start_all(copies)
    sum_ref[...] = add_low(own_ref[...], got_ref[...])
    for tap in range(3):
        moved = by_frames(grad_ref[...], tap - 1)
        for start in range(0, features, channels):
            if tap == 0:
                copies[start // channels].wait()
            part = low(product(held[start : start + channels], moved))
            store_rows(buffer, place_ref, part, tap * features + start, buffer.shape[2])
    wait_all(hand_out(buffer, send_ref, keep_ref, out_sems))


def map_back(places_ref, grad_ref, weight_ref, lin_c_grad_ref, out_ref, moved, held_lin, held_out, sems):
    sites, features = held_out.shape
    channels = grad_ref.shape[1]
    copies = start_all([pltpu.make_async_copy(lin_c_grad_ref, held_lin, sems.at[0])])
    for tap in range(3):
        moved[tap] = by_frames(grad_ref[...], tap - 1)
    wait_all(copies)
    groups = channels // LANE_ROWS

    def chunk(number, carry):
        columns = pl.ds(pl.multiple_of(number * channels, channels), channels)
        total = wide(held_lin[:, columns])
        for tap in range(3):
            rows = pl.ds(tap * (features // LANE_ROWS) + number * groups, groups)
            total = total + dot_nt(moved[tap], weight_ref[rows].reshape(channels, channels))
        held_out[:, columns] = low(total)
        pltpu.make_async_copy(held_out.at[:, columns], out_ref.at[:, columns], sems.at[1 + number]).start()
        return carry

    lax.fori_loop(0, features // channels, chunk, 0)
    copies = []
    for number in range(features // channels):
        columns = pl.ds(number * channels, channels)
        copies.append(pltpu.make_async_copy(held_out.at[:, columns], out_ref.at[:, columns], sems.at[1 + number]))
    wait_all(copies)


COST = 1.5e10
WINDOW = 0.1
FIRST_LIMIT = 52
F32 = jnp.float32
BF16 = jnp.bfloat16
ANY = pl.BlockSpec(memory_space=pl.ANY)
SCALAR = pl.BlockSpec(memory_space=pltpu.SMEM)
HELD = pl.BlockSpec(memory_space=pltpu.VMEM)


def shape_of(dims, kind):
    return jax.ShapeDtypeStruct(dims, kind)


def add_low(left, right):
    return left + right


class Blocks:
    def __init__(self, ref, first, dims, rows):
        self.ref, self.first, self.dims, self.rows = ref, first, dims, rows

    @property
    def shape(self):
        return self.dims

    def span(self, index):
        index = index if isinstance(index, tuple) else (index,)
        flat = 0
        for place, size in zip(index, self.dims):
            flat = flat * size + place
        return pl.ds(pl.multiple_of(self.first + flat * self.rows, LANE_ROWS), self.rows)

    def __getitem__(self, index):
        return self.ref[self.span(index)]

    def __setitem__(self, index, value):
        self.ref[self.span(index)] = value


def after_last(places_ref, keep_ref, got_ref, keep_one, send_one, keep_two, send_two):
    half = keep_ref.shape[0] // 2
    across, inner = places_ref[0], places_ref[1]

    def one(number, carry):
        for place in range(2):
            keep_one[number, place] = add_low(keep_ref[number, place, across], got_ref[number, place, across])
            send_one[number, place] = add_low(keep_ref[number, place, 1 - across], got_ref[number, place, 1 - across])
            later = number + half
            keep_two[number, place] = add_low(keep_ref[later, inner, place], got_ref[later, inner, place])
            send_two[number, place] = add_low(keep_ref[later, 1 - inner, place], got_ref[later, 1 - inner, place])
        return carry

    lax.fori_loop(0, half, one, 0)


def after_cross(places_ref, keep_one, got_one, keep_two, got_two, kept_one, send_one, kept_two, send_two):
    across, inner = places_ref[0], places_ref[1]

    def one(number, carry):
        kept_one[number] = add_low(keep_one[number, inner], got_one[number, inner])
        send_one[number] = add_low(keep_one[number, 1 - inner], got_one[number, 1 - inner])
        kept_two[number] = add_low(keep_two[number, across], got_two[number, across])
        send_two[number] = add_low(keep_two[number, 1 - across], got_two[number, 1 - across])
        return carry

    lax.fori_loop(0, keep_two.shape[0], one, 0)


def after_plane(places_ref, keep_one, got_one, keep_two, got_two, kept_ref, sends):
    half = keep_one.shape[0]
    outer = places_ref[2]

    def block(place, target):
        @pl.when(place < half)
        def _():
            target[...] = add_low(keep_one[lax.rem(place, half)], got_one[lax.rem(place, half)])

        @pl.when(place >= half)
        def _():
            target[...] = add_low(keep_two[lax.rem(place, half)], got_two[lax.rem(place, half)])

    block(outer, kept_ref)
    for step, target in enumerate(sends):
        block(outer ^ (step + 1), target)


def total_of(refs):
    total = wide(refs[0][...])
    for ref in refs[1:]:
        total = total + wide(ref[...])
    return total


def kept_blocks(ref, half, rows, rows_a):
    pairs = 2 * half * rows_a
    return (
        Blocks(ref, 0, (half, 2), rows_a),
        Blocks(ref, pairs, (half, 2), rows_a),
        Blocks(ref, 2 * pairs, (half,), rows),
        Blocks(ref, 2 * pairs + half * rows, (half,), rows),
    )


def round_two(
    places_ref, keep_one, got_one, keep_two, got_two, keep_a, got_a, kept_ref, across_ref, inner_ref
):
    half, rows, rows_a = keep_one.shape[0], keep_one.shape[2], keep_a.shape[3]
    below = 2 * half * rows_a
    keep_a_one, keep_a_two, kept_one, kept_two = kept_blocks(kept_ref, half, rows, rows_a)
    after_last(
        places_ref, keep_a, got_a, keep_a_one, Blocks(across_ref, 0, (half, 2), rows_a), keep_a_two,
        Blocks(inner_ref, 0, (half, 2), rows_a),
    )
    after_cross(
        places_ref, keep_one, got_one, keep_two, got_two, kept_one, Blocks(inner_ref, below, (half,), rows), kept_two,
        Blocks(across_ref, below, (half,), rows),
    )


def bank_spans(lines, width, channels):
    groups = channels // width
    step = -(-lines // (groups * LANE_ROWS)) * LANE_ROWS
    return [(first, min(first + step, lines)) for first in range(0, lines, step)], step


def store_narrow(target, first, value, channels):
    lines, width = value.shape
    spans, step = bank_spans(lines, width, channels)
    target[first : first + step] = jnp.zeros((step, channels), BF16)
    for number, (begin, end) in enumerate(spans):
        target[first : first + end - begin, number * width : (number + 1) * width] = value[begin:end]


def load_narrow(value, first, lines, width):
    spans, _ = bank_spans(lines, width, value.shape[1])
    pieces = [
        value[first : first + end - begin, number * width : (number + 1) * width]
        for number, (begin, end) in enumerate(spans)
    ]
    return jnp.concatenate(pieces, axis=0)


def round_three(sizes, count, split, places_ref, held_ref, got_across, got_inner, *refs):
    half, rows, rows_a = sizes
    region_refs, refs = (refs[:2], refs[2:]) if split else (refs[:1], refs[1:])
    bank_refs, refs = (refs[:count], refs[count:]) if split else (refs[:1], refs[1:])
    kept_ref, across_ref, inner_ref, *sends = refs
    channels = kept_ref.shape[1]
    below = 2 * half * rows_a
    keep_a_one, keep_a_two, kept_one, kept_two = kept_blocks(held_ref, half, rows, rows_a)
    after_plane(
        places_ref, kept_one, Blocks(got_inner, below, (half,), rows), kept_two, Blocks(got_across, below, (half,), rows),
        kept_ref.at[pl.ds(0, rows)], sends,
    )
    after_cross(
        places_ref, keep_a_one, Blocks(got_across, 0, (half, 2), rows_a), keep_a_two,
        Blocks(got_inner, 0, (half, 2), rows_a), Blocks(kept_ref, rows, (half,), rows_a),
        Blocks(inner_ref, 0, (half,), rows_a), Blocks(kept_ref, rows + half * rows_a, (half,), rows_a),
        Blocks(across_ref, 0, (half,), rows_a),
    )
    across_ref[half * rows_a :] = low(total_of(region_refs))
    inner = places_ref[7] if split else 0
    keep = total_of([ref.at[inner] for ref in bank_refs])
    at = rows + 2 * half * rows_a
    store_narrow(kept_ref, at, low(keep), channels)
    if split:
        send = total_of([ref.at[1 - inner] for ref in bank_refs])
        store_narrow(inner_ref, half * rows_a, low(send), channels)
    else:
        inner_ref[half * rows_a :] = kept_ref[at:]


def round_four(sizes, count, split, widths, places_ref, held_ref, *refs):
    half, rows, rows_a = sizes
    plane_refs, refs = [held_ref.at[pl.ds(0, rows)], *refs[: count - 1]], refs[count - 1 :]
    across_ref, got_across, got_inner, done_ref, kept_a_ref = refs[:5]
    sends, (reduce_ref, query_ref, out_ref, head_ref) = refs[5 : 4 + count], refs[4 + count :]
    kept_a_one = Blocks(held_ref, rows, (half,), rows_a)
    kept_a_two = Blocks(held_ref, rows + half * rows_a, (half,), rows_a)
    bank_keep = held_ref[rows + 2 * half * rows_a :]
    below = half * rows_a
    after_plane(
        places_ref, kept_a_one, Blocks(got_inner, 0, (half,), rows_a), kept_a_two,
        Blocks(got_across, 0, (half,), rows_a), kept_a_ref, sends,
    )
    done_ref[:rows] = low(total_of(plane_refs))
    done_ref[rows:] = add_low(bank_keep, got_inner[below:]) if split else bank_keep
    region = wide(across_ref[below:]) + wide(got_across[below:]) if split else wide(across_ref[below:])
    _, _, feature_rows, channel_rows, _, joined_rows = widths
    reduce_ref[...] = region[:feature_rows]
    query_ref[...] = region[feature_rows : feature_rows + channel_rows]
    out_ref[...] = region[feature_rows + channel_rows : feature_rows + 2 * channel_rows]
    head = load_narrow(region, feature_rows + 2 * channel_rows, joined_rows, TILE)
    head_ref[...] = head[:, : head_ref.shape[1]]


def round_last(count, places_ref, *refs):
    part_ref, both = refs[-1 if len(refs) == count + 1 else -2], refs[-1]
    part_ref[...] = low(total_of(refs[:count]))
    if len(refs) > count + 1:
        for number, ref in enumerate(refs[count : count + 2]):
            both[number] = ref[...]


def sum_swap(places_ref, *refs):
    refs[-1][...] = low(total_of(refs[:-1]))


def front_pack(groups_a, groups_b, places_ref, conv_a_ref, conv_b_ref, conv_c_ref, own_a_ref, own_ref, sems):
    place = places_ref[9]
    chunks = own_ref.shape[0] - groups_b
    channels = own_ref.shape[2]
    copies = [
        pltpu.make_async_copy(conv_b_ref.at[pl.ds(place * groups_b, groups_b)], own_ref.at[pl.ds(0, groups_b)], sems.at[0]),
        pltpu.make_async_copy(conv_a_ref.at[pl.ds(place * groups_a, groups_a)], own_a_ref, sems.at[1]),
    ]
    for chunk in range(chunks):
        copies.append(
            pltpu.make_async_copy(
                conv_c_ref.at[place, :, pl.ds(chunk * channels, channels)], own_ref.at[groups_b + chunk], sems.at[2 + chunk]
            )
        )
    wait_all(start_all(copies))


def front_turn(places_ref, map_ref, bank_ref, turned_map_ref, turned_bank_ref):
    sites, features = map_ref.shape
    for start in range(0, features, sites):
        turned_map_ref[start : start + sites] = map_ref[:, start : start + sites].T
        turned_bank_ref[start : start + sites] = bank_ref[:, start : start + sites].T


def front_bank(places_ref, bank_ref, w_bank_ref, w_key_ref, w_value_ref, keys_ref, values_ref, turned_memory_ref):
    memory = low(product(bank_ref[...], w_bank_ref[...]))
    keys_ref[...] = low(product(memory, w_key_ref[...]))
    values_ref[...] = low(product(memory, w_value_ref[...]))
    turned_memory_ref[...] = memory.T


def front_head(
    places_ref, index_ref, weight_ref, logit_grad_ref, w_head_ref, w_out_ref,
    pool_ref, joined_grad_ref, hidden_grad_ref, branch_grad_ref,
):
    own, taps = index_ref.shape
    sites = pool_ref.shape[1]
    channels = hidden_grad_ref.shape[1]
    features = w_head_ref.shape[0] - channels
    column = lax.broadcasted_iota(jnp.int32, (own, sites), 1)
    pool = jnp.zeros((own, sites), F32)
    for tap in range(taps):
        weight = wide(weight_ref[:, tap : tap + 1])
        pool = pool + jnp.where(column == index_ref[:, tap : tap + 1], weight, 0.0)
    pool_ref[...] = low(pool)
    logit_grad = logit_grad_ref[pl.ds(pl.multiple_of(places_ref[8], LANE_ROWS), own)]
    joined_grad = dot_nt(logit_grad, w_head_ref[...])
    joined_grad_ref[...] = joined_grad
    hidden_grad_ref[...] = dot_nt(low(joined_grad[:, features:]), w_out_ref[...])
    branch_grad_ref[...] = low(dot_nt(logit_grad_ref[...], w_head_ref[features:]))


def region_pack(
    places_ref, regions_ref, reduced_ref, hidden_ref, query_grad_ref, reduced_grad_ref, w_out_ref, w_head_ref,
    logits_ref, message_ref,
):
    count = message_ref.shape[0]
    channels = reduced_ref.shape[1]
    reduced = reduced_ref[...]
    merged = low(reduced + product(hidden_ref[...], w_out_ref[...]))
    joined = jnp.concatenate([regions_ref[...], merged], axis=1)
    logits_ref[...] = low(product(joined, w_head_ref[...]))[:, : logits_ref.shape[1]]
    reduced_low = low(reduced)
    parts = [regions_ref[...], reduced_low, hidden_ref[...], joined]
    shared = [reduced_grad_ref[...], query_grad_ref[...]]
    for place in range(count):
        pieces = list(shared)
        for part in parts:
            width = part.shape[1] // count
            pieces.append(part[:, place * width : (place + 1) * width])
        spare = message_ref.shape[2] - sum(piece.shape[1] for piece in pieces)
        if spare:
            pieces.append(jnp.zeros((reduced.shape[0], spare), BF16))
        message_ref[place] = jnp.concatenate(pieces, axis=1)


def key_value_parts(places_ref, score_grad_ref, queries_ref, weights_ref, arrived_ref, out_ref):
    keys_here = score_grad_ref.shape[1]
    out_ref[:keys_here] = low(dot_tn(score_grad_ref[...], queries_ref[...]))
    out_ref[keys_here:] = low(dot_tn(weights_ref[...], arrived_ref[:, : queries_ref.shape[1]]))


def region_sums(widths, places_ref, group_ref, branch_grad_ref, logit_grad_ref, out_ref):
    ends, start = [], 0
    for width in widths:
        ends.append((start, start + width))
        start += width
    reduced_grad, query_grad, regions, reduced, hidden, joined = [group_ref[:, begin:end] for begin, end in ends]
    first, second = widths[2], widths[2] + widths[3]
    third = second + widths[4]
    channels = reduced_grad.shape[1]
    out_ref[:first] = low(dot_tn(regions, reduced_grad))
    out_ref[first:second] = low(dot_tn(reduced, query_grad))
    out_ref[second:third] = low(dot_tn(hidden, branch_grad_ref[...]))
    head = low(dot_tn(joined, logit_grad_ref[...]))
    store_narrow(out_ref, third, head, channels)


def bank_back(
    places_ref, sums_ref, w_key_ref, w_value_ref, w_bank_ref, turned_bank_ref, turned_memory_ref, *refs
):
    vectors, bank_grad_ref, outs, (message_ref, grads) = refs[:8], refs[8], refs[9:-2], refs[-2:]
    keys_here, features = bank_grad_ref.shape
    channels = sums_ref.shape[1]
    count, _, width = message_ref.shape
    key_low, value_low = sums_ref[:keys_here], sums_ref[keys_here:]
    memory_grad = low(dot_nt(key_low, w_key_ref[...]) + dot_nt(value_low, w_value_ref[...]))
    for start in range(0, features, channels):
        bank_grad_ref[:, start : start + channels] = low(dot_nt(memory_grad, w_bank_ref[start : start + channels]))
    grads[:keys_here] = memory_grad
    grads[keys_here : 2 * keys_here] = key_low
    grads[2 * keys_here :] = value_low

    def columns(rows):
        if width % TILE == 0:
            return grads[rows, pl.ds(pl.multiple_of(places_ref[4] * width, width), width)]
        picked = grads[rows, :width]
        for number in range(1, channels // width):
            picked = jnp.where(places_ref[4] == number, grads[rows, number * width : (number + 1) * width], picked)
        return picked

    feature_rows, channel_rows = features // count, channels // count
    part = low(product(turned_bank_ref[...], columns(pl.ds(0, keys_here))))
    message_ref[:, :feature_rows] = part.reshape(count, feature_rows, width)
    at = feature_rows
    for number in (1, 2):
        part = low(product(turned_memory_ref[...], columns(pl.ds(number * keys_here, keys_here))))
        message_ref[:, at : at + channel_rows] = part.reshape(count, channel_rows, width)
        at += channel_rows
    spare = message_ref.shape[1] - at
    for place in range(count):
        row = []
        for vector_ref in vectors:
            share = vector_ref.shape[1] // count
            row.append(vector_ref[:, place * share : (place + 1) * share])
        total = sum(piece.shape[1] for piece in row)
        lines = -(-total // width)
        if lines * width > total:
            row.append(jnp.zeros((1, lines * width - total), F32))
        row = jnp.concatenate(row, axis=1)
        tile = [row[:, line * width : (line + 1) * width] for line in range(lines)]
        tile.append(jnp.zeros((spare - lines, width), F32))
        message_ref[place, at:] = low(jnp.concatenate(tile, axis=0))
    inner = outs[0].shape[0]
    for step, out_ref in enumerate(outs):
        out_ref[...] = message_ref[pl.ds((places_ref[6] ^ step) * inner, inner)]


def finish(shape_info, places_ref, part_ref, *refs):
    rows_b, rows_c, feature_rows, channel_rows, lines, split = shape_info
    if split:
        own_ref, got_ref, refs = refs[0], refs[1], refs[2:]
        weight_refs = [own_ref.at[0], got_ref.at[0], own_ref.at[1], got_ref.at[1]]
        bank_refs, first = weight_refs, rows_b + rows_c
    else:
        weight_refs, bank_refs, refs, first = refs[:1], refs[1:-14], refs[-14:], 0
    conv_a_ref, conv_b_ref, conv_c_ref, bank_out_ref, key_ref, value_ref = refs[:6]
    vectors = refs[6:]
    conv_a_ref[...] = wide(part_ref[...]).reshape(conv_a_ref.shape)
    channels = weight_refs[0].shape[1]
    width = channels // len(bank_refs)

    def spot(number, size):
        if not split:
            return pl.ds(number * size, size)
        return pl.ds(pl.multiple_of((places_ref[4] ^ number) * size, size), size)

    for number, ref in enumerate(weight_refs):
        conv_b_ref[spot(number, rows_b)] = wide(ref[:rows_b])
        for chunk in range(rows_c // LANE_ROWS):
            begin = rows_b + chunk * LANE_ROWS
            conv_c_ref[spot(number, LANE_ROWS), chunk * channels : (chunk + 1) * channels] = wide(
                ref[begin : begin + LANE_ROWS]
            )
    tile = None
    at = feature_rows + 2 * channel_rows
    for number, ref in enumerate(bank_refs):
        bank = wide(load_narrow(ref, first, lines, width))
        columns = spot(number, width)
        bank_out_ref[:, columns] = bank[:feature_rows]
        key_ref[:, columns] = bank[feature_rows : feature_rows + channel_rows]
        value_ref[:, columns] = bank[feature_rows + channel_rows : at]
        tile = bank[at:] if tile is None else tile + bank[at:]
    total = sum(ref.shape[1] for ref in vectors)
    row = jnp.concatenate([tile[line : line + 1] for line in range(-(-total // width))], axis=1)
    at = 0
    for ref in vectors:
        ref[...] = row[:, at : at + ref.shape[1]]
        at += ref.shape[1]


def run_kernel(
    kernel, places, arrays, shapes, name, micros, scratch=(), raw_in=(), raw_out=(), fetched=(), limit=8
):
    count_in, count_out, fetched = len(arrays), len(shapes), list(fetched)

    def wrapped(*refs):
        places_ref, ins = refs[0], list(refs[1 : 1 + count_in])
        out_places, outs = refs[1 + count_in], refs[2 + count_in : 2 + count_in + count_out]
        extra = refs[2 + count_in + count_out :]
        if fetched:
            held, sems, extra = extra[: len(fetched)], extra[len(fetched)], extra[len(fetched) + 1 :]
            copies = start_all(
                [pltpu.make_async_copy(ins[number], held[slot], sems.at[slot]) for slot, number in enumerate(fetched)]
            )
        for number in range(places.shape[0]):
            out_places[number] = places_ref[number]
        if fetched:
            wait_all(copies)
            for slot, number in enumerate(fetched):
                ins[number] = held[slot]
        kernel(places_ref, *ins, *outs, *extra)

    outside = [*raw_in, *fetched]
    buffers = [pltpu.VMEM(arrays[number].shape, arrays[number].dtype) for number in fetched]
    if fetched:
        buffers.append(pltpu.SemaphoreType.DMA((len(fetched),)))
    return pl.pallas_call(
        wrapped,
        out_shape=[shape_of(places.shape, jnp.int32)] + list(shapes),
        in_specs=[SCALAR] + [ANY if number in outside else HELD for number in range(count_in)],
        out_specs=[SCALAR] + [ANY if number in raw_out else HELD for number in range(count_out)],
        scratch_shapes=buffers + list(scratch),
        compiler_params=params(limit),
        cost_estimate=pl.CostEstimate(
            flops=int(micros * COST), bytes_accessed=int(micros * COST / 1000), transcendentals=0
        ),
        name=name,
    )(places, *arrays)


def run_first_conv(places, feature_map, sources, scale, shift):
    sites, channels = feature_map.shape[0], sources[0].shape[3]
    groups = sources[0].shape[1]
    blocks = sum(source.shape[0] for source in sources)
    return pl.pallas_call(
        first_conv,
        out_shape=[
            shape_of((sites, channels), F32),
            shape_of((sites, channels), BF16),
            shape_of((blocks * groups, LANE_ROWS, channels), BF16),
        ],
        in_specs=[SCALAR, HELD] + [ANY] * len(sources) + [HELD] * 2,
        out_specs=[ANY, HELD, ANY],
        scratch_shapes=[
            pltpu.VMEM((blocks * groups, LANE_ROWS, channels), BF16),
            pltpu.VMEM((sites, channels), F32),
            pltpu.SemaphoreType.DMA((blocks,)),
            pltpu.SemaphoreType.DMA((2,)),
        ],
        compiler_params=params(FIRST_LIMIT),
        cost_estimate=pl.CostEstimate(flops=int(6 * COST), bytes_accessed=int(6 * COST / 1000), transcendentals=0),
        name="first_conv",
    )(places, feature_map, *sources, scale.reshape(1, -1), shift.reshape(1, -1))


def run_later_convs(
    act_a, feature_map, packed, scale_b, shift_b, scale_c, shift_c, pooling, w_reduce, w_query, groups_b, groups_c
):
    sites, channels = act_a.shape
    features = feature_map.shape[1]
    blocks = packed.shape[0]
    own = pooling.shape[0]
    group = lax.axis_size("bank")
    return pl.pallas_call(
        later_convs,
        out_shape=[
            jax.ShapeDtypeStruct((sites, channels), jnp.float32),
            jax.ShapeDtypeStruct((sites, channels), jnp.bfloat16),
            jax.ShapeDtypeStruct((sites, features), jnp.float32),
            jax.ShapeDtypeStruct((own, features), jnp.bfloat16),
            jax.ShapeDtypeStruct((own, channels), jnp.float32),
            jax.ShapeDtypeStruct((group, own, channels), jnp.bfloat16),
        ],
        in_specs=[HELD] + [ANY] * 2 + [HELD] * 5 + [ANY, HELD],
        out_specs=[ANY] * 5 + [HELD],
        scratch_shapes=[
            pltpu.VMEM((blocks * groups_b, LANE_ROWS, channels), jnp.bfloat16),
            pltpu.VMEM((groups_c, blocks, LANE_ROWS, channels), jnp.bfloat16),
            pltpu.VMEM((sites, channels), jnp.bfloat16),
            pltpu.VMEM((sites, features), jnp.bfloat16),
            pltpu.VMEM((sites, features), jnp.float32),
            pltpu.VMEM(w_reduce.shape, jnp.bfloat16),
            pltpu.VMEM((sites, channels), jnp.float32),
            pltpu.VMEM((sites, channels), jnp.bfloat16),
            pltpu.VMEM((own, features), jnp.bfloat16),
            pltpu.VMEM((own, channels), jnp.float32),
            pltpu.SemaphoreType.DMA((blocks,)),
            pltpu.SemaphoreType.DMA((blocks,)),
            pltpu.SemaphoreType.DMA((6 + groups_c,)),
        ],
        compiler_params=params(52),
        cost_estimate=pl.CostEstimate(flops=int(15 * COST), bytes_accessed=int(15 * COST / 1000), transcendentals=0),
        name="later_convs",
    )(
        act_a, feature_map, packed, scale_b.reshape(1, -1), shift_b.reshape(1, -1), scale_c.reshape(1, -1),
        shift_c.reshape(1, -1), pooling, w_reduce, w_query,
    )


def body(
    feature_map,
    bank,
    region_time,
    roi_index,
    roi_weight,
    conv_a,
    scale_a,
    shift_a,
    conv_b,
    scale_b,
    shift_b,
    conv_c,
    scale_c,
    shift_c,
    w_reduce,
    w_bank,
    w_query,
    w_key,
    w_value,
    ln_gain,
    ln_shift,
    w_out,
    w_head,
    logit_grad,
):
    site_count = feature_map.shape[0]
    feature_count = feature_map.shape[1]
    channels = w_query.shape[0]
    classes = w_head.shape[1]
    keys_here = bank.shape[0]
    own_count = roi_index.shape[0]
    bank_count = lax.axis_size("bank")
    bank_place = lax.axis_index("bank")
    dp_count = lax.axis_size("dp")
    dp_place = lax.axis_index("dp")
    first_row = bank_place * own_count
    half_span = keys_here * bank_count // 2
    group_rows = bank_count * own_count
    chunks = feature_count // channels
    shards = (conv_a, conv_b, conv_c)
    split = dp_count // 2 == 2 and bank_count // 2 == 4 and all(shard.shape[0] % (LANE_ROWS * dp_count) == 0 for shard in shards)
    axes = block_axes(split, dp_count, bank_count)
    outer, inner, across, last = axes
    outer_count = outer.size if split else 1
    blocks = bank_count * dp_count if split else bank_count
    halves = tuple(axis.size for axis in axes[:3])
    places_here = jnp.stack([across.place(), inner.place(), outer.place(), last.place(), dp_place, bank_place * keys_here, outer.place() if split else 0 * bank_place, inner.place(), first_row, dp_place if split else 0 * dp_place])

    parts = dp_count if split else 1
    rows_a, rows_b, rows_c = [shard.shape[0] // parts for shard in shards]
    groups_a, groups_b, groups_c = rows_a // LANE_ROWS, rows_b // LANE_ROWS, chunks
    places, own_a, own_packed = run_kernel(
        functools.partial(front_pack, groups_a, groups_b),
        places_here,
        [shard.reshape(-1, LANE_ROWS, shard.shape[1]) for shard in shards],
        [shape_of((groups_a, LANE_ROWS, channels), BF16), shape_of((groups_b + chunks, LANE_ROWS, channels), BF16)],
        "front_pack",
        1,
        scratch=[pltpu.SemaphoreType.DMA((2 + chunks,))],
        raw_in=(0, 1, 2),
        raw_out=(0, 1),
    )
    packed = lax.all_gather(own_packed, ("bank", "dp") if split else "bank", axis=0, tiled=False)
    packed = packed.reshape((blocks,) + own_packed.shape)
    spare = ((0, 0), (0, TILE - classes))
    wide_head, wide_logit_grad = jnp.pad(w_head, spare), jnp.pad(logit_grad, spare)
    front = {}

    def turn(places):
        places, front["turned_map"], front["turned_bank"] = run_kernel(
            front_turn,
            places,
            [feature_map, bank],
            [shape_of((feature_count, site_count), BF16), shape_of((feature_count, keys_here), BF16)],
            "front_turn",
            6,
            limit=16,
        )
        return places

    def project(places):
        inside = shape_of((keys_here, channels), BF16)
        places, front["keys"], front["values"], front["turned_memory"] = run_kernel(
            front_bank,
            places,
            [bank, w_bank, w_key, w_value],
            [inside, inside, shape_of((channels, keys_here), BF16)],
            "front_bank",
            6,
            limit=16,
        )
        return places

    def head(places):
        places, front["pooling"], front["joined_grad"], front["hidden_grad"], front["group_branch_grad"] = run_kernel(
            front_head,
            places,
            [roi_index, roi_weight, wide_logit_grad, wide_head, w_out],
            [
                shape_of((own_count, site_count), BF16),
                shape_of((own_count, w_head.shape[0]), F32),
                shape_of((own_count, channels), F32),
                shape_of((group_rows, channels), BF16),
            ],
            "front_head",
            4,
            limit=16,
        )
        return places

    if split:
        places, sources = gather_blocks(own_a, axes, places, [turn, project, head])
    else:
        places, sources = head(project(turn(places))), [lax.all_gather(own_a, "bank", axis=0, tiled=False)]
    turned_map, turned_bank, turned_memory = front["turned_map"], front["turned_bank"], front["turned_memory"]
    keys, values, pooling = front["keys"], front["values"], front["pooling"]
    joined_grad, hidden_grad, group_branch_grad = front["joined_grad"], front["hidden_grad"], front["group_branch_grad"]
    time_column = region_time.reshape(-1, 1)
    scales = jnp.stack([scale_b, shift_b, scale_a, shift_a])
    places, time_column, scales, *sources = lax.optimization_barrier((places, time_column, scales, *sources))

    pre_a, act_a, weight_a = run_first_conv(places, feature_map, sources, scale_a, shift_a)
    pre_b, act_b, pre_c, regions, reduced, own_queries = run_later_convs(
        act_a, feature_map, packed, scale_b, shift_b, scale_c, shift_c, pooling, w_reduce, w_query, groups_b, groups_c
    )
    queries = to_owners(own_queries).reshape(group_rows, channels)
    places, message, scores = run_kernel(
        functools.partial(attend, half_span),
        places,
        [queries, keys, values, time_column],
        [shape_of((group_rows, channels + TILE), BF16), shape_of((group_rows, keys_here), F32)],
        "attend",
        2,
    )
    arrived = to_owners(message.reshape(bank_count, own_count, channels + TILE))
    row = shape_of((1, channels), F32)
    places, message, hidden_low, gain_part, shift_part = run_kernel(
        merge_rows,
        places,
        [arrived, hidden_grad, ln_gain.reshape(1, -1), ln_shift.reshape(1, -1)],
        [shape_of(arrived.shape, BF16), shape_of((own_count, channels), BF16), row, row],
        "merge_rows",
        2,
    )
    arrived = to_owners(message).reshape(group_rows, channels + TILE)
    maps = (site_count, feature_count)
    inside = (site_count, channels)
    places, slope_c = run_kernel(
        slopes_outer,
        places,
        [scale_c.reshape(1, -1), shift_c.reshape(1, -1), pre_c, feature_map],
        [shape_of(maps, BF16)],
        "slopes_outer",
        WINDOW,
        scratch=[
            pltpu.VMEM(maps, F32), pltpu.VMEM(maps, BF16), pltpu.VMEM(maps, BF16), pltpu.SemaphoreType.DMA((3, chunks))
        ],
        raw_in=(2, 3),
        raw_out=(0,),
        limit=52,
    )
    group_shape = shape_of((group_rows, channels), BF16)
    weight_shape = shape_of((group_rows, keys_here), BF16)
    places, query_part, score_grad, weights_low = run_kernel(
        attend_back,
        places,
        [arrived, scores, keys, values],
        [group_shape, weight_shape, weight_shape],
        "attend_back",
        2,
    )
    query_parts = to_owners(query_part.reshape(bank_count, own_count, channels))
    places, key_value = run_kernel(
        key_value_parts,
        places,
        [score_grad, queries, weights_low, arrived],
        [shape_of((2 * keys_here, channels), BF16)],
        "key_value_parts",
        3,
    )

    def dp_swap(value, step):
        return lax.ppermute(value, "dp", [(i, i ^ step) for i in range(dp_count)])

    key_value_got = dp_swap(key_value, 1)

    def summed_swap(places, own, got):
        places, own = run_kernel(
            sum_swap, places, [own, got], [shape_of(own.shape, BF16)], "sum_swap", 2
        )
        return places, own

    places, key_value = summed_swap(places, key_value, key_value_got)
    step = 2
    while step * 2 < dp_count:
        places, key_value = summed_swap(places, key_value, dp_swap(key_value, step))
        step *= 2
    key_value_got = dp_swap(key_value, step)
    own_shape = shape_of((own_count, channels), BF16)
    places, query_grad, reduced_grad, regions_grad = run_kernel(
        region_back,
        places,
        [query_parts, joined_grad, w_query, w_reduce],
        [own_shape, own_shape, shape_of((own_count, feature_count), BF16)],
        "region_back",
        3,
    )
    half_blocks = blocks // 2
    rows_bc = rows_b + groups_c * LANE_ROWS
    wide_row = shape_of((1, feature_count), F32)
    (
        places, send_bc, keep_bc, lin_c_grad, pre_a_grad,
        scale_c_part, shift_c_part, scale_b_part, shift_b_part, scale_a_part, shift_a_part,
    ) = run_kernel(
        functools.partial(later_back, 0, groups_b),
        places,
        [
            regions_grad, pooling, scale_c.reshape(1, -1), scales, pre_c, slope_c, act_b, pre_b, act_a, pre_a, packed,
        ],
        [shape_of((half_blocks, rows_bc, channels), BF16)] * 2
        + [shape_of(maps, BF16), shape_of(inside, BF16), wide_row, wide_row]
        + [row] * 4,
        "later_back",
        28,
        scratch=[
            pltpu.VMEM((blocks * groups_b, LANE_ROWS, channels), BF16),
            pltpu.VMEM((groups_c, blocks, LANE_ROWS, channels), BF16),
            pltpu.VMEM((2, half_blocks, rows_bc, channels), BF16),
            pltpu.VMEM(inside, F32),
            pltpu.VMEM(inside, BF16),
            pltpu.VMEM((channels, site_count), BF16),
            pltpu.VMEM(inside, F32),
            pltpu.VMEM(inside, F32),
            pltpu.VMEM(maps, F32),
            pltpu.VMEM(maps, BF16),
            pltpu.VMEM(inside, BF16),
            pltpu.VMEM(inside, F32),
            pltpu.VMEM(inside, BF16),
            pltpu.VMEM(inside, F32),
            pltpu.VMEM(maps, BF16),
            pltpu.SemaphoreType.DMA((blocks,)),
            pltpu.SemaphoreType.DMA((blocks,)),
            pltpu.SemaphoreType.DMA((2,)),
            pltpu.SemaphoreType.DMA((4 + 3 * chunks,)),
        ],
        raw_in=range(4, 11),
        raw_out=(0, 1, 2),
        limit=40,
    )
    got_bc = last.swap(send_bc, 1)

    def parted(value):
        return value.reshape(halves + value.shape[1:])

    places, send_a, keep_a, key_value = run_kernel(
        first_back,
        places,
        [pre_a_grad, key_value, key_value_got, turned_map],
        [shape_of((half_blocks, rows_a, channels), BF16)] * 2 + [shape_of(key_value.shape, BF16)],
        "first_back",
        6,
        scratch=[
            pltpu.VMEM((2, half_blocks, rows_a, channels), BF16),
            pltpu.VMEM(turned_map.shape, BF16),
            pltpu.SemaphoreType.DMA((chunks,)),
            pltpu.SemaphoreType.DMA((2,)),
        ],
        raw_in=(3,),
        raw_out=(0, 1),
        limit=20,
    )
    got_a = last.swap(send_a, 1)
    half = outer.size // 2
    plane_shape = (half, 2, rows_bc, channels)
    places, keep_one, send_one, keep_two, send_two = run_kernel(
        after_last, places, [parted(keep_bc), parted(got_bc)], [shape_of(plane_shape, BF16)] * 4, "round_one", 4
    )
    got_one, got_two = across.swap(send_one, 1), inner.swap(send_two, 1)
    feature_rows, channel_rows = feature_count // bank_count, channels // bank_count
    joined_rows = (feature_count + channels) // bank_count
    widths = (channels, channels, feature_rows, channel_rows, channel_rows, joined_rows)
    message_width = -(-sum(widths) // TILE) * TILE
    places, logits_out, message = run_kernel(
        region_pack,
        places,
        [regions, reduced, hidden_low, query_grad, reduced_grad, w_out, wide_head],
        [shape_of((own_count, classes), BF16), shape_of((bank_count, own_count, message_width), BF16)],
        "region_pack",
        WINDOW,
    )
    group = to_owners(message).reshape(group_rows, message_width)

    places, map_grad = run_kernel(
        map_back,
        places,
        [pre_a_grad, weight_a, lin_c_grad],
        [shape_of(maps, BF16)],
        "map_back",
        WINDOW,
        scratch=[
            pltpu.VMEM((3,) + inside, BF16),
            pltpu.VMEM(maps, BF16),
            pltpu.VMEM(maps, BF16),
            pltpu.SemaphoreType.DMA((1 + chunks,)),
        ],
        raw_in=(2,),
        raw_out=(0,),
        limit=12,
    )
    kept_shape = shape_of((2 * half * (2 * rows_a + rows_bc), channels), BF16)
    both = shape_of((half * (2 * rows_a + rows_bc), channels), BF16)
    places, held, send_across, send_inner = run_kernel(
        round_two,
        places,
        [keep_one, got_one, keep_two, got_two, parted(keep_a), parted(got_a)],
        [kept_shape, both, both],
        "round_two",
        5,
    )
    got_across, got_inner = across.swap(send_across, 1), inner.swap(send_inner, 1)
    vectors = [
        gain_part, shift_part, scale_a_part, shift_a_part, scale_b_part, shift_b_part, scale_c_part, shift_c_part
    ]
    width = channels // dp_count
    lines = -(-sum(vector.shape[1] for vector in vectors) // (bank_count * width))
    lines = -(-lines // LANE_ROWS) * LANE_ROWS
    bank_lines = feature_rows + 2 * channel_rows + lines
    bank_step = bank_spans(bank_lines, width, channels)[1]
    region_lines = feature_rows + 2 * channel_rows + bank_spans(joined_rows, TILE, channels)[1]
    places, bank_grad, *bank_pieces = run_kernel(
        bank_back,
        places,
        [key_value, w_key, w_value, w_bank, turned_bank, turned_memory] + vectors,
        [shape_of(bank.shape, BF16)]
        + [shape_of((bank_count // outer_count, bank_lines, width), BF16)] * outer_count,
        "bank_back",
        WINDOW,
        scratch=[
            pltpu.VMEM((bank_count, bank_lines, width), BF16),
            pltpu.VMEM((3 * keys_here, channels), BF16),
        ],
        limit=8,
    )
    places, region_parts = run_kernel(
        functools.partial(region_sums, widths),
        places,
        [group, group_branch_grad, wide_logit_grad],
        [shape_of((region_lines, channels), BF16)],
        "region_sums",
        WINDOW,
    )
    region_both = [region_parts, dp_swap(region_parts, 1)] if split else [lax.psum(region_parts, "dp")]
    if split:
        bank_parts = [bank_pieces[0]] + [outer.swap(piece, step + 1) for step, piece in enumerate(bank_pieces[1:])]
    else:
        bank_parts = [low(jnp.sum(wide(to_owners(bank_pieces[0])), axis=0, keepdims=True))]
    sizes = (half, rows_bc, rows_a)
    places, held, send_across, send_inner, *pieces_bc = run_kernel(
        functools.partial(round_three, sizes, outer.size, split),
        places,
        [held, got_across, got_inner] + region_both + bank_parts,
        [
            shape_of((rows_bc + 2 * half * rows_a + bank_step, channels), BF16),
            shape_of((half * rows_a + region_lines, channels), BF16),
            shape_of((half * rows_a + bank_step, channels), BF16),
        ]
        + [shape_of((rows_bc, channels), BF16)] * (outer.size - 1),
        "round_three",
        5,
    )
    got_across, got_inner = across.swap(send_across, 1), inner.swap(send_inner, 1)
    got_bc = [outer.swap(piece, step + 1) for step, piece in enumerate(pieces_bc)]
    row_block = shape_of((channel_rows, channels), F32)
    results = run_kernel(
        functools.partial(round_four, sizes, outer.size, split, widths),
        places,
        [held, *got_bc, send_across, got_across, got_inner],
        [shape_of((rows_bc + bank_step, channels), BF16)]
        + [shape_of((rows_a, channels), BF16)] * outer.size
        + [shape_of((feature_rows, channels), F32), row_block, row_block, shape_of((joined_rows, classes), F32)],
        "round_four",
        4,
    )
    places, done, kept_a, *pieces_a = results[: 2 + outer.size]
    reduce_weight_grad, query_weight_grad, out_weight_grad, head_weight_grad = results[2 + outer.size :]
    got_a = [outer.swap(piece, step + 1) for step, piece in enumerate(pieces_a)]
    done_both = [done, across.swap(done, 1)] if split else []
    row_block = shape_of((channel_rows, channels), F32)
    places, part_a, *both = run_kernel(
        functools.partial(round_last, outer.size),
        places,
        [kept_a, *got_a, *done_both],
        [shape_of((rows_a, channels), BF16)] + [shape_of((2,) + done.shape, BF16)] * len(done_both[1:]),
        "round_last",
        2,
    )
    if split:
        done_a = lax.all_gather(part_a, "dp", axis=0, tiled=False)
        done_all = [both[0], last.swap(both[0], 1)]
    else:
        done_a = lax.psum(part_a, "dp")
        bank_all = lax.all_gather(done[rows_bc:], "dp", axis=0, tiled=False)
        done_all = [lax.psum(done[:rows_bc], "dp")] + [bank_all[place] for place in range(dp_count)]
    info = (rows_b, groups_c * LANE_ROWS, feature_rows, channel_rows, bank_lines, split)
    results = run_kernel(
        functools.partial(finish, info),
        places,
        [done_a, *done_all],
        [shape_of(conv_a.shape, F32), shape_of(conv_b.shape, F32), shape_of(conv_c.shape, F32)]
        + [shape_of((feature_rows, channels), F32), row_block, row_block]
        + [shape_of((1, vector.shape[1] // bank_count), F32) for vector in vectors],
        "finish",
        3,
    )
    places, conv_a_grad, conv_b_grad, conv_c_grad, bank_weight_grad, key_weight_grad, value_weight_grad = results[:7]
    small = [value.reshape(-1) for value in results[7:]]
    gain_grad, shift_grad = small[:2]
    scale_a_grad, shift_a_grad, scale_b_grad, shift_b_grad, scale_c_grad, shift_c_grad = small[2:]
    return (
        logits_out,
        map_grad,
        bank_grad,
        conv_a_grad,
        scale_a_grad,
        shift_a_grad,
        conv_b_grad,
        scale_b_grad,
        shift_b_grad,
        conv_c_grad,
        scale_c_grad,
        shift_c_grad,
        reduce_weight_grad,
        bank_weight_grad,
        query_weight_grad,
        key_weight_grad,
        value_weight_grad,
        gain_grad,
        shift_grad,
        out_weight_grad,
        head_weight_grad,
    )


def solution(mesh):
    in_specs = (
        P(("dp", "bank"), None),
        P("bank", None),
        P("dp"),
        P(("dp", "bank"), None),
        P(("dp", "bank"), None),
        P("bank", None),
        P(),
        P(),
        P("bank", None),
        P(),
        P(),
        P("bank", None),
        P(),
        P(),
        P(),
        P(),
        P(),
        P(),
        P(),
        P(),
        P(),
        P(),
        P(),
        P("dp", None),
    )
    out_specs = (
        P(("dp", "bank"), None),
        P(("dp", "bank"), None),
        P("bank", None),
        P("bank", None),
        P("bank"),
        P("bank"),
        P("bank", None),
        P("bank"),
        P("bank"),
        P("bank", None),
        P("bank"),
        P("bank"),
        P("bank", None),
        P("bank", None),
        P("bank", None),
        P("bank", None),
        P("bank", None),
        P("bank"),
        P("bank"),
        P("bank", None),
        P("bank", None),
    )
    return jax.shard_map(body, mesh=mesh, in_specs=in_specs, out_specs=out_specs, check_vma=False)
```

```python
import functools

import jax
import jax.numpy as jnp
from jax import lax
from jax.experimental import pallas as pl
from jax.experimental.pallas import tpu as pltpu
from jax.sharding import PartitionSpec as P

FRAMES = 4
SIDE = 8
LANE_ROWS = 16
TILE = 128
ROOT = 0.7978845608028654
CUBIC = 0.044715

epsilon = 1e-05
masked_score = -1e30
places = [(-1, -1), (-1, 0), (-1, 1), (0, -1), (0, 0), (0, 1), (1, -1), (1, 0), (1, 1)]


def product(left, right):
    return jnp.dot(left, right, preferred_element_type=jnp.float32)


def low(value):
    return value.astype(jnp.bfloat16)


def wide(value):
    return value.astype(jnp.float32)


class SubAxis:
    def __init__(self, name, size, stride):
        self.name, self.size, self.stride = name, size, stride

    def place(self):
        return lax.rem(lax.axis_index(self.name) // self.stride, self.size)

    def swap(self, value, step):
        count = lax.axis_size(self.name)
        pairs = [(i, i ^ (step * self.stride)) for i in range(count)]
        return lax.ppermute(value, self.name, pairs)


def block_axes(split, dp_count, bank_count):
    if split:
        return (
            SubAxis("bank", bank_count // 2, 2),
            SubAxis("bank", 2, 1),
            SubAxis("dp", dp_count // 2, 2),
            SubAxis("dp", 2, 1),
        )
    return (
        SubAxis("bank", bank_count // 8, 8),
        SubAxis("bank", 2, 4),
        SubAxis("bank", 2, 2),
        SubAxis("bank", 2, 1),
    )


def gather_blocks(own, axes, places, steps):
    outer, inner, across, last = axes
    blocks = [own] + [outer.swap(own, step) for step in range(1, outer.size)]
    places = steps[0](places)
    *blocks, places = lax.optimization_barrier((*blocks, places))
    blocks = jnp.stack(blocks)
    half = outer.size // 2
    first, second = blocks[:half], blocks[half:]
    got_first, got_second = across.swap(first, 1), inner.swap(second, 1)
    places = steps[1](places)
    first, got_first, second, got_second, places = lax.optimization_barrier((first, got_first, second, got_second, places))
    first, second = jnp.concatenate([first, got_first]), jnp.concatenate([second, got_second])
    got_first, got_second = inner.swap(first, 1), across.swap(second, 1)
    places = steps[2](places)
    first, got_first, second, got_second, places = lax.optimization_barrier((first, got_first, second, got_second, places))
    near = jnp.concatenate([first, got_first, second, got_second])
    return places, [near, last.swap(near, 1)]


def to_owners(value):
    return lax.all_to_all(value, "bank", split_axis=0, concat_axis=0, tiled=True)


def to_group(value):
    count = lax.axis_size("bank")
    return to_owners(jnp.broadcast_to(value[None], (count,) + value.shape))


def params(mib):
    return pltpu.CompilerParams(vmem_limit_bytes=mib * 1024 * 1024)


def gelu_of(x):
    return 0.5 * x * (1.0 + jnp.tanh(ROOT * (x + CUBIC * x * x * x)))


def gelu_slope(x):
    square = x * x
    bent = jnp.tanh(ROOT * x * (1.0 + CUBIC * square))
    return 0.5 * (1.0 + bent) + 0.5 * ROOT * x * (1.0 - bent * bent) * (1.0 + 3.0 * CUBIC * square)


def by_rows(count, step, work):
    def one(number, carry):
        work(pl.ds(pl.multiple_of(number * step, step), step))
        return carry

    lax.fori_loop(0, count // step, one, 0)


def dot_tn(left, right):
    return lax.dot_general(
        left, right, (((0,), (0,)), ((), ())), preferred_element_type=jnp.float32
    )


def dot_nt(left, right):
    return lax.dot_general(
        left, right, (((1,), (1,)), ((), ())), preferred_element_type=jnp.float32
    )


def in_rows(value, step):
    if step == 0:
        return value
    sites, width = value.shape
    tall = value.reshape(sites // (SIDE * SIDE), SIDE, SIDE, width)
    edge = jnp.zeros_like(tall[:, :1])
    if step > 0:
        tall = jnp.concatenate([tall[:, 1:], edge], axis=1)
    else:
        tall = jnp.concatenate([edge, tall[:, :-1]], axis=1)
    return tall.reshape(sites, width)


def in_columns(value, step):
    if step == 0:
        return value
    sites = value.shape[0]
    turned = pltpu.roll(value, (-step) % sites, 0)
    column = lax.broadcasted_iota(jnp.int32, value.shape, 0) % SIDE
    keep = column != (SIDE - 1 if step > 0 else 0)
    return jnp.where(keep, turned, 0.0)


def fetch(source, target, sems, first, groups):
    copies = []
    for block in range(source.shape[0]):
        copies.append(
            pltpu.make_async_copy(
                source.at[block, pl.ds(first, groups)],
                target.at[pl.ds(block * groups, groups)],
                sems.at[block],
            )
        )
    return copies


def fetch_columns(source, target, sems, first, groups):
    return [
        pltpu.make_async_copy(
            source.at[block, pl.ds(first, groups)], target.at[:, block], sems.at[block]
        )
        for block in range(source.shape[0])
    ]


def start_all(copies):
    for copy in copies:
        copy.start()
    return copies


def wait_all(copies):
    for copy in copies:
        copy.wait()


def gathered_spot(places_ref, number, far):
    second, rest = divmod(number, 8)
    high, low_bits = divmod(rest, 4)
    middle, step = divmod(low_bits, 2)
    across, inner = (high, middle) if second else (middle, high)
    outer = (places_ref[2] ^ (2 * second + step)) * 2 + (places_ref[1] ^ inner)
    return (outer * 2 + (places_ref[0] ^ across)) * 2 + (places_ref[3] ^ far)


def first_conv(places_ref, fm_ref, *refs):
    sources, refs = refs[:-9], refs[-9:]
    scale_ref, shift_ref, pre_out_ref, act_ref, weight_out_ref, weight, pre_ref, sems, out_sems = refs
    sites, features = fm_ref.shape
    channels = act_ref.shape[1]
    groups = sources[0].shape[1]
    copies = []
    for far, source in enumerate(sources):
        for number in range(source.shape[0]):
            block = gathered_spot(places_ref, number, far) if len(sources) > 1 else number
            target = weight.at[pl.ds(block * groups, groups)]
            copies.append(pltpu.make_async_copy(source.at[number], target, sems.at[len(copies)]))
    start_all(copies)
    clip = FRAMES * SIDE * SIDE
    frame = SIDE * SIDE
    wait_all(copies)
    out = start_all([pltpu.make_async_copy(weight, weight_out_ref, out_sems.at[1])])

    def tap(number):
        begin = number * features // LANE_ROWS
        return weight[begin : begin + features // LANE_ROWS].reshape(features, channels)

    before = tap(0)
    for start in range(0, sites, clip):
        pre_ref[start : start + frame] = jnp.zeros((frame, channels), jnp.float32)
        pre_ref[start + frame : start + clip] = product(fm_ref[start : start + clip - frame], before)
    pre_ref[...] += product(fm_ref[...], tap(1))
    after = tap(2)
    for start in range(0, sites, clip):
        pre_ref[start : start + clip - frame] += product(fm_ref[start + frame : start + clip], after)

    def finish(rows):
        act_ref[rows] = low(gelu_of(pre_ref[rows] * scale_ref[...] + shift_ref[...]))

    out += start_all([pltpu.make_async_copy(pre_ref, pre_out_ref, out_sems.at[0])])
    by_rows(sites, 128, finish)
    wait_all(out)


def later_convs(
    act_a_ref, fm_ref, packed_ref, scale_b_ref, shift_b_ref, scale_c_ref, shift_c_ref, pool_ref, w_reduce_ref, w_query_far_ref,
    pre_b_out_ref, act_b_out_ref, pre_c_ref, regions_out_ref, reduced_out_ref, queries_ref,
    weight_b, weight_c, out_low, held_map, held_pre, held_reduce, pre_b_ref, act_b_ref, regions_ref, reduced_ref, w_query_ref, sems_b, sems_c, sems,
):
    sites, channels = act_a_ref.shape
    blocks = packed_ref.shape[0]
    groups_b = weight_b.shape[0] // blocks
    groups_c = weight_c.shape[0]
    groups_a = packed_ref.shape[1] - groups_b - groups_c
    copies_b = start_all(fetch(packed_ref, weight_b, sems_b, groups_a, groups_b))
    copies_c = start_all(fetch_columns(packed_ref, weight_c, sems_c, groups_a + groups_b, groups_c))
    others = start_all(
        [
            pltpu.make_async_copy(fm_ref, held_map, sems.at[0]),
            pltpu.make_async_copy(w_reduce_ref, held_reduce, sems.at[1]),
            pltpu.make_async_copy(w_query_far_ref, w_query_ref, sems.at[6 + groups_c]),
        ]
    )
    act_a = act_a_ref[...]
    block_rows = groups_b * LANE_ROWS
    sums = {-1: None, 0: None, 1: None}
    waited = 0
    for number, (rise, slide) in enumerate(places):
        while waited < len(copies_b) and waited * block_rows < (number + 1) * channels:
            copies_b[waited].wait()
            waited += 1
        begin = number * channels // LANE_ROWS
        tap = weight_b[begin : begin + channels // LANE_ROWS].reshape(channels, channels)
        part = in_rows(product(act_a, tap), rise)
        sums[slide] = part if sums[slide] is None else sums[slide] + part
    pre_b_ref[...] = sums[0] + in_columns(sums[1], 1) + in_columns(sums[-1], -1)

    outs = start_all([pltpu.make_async_copy(pre_b_ref, pre_b_out_ref, sems.at[2 + groups_c])])

    def finish(rows):
        act_b_ref[rows] = low(gelu_of(pre_b_ref[rows] * scale_b_ref[...] + shift_b_ref[...]))

    by_rows(sites, 128, finish)
    outs += start_all([pltpu.make_async_copy(act_b_ref, act_b_out_ref, sems.at[3 + groups_c])])
    wait_all(copies_c + others)
    reduced_ref[...] = jnp.zeros_like(reduced_ref)

    def chunk(number, carry):
        columns = pl.ds(pl.multiple_of(number * channels, channels), channels)
        held_pre[:, columns] = product(act_b_ref[...], weight_c[number].reshape(channels, channels))
        pltpu.make_async_copy(held_pre.at[:, columns], pre_c_ref.at[:, columns], sems.at[2 + number]).start()

        def finish_c(rows):
            linear = wide(held_map[rows, columns]) + held_pre[rows, columns] * scale_c_ref[:, columns] + shift_c_ref[:, columns]
            out_low[rows] = low(gelu_of(linear))

        by_rows(sites, 128, finish_c)
        part = low(product(pool_ref[...], out_low[...]))
        regions_ref[:, columns] = part
        reduced_ref[...] += product(part, held_reduce[columns])
        return carry

    lax.fori_loop(0, groups_c, chunk, 0)
    outs += start_all(
        [
            pltpu.make_async_copy(regions_ref, regions_out_ref, sems.at[4 + groups_c]),
            pltpu.make_async_copy(reduced_ref, reduced_out_ref, sems.at[5 + groups_c]),
        ]
    )
    queries = low(product(low(reduced_ref[...]), w_query_ref[...]))
    for place in range(queries_ref.shape[0]):
        queries_ref[place] = queries
    for number in range(groups_c):
        columns = pl.ds(number * channels, channels)
        outs.append(pltpu.make_async_copy(held_pre.at[:, columns], pre_c_ref.at[:, columns], sems.at[2 + number]))
    wait_all(outs)


def column_tile(columns, shape):
    lane = lax.broadcasted_iota(jnp.int32, shape, len(shape) - 1)
    tile = jnp.zeros(shape, jnp.float32)
    for number, column in enumerate(columns):
        rest = column
        for third in range(3):
            piece = wide(low(rest))
            tile = jnp.where(lane == 3 * number + third, piece, tile)
            rest = rest - piece
    return low(tile)


def from_tile(tile, number):
    lane = lax.broadcasted_iota(jnp.int32, tile.shape, tile.ndim - 1)
    picked = jnp.where((lane >= 3 * number) & (lane < 3 * number + 3), wide(tile), 0.0)
    return jnp.sum(picked, axis=-1, keepdims=True)


def attend(half_span, places_ref, queries_ref, keys_ref, values_ref, time_ref, message_ref, scores_ref):
    channels = queries_ref.shape[1]
    positions = places_ref[5] + lax.broadcasted_iota(jnp.int32, scores_ref.shape, 1)
    visible = jnp.abs(time_ref[...] - positions) <= half_span
    scores = dot_nt(queries_ref[...], keys_ref[...]) * (channels ** (-0.5))
    scores = jnp.where(visible, scores, masked_score)
    scores_ref[...] = scores
    top = jnp.max(scores, axis=1, keepdims=True)
    weights = jnp.exp(scores - top)
    total = jnp.sum(weights, axis=1, keepdims=True)
    message_ref[:, :channels] = low(product(low(weights), values_ref[...]))
    message_ref[:, channels:] = column_tile([top, total], (scores.shape[0], TILE))


def merge_rows(places_ref, arrived_ref, hidden_grad_ref, gain_ref, shift_ref, message_ref, hidden_ref, gain_out_ref, shift_out_ref):
    count, own, packed = arrived_ref.shape
    channels = hidden_grad_ref.shape[1]
    tops = from_tile(arrived_ref[:, :, channels:], 0)
    totals = from_tile(arrived_ref[:, :, channels:], 1)
    top = jnp.max(tops, axis=0)
    factors = jnp.exp(tops - top[None])
    total = jnp.sum(factors * totals, axis=0)
    numer = jnp.sum(factors * wide(arrived_ref[:, :, :channels]), axis=0)
    attended = numer / total
    centred = attended - jnp.mean(attended, axis=1, keepdims=True)
    spread = lax.rsqrt(jnp.mean(centred * centred, axis=1, keepdims=True) + epsilon)
    unit = centred * spread
    normed = unit * gain_ref[...] + shift_ref[...]
    hidden_ref[...] = low(gelu_of(normed))
    normed_grad = hidden_grad_ref[...] * gelu_slope(normed)
    gain_out_ref[...] = jnp.sum(normed_grad * unit, axis=0, keepdims=True)
    shift_out_ref[...] = jnp.sum(normed_grad, axis=0, keepdims=True)
    unit_grad = normed_grad * gain_ref[...]
    attended_grad = spread * (
        unit_grad
        - jnp.mean(unit_grad, axis=1, keepdims=True)
        - unit * jnp.mean(unit_grad * unit, axis=1, keepdims=True)
    )
    centre = jnp.sum(attended_grad * attended, axis=1, keepdims=True) / total
    numer_grad = low(attended_grad / total)
    tile = column_tile([top, centre], (own, TILE))
    for place in range(count):
        message_ref[place, :, :channels] = numer_grad
        message_ref[place, :, channels:] = tile


def attend_back(places_ref, arrived_ref, scores_ref, keys_ref, values_ref, part_ref, score_grad_ref, weights_ref):
    channels = keys_ref.shape[1]
    top = from_tile(arrived_ref[:, channels:], 0)
    centre = from_tile(arrived_ref[:, channels:], 1)
    weights = jnp.exp(scores_ref[...] - top)
    weights_ref[...] = low(weights)
    prob_grad = dot_nt(arrived_ref[:, :channels], values_ref[...])
    score_grad = low(weights * (prob_grad - centre) * (channels ** (-0.5)))
    score_grad_ref[...] = score_grad
    part_ref[...] = low(product(score_grad, keys_ref[...]))


def half_of(place_ref, bit):
    return jnp.where(place_ref[3] == bit, 1, 0)


def fold(value):
    return jnp.sum(value.reshape(value.shape[0] // 8, 8, value.shape[1]), axis=0)


def region_back(
    places_ref, arrived_ref, joined_grad_ref, w_query_ref, w_reduce_ref, query_grad_ref, reduced_grad_ref, regions_grad_ref
):
    features = regions_grad_ref.shape[1]
    query_grad = low(jnp.sum(wide(arrived_ref[...]), axis=0))
    query_grad_ref[...] = query_grad
    reduced_grad = low(joined_grad_ref[:, features:] + dot_nt(query_grad, w_query_ref[...]))
    reduced_grad_ref[...] = reduced_grad
    regions_grad_ref[...] = low(joined_grad_ref[:, :features] + dot_nt(reduced_grad, w_reduce_ref[...]))


def hand_out(buffer, send_ref, keep_ref, sems):
    return start_all(
        [
            pltpu.make_async_copy(buffer.at[number], target, sems.at[number])
            for number, target in enumerate((send_ref, keep_ref))
        ]
    )


def store_rows(buffer, place_ref, value, first, rows):
    at, end = first, first + value.shape[0]
    while at < end:
        block, offset = divmod(at, rows)
        count = min(rows - offset, end - at)
        buffer[half_of(place_ref, block % 2), block // 2, offset : offset + count] = value[at - first : at - first + count]
        at += count


def slopes_outer(places_ref, scale_ref, shift_ref, pre_ref, map_ref, out_ref, held_pre, held_map, held_out, sems):
    sites, features = held_map.shape
    chunks = sems.shape[1]
    width = features // chunks

    def part_of(source, target, number, row):
        columns = pl.ds(pl.multiple_of(number * width, width), width)
        return pltpu.make_async_copy(source.at[:, columns], target.at[:, columns], sems.at[row, number])

    for number in range(chunks):
        start_all([part_of(pre_ref, held_pre, number, 0), part_of(map_ref, held_map, number, 1)])

    def chunk(number, carry):
        columns = pl.ds(pl.multiple_of(number * width, width), width)
        wait_all([part_of(pre_ref, held_pre, number, 0), part_of(map_ref, held_map, number, 1)])

        def one(rows):
            linear = wide(held_map[rows, columns]) + held_pre[rows, columns] * scale_ref[:, columns] + shift_ref[:, columns]
            held_out[rows, columns] = low(gelu_slope(linear))

        by_rows(sites, 128, one)
        part_of(held_out, out_ref, number, 2).start()
        return carry

    lax.fori_loop(0, chunks, chunk, 0)
    wait_all([part_of(held_out, out_ref, number, 2) for number in range(chunks)])


def slope_back(upstream_ref, pre_ref, scale_ref, shift_ref, out_ref, scale_out_ref, shift_out_ref):
    sites, channels = pre_ref.shape

    def one(step, sums):
        rows = pl.ds(pl.multiple_of(step * 128, 128), 128)
        pre = pre_ref[rows]
        grad = upstream_ref[rows] * gelu_slope(pre * scale_ref[...] + shift_ref[...])
        out_ref[rows] = low(grad * scale_ref[...]).astype(out_ref.dtype)
        return sums[0] + fold(grad * pre), sums[1] + fold(grad)

    zero = jnp.zeros((8, channels), jnp.float32)
    scale_sum, shift_sum = lax.fori_loop(0, sites // 128, one, (zero, zero))
    scale_out_ref[...] = jnp.sum(scale_sum, axis=0, keepdims=True)
    shift_out_ref[...] = jnp.sum(shift_sum, axis=0, keepdims=True)


def later_back(
    groups_a, groups_b, place_ref, regions_grad_ref, pool_ref, scale_ref, scales_ref, pre_c_ref, slope_ref, act_b_ref,
    pre_b_ref, act_a_ref, pre_a_ref, packed_ref,
    send_ref, keep_ref, lin_c_grad_ref, pre_a_grad_ref, scale_c_out_ref, shift_c_out_ref, scale_b_out_ref, shift_b_out_ref,
    scale_a_out_ref, shift_a_out_ref,
    weight_b, weight_c, buffer, out_grad, pre_grad, turned, act_grad, wide_grad,
    held_pre_c, held_map, held_act_b, held_pre_b, held_act_a, held_pre_a, held_lin, sems_b, sems_c, out_sems, sems,
):
    sites, features = held_map.shape
    channels = held_act_b.shape[1]
    chunks, blocks = weight_c.shape[0], weight_c.shape[1]
    rows_b = groups_b * LANE_ROWS

    def part_of(source, target, number, sem):
        columns = pl.ds(pl.multiple_of(number * channels, channels), channels)
        return pltpu.make_async_copy(source.at[:, columns], target.at[:, columns], sems.at[sem + number])

    early = start_all([pltpu.make_async_copy(act_b_ref, held_act_b, sems.at[0])])
    copies_c = start_all(fetch_columns(packed_ref, weight_c, sems_c, groups_a + groups_b, chunks))
    for number in range(chunks):
        part_of(pre_c_ref, held_pre_c, number, 4).start()
        part_of(slope_ref, held_map, number, 4 + chunks).start()
    late = start_all(
        [
            pltpu.make_async_copy(pre_b_ref, held_pre_b, sems.at[1]),
            pltpu.make_async_copy(act_a_ref, held_act_a, sems.at[2]),
            pltpu.make_async_copy(pre_a_ref, held_pre_a, sems.at[3]),
        ]
    )
    copies_b = start_all(fetch(packed_ref, weight_b, sems_b, groups_a, groups_b))
    scale_b_ref, shift_b_ref, scale_a_ref, shift_a_ref = [scales_ref.at[pl.ds(number, 1)] for number in range(4)]
    act_grad[...] = jnp.zeros_like(act_grad)
    wait_all(early)
    turned[...] = held_act_b[...].T
    wait_all(copies_c)

    def chunk(number, carry):
        columns = pl.ds(pl.multiple_of(number * channels, channels), channels)
        out_grad[...] = dot_tn(pool_ref[...], regions_grad_ref[:, columns])
        part_of(pre_c_ref, held_pre_c, number, 4).wait()
        part_of(slope_ref, held_map, number, 4 + chunks).wait()

        def one(step, sums):
            rows = pl.ds(pl.multiple_of(step * 128, 128), 128)
            pre = held_pre_c[rows, columns]
            scale = scale_ref[:, columns]
            grad = out_grad[rows] * wide(held_map[rows, columns])
            held_lin[rows, columns] = low(grad)
            pre_grad[rows] = low(grad * scale)
            return sums[0] + fold(grad * pre), sums[1] + fold(grad)

        zero = jnp.zeros((8, channels), jnp.float32)
        scale_sum, shift_sum = lax.fori_loop(0, sites // 128, one, (zero, zero))
        part_of(held_lin, lin_c_grad_ref, number, 4 + 2 * chunks).start()
        scale_c_out_ref[:, columns] = jnp.sum(scale_sum, axis=0, keepdims=True)
        shift_c_out_ref[:, columns] = jnp.sum(shift_sum, axis=0, keepdims=True)
        part = low(product(turned[...], pre_grad[...])).reshape(blocks // 2, 2, LANE_ROWS, channels)
        rows = pl.ds(pl.multiple_of(rows_b + number * LANE_ROWS, LANE_ROWS), LANE_ROWS)
        for bit in range(2):
            buffer[half_of(place_ref, bit), :, rows] = part[:, bit]
        act_grad[...] += dot_nt(pre_grad[...], weight_c[number].reshape(channels, channels))
        return carry

    lax.fori_loop(0, chunks, chunk, 0)
    wait_all(late)
    slope_back(act_grad, held_pre_b, scale_b_ref, shift_b_ref, wide_grad, scale_b_out_ref, shift_b_out_ref)
    turned[...] = held_act_a[...].T
    wait_all(copies_b)
    for slide in (-1, 0, 1):
        slid = in_columns(wide_grad[...], -slide)
        for number, place in enumerate(places):
            if place[1] != slide:
                continue
            moved = low(in_rows(slid, -place[0]))
            store_rows(buffer, place_ref, low(product(turned[...], moved)), number * channels, rows_b)
            begin = number * channels // LANE_ROWS
            tap = weight_b[begin : begin + channels // LANE_ROWS].reshape(channels, channels)
            part = dot_nt(moved, tap)
            if slide == -1 and place[0] == -1:
                act_grad[...] = part
            else:
                act_grad[...] += part
    copies = hand_out(buffer, send_ref, keep_ref, out_sems)
    slope_back(act_grad, held_pre_a, scale_a_ref, shift_a_ref, pre_a_grad_ref, scale_a_out_ref, shift_a_out_ref)
    wait_all(copies)
    for number in range(chunks):
        part_of(held_lin, lin_c_grad_ref, number, 4 + 2 * chunks).wait()


def by_frames(grad, offset):
    if offset == 0:
        return grad
    sites, width = grad.shape
    tall = grad.reshape(sites // (FRAMES * SIDE * SIDE), FRAMES, SIDE * SIDE, width)
    edge = jnp.zeros_like(tall[:, :1])
    if offset > 0:
        tall = jnp.concatenate([edge, tall[:, :-1]], axis=1)
    else:
        tall = jnp.concatenate([tall[:, 1:], edge], axis=1)
    return tall.reshape(sites, width)


def first_back(place_ref, grad_ref, own_ref, got_ref, turned_ref, send_ref, keep_ref, sum_ref, buffer, held, sems, out_sems):
    features, sites = held.shape
    channels = grad_ref.shape[1]
    copies = [
        pltpu.make_async_copy(turned_ref.at[pl.ds(start, channels)], held.at[pl.ds(start, channels)], sems.at[start // channels])
        for start in range(0, features, channels)
    ]
    start_all(copies)
    sum_ref[...] = add_low(own_ref[...], got_ref[...])
    for tap in range(3):
        moved = by_frames(grad_ref[...], tap - 1)
        for start in range(0, features, channels):
            if tap == 0:
                copies[start // channels].wait()
            part = low(product(held[start : start + channels], moved))
            store_rows(buffer, place_ref, part, tap * features + start, buffer.shape[2])
    wait_all(hand_out(buffer, send_ref, keep_ref, out_sems))


def map_back(places_ref, grad_ref, weight_ref, lin_c_grad_ref, out_ref, moved, held_lin, held_out, sems):
    sites, features = held_out.shape
    channels = grad_ref.shape[1]
    copies = start_all([pltpu.make_async_copy(lin_c_grad_ref, held_lin, sems.at[0])])
    for tap in range(3):
        moved[tap] = by_frames(grad_ref[...], tap - 1)
    wait_all(copies)
    groups = channels // LANE_ROWS

    def chunk(number, carry):
        columns = pl.ds(pl.multiple_of(number * channels, channels), channels)
        total = wide(held_lin[:, columns])
        for tap in range(3):
            rows = pl.ds(tap * (features // LANE_ROWS) + number * groups, groups)
            total = total + dot_nt(moved[tap], weight_ref[rows].reshape(channels, channels))
        held_out[:, columns] = low(total)
        pltpu.make_async_copy(held_out.at[:, columns], out_ref.at[:, columns], sems.at[1 + number]).start()
        return carry

    lax.fori_loop(0, features // channels, chunk, 0)
    copies = []
    for number in range(features // channels):
        columns = pl.ds(number * channels, channels)
        copies.append(pltpu.make_async_copy(held_out.at[:, columns], out_ref.at[:, columns], sems.at[1 + number]))
    wait_all(copies)


COST = 1.5e10
WINDOW = 0.1
FIRST_LIMIT = 52
F32 = jnp.float32
BF16 = jnp.bfloat16
ANY = pl.BlockSpec(memory_space=pl.ANY)
SCALAR = pl.BlockSpec(memory_space=pltpu.SMEM)
HELD = pl.BlockSpec(memory_space=pltpu.VMEM)


def shape_of(dims, kind):
    return jax.ShapeDtypeStruct(dims, kind)


def add_low(left, right):
    return left + right


class Blocks:
    def __init__(self, ref, first, dims, rows):
        self.ref, self.first, self.dims, self.rows = ref, first, dims, rows

    @property
    def shape(self):
        return self.dims

    def span(self, index):
        index = index if isinstance(index, tuple) else (index,)
        flat = 0
        for place, size in zip(index, self.dims):
            flat = flat * size + place
        return pl.ds(pl.multiple_of(self.first + flat * self.rows, LANE_ROWS), self.rows)

    def __getitem__(self, index):
        return self.ref[self.span(index)]

    def __setitem__(self, index, value):
        self.ref[self.span(index)] = value


def after_last(places_ref, keep_ref, got_ref, keep_one, send_one, keep_two, send_two):
    half = keep_ref.shape[0] // 2
    across, inner = places_ref[0], places_ref[1]

    def one(number, carry):
        for place in range(2):
            keep_one[number, place] = add_low(keep_ref[number, place, across], got_ref[number, place, across])
            send_one[number, place] = add_low(keep_ref[number, place, 1 - across], got_ref[number, place, 1 - across])
            later = number + half
            keep_two[number, place] = add_low(keep_ref[later, inner, place], got_ref[later, inner, place])
            send_two[number, place] = add_low(keep_ref[later, 1 - inner, place], got_ref[later, 1 - inner, place])
        return carry

    lax.fori_loop(0, half, one, 0)


def after_cross(places_ref, keep_one, got_one, keep_two, got_two, kept_one, send_one, kept_two, send_two):
    across, inner = places_ref[0], places_ref[1]

    def one(number, carry):
        kept_one[number] = add_low(keep_one[number, inner], got_one[number, inner])
        send_one[number] = add_low(keep_one[number, 1 - inner], got_one[number, 1 - inner])
        kept_two[number] = add_low(keep_two[number, across], got_two[number, across])
        send_two[number] = add_low(keep_two[number, 1 - across], got_two[number, 1 - across])
        return carry

    lax.fori_loop(0, keep_two.shape[0], one, 0)


def after_plane(places_ref, keep_one, got_one, keep_two, got_two, kept_ref, sends):
    half = keep_one.shape[0]
    outer = places_ref[2]

    def block(place, target):
        @pl.when(place < half)
        def _():
            target[...] = add_low(keep_one[lax.rem(place, half)], got_one[lax.rem(place, half)])

        @pl.when(place >= half)
        def _():
            target[...] = add_low(keep_two[lax.rem(place, half)], got_two[lax.rem(place, half)])

    block(outer, kept_ref)
    for step, target in enumerate(sends):
        block(outer ^ (step + 1), target)


def total_of(refs):
    total = wide(refs[0][...])
    for ref in refs[1:]:
        total = total + wide(ref[...])
    return total


def kept_blocks(ref, half, rows, rows_a):
    pairs = 2 * half * rows_a
    return (
        Blocks(ref, 0, (half, 2), rows_a),
        Blocks(ref, pairs, (half, 2), rows_a),
        Blocks(ref, 2 * pairs, (half,), rows),
        Blocks(ref, 2 * pairs + half * rows, (half,), rows),
    )


def round_two(
    places_ref, keep_one, got_one, keep_two, got_two, keep_a, got_a, kept_ref, across_ref, inner_ref
):
    half, rows, rows_a = keep_one.shape[0], keep_one.shape[2], keep_a.shape[3]
    below = 2 * half * rows_a
    keep_a_one, keep_a_two, kept_one, kept_two = kept_blocks(kept_ref, half, rows, rows_a)
    after_last(
        places_ref, keep_a, got_a, keep_a_one, Blocks(across_ref, 0, (half, 2), rows_a), keep_a_two,
        Blocks(inner_ref, 0, (half, 2), rows_a),
    )
    after_cross(
        places_ref, keep_one, got_one, keep_two, got_two, kept_one, Blocks(inner_ref, below, (half,), rows), kept_two,
        Blocks(across_ref, below, (half,), rows),
    )


def bank_spans(lines, width, channels):
    groups = channels // width
    step = -(-lines // (groups * LANE_ROWS)) * LANE_ROWS
    return [(first, min(first + step, lines)) for first in range(0, lines, step)], step


def store_narrow(target, first, value, channels):
    lines, width = value.shape
    spans, step = bank_spans(lines, width, channels)
    target[first : first + step] = jnp.zeros((step, channels), BF16)
    for number, (begin, end) in enumerate(spans):
        target[first : first + end - begin, number * width : (number + 1) * width] = value[begin:end]


def load_narrow(value, first, lines, width):
    spans, _ = bank_spans(lines, width, value.shape[1])
    pieces = [
        value[first : first + end - begin, number * width : (number + 1) * width]
        for number, (begin, end) in enumerate(spans)
    ]
    return jnp.concatenate(pieces, axis=0)


def round_three(sizes, count, split, places_ref, held_ref, got_across, got_inner, *refs):
    half, rows, rows_a = sizes
    region_refs, refs = (refs[:2], refs[2:]) if split else (refs[:1], refs[1:])
    bank_refs, refs = (refs[:count], refs[count:]) if split else (refs[:1], refs[1:])
    kept_ref, across_ref, inner_ref, *sends = refs
    channels = kept_ref.shape[1]
    below = 2 * half * rows_a
    keep_a_one, keep_a_two, kept_one, kept_two = kept_blocks(held_ref, half, rows, rows_a)
    after_plane(
        places_ref, kept_one, Blocks(got_inner, below, (half,), rows), kept_two, Blocks(got_across, below, (half,), rows),
        kept_ref.at[pl.ds(0, rows)], sends,
    )
    after_cross(
        places_ref, keep_a_one, Blocks(got_across, 0, (half, 2), rows_a), keep_a_two,
        Blocks(got_inner, 0, (half, 2), rows_a), Blocks(kept_ref, rows, (half,), rows_a),
        Blocks(inner_ref, 0, (half,), rows_a), Blocks(kept_ref, rows + half * rows_a, (half,), rows_a),
        Blocks(across_ref, 0, (half,), rows_a),
    )
    across_ref[half * rows_a :] = low(total_of(region_refs))
    inner = places_ref[7] if split else 0
    keep = total_of([ref.at[inner] for ref in bank_refs])
    at = rows + 2 * half * rows_a
    store_narrow(kept_ref, at, low(keep), channels)
    if split:
        send = total_of([ref.at[1 - inner] for ref in bank_refs])
        store_narrow(inner_ref, half * rows_a, low(send), channels)
    else:
        inner_ref[half * rows_a :] = kept_ref[at:]


def round_four(sizes, count, split, widths, places_ref, held_ref, *refs):
    half, rows, rows_a = sizes
    plane_refs, refs = [held_ref.at[pl.ds(0, rows)], *refs[: count - 1]], refs[count - 1 :]
    across_ref, got_across, got_inner, done_ref, kept_a_ref = refs[:5]
    sends, (reduce_ref, query_ref, out_ref, head_ref) = refs[5 : 4 + count], refs[4 + count :]
    kept_a_one = Blocks(held_ref, rows, (half,), rows_a)
    kept_a_two = Blocks(held_ref, rows + half * rows_a, (half,), rows_a)
    bank_keep = held_ref[rows + 2 * half * rows_a :]
    below = half * rows_a
    after_plane(
        places_ref, kept_a_one, Blocks(got_inner, 0, (half,), rows_a), kept_a_two,
        Blocks(got_across, 0, (half,), rows_a), kept_a_ref, sends,
    )
    done_ref[:rows] = low(total_of(plane_refs))
    done_ref[rows:] = add_low(bank_keep, got_inner[below:]) if split else bank_keep
    region = wide(across_ref[below:]) + wide(got_across[below:]) if split else wide(across_ref[below:])
    _, _, feature_rows, channel_rows, _, joined_rows = widths
    reduce_ref[...] = region[:feature_rows]
    query_ref[...] = region[feature_rows : feature_rows + channel_rows]
    out_ref[...] = region[feature_rows + channel_rows : feature_rows + 2 * channel_rows]
    head = load_narrow(region, feature_rows + 2 * channel_rows, joined_rows, TILE)
    head_ref[...] = head[:, : head_ref.shape[1]]


def round_last(count, places_ref, *refs):
    part_ref, both = refs[-1 if len(refs) == count + 1 else -2], refs[-1]
    part_ref[...] = low(total_of(refs[:count]))
    if len(refs) > count + 1:
        for number, ref in enumerate(refs[count : count + 2]):
            both[number] = ref[...]


def sum_swap(places_ref, *refs):
    refs[-1][...] = low(total_of(refs[:-1]))


def front_pack(groups_a, groups_b, places_ref, conv_a_ref, conv_b_ref, conv_c_ref, own_a_ref, own_ref, sems):
    place = places_ref[9]
    chunks = own_ref.shape[0] - groups_b
    channels = own_ref.shape[2]
    copies = [
        pltpu.make_async_copy(conv_b_ref.at[pl.ds(place * groups_b, groups_b)], own_ref.at[pl.ds(0, groups_b)], sems.at[0]),
        pltpu.make_async_copy(conv_a_ref.at[pl.ds(place * groups_a, groups_a)], own_a_ref, sems.at[1]),
    ]
    for chunk in range(chunks):
        copies.append(
            pltpu.make_async_copy(
                conv_c_ref.at[place, :, pl.ds(chunk * channels, channels)], own_ref.at[groups_b + chunk], sems.at[2 + chunk]
            )
        )
    wait_all(start_all(copies))


def front_turn(places_ref, map_ref, bank_ref, turned_map_ref, turned_bank_ref):
    sites, features = map_ref.shape
    for start in range(0, features, sites):
        turned_map_ref[start : start + sites] = map_ref[:, start : start + sites].T
        turned_bank_ref[start : start + sites] = bank_ref[:, start : start + sites].T


def front_bank(places_ref, bank_ref, w_bank_ref, w_key_ref, w_value_ref, keys_ref, values_ref, turned_memory_ref):
    memory = low(product(bank_ref[...], w_bank_ref[...]))
    keys_ref[...] = low(product(memory, w_key_ref[...]))
    values_ref[...] = low(product(memory, w_value_ref[...]))
    turned_memory_ref[...] = memory.T


def front_head(
    places_ref, index_ref, weight_ref, logit_grad_ref, w_head_ref, w_out_ref,
    pool_ref, joined_grad_ref, hidden_grad_ref, branch_grad_ref,
):
    own, taps = index_ref.shape
    sites = pool_ref.shape[1]
    channels = hidden_grad_ref.shape[1]
    features = w_head_ref.shape[0] - channels
    column = lax.broadcasted_iota(jnp.int32, (own, sites), 1)
    pool = jnp.zeros((own, sites), F32)
    for tap in range(taps):
        weight = wide(weight_ref[:, tap : tap + 1])
        pool = pool + jnp.where(column == index_ref[:, tap : tap + 1], weight, 0.0)
    pool_ref[...] = low(pool)
    logit_grad = logit_grad_ref[pl.ds(pl.multiple_of(places_ref[8], LANE_ROWS), own)]
    joined_grad = dot_nt(logit_grad, w_head_ref[...])
    joined_grad_ref[...] = joined_grad
    hidden_grad_ref[...] = dot_nt(low(joined_grad[:, features:]), w_out_ref[...])
    branch_grad_ref[...] = low(dot_nt(logit_grad_ref[...], w_head_ref[features:]))


def region_pack(
    places_ref, regions_ref, reduced_ref, hidden_ref, query_grad_ref, reduced_grad_ref, w_out_ref, w_head_ref,
    logits_ref, message_ref,
):
    count = message_ref.shape[0]
    channels = reduced_ref.shape[1]
    reduced = reduced_ref[...]
    merged = low(reduced + product(hidden_ref[...], w_out_ref[...]))
    joined = jnp.concatenate([regions_ref[...], merged], axis=1)
    logits_ref[...] = low(product(joined, w_head_ref[...]))[:, : logits_ref.shape[1]]
    reduced_low = low(reduced)
    parts = [regions_ref[...], reduced_low, hidden_ref[...], joined]
    shared = [reduced_grad_ref[...], query_grad_ref[...]]
    for place in range(count):
        pieces = list(shared)
        for part in parts:
            width = part.shape[1] // count
            pieces.append(part[:, place * width : (place + 1) * width])
        spare = message_ref.shape[2] - sum(piece.shape[1] for piece in pieces)
        if spare:
            pieces.append(jnp.zeros((reduced.shape[0], spare), BF16))
        message_ref[place] = jnp.concatenate(pieces, axis=1)


def key_value_parts(places_ref, score_grad_ref, queries_ref, weights_ref, arrived_ref, out_ref):
    keys_here = score_grad_ref.shape[1]
    out_ref[:keys_here] = low(dot_tn(score_grad_ref[...], queries_ref[...]))
    out_ref[keys_here:] = low(dot_tn(weights_ref[...], arrived_ref[:, : queries_ref.shape[1]]))


def region_sums(widths, places_ref, group_ref, branch_grad_ref, logit_grad_ref, out_ref):
    ends, start = [], 0
    for width in widths:
        ends.append((start, start + width))
        start += width
    reduced_grad, query_grad, regions, reduced, hidden, joined = [group_ref[:, begin:end] for begin, end in ends]
    first, second = widths[2], widths[2] + widths[3]
    third = second + widths[4]
    channels = reduced_grad.shape[1]
    out_ref[:first] = low(dot_tn(regions, reduced_grad))
    out_ref[first:second] = low(dot_tn(reduced, query_grad))
    out_ref[second:third] = low(dot_tn(hidden, branch_grad_ref[...]))
    head = low(dot_tn(joined, logit_grad_ref[...]))
    store_narrow(out_ref, third, head, channels)


def bank_back(
    places_ref, sums_ref, w_key_ref, w_value_ref, w_bank_ref, turned_bank_ref, turned_memory_ref, *refs
):
    vectors, bank_grad_ref, outs, (message_ref, grads) = refs[:8], refs[8], refs[9:-2], refs[-2:]
    keys_here, features = bank_grad_ref.shape
    channels = sums_ref.shape[1]
    count, _, width = message_ref.shape
    key_low, value_low = sums_ref[:keys_here], sums_ref[keys_here:]
    memory_grad = low(dot_nt(key_low, w_key_ref[...]) + dot_nt(value_low, w_value_ref[...]))
    for start in range(0, features, channels):
        bank_grad_ref[:, start : start + channels] = low(dot_nt(memory_grad, w_bank_ref[start : start + channels]))
    grads[:keys_here] = memory_grad
    grads[keys_here : 2 * keys_here] = key_low
    grads[2 * keys_here :] = value_low

    def columns(rows):
        if width % TILE == 0:
            return grads[rows, pl.ds(pl.multiple_of(places_ref[4] * width, width), width)]
        picked = grads[rows, :width]
        for number in range(1, channels // width):
            picked = jnp.where(places_ref[4] == number, grads[rows, number * width : (number + 1) * width], picked)
        return picked

    feature_rows, channel_rows = features // count, channels // count
    part = low(product(turned_bank_ref[...], columns(pl.ds(0, keys_here))))
    message_ref[:, :feature_rows] = part.reshape(count, feature_rows, width)
    at = feature_rows
    for number in (1, 2):
        part = low(product(turned_memory_ref[...], columns(pl.ds(number * keys_here, keys_here))))
        message_ref[:, at : at + channel_rows] = part.reshape(count, channel_rows, width)
        at += channel_rows
    spare = message_ref.shape[1] - at
    for place in range(count):
        row = []
        for vector_ref in vectors:
            share = vector_ref.shape[1] // count
            row.append(vector_ref[:, place * share : (place + 1) * share])
        total = sum(piece.shape[1] for piece in row)
        lines = -(-total // width)
        if lines * width > total:
            row.append(jnp.zeros((1, lines * width - total), F32))
        row = jnp.concatenate(row, axis=1)
        tile = [row[:, line * width : (line + 1) * width] for line in range(lines)]
        tile.append(jnp.zeros((spare - lines, width), F32))
        message_ref[place, at:] = low(jnp.concatenate(tile, axis=0))
    inner = outs[0].shape[0]
    for step, out_ref in enumerate(outs):
        out_ref[...] = message_ref[pl.ds((places_ref[6] ^ step) * inner, inner)]


def finish(shape_info, places_ref, part_ref, *refs):
    rows_b, rows_c, feature_rows, channel_rows, lines, split = shape_info
    if split:
        own_ref, got_ref, refs = refs[0], refs[1], refs[2:]
        weight_refs = [own_ref.at[0], got_ref.at[0], own_ref.at[1], got_ref.at[1]]
        bank_refs, first = weight_refs, rows_b + rows_c
    else:
        weight_refs, bank_refs, refs, first = refs[:1], refs[1:-14], refs[-14:], 0
    conv_a_ref, conv_b_ref, conv_c_ref, bank_out_ref, key_ref, value_ref = refs[:6]
    vectors = refs[6:]
    conv_a_ref[...] = wide(part_ref[...]).reshape(conv_a_ref.shape)
    channels = weight_refs[0].shape[1]
    width = channels // len(bank_refs)

    def spot(number, size):
        if not split:
            return pl.ds(number * size, size)
        return pl.ds(pl.multiple_of((places_ref[4] ^ number) * size, size), size)

    for number, ref in enumerate(weight_refs):
        conv_b_ref[spot(number, rows_b)] = wide(ref[:rows_b])
        for chunk in range(rows_c // LANE_ROWS):
            begin = rows_b + chunk * LANE_ROWS
            conv_c_ref[spot(number, LANE_ROWS), chunk * channels : (chunk + 1) * channels] = wide(
                ref[begin : begin + LANE_ROWS]
            )
    tile = None
    at = feature_rows + 2 * channel_rows
    for number, ref in enumerate(bank_refs):
        bank = wide(load_narrow(ref, first, lines, width))
        columns = spot(number, width)
        bank_out_ref[:, columns] = bank[:feature_rows]
        key_ref[:, columns] = bank[feature_rows : feature_rows + channel_rows]
        value_ref[:, columns] = bank[feature_rows + channel_rows : at]
        tile = bank[at:] if tile is None else tile + bank[at:]
    total = sum(ref.shape[1] for ref in vectors)
    row = jnp.concatenate([tile[line : line + 1] for line in range(-(-total // width))], axis=1)
    at = 0
    for ref in vectors:
        ref[...] = row[:, at : at + ref.shape[1]]
        at += ref.shape[1]


def run_kernel(
    kernel, places, arrays, shapes, name, micros, scratch=(), raw_in=(), raw_out=(), fetched=(), limit=8
):
    count_in, count_out, fetched = len(arrays), len(shapes), list(fetched)

    def wrapped(*refs):
        places_ref, ins = refs[0], list(refs[1 : 1 + count_in])
        out_places, outs = refs[1 + count_in], refs[2 + count_in : 2 + count_in + count_out]
        extra = refs[2 + count_in + count_out :]
        if fetched:
            held, sems, extra = extra[: len(fetched)], extra[len(fetched)], extra[len(fetched) + 1 :]
            copies = start_all(
                [pltpu.make_async_copy(ins[number], held[slot], sems.at[slot]) for slot, number in enumerate(fetched)]
            )
        for number in range(places.shape[0]):
            out_places[number] = places_ref[number]
        if fetched:
            wait_all(copies)
            for slot, number in enumerate(fetched):
                ins[number] = held[slot]
        kernel(places_ref, *ins, *outs, *extra)

    outside = [*raw_in, *fetched]
    buffers = [pltpu.VMEM(arrays[number].shape, arrays[number].dtype) for number in fetched]
    if fetched:
        buffers.append(pltpu.SemaphoreType.DMA((len(fetched),)))
    return pl.pallas_call(
        wrapped,
        out_shape=[shape_of(places.shape, jnp.int32)] + list(shapes),
        in_specs=[SCALAR] + [ANY if number in outside else HELD for number in range(count_in)],
        out_specs=[SCALAR] + [ANY if number in raw_out else HELD for number in range(count_out)],
        scratch_shapes=buffers + list(scratch),
        compiler_params=params(limit),
        cost_estimate=pl.CostEstimate(
            flops=int(micros * COST), bytes_accessed=int(micros * COST / 1000), transcendentals=0
        ),
        name=name,
    )(places, *arrays)


def run_first_conv(places, feature_map, sources, scale, shift):
    sites, channels = feature_map.shape[0], sources[0].shape[3]
    groups = sources[0].shape[1]
    blocks = sum(source.shape[0] for source in sources)
    return pl.pallas_call(
        first_conv,
        out_shape=[
            shape_of((sites, channels), F32),
            shape_of((sites, channels), BF16),
            shape_of((blocks * groups, LANE_ROWS, channels), BF16),
        ],
        in_specs=[SCALAR, HELD] + [ANY] * len(sources) + [HELD] * 2,
        out_specs=[ANY, HELD, ANY],
        scratch_shapes=[
            pltpu.VMEM((blocks * groups, LANE_ROWS, channels), BF16),
            pltpu.VMEM((sites, channels), F32),
            pltpu.SemaphoreType.DMA((blocks,)),
            pltpu.SemaphoreType.DMA((2,)),
        ],
        compiler_params=params(FIRST_LIMIT),
        cost_estimate=pl.CostEstimate(flops=int(6 * COST), bytes_accessed=int(6 * COST / 1000), transcendentals=0),
        name="first_conv",
    )(places, feature_map, *sources, scale.reshape(1, -1), shift.reshape(1, -1))


def run_later_convs(
    act_a, feature_map, packed, scale_b, shift_b, scale_c, shift_c, pooling, w_reduce, w_query, groups_b, groups_c
):
    sites, channels = act_a.shape
    features = feature_map.shape[1]
    blocks = packed.shape[0]
    own = pooling.shape[0]
    group = lax.axis_size("bank")
    return pl.pallas_call(
        later_convs,
        out_shape=[
            jax.ShapeDtypeStruct((sites, channels), jnp.float32),
            jax.ShapeDtypeStruct((sites, channels), jnp.bfloat16),
            jax.ShapeDtypeStruct((sites, features), jnp.float32),
            jax.ShapeDtypeStruct((own, features), jnp.bfloat16),
            jax.ShapeDtypeStruct((own, channels), jnp.float32),
            jax.ShapeDtypeStruct((group, own, channels), jnp.bfloat16),
        ],
        in_specs=[HELD] + [ANY] * 2 + [HELD] * 5 + [ANY] * 2,
        out_specs=[ANY] * 5 + [HELD],
        scratch_shapes=[
            pltpu.VMEM((blocks * groups_b, LANE_ROWS, channels), jnp.bfloat16),
            pltpu.VMEM((groups_c, blocks, LANE_ROWS, channels), jnp.bfloat16),
            pltpu.VMEM((sites, channels), jnp.bfloat16),
            pltpu.VMEM((sites, features), jnp.bfloat16),
            pltpu.VMEM((sites, features), jnp.float32),
            pltpu.VMEM(w_reduce.shape, jnp.bfloat16),
            pltpu.VMEM((sites, channels), jnp.float32),
            pltpu.VMEM((sites, channels), jnp.bfloat16),
            pltpu.VMEM((own, features), jnp.bfloat16),
            pltpu.VMEM((own, channels), jnp.float32),
            pltpu.VMEM(w_query.shape, jnp.bfloat16),
            pltpu.SemaphoreType.DMA((blocks,)),
            pltpu.SemaphoreType.DMA((blocks,)),
            pltpu.SemaphoreType.DMA((7 + groups_c,)),
        ],
        compiler_params=params(52),
        cost_estimate=pl.CostEstimate(flops=int(15 * COST), bytes_accessed=int(15 * COST / 1000), transcendentals=0),
        name="later_convs",
    )(
        act_a, feature_map, packed, scale_b.reshape(1, -1), shift_b.reshape(1, -1), scale_c.reshape(1, -1),
        shift_c.reshape(1, -1), pooling, w_reduce, w_query,
    )


def body(
    feature_map,
    bank,
    region_time,
    roi_index,
    roi_weight,
    conv_a,
    scale_a,
    shift_a,
    conv_b,
    scale_b,
    shift_b,
    conv_c,
    scale_c,
    shift_c,
    w_reduce,
    w_bank,
    w_query,
    w_key,
    w_value,
    ln_gain,
    ln_shift,
    w_out,
    w_head,
    logit_grad,
):
    site_count = feature_map.shape[0]
    feature_count = feature_map.shape[1]
    channels = w_query.shape[0]
    classes = w_head.shape[1]
    keys_here = bank.shape[0]
    own_count = roi_index.shape[0]
    bank_count = lax.axis_size("bank")
    bank_place = lax.axis_index("bank")
    dp_count = lax.axis_size("dp")
    dp_place = lax.axis_index("dp")
    first_row = bank_place * own_count
    half_span = keys_here * bank_count // 2
    group_rows = bank_count * own_count
    chunks = feature_count // channels
    shards = (conv_a, conv_b, conv_c)
    split = dp_count // 2 == 2 and bank_count // 2 == 4 and all(shard.shape[0] % (LANE_ROWS * dp_count) == 0 for shard in shards)
    axes = block_axes(split, dp_count, bank_count)
    outer, inner, across, last = axes
    outer_count = outer.size if split else 1
    blocks = bank_count * dp_count if split else bank_count
    halves = tuple(axis.size for axis in axes[:3])
    places_here = jnp.stack([across.place(), inner.place(), outer.place(), last.place(), dp_place, bank_place * keys_here, outer.place() if split else 0 * bank_place, inner.place(), first_row, dp_place if split else 0 * dp_place])

    parts = dp_count if split else 1
    rows_a, rows_b, rows_c = [shard.shape[0] // parts for shard in shards]
    groups_a, groups_b, groups_c = rows_a // LANE_ROWS, rows_b // LANE_ROWS, chunks
    places, own_a, own_packed = run_kernel(
        functools.partial(front_pack, groups_a, groups_b),
        places_here,
        [shard.reshape(-1, LANE_ROWS, shard.shape[1]) for shard in shards],
        [shape_of((groups_a, LANE_ROWS, channels), BF16), shape_of((groups_b + chunks, LANE_ROWS, channels), BF16)],
        "front_pack",
        1,
        scratch=[pltpu.SemaphoreType.DMA((2 + chunks,))],
        raw_in=(0, 1, 2),
        raw_out=(0, 1),
    )
    packed = lax.all_gather(own_packed, ("bank", "dp") if split else "bank", axis=0, tiled=False)
    packed = packed.reshape((blocks,) + own_packed.shape)
    spare = ((0, 0), (0, TILE - classes))
    wide_head, wide_logit_grad = jnp.pad(w_head, spare), jnp.pad(logit_grad, spare)
    front = {}

    def turn(places):
        places, front["turned_map"], front["turned_bank"] = run_kernel(
            front_turn,
            places,
            [feature_map, bank],
            [shape_of((feature_count, site_count), BF16), shape_of((feature_count, keys_here), BF16)],
            "front_turn",
            6,
            limit=16,
        )
        return places

    def project(places):
        inside = shape_of((keys_here, channels), BF16)
        places, front["keys"], front["values"], front["turned_memory"] = run_kernel(
            front_bank,
            places,
            [bank, w_bank, w_key, w_value],
            [inside, inside, shape_of((channels, keys_here), BF16)],
            "front_bank",
            6,
            limit=16,
        )
        return places

    def head(places):
        places, front["pooling"], front["joined_grad"], front["hidden_grad"], front["group_branch_grad"] = run_kernel(
            front_head,
            places,
            [roi_index, roi_weight, wide_logit_grad, wide_head, w_out],
            [
                shape_of((own_count, site_count), BF16),
                shape_of((own_count, w_head.shape[0]), F32),
                shape_of((own_count, channels), F32),
                shape_of((group_rows, channels), BF16),
            ],
            "front_head",
            4,
            limit=16,
        )
        return places

    if split:
        places, sources = gather_blocks(own_a, axes, places, [turn, project, head])
    else:
        places, sources = head(project(turn(places))), [lax.all_gather(own_a, "bank", axis=0, tiled=False)]
    turned_map, turned_bank, turned_memory = front["turned_map"], front["turned_bank"], front["turned_memory"]
    keys, values, pooling = front["keys"], front["values"], front["pooling"]
    joined_grad, hidden_grad, group_branch_grad = front["joined_grad"], front["hidden_grad"], front["group_branch_grad"]
    time_column = region_time.reshape(-1, 1)
    scales = jnp.stack([scale_b, shift_b, scale_a, shift_a])
    places, time_column, scales, *sources = lax.optimization_barrier((places, time_column, scales, *sources))

    pre_a, act_a, weight_a = run_first_conv(places, feature_map, sources, scale_a, shift_a)
    pre_b, act_b, pre_c, regions, reduced, own_queries = run_later_convs(
        act_a, feature_map, packed, scale_b, shift_b, scale_c, shift_c, pooling, w_reduce, w_query, groups_b, groups_c
    )
    queries = to_owners(own_queries).reshape(group_rows, channels)
    places, message, scores = run_kernel(
        functools.partial(attend, half_span),
        places,
        [queries, keys, values, time_column],
        [shape_of((group_rows, channels + TILE), BF16), shape_of((group_rows, keys_here), F32)],
        "attend",
        2,
    )
    arrived = to_owners(message.reshape(bank_count, own_count, channels + TILE))
    row = shape_of((1, channels), F32)
    places, message, hidden_low, gain_part, shift_part = run_kernel(
        merge_rows,
        places,
        [arrived, hidden_grad, ln_gain.reshape(1, -1), ln_shift.reshape(1, -1)],
        [shape_of(arrived.shape, BF16), shape_of((own_count, channels), BF16), row, row],
        "merge_rows",
        2,
    )
    arrived = to_owners(message).reshape(group_rows, channels + TILE)
    maps = (site_count, feature_count)
    inside = (site_count, channels)
    places, slope_c = run_kernel(
        slopes_outer,
        places,
        [scale_c.reshape(1, -1), shift_c.reshape(1, -1), pre_c, feature_map],
        [shape_of(maps, BF16)],
        "slopes_outer",
        WINDOW,
        scratch=[
            pltpu.VMEM(maps, F32), pltpu.VMEM(maps, BF16), pltpu.VMEM(maps, BF16), pltpu.SemaphoreType.DMA((3, chunks))
        ],
        raw_in=(2, 3),
        raw_out=(0,),
        limit=52,
    )
    group_shape = shape_of((group_rows, channels), BF16)
    weight_shape = shape_of((group_rows, keys_here), BF16)
    places, query_part, score_grad, weights_low = run_kernel(
        attend_back,
        places,
        [arrived, scores, keys, values],
        [group_shape, weight_shape, weight_shape],
        "attend_back",
        2,
    )
    query_parts = to_owners(query_part.reshape(bank_count, own_count, channels))
    places, key_value = run_kernel(
        key_value_parts,
        places,
        [score_grad, queries, weights_low, arrived],
        [shape_of((2 * keys_here, channels), BF16)],
        "key_value_parts",
        3,
    )

    def dp_swap(value, step):
        return lax.ppermute(value, "dp", [(i, i ^ step) for i in range(dp_count)])

    key_value_got = dp_swap(key_value, 1)

    def summed_swap(places, own, got):
        places, own = run_kernel(
            sum_swap, places, [own, got], [shape_of(own.shape, BF16)], "sum_swap", 2
        )
        return places, own

    places, key_value = summed_swap(places, key_value, key_value_got)
    step = 2
    while step * 2 < dp_count:
        places, key_value = summed_swap(places, key_value, dp_swap(key_value, step))
        step *= 2
    key_value_got = dp_swap(key_value, step)
    own_shape = shape_of((own_count, channels), BF16)
    places, query_grad, reduced_grad, regions_grad = run_kernel(
        region_back,
        places,
        [query_parts, joined_grad, w_query, w_reduce],
        [own_shape, own_shape, shape_of((own_count, feature_count), BF16)],
        "region_back",
        3,
    )
    half_blocks = blocks // 2
    rows_bc = rows_b + groups_c * LANE_ROWS
    wide_row = shape_of((1, feature_count), F32)
    (
        places, send_bc, keep_bc, lin_c_grad, pre_a_grad,
        scale_c_part, shift_c_part, scale_b_part, shift_b_part, scale_a_part, shift_a_part,
    ) = run_kernel(
        functools.partial(later_back, 0, groups_b),
        places,
        [
            regions_grad, pooling, scale_c.reshape(1, -1), scales, pre_c, slope_c, act_b, pre_b, act_a, pre_a, packed,
        ],
        [shape_of((half_blocks, rows_bc, channels), BF16)] * 2
        + [shape_of(maps, BF16), shape_of(inside, BF16), wide_row, wide_row]
        + [row] * 4,
        "later_back",
        28,
        scratch=[
            pltpu.VMEM((blocks * groups_b, LANE_ROWS, channels), BF16),
            pltpu.VMEM((groups_c, blocks, LANE_ROWS, channels), BF16),
            pltpu.VMEM((2, half_blocks, rows_bc, channels), BF16),
            pltpu.VMEM(inside, F32),
            pltpu.VMEM(inside, BF16),
            pltpu.VMEM((channels, site_count), BF16),
            pltpu.VMEM(inside, F32),
            pltpu.VMEM(inside, F32),
            pltpu.VMEM(maps, F32),
            pltpu.VMEM(maps, BF16),
            pltpu.VMEM(inside, BF16),
            pltpu.VMEM(inside, F32),
            pltpu.VMEM(inside, BF16),
            pltpu.VMEM(inside, F32),
            pltpu.VMEM(maps, BF16),
            pltpu.SemaphoreType.DMA((blocks,)),
            pltpu.SemaphoreType.DMA((blocks,)),
            pltpu.SemaphoreType.DMA((2,)),
            pltpu.SemaphoreType.DMA((4 + 3 * chunks,)),
        ],
        raw_in=range(4, 11),
        raw_out=(0, 1, 2),
        limit=40,
    )
    got_bc = last.swap(send_bc, 1)

    def parted(value):
        return value.reshape(halves + value.shape[1:])

    places, send_a, keep_a, key_value = run_kernel(
        first_back,
        places,
        [pre_a_grad, key_value, key_value_got, turned_map],
        [shape_of((half_blocks, rows_a, channels), BF16)] * 2 + [shape_of(key_value.shape, BF16)],
        "first_back",
        6,
        scratch=[
            pltpu.VMEM((2, half_blocks, rows_a, channels), BF16),
            pltpu.VMEM(turned_map.shape, BF16),
            pltpu.SemaphoreType.DMA((chunks,)),
            pltpu.SemaphoreType.DMA((2,)),
        ],
        raw_in=(3,),
        raw_out=(0, 1),
        limit=20,
    )
    got_a = last.swap(send_a, 1)
    half = outer.size // 2
    plane_shape = (half, 2, rows_bc, channels)
    places, keep_one, send_one, keep_two, send_two = run_kernel(
        after_last, places, [parted(keep_bc), parted(got_bc)], [shape_of(plane_shape, BF16)] * 4, "round_one", 4
    )
    got_one, got_two = across.swap(send_one, 1), inner.swap(send_two, 1)
    feature_rows, channel_rows = feature_count // bank_count, channels // bank_count
    joined_rows = (feature_count + channels) // bank_count
    widths = (channels, channels, feature_rows, channel_rows, channel_rows, joined_rows)
    message_width = -(-sum(widths) // TILE) * TILE
    places, logits_out, message = run_kernel(
        region_pack,
        places,
        [regions, reduced, hidden_low, query_grad, reduced_grad, w_out, wide_head],
        [shape_of((own_count, classes), BF16), shape_of((bank_count, own_count, message_width), BF16)],
        "region_pack",
        WINDOW,
    )
    group = to_owners(message).reshape(group_rows, message_width)

    places, map_grad = run_kernel(
        map_back,
        places,
        [pre_a_grad, weight_a, lin_c_grad],
        [shape_of(maps, BF16)],
        "map_back",
        WINDOW,
        scratch=[
            pltpu.VMEM((3,) + inside, BF16),
            pltpu.VMEM(maps, BF16),
            pltpu.VMEM(maps, BF16),
            pltpu.SemaphoreType.DMA((1 + chunks,)),
        ],
        raw_in=(2,),
        raw_out=(0,),
        limit=12,
    )
    kept_shape = shape_of((2 * half * (2 * rows_a + rows_bc), channels), BF16)
    both = shape_of((half * (2 * rows_a + rows_bc), channels), BF16)
    places, held, send_across, send_inner = run_kernel(
        round_two,
        places,
        [keep_one, got_one, keep_two, got_two, parted(keep_a), parted(got_a)],
        [kept_shape, both, both],
        "round_two",
        5,
    )
    got_across, got_inner = across.swap(send_across, 1), inner.swap(send_inner, 1)
    vectors = [
        gain_part, shift_part, scale_a_part, shift_a_part, scale_b_part, shift_b_part, scale_c_part, shift_c_part
    ]
    width = channels // dp_count
    lines = -(-sum(vector.shape[1] for vector in vectors) // (bank_count * width))
    lines = -(-lines // LANE_ROWS) * LANE_ROWS
    bank_lines = feature_rows + 2 * channel_rows + lines
    bank_step = bank_spans(bank_lines, width, channels)[1]
    region_lines = feature_rows + 2 * channel_rows + bank_spans(joined_rows, TILE, channels)[1]
    places, bank_grad, *bank_pieces = run_kernel(
        bank_back,
        places,
        [key_value, w_key, w_value, w_bank, turned_bank, turned_memory] + vectors,
        [shape_of(bank.shape, BF16)]
        + [shape_of((bank_count // outer_count, bank_lines, width), BF16)] * outer_count,
        "bank_back",
        WINDOW,
        scratch=[
            pltpu.VMEM((bank_count, bank_lines, width), BF16),
            pltpu.VMEM((3 * keys_here, channels), BF16),
        ],
        limit=8,
    )
    places, region_parts = run_kernel(
        functools.partial(region_sums, widths),
        places,
        [group, group_branch_grad, wide_logit_grad],
        [shape_of((region_lines, channels), BF16)],
        "region_sums",
        WINDOW,
    )
    region_both = [region_parts, dp_swap(region_parts, 1)] if split else [lax.psum(region_parts, "dp")]
    if split:
        bank_parts = [bank_pieces[0]] + [outer.swap(piece, step + 1) for step, piece in enumerate(bank_pieces[1:])]
    else:
        bank_parts = [low(jnp.sum(wide(to_owners(bank_pieces[0])), axis=0, keepdims=True))]
    sizes = (half, rows_bc, rows_a)
    places, held, send_across, send_inner, *pieces_bc = run_kernel(
        functools.partial(round_three, sizes, outer.size, split),
        places,
        [held, got_across, got_inner] + region_both + bank_parts,
        [
            shape_of((rows_bc + 2 * half * rows_a + bank_step, channels), BF16),
            shape_of((half * rows_a + region_lines, channels), BF16),
            shape_of((half * rows_a + bank_step, channels), BF16),
        ]
        + [shape_of((rows_bc, channels), BF16)] * (outer.size - 1),
        "round_three",
        5,
    )
    got_across, got_inner = across.swap(send_across, 1), inner.swap(send_inner, 1)
    got_bc = [outer.swap(piece, step + 1) for step, piece in enumerate(pieces_bc)]
    row_block = shape_of((channel_rows, channels), F32)
    results = run_kernel(
        functools.partial(round_four, sizes, outer.size, split, widths),
        places,
        [held, *got_bc, send_across, got_across, got_inner],
        [shape_of((rows_bc + bank_step, channels), BF16)]
        + [shape_of((rows_a, channels), BF16)] * outer.size
        + [shape_of((feature_rows, channels), F32), row_block, row_block, shape_of((joined_rows, classes), F32)],
        "round_four",
        4,
    )
    places, done, kept_a, *pieces_a = results[: 2 + outer.size]
    reduce_weight_grad, query_weight_grad, out_weight_grad, head_weight_grad = results[2 + outer.size :]
    got_a = [outer.swap(piece, step + 1) for step, piece in enumerate(pieces_a)]
    done_both = [done, across.swap(done, 1)] if split else []
    row_block = shape_of((channel_rows, channels), F32)
    places, part_a, *both = run_kernel(
        functools.partial(round_last, outer.size),
        places,
        [kept_a, *got_a, *done_both],
        [shape_of((rows_a, channels), BF16)] + [shape_of((2,) + done.shape, BF16)] * len(done_both[1:]),
        "round_last",
        2,
    )
    if split:
        done_a = lax.all_gather(part_a, "dp", axis=0, tiled=False)
        done_all = [both[0], last.swap(both[0], 1)]
    else:
        done_a = lax.psum(part_a, "dp")
        bank_all = lax.all_gather(done[rows_bc:], "dp", axis=0, tiled=False)
        done_all = [lax.psum(done[:rows_bc], "dp")] + [bank_all[place] for place in range(dp_count)]
    info = (rows_b, groups_c * LANE_ROWS, feature_rows, channel_rows, bank_lines, split)
    results = run_kernel(
        functools.partial(finish, info),
        places,
        [done_a, *done_all],
        [shape_of(conv_a.shape, F32), shape_of(conv_b.shape, F32), shape_of(conv_c.shape, F32)]
        + [shape_of((feature_rows, channels), F32), row_block, row_block]
        + [shape_of((1, vector.shape[1] // bank_count), F32) for vector in vectors],
        "finish",
        3,
    )
    places, conv_a_grad, conv_b_grad, conv_c_grad, bank_weight_grad, key_weight_grad, value_weight_grad = results[:7]
    small = [value.reshape(-1) for value in results[7:]]
    gain_grad, shift_grad = small[:2]
    scale_a_grad, shift_a_grad, scale_b_grad, shift_b_grad, scale_c_grad, shift_c_grad = small[2:]
    return (
        logits_out,
        map_grad,
        bank_grad,
        conv_a_grad,
        scale_a_grad,
        shift_a_grad,
        conv_b_grad,
        scale_b_grad,
        shift_b_grad,
        conv_c_grad,
        scale_c_grad,
        shift_c_grad,
        reduce_weight_grad,
        bank_weight_grad,
        query_weight_grad,
        key_weight_grad,
        value_weight_grad,
        gain_grad,
        shift_grad,
        out_weight_grad,
        head_weight_grad,
    )


def solution(mesh):
    in_specs = (
        P(("dp", "bank"), None),
        P("bank", None),
        P("dp"),
        P(("dp", "bank"), None),
        P(("dp", "bank"), None),
        P("bank", None),
        P(),
        P(),
        P("bank", None),
        P(),
        P(),
        P("bank", None),
        P(),
        P(),
        P(),
        P(),
        P(),
        P(),
        P(),
        P(),
        P(),
        P(),
        P(),
        P("dp", None),
    )
    out_specs = (
        P(("dp", "bank"), None),
        P(("dp", "bank"), None),
        P("bank", None),
        P("bank", None),
        P("bank"),
        P("bank"),
        P("bank", None),
        P("bank"),
        P("bank"),
        P("bank", None),
        P("bank"),
        P("bank"),
        P("bank", None),
        P("bank", None),
        P("bank", None),
        P("bank", None),
        P("bank", None),
        P("bank"),
        P("bank"),
        P("bank", None),
        P("bank", None),
    )
    return jax.shard_map(body, mesh=mesh, in_specs=in_specs, out_specs=out_specs, check_vma=False)
```

```python
import functools

import jax
import jax.numpy as jnp
from jax import lax
from jax.experimental import pallas as pl
from jax.experimental.pallas import tpu as pltpu
from jax.sharding import PartitionSpec as P

FRAMES = 4
SIDE = 8
LANE_ROWS = 16
TILE = 128
ROOT = 0.7978845608028654
CUBIC = 0.044715

epsilon = 1e-05
masked_score = -1e30
places = [(-1, -1), (-1, 0), (-1, 1), (0, -1), (0, 0), (0, 1), (1, -1), (1, 0), (1, 1)]


def product(left, right):
    return jnp.dot(left, right, preferred_element_type=jnp.float32)


def low(value):
    return value.astype(jnp.bfloat16)


def wide(value):
    return value.astype(jnp.float32)


class SubAxis:
    def __init__(self, name, size, stride):
        self.name, self.size, self.stride = name, size, stride

    def place(self):
        return lax.rem(lax.axis_index(self.name) // self.stride, self.size)

    def swap(self, value, step):
        count = lax.axis_size(self.name)
        pairs = [(i, i ^ (step * self.stride)) for i in range(count)]
        return lax.ppermute(value, self.name, pairs)


def block_axes(split, dp_count, bank_count):
    if split:
        return (
            SubAxis("bank", bank_count // 2, 2),
            SubAxis("bank", 2, 1),
            SubAxis("dp", dp_count // 2, 2),
            SubAxis("dp", 2, 1),
        )
    return (
        SubAxis("bank", bank_count // 8, 8),
        SubAxis("bank", 2, 4),
        SubAxis("bank", 2, 2),
        SubAxis("bank", 2, 1),
    )


def gather_blocks(own, axes, places, steps):
    outer, inner, across, last = axes
    blocks = [own] + [outer.swap(own, step) for step in range(1, outer.size)]
    places = steps[0](places)
    *blocks, places = lax.optimization_barrier((*blocks, places))
    blocks = jnp.stack(blocks)
    half = outer.size // 2
    first, second = blocks[:half], blocks[half:]
    got_first, got_second = across.swap(first, 1), inner.swap(second, 1)
    places = steps[1](places)
    first, got_first, second, got_second, places = lax.optimization_barrier((first, got_first, second, got_second, places))
    first, second = jnp.concatenate([first, got_first]), jnp.concatenate([second, got_second])
    got_first, got_second = inner.swap(first, 1), across.swap(second, 1)
    places = steps[2](places)
    first, got_first, second, got_second, places = lax.optimization_barrier((first, got_first, second, got_second, places))
    near = jnp.concatenate([first, got_first, second, got_second])
    return places, [near, last.swap(near, 1)]


def to_owners(value):
    return lax.all_to_all(value, "bank", split_axis=0, concat_axis=0, tiled=True)


def to_group(value):
    count = lax.axis_size("bank")
    return to_owners(jnp.broadcast_to(value[None], (count,) + value.shape))


def params(mib):
    return pltpu.CompilerParams(vmem_limit_bytes=mib * 1024 * 1024)


def gelu_of(x):
    return 0.5 * x * (1.0 + jnp.tanh(ROOT * (x + CUBIC * x * x * x)))


def gelu_slope(x):
    square = x * x
    bent = jnp.tanh(ROOT * x * (1.0 + CUBIC * square))
    return 0.5 * (1.0 + bent) + 0.5 * ROOT * x * (1.0 - bent * bent) * (1.0 + 3.0 * CUBIC * square)


def by_rows(count, step, work):
    def one(number, carry):
        work(pl.ds(pl.multiple_of(number * step, step), step))
        return carry

    lax.fori_loop(0, count // step, one, 0)


def dot_tn(left, right):
    return lax.dot_general(
        left, right, (((0,), (0,)), ((), ())), preferred_element_type=jnp.float32
    )


def dot_nt(left, right):
    return lax.dot_general(
        left, right, (((1,), (1,)), ((), ())), preferred_element_type=jnp.float32
    )


def in_rows(value, step):
    if step == 0:
        return value
    sites, width = value.shape
    tall = value.reshape(sites // (SIDE * SIDE), SIDE, SIDE, width)
    edge = jnp.zeros_like(tall[:, :1])
    if step > 0:
        tall = jnp.concatenate([tall[:, 1:], edge], axis=1)
    else:
        tall = jnp.concatenate([edge, tall[:, :-1]], axis=1)
    return tall.reshape(sites, width)


def in_columns(value, step):
    if step == 0:
        return value
    sites = value.shape[0]
    turned = pltpu.roll(value, (-step) % sites, 0)
    column = lax.broadcasted_iota(jnp.int32, value.shape, 0) % SIDE
    keep = column != (SIDE - 1 if step > 0 else 0)
    return jnp.where(keep, turned, 0.0)


def fetch(source, target, sems, first, groups):
    copies = []
    for block in range(source.shape[0]):
        copies.append(
            pltpu.make_async_copy(
                source.at[block, pl.ds(first, groups)],
                target.at[pl.ds(block * groups, groups)],
                sems.at[block],
            )
        )
    return copies


def fetch_columns(source, target, sems, first, groups):
    return [
        pltpu.make_async_copy(
            source.at[block, pl.ds(first, groups)], target.at[:, block], sems.at[block]
        )
        for block in range(source.shape[0])
    ]


def start_all(copies):
    for copy in copies:
        copy.start()
    return copies


def wait_all(copies):
    for copy in copies:
        copy.wait()


def gathered_spot(places_ref, number, far):
    second, rest = divmod(number, 8)
    high, low_bits = divmod(rest, 4)
    middle, step = divmod(low_bits, 2)
    across, inner = (high, middle) if second else (middle, high)
    outer = (places_ref[2] ^ (2 * second + step)) * 2 + (places_ref[1] ^ inner)
    return (outer * 2 + (places_ref[0] ^ across)) * 2 + (places_ref[3] ^ far)


def first_conv(places_ref, fm_ref, *refs):
    sources, refs = refs[:-9], refs[-9:]
    scale_ref, shift_ref, pre_out_ref, act_ref, weight_out_ref, weight, pre_ref, sems, out_sems = refs
    sites, features = fm_ref.shape
    channels = act_ref.shape[1]
    groups = sources[0].shape[1]
    copies = []
    for far, source in enumerate(sources):
        for number in range(source.shape[0]):
            block = gathered_spot(places_ref, number, far) if len(sources) > 1 else number
            target = weight.at[pl.ds(block * groups, groups)]
            copies.append(pltpu.make_async_copy(source.at[number], target, sems.at[len(copies)]))
    start_all(copies)
    clip = FRAMES * SIDE * SIDE
    frame = SIDE * SIDE
    wait_all(copies)
    out = start_all([pltpu.make_async_copy(weight, weight_out_ref, out_sems.at[1])])

    def tap(number):
        begin = number * features // LANE_ROWS
        return weight[begin : begin + features // LANE_ROWS].reshape(features, channels)

    before = tap(0)
    for start in range(0, sites, clip):
        pre_ref[start : start + frame] = jnp.zeros((frame, channels), jnp.float32)
        pre_ref[start + frame : start + clip] = product(fm_ref[start : start + clip - frame], before)
    pre_ref[...] += product(fm_ref[...], tap(1))
    after = tap(2)
    for start in range(0, sites, clip):
        pre_ref[start : start + clip - frame] += product(fm_ref[start + frame : start + clip], after)

    def finish(rows):
        act_ref[rows] = low(gelu_of(pre_ref[rows] * scale_ref[...] + shift_ref[...]))

    out += start_all([pltpu.make_async_copy(pre_ref, pre_out_ref, out_sems.at[0])])
    by_rows(sites, 128, finish)
    wait_all(out)


def later_convs(
    act_a_ref, fm_ref, packed_ref, scale_b_ref, shift_b_ref, scale_c_ref, shift_c_ref, pool_ref, w_reduce_ref, w_query_far_ref,
    pre_b_out_ref, act_b_out_ref, pre_c_ref, regions_out_ref, reduced_out_ref, queries_ref,
    weight_b, weight_c, out_low, held_map, held_pre, held_reduce, pre_b_ref, act_b_ref, regions_ref, reduced_ref, w_query_ref, sems_b, sems_c, sems,
):
    sites, channels = act_a_ref.shape
    blocks = packed_ref.shape[0]
    groups_b = weight_b.shape[0] // blocks
    groups_c = weight_c.shape[0]
    groups_a = packed_ref.shape[1] - groups_b - groups_c
    copies_b = start_all(fetch(packed_ref, weight_b, sems_b, groups_a, groups_b))
    copies_c = start_all(fetch_columns(packed_ref, weight_c, sems_c, groups_a + groups_b, groups_c))
    others = start_all(
        [
            pltpu.make_async_copy(fm_ref, held_map, sems.at[0]),
            pltpu.make_async_copy(w_reduce_ref, held_reduce, sems.at[1]),
            pltpu.make_async_copy(w_query_far_ref, w_query_ref, sems.at[6 + groups_c]),
        ]
    )
    act_a = act_a_ref[...]
    block_rows = groups_b * LANE_ROWS
    sums = {-1: None, 0: None, 1: None}
    waited = 0
    for number, (rise, slide) in enumerate(places):
        while waited < len(copies_b) and waited * block_rows < (number + 1) * channels:
            copies_b[waited].wait()
            waited += 1
        begin = number * channels // LANE_ROWS
        tap = weight_b[begin : begin + channels // LANE_ROWS].reshape(channels, channels)
        part = in_rows(product(act_a, tap), rise)
        sums[slide] = part if sums[slide] is None else sums[slide] + part
    pre_b_ref[...] = sums[0] + in_columns(sums[1], 1) + in_columns(sums[-1], -1)

    outs = start_all([pltpu.make_async_copy(pre_b_ref, pre_b_out_ref, sems.at[2 + groups_c])])

    def finish(rows):
        act_b_ref[rows] = low(gelu_of(pre_b_ref[rows] * scale_b_ref[...] + shift_b_ref[...]))

    by_rows(sites, 128, finish)
    outs += start_all([pltpu.make_async_copy(act_b_ref, act_b_out_ref, sems.at[3 + groups_c])])
    wait_all(copies_c + others)
    reduced_ref[...] = jnp.zeros_like(reduced_ref)

    def chunk(number, carry):
        columns = pl.ds(pl.multiple_of(number * channels, channels), channels)
        held_pre[:, columns] = product(act_b_ref[...], weight_c[number].reshape(channels, channels))
        pltpu.make_async_copy(held_pre.at[:, columns], pre_c_ref.at[:, columns], sems.at[2 + number]).start()

        def finish_c(rows):
            linear = wide(held_map[rows, columns]) + held_pre[rows, columns] * scale_c_ref[:, columns] + shift_c_ref[:, columns]
            out_low[rows] = low(gelu_of(linear))

        by_rows(sites, 128, finish_c)
        part = low(product(pool_ref[...], out_low[...]))
        regions_ref[:, columns] = part
        reduced_ref[...] += product(part, held_reduce[columns])
        return carry

    lax.fori_loop(0, groups_c, chunk, 0)
    outs += start_all(
        [
            pltpu.make_async_copy(regions_ref, regions_out_ref, sems.at[4 + groups_c]),
            pltpu.make_async_copy(reduced_ref, reduced_out_ref, sems.at[5 + groups_c]),
        ]
    )
    queries = low(product(low(reduced_ref[...]), w_query_ref[...]))
    for place in range(queries_ref.shape[0]):
        queries_ref[place] = queries
    for number in range(groups_c):
        columns = pl.ds(number * channels, channels)
        outs.append(pltpu.make_async_copy(held_pre.at[:, columns], pre_c_ref.at[:, columns], sems.at[2 + number]))
    wait_all(outs)


def column_tile(columns, shape):
    lane = lax.broadcasted_iota(jnp.int32, shape, len(shape) - 1)
    tile = jnp.zeros(shape, jnp.float32)
    for number, column in enumerate(columns):
        rest = column
        for third in range(3):
            piece = wide(low(rest))
            tile = jnp.where(lane == 3 * number + third, piece, tile)
            rest = rest - piece
    return low(tile)


def from_tile(tile, number):
    lane = lax.broadcasted_iota(jnp.int32, tile.shape, tile.ndim - 1)
    picked = jnp.where((lane >= 3 * number) & (lane < 3 * number + 3), wide(tile), 0.0)
    return jnp.sum(picked, axis=-1, keepdims=True)


def attend(half_span, places_ref, queries_ref, keys_ref, values_ref, time_ref, message_ref, scores_ref):
    channels = queries_ref.shape[1]
    positions = places_ref[5] + lax.broadcasted_iota(jnp.int32, scores_ref.shape, 1)
    visible = jnp.abs(time_ref[...] - positions) <= half_span
    scores = dot_nt(queries_ref[...], keys_ref[...]) * (channels ** (-0.5))
    scores = jnp.where(visible, scores, masked_score)
    scores_ref[...] = scores
    top = jnp.max(scores, axis=1, keepdims=True)
    weights = jnp.exp(scores - top)
    total = jnp.sum(weights, axis=1, keepdims=True)
    message_ref[:, :channels] = low(product(low(weights), values_ref[...]))
    message_ref[:, channels:] = column_tile([top, total], (scores.shape[0], TILE))


def merge_rows(places_ref, arrived_ref, hidden_grad_ref, gain_ref, shift_ref, message_ref, hidden_ref, gain_out_ref, shift_out_ref):
    count, own, packed = arrived_ref.shape
    channels = hidden_grad_ref.shape[1]
    tops = from_tile(arrived_ref[:, :, channels:], 0)
    totals = from_tile(arrived_ref[:, :, channels:], 1)
    top = jnp.max(tops, axis=0)
    factors = jnp.exp(tops - top[None])
    total = jnp.sum(factors * totals, axis=0)
    numer = jnp.sum(factors * wide(arrived_ref[:, :, :channels]), axis=0)
    attended = numer / total
    centred = attended - jnp.mean(attended, axis=1, keepdims=True)
    spread = lax.rsqrt(jnp.mean(centred * centred, axis=1, keepdims=True) + epsilon)
    unit = centred * spread
    normed = unit * gain_ref[...] + shift_ref[...]
    hidden_ref[...] = low(gelu_of(normed))
    normed_grad = hidden_grad_ref[...] * gelu_slope(normed)
    gain_out_ref[...] = jnp.sum(normed_grad * unit, axis=0, keepdims=True)
    shift_out_ref[...] = jnp.sum(normed_grad, axis=0, keepdims=True)
    unit_grad = normed_grad * gain_ref[...]
    attended_grad = spread * (
        unit_grad
        - jnp.mean(unit_grad, axis=1, keepdims=True)
        - unit * jnp.mean(unit_grad * unit, axis=1, keepdims=True)
    )
    centre = jnp.sum(attended_grad * attended, axis=1, keepdims=True) / total
    numer_grad = low(attended_grad / total)
    tile = column_tile([top, centre], (own, TILE))
    for place in range(count):
        message_ref[place, :, :channels] = numer_grad
        message_ref[place, :, channels:] = tile


def attend_back(places_ref, arrived_ref, scores_ref, keys_ref, values_ref, queries_ref, part_ref, sums_ref):
    keys_here, channels = keys_ref.shape
    top = from_tile(arrived_ref[:, channels:], 0)
    centre = from_tile(arrived_ref[:, channels:], 1)
    numer_grad = arrived_ref[:, :channels]
    weights = jnp.exp(scores_ref[...] - top)
    prob_grad = dot_nt(numer_grad, values_ref[...])
    score_grad = low(weights * (prob_grad - centre) * (channels ** (-0.5)))
    part_ref[...] = low(product(score_grad, keys_ref[...]))
    sums_ref[:keys_here] = low(dot_tn(score_grad, queries_ref[...]))
    sums_ref[keys_here:] = low(dot_tn(low(weights), numer_grad))


def half_of(place_ref, bit):
    return jnp.where(place_ref[3] == bit, 1, 0)


def fold(value):
    return jnp.sum(value.reshape(value.shape[0] // 8, 8, value.shape[1]), axis=0)


def region_back(
    places_ref, arrived_ref, joined_grad_ref, w_query_ref, w_reduce_ref, query_grad_ref, reduced_grad_ref, regions_grad_ref
):
    features = regions_grad_ref.shape[1]
    query_grad = low(jnp.sum(wide(arrived_ref[...]), axis=0))
    query_grad_ref[...] = query_grad
    reduced_grad = low(joined_grad_ref[:, features:] + dot_nt(query_grad, w_query_ref[...]))
    reduced_grad_ref[...] = reduced_grad
    regions_grad_ref[...] = low(joined_grad_ref[:, :features] + dot_nt(reduced_grad, w_reduce_ref[...]))


def hand_out(buffer, send_ref, keep_ref, sems):
    return start_all(
        [
            pltpu.make_async_copy(buffer.at[number], target, sems.at[number])
            for number, target in enumerate((send_ref, keep_ref))
        ]
    )


def store_rows(buffer, place_ref, value, first, rows):
    at, end = first, first + value.shape[0]
    while at < end:
        block, offset = divmod(at, rows)
        count = min(rows - offset, end - at)
        buffer[half_of(place_ref, block % 2), block // 2, offset : offset + count] = value[at - first : at - first + count]
        at += count


def slopes_outer(places_ref, scale_ref, shift_ref, pre_ref, map_ref, out_ref, held_pre, held_map, held_out, sems):
    sites, features = held_map.shape
    chunks = sems.shape[1]
    width = features // chunks

    def part_of(source, target, number, row):
        columns = pl.ds(pl.multiple_of(number * width, width), width)
        return pltpu.make_async_copy(source.at[:, columns], target.at[:, columns], sems.at[row, number])

    for number in range(chunks):
        start_all([part_of(pre_ref, held_pre, number, 0), part_of(map_ref, held_map, number, 1)])

    def chunk(number, carry):
        columns = pl.ds(pl.multiple_of(number * width, width), width)
        wait_all([part_of(pre_ref, held_pre, number, 0), part_of(map_ref, held_map, number, 1)])

        def one(rows):
            linear = wide(held_map[rows, columns]) + held_pre[rows, columns] * scale_ref[:, columns] + shift_ref[:, columns]
            held_out[rows, columns] = low(gelu_slope(linear))

        by_rows(sites, 128, one)
        part_of(held_out, out_ref, number, 2).start()
        return carry

    lax.fori_loop(0, chunks, chunk, 0)
    wait_all([part_of(held_out, out_ref, number, 2) for number in range(chunks)])


def slope_back(upstream_ref, pre_ref, scale_ref, shift_ref, out_ref, scale_out_ref, shift_out_ref):
    sites, channels = pre_ref.shape

    def one(step, sums):
        rows = pl.ds(pl.multiple_of(step * 128, 128), 128)
        pre = pre_ref[rows]
        grad = upstream_ref[rows] * gelu_slope(pre * scale_ref[...] + shift_ref[...])
        out_ref[rows] = low(grad * scale_ref[...]).astype(out_ref.dtype)
        return sums[0] + fold(grad * pre), sums[1] + fold(grad)

    zero = jnp.zeros((8, channels), jnp.float32)
    scale_sum, shift_sum = lax.fori_loop(0, sites // 128, one, (zero, zero))
    scale_out_ref[...] = jnp.sum(scale_sum, axis=0, keepdims=True)
    shift_out_ref[...] = jnp.sum(shift_sum, axis=0, keepdims=True)


def later_back(
    groups_a, groups_b, place_ref, regions_grad_ref, pool_ref, scale_ref, scales_ref, pre_c_ref, slope_ref, act_b_ref,
    pre_b_ref, act_a_ref, pre_a_ref, packed_ref,
    send_ref, keep_ref, lin_c_grad_ref, pre_a_grad_ref, scale_c_out_ref, shift_c_out_ref, scale_b_out_ref, shift_b_out_ref,
    scale_a_out_ref, shift_a_out_ref,
    weight_b, weight_c, buffer, out_grad, pre_grad, turned, act_grad, wide_grad,
    held_pre_c, held_map, held_act_b, held_pre_b, held_act_a, held_pre_a, held_lin, sems_b, sems_c, out_sems, sems,
):
    sites, features = held_map.shape
    channels = held_act_b.shape[1]
    chunks, blocks = weight_c.shape[0], weight_c.shape[1]
    rows_b = groups_b * LANE_ROWS

    def part_of(source, target, number, sem):
        columns = pl.ds(pl.multiple_of(number * channels, channels), channels)
        return pltpu.make_async_copy(source.at[:, columns], target.at[:, columns], sems.at[sem + number])

    early = start_all([pltpu.make_async_copy(act_b_ref, held_act_b, sems.at[0])])
    copies_c = start_all(fetch_columns(packed_ref, weight_c, sems_c, groups_a + groups_b, chunks))
    for number in range(chunks):
        part_of(pre_c_ref, held_pre_c, number, 4).start()
        part_of(slope_ref, held_map, number, 4 + chunks).start()
    late = start_all(
        [
            pltpu.make_async_copy(pre_b_ref, held_pre_b, sems.at[1]),
            pltpu.make_async_copy(act_a_ref, held_act_a, sems.at[2]),
            pltpu.make_async_copy(pre_a_ref, held_pre_a, sems.at[3]),
        ]
    )
    copies_b = start_all(fetch(packed_ref, weight_b, sems_b, groups_a, groups_b))
    scale_b_ref, shift_b_ref, scale_a_ref, shift_a_ref = [scales_ref.at[pl.ds(number, 1)] for number in range(4)]
    act_grad[...] = jnp.zeros_like(act_grad)
    wait_all(early)
    turned[...] = held_act_b[...].T
    wait_all(copies_c)

    def chunk(number, carry):
        columns = pl.ds(pl.multiple_of(number * channels, channels), channels)
        out_grad[...] = dot_tn(pool_ref[...], regions_grad_ref[:, columns])
        part_of(pre_c_ref, held_pre_c, number, 4).wait()
        part_of(slope_ref, held_map, number, 4 + chunks).wait()

        def one(step, sums):
            rows = pl.ds(pl.multiple_of(step * 128, 128), 128)
            pre = held_pre_c[rows, columns]
            scale = scale_ref[:, columns]
            grad = out_grad[rows] * wide(held_map[rows, columns])
            held_lin[rows, columns] = low(grad)
            pre_grad[rows] = low(grad * scale)
            return sums[0] + fold(grad * pre), sums[1] + fold(grad)

        zero = jnp.zeros((8, channels), jnp.float32)
        scale_sum, shift_sum = lax.fori_loop(0, sites // 128, one, (zero, zero))
        part_of(held_lin, lin_c_grad_ref, number, 4 + 2 * chunks).start()
        scale_c_out_ref[:, columns] = jnp.sum(scale_sum, axis=0, keepdims=True)
        shift_c_out_ref[:, columns] = jnp.sum(shift_sum, axis=0, keepdims=True)
        part = low(product(turned[...], pre_grad[...])).reshape(blocks // 2, 2, LANE_ROWS, channels)
        rows = pl.ds(pl.multiple_of(rows_b + number * LANE_ROWS, LANE_ROWS), LANE_ROWS)
        for bit in range(2):
            buffer[half_of(place_ref, bit), :, rows] = part[:, bit]
        act_grad[...] += dot_nt(pre_grad[...], weight_c[number].reshape(channels, channels))
        return carry

    lax.fori_loop(0, chunks, chunk, 0)
    wait_all(late)
    slope_back(act_grad, held_pre_b, scale_b_ref, shift_b_ref, wide_grad, scale_b_out_ref, shift_b_out_ref)
    turned[...] = held_act_a[...].T
    wait_all(copies_b)
    for slide in (-1, 0, 1):
        slid = in_columns(wide_grad[...], -slide)
        for number, place in enumerate(places):
            if place[1] != slide:
                continue
            moved = low(in_rows(slid, -place[0]))
            store_rows(buffer, place_ref, low(product(turned[...], moved)), number * channels, rows_b)
            begin = number * channels // LANE_ROWS
            tap = weight_b[begin : begin + channels // LANE_ROWS].reshape(channels, channels)
            part = dot_nt(moved, tap)
            if slide == -1 and place[0] == -1:
                act_grad[...] = part
            else:
                act_grad[...] += part
    copies = hand_out(buffer, send_ref, keep_ref, out_sems)
    slope_back(act_grad, held_pre_a, scale_a_ref, shift_a_ref, pre_a_grad_ref, scale_a_out_ref, shift_a_out_ref)
    wait_all(copies)
    for number in range(chunks):
        part_of(held_lin, lin_c_grad_ref, number, 4 + 2 * chunks).wait()


def by_frames(grad, offset):
    if offset == 0:
        return grad
    sites, width = grad.shape
    tall = grad.reshape(sites // (FRAMES * SIDE * SIDE), FRAMES, SIDE * SIDE, width)
    edge = jnp.zeros_like(tall[:, :1])
    if offset > 0:
        tall = jnp.concatenate([edge, tall[:, :-1]], axis=1)
    else:
        tall = jnp.concatenate([tall[:, 1:], edge], axis=1)
    return tall.reshape(sites, width)


def first_back(place_ref, grad_ref, own_ref, got_ref, turned_ref, send_ref, keep_ref, sum_ref, buffer, held, sems, out_sems):
    features, sites = held.shape
    channels = grad_ref.shape[1]
    copies = [
        pltpu.make_async_copy(turned_ref.at[pl.ds(start, channels)], held.at[pl.ds(start, channels)], sems.at[start // channels])
        for start in range(0, features, channels)
    ]
    start_all(copies)
    sum_ref[...] = add_low(own_ref[...], got_ref[...])
    for tap in range(3):
        moved = by_frames(grad_ref[...], tap - 1)
        for start in range(0, features, channels):
            if tap == 0:
                copies[start // channels].wait()
            part = low(product(held[start : start + channels], moved))
            store_rows(buffer, place_ref, part, tap * features + start, buffer.shape[2])
    wait_all(hand_out(buffer, send_ref, keep_ref, out_sems))


def map_back(places_ref, grad_ref, weight_ref, lin_c_grad_ref, out_ref, moved, held_lin, held_out, sems):
    sites, features = held_out.shape
    channels = grad_ref.shape[1]
    copies = start_all([pltpu.make_async_copy(lin_c_grad_ref, held_lin, sems.at[0])])
    for tap in range(3):
        moved[tap] = by_frames(grad_ref[...], tap - 1)
    wait_all(copies)
    groups = channels // LANE_ROWS

    def chunk(number, carry):
        columns = pl.ds(pl.multiple_of(number * channels, channels), channels)
        total = wide(held_lin[:, columns])
        for tap in range(3):
            rows = pl.ds(tap * (features // LANE_ROWS) + number * groups, groups)
            total = total + dot_nt(moved[tap], weight_ref[rows].reshape(channels, channels))
        held_out[:, columns] = low(total)
        pltpu.make_async_copy(held_out.at[:, columns], out_ref.at[:, columns], sems.at[1 + number]).start()
        return carry

    lax.fori_loop(0, features // channels, chunk, 0)
    copies = []
    for number in range(features // channels):
        columns = pl.ds(number * channels, channels)
        copies.append(pltpu.make_async_copy(held_out.at[:, columns], out_ref.at[:, columns], sems.at[1 + number]))
    wait_all(copies)


COST = 1.5e10
WINDOW = 0.1
FIRST_LIMIT = 52
F32 = jnp.float32
BF16 = jnp.bfloat16
ANY = pl.BlockSpec(memory_space=pl.ANY)
SCALAR = pl.BlockSpec(memory_space=pltpu.SMEM)
HELD = pl.BlockSpec(memory_space=pltpu.VMEM)


def shape_of(dims, kind):
    return jax.ShapeDtypeStruct(dims, kind)


def add_low(left, right):
    return left + right


class Blocks:
    def __init__(self, ref, first, dims, rows):
        self.ref, self.first, self.dims, self.rows = ref, first, dims, rows

    @property
    def shape(self):
        return self.dims

    def span(self, index):
        index = index if isinstance(index, tuple) else (index,)
        flat = 0
        for place, size in zip(index, self.dims):
            flat = flat * size + place
        return pl.ds(pl.multiple_of(self.first + flat * self.rows, LANE_ROWS), self.rows)

    def __getitem__(self, index):
        return self.ref[self.span(index)]

    def __setitem__(self, index, value):
        self.ref[self.span(index)] = value


def after_last(places_ref, keep_ref, got_ref, keep_one, send_one, keep_two, send_two):
    half = keep_ref.shape[0] // 2
    across, inner = places_ref[0], places_ref[1]

    def one(number, carry):
        for place in range(2):
            keep_one[number, place] = add_low(keep_ref[number, place, across], got_ref[number, place, across])
            send_one[number, place] = add_low(keep_ref[number, place, 1 - across], got_ref[number, place, 1 - across])
            later = number + half
            keep_two[number, place] = add_low(keep_ref[later, inner, place], got_ref[later, inner, place])
            send_two[number, place] = add_low(keep_ref[later, 1 - inner, place], got_ref[later, 1 - inner, place])
        return carry

    lax.fori_loop(0, half, one, 0)


def after_cross(places_ref, keep_one, got_one, keep_two, got_two, kept_one, send_one, kept_two, send_two):
    across, inner = places_ref[0], places_ref[1]

    def one(number, carry):
        kept_one[number] = add_low(keep_one[number, inner], got_one[number, inner])
        send_one[number] = add_low(keep_one[number, 1 - inner], got_one[number, 1 - inner])
        kept_two[number] = add_low(keep_two[number, across], got_two[number, across])
        send_two[number] = add_low(keep_two[number, 1 - across], got_two[number, 1 - across])
        return carry

    lax.fori_loop(0, keep_two.shape[0], one, 0)


def after_plane(places_ref, keep_one, got_one, keep_two, got_two, kept_ref, sends):
    half = keep_one.shape[0]
    outer = places_ref[2]

    def block(place, target):
        @pl.when(place < half)
        def _():
            target[...] = add_low(keep_one[lax.rem(place, half)], got_one[lax.rem(place, half)])

        @pl.when(place >= half)
        def _():
            target[...] = add_low(keep_two[lax.rem(place, half)], got_two[lax.rem(place, half)])

    block(outer, kept_ref)
    for step, target in enumerate(sends):
        block(outer ^ (step + 1), target)


def total_of(refs):
    total = wide(refs[0][...])
    for ref in refs[1:]:
        total = total + wide(ref[...])
    return total


def kept_blocks(ref, half, rows, rows_a):
    pairs = 2 * half * rows_a
    return (
        Blocks(ref, 0, (half, 2), rows_a),
        Blocks(ref, pairs, (half, 2), rows_a),
        Blocks(ref, 2 * pairs, (half,), rows),
        Blocks(ref, 2 * pairs + half * rows, (half,), rows),
    )


def round_two(
    places_ref, keep_one, got_one, keep_two, got_two, keep_a, got_a, kept_ref, across_ref, inner_ref
):
    half, rows, rows_a = keep_one.shape[0], keep_one.shape[2], keep_a.shape[3]
    below = 2 * half * rows_a
    keep_a_one, keep_a_two, kept_one, kept_two = kept_blocks(kept_ref, half, rows, rows_a)
    after_last(
        places_ref, keep_a, got_a, keep_a_one, Blocks(across_ref, 0, (half, 2), rows_a), keep_a_two,
        Blocks(inner_ref, 0, (half, 2), rows_a),
    )
    after_cross(
        places_ref, keep_one, got_one, keep_two, got_two, kept_one, Blocks(inner_ref, below, (half,), rows), kept_two,
        Blocks(across_ref, below, (half,), rows),
    )


def bank_spans(lines, width, channels):
    groups = channels // width
    step = -(-lines // (groups * LANE_ROWS)) * LANE_ROWS
    return [(first, min(first + step, lines)) for first in range(0, lines, step)], step


def store_narrow(target, first, value, channels):
    lines, width = value.shape
    spans, step = bank_spans(lines, width, channels)
    target[first : first + step] = jnp.zeros((step, channels), BF16)
    for number, (begin, end) in enumerate(spans):
        target[first : first + end - begin, number * width : (number + 1) * width] = value[begin:end]


def load_narrow(value, first, lines, width):
    spans, _ = bank_spans(lines, width, value.shape[1])
    pieces = [
        value[first : first + end - begin, number * width : (number + 1) * width]
        for number, (begin, end) in enumerate(spans)
    ]
    return jnp.concatenate(pieces, axis=0)


def round_three(sizes, count, split, places_ref, held_ref, got_across, got_inner, *refs):
    half, rows, rows_a = sizes
    region_refs, refs = (refs[:2], refs[2:]) if split else (refs[:1], refs[1:])
    bank_refs, refs = (refs[:count], refs[count:]) if split else (refs[:1], refs[1:])
    kept_ref, across_ref, inner_ref, *sends = refs
    channels = kept_ref.shape[1]
    below = 2 * half * rows_a
    keep_a_one, keep_a_two, kept_one, kept_two = kept_blocks(held_ref, half, rows, rows_a)
    after_plane(
        places_ref, kept_one, Blocks(got_inner, below, (half,), rows), kept_two, Blocks(got_across, below, (half,), rows),
        kept_ref.at[pl.ds(0, rows)], sends,
    )
    after_cross(
        places_ref, keep_a_one, Blocks(got_across, 0, (half, 2), rows_a), keep_a_two,
        Blocks(got_inner, 0, (half, 2), rows_a), Blocks(kept_ref, rows, (half,), rows_a),
        Blocks(inner_ref, 0, (half,), rows_a), Blocks(kept_ref, rows + half * rows_a, (half,), rows_a),
        Blocks(across_ref, 0, (half,), rows_a),
    )
    across_ref[half * rows_a :] = low(total_of(region_refs))
    inner = places_ref[7] if split else 0
    keep = total_of([ref.at[inner] for ref in bank_refs])
    at = rows + 2 * half * rows_a
    store_narrow(kept_ref, at, low(keep), channels)
    if split:
        send = total_of([ref.at[1 - inner] for ref in bank_refs])
        store_narrow(inner_ref, half * rows_a, low(send), channels)
    else:
        inner_ref[half * rows_a :] = kept_ref[at:]


def round_four(sizes, count, split, widths, places_ref, held_ref, *refs):
    half, rows, rows_a = sizes
    plane_refs, refs = [held_ref.at[pl.ds(0, rows)], *refs[: count - 1]], refs[count - 1 :]
    across_ref, got_across, got_inner, done_ref, kept_a_ref = refs[:5]
    sends, (reduce_ref, query_ref, out_ref, head_ref) = refs[5 : 4 + count], refs[4 + count :]
    kept_a_one = Blocks(held_ref, rows, (half,), rows_a)
    kept_a_two = Blocks(held_ref, rows + half * rows_a, (half,), rows_a)
    bank_keep = held_ref[rows + 2 * half * rows_a :]
    below = half * rows_a
    after_plane(
        places_ref, kept_a_one, Blocks(got_inner, 0, (half,), rows_a), kept_a_two,
        Blocks(got_across, 0, (half,), rows_a), kept_a_ref, sends,
    )
    done_ref[:rows] = low(total_of(plane_refs))
    done_ref[rows:] = add_low(bank_keep, got_inner[below:]) if split else bank_keep
    region = wide(across_ref[below:]) + wide(got_across[below:]) if split else wide(across_ref[below:])
    _, _, feature_rows, channel_rows, _, joined_rows = widths
    reduce_ref[...] = region[:feature_rows]
    query_ref[...] = region[feature_rows : feature_rows + channel_rows]
    out_ref[...] = region[feature_rows + channel_rows : feature_rows + 2 * channel_rows]
    head = load_narrow(region, feature_rows + 2 * channel_rows, joined_rows, TILE)
    head_ref[...] = head[:, : head_ref.shape[1]]


def round_last(count, places_ref, *refs):
    part_ref, both = refs[-1 if len(refs) == count + 1 else -2], refs[-1]
    part_ref[...] = low(total_of(refs[:count]))
    if len(refs) > count + 1:
        for number, ref in enumerate(refs[count : count + 2]):
            both[number] = ref[...]


def sum_swap(places_ref, *refs):
    refs[-1][...] = low(total_of(refs[:-1]))


def front_pack(groups_a, groups_b, places_ref, conv_a_ref, conv_b_ref, conv_c_ref, own_a_ref, own_ref, sems):
    place = places_ref[9]
    chunks = own_ref.shape[0] - groups_b
    channels = own_ref.shape[2]
    copies = [
        pltpu.make_async_copy(conv_b_ref.at[pl.ds(place * groups_b, groups_b)], own_ref.at[pl.ds(0, groups_b)], sems.at[0]),
        pltpu.make_async_copy(conv_a_ref.at[pl.ds(place * groups_a, groups_a)], own_a_ref, sems.at[1]),
    ]
    for chunk in range(chunks):
        copies.append(
            pltpu.make_async_copy(
                conv_c_ref.at[place, :, pl.ds(chunk * channels, channels)], own_ref.at[groups_b + chunk], sems.at[2 + chunk]
            )
        )
    wait_all(start_all(copies))


def front_turn(places_ref, map_ref, bank_ref, turned_map_ref, turned_bank_ref):
    sites, features = map_ref.shape
    for start in range(0, features, sites):
        turned_map_ref[start : start + sites] = map_ref[:, start : start + sites].T
        turned_bank_ref[start : start + sites] = bank_ref[:, start : start + sites].T


def front_bank(places_ref, bank_ref, w_bank_ref, w_key_ref, w_value_ref, keys_ref, values_ref, turned_memory_ref):
    memory = low(product(bank_ref[...], w_bank_ref[...]))
    keys_ref[...] = low(product(memory, w_key_ref[...]))
    values_ref[...] = low(product(memory, w_value_ref[...]))
    turned_memory_ref[...] = memory.T


def front_head(
    places_ref, index_ref, weight_ref, logit_grad_ref, w_head_ref, w_out_ref,
    pool_ref, joined_grad_ref, hidden_grad_ref, branch_grad_ref,
):
    own, taps = index_ref.shape
    sites = pool_ref.shape[1]
    channels = hidden_grad_ref.shape[1]
    features = w_head_ref.shape[0] - channels
    column = lax.broadcasted_iota(jnp.int32, (own, sites), 1)
    pool = jnp.zeros((own, sites), F32)
    for tap in range(taps):
        weight = wide(weight_ref[:, tap : tap + 1])
        pool = pool + jnp.where(column == index_ref[:, tap : tap + 1], weight, 0.0)
    pool_ref[...] = low(pool)
    logit_grad = logit_grad_ref[pl.ds(pl.multiple_of(places_ref[8], LANE_ROWS), own)]
    joined_grad = dot_nt(logit_grad, w_head_ref[...])
    joined_grad_ref[...] = joined_grad
    hidden_grad_ref[...] = dot_nt(low(joined_grad[:, features:]), w_out_ref[...])
    branch_grad_ref[...] = low(dot_nt(logit_grad_ref[...], w_head_ref[features:]))


def region_pack(
    places_ref, regions_ref, reduced_ref, hidden_ref, query_grad_ref, reduced_grad_ref, w_out_ref, w_head_ref,
    logits_ref, message_ref,
):
    count = message_ref.shape[0]
    channels = reduced_ref.shape[1]
    reduced = reduced_ref[...]
    merged = low(reduced + product(hidden_ref[...], w_out_ref[...]))
    joined = jnp.concatenate([regions_ref[...], merged], axis=1)
    logits_ref[...] = low(product(joined, w_head_ref[...]))[:, : logits_ref.shape[1]]
    reduced_low = low(reduced)
    parts = [regions_ref[...], reduced_low, hidden_ref[...], joined]
    shared = [reduced_grad_ref[...], query_grad_ref[...]]
    for place in range(count):
        pieces = list(shared)
        for part in parts:
            width = part.shape[1] // count
            pieces.append(part[:, place * width : (place + 1) * width])
        spare = message_ref.shape[2] - sum(piece.shape[1] for piece in pieces)
        if spare:
            pieces.append(jnp.zeros((reduced.shape[0], spare), BF16))
        message_ref[place] = jnp.concatenate(pieces, axis=1)


def region_sums(widths, places_ref, group_ref, branch_grad_ref, logit_grad_ref, out_ref):
    ends, start = [], 0
    for width in widths:
        ends.append((start, start + width))
        start += width
    reduced_grad, query_grad, regions, reduced, hidden, joined = [group_ref[:, begin:end] for begin, end in ends]
    first, second = widths[2], widths[2] + widths[3]
    third = second + widths[4]
    channels = reduced_grad.shape[1]
    out_ref[:first] = low(dot_tn(regions, reduced_grad))
    out_ref[first:second] = low(dot_tn(reduced, query_grad))
    out_ref[second:third] = low(dot_tn(hidden, branch_grad_ref[...]))
    head = low(dot_tn(joined, logit_grad_ref[...]))
    store_narrow(out_ref, third, head, channels)


def bank_back(
    places_ref, sums_ref, w_key_ref, w_value_ref, w_bank_ref, turned_bank_ref, turned_memory_ref, *refs
):
    vectors, bank_grad_ref, outs, (message_ref, grads) = refs[:8], refs[8], refs[9:-2], refs[-2:]
    keys_here, features = bank_grad_ref.shape
    channels = sums_ref.shape[1]
    count, _, width = message_ref.shape
    key_low, value_low = sums_ref[:keys_here], sums_ref[keys_here:]
    memory_grad = low(dot_nt(key_low, w_key_ref[...]) + dot_nt(value_low, w_value_ref[...]))
    for start in range(0, features, channels):
        bank_grad_ref[:, start : start + channels] = low(dot_nt(memory_grad, w_bank_ref[start : start + channels]))
    grads[:keys_here] = memory_grad
    grads[keys_here : 2 * keys_here] = key_low
    grads[2 * keys_here :] = value_low

    def columns(rows):
        if width % TILE == 0:
            return grads[rows, pl.ds(pl.multiple_of(places_ref[4] * width, width), width)]
        picked = grads[rows, :width]
        for number in range(1, channels // width):
            picked = jnp.where(places_ref[4] == number, grads[rows, number * width : (number + 1) * width], picked)
        return picked

    feature_rows, channel_rows = features // count, channels // count
    part = low(product(turned_bank_ref[...], columns(pl.ds(0, keys_here))))
    message_ref[:, :feature_rows] = part.reshape(count, feature_rows, width)
    at = feature_rows
    for number in (1, 2):
        part = low(product(turned_memory_ref[...], columns(pl.ds(number * keys_here, keys_here))))
        message_ref[:, at : at + channel_rows] = part.reshape(count, channel_rows, width)
        at += channel_rows
    spare = message_ref.shape[1] - at
    for place in range(count):
        row = []
        for vector_ref in vectors:
            share = vector_ref.shape[1] // count
            row.append(vector_ref[:, place * share : (place + 1) * share])
        total = sum(piece.shape[1] for piece in row)
        lines = -(-total // width)
        if lines * width > total:
            row.append(jnp.zeros((1, lines * width - total), F32))
        row = jnp.concatenate(row, axis=1)
        tile = [row[:, line * width : (line + 1) * width] for line in range(lines)]
        tile.append(jnp.zeros((spare - lines, width), F32))
        message_ref[place, at:] = low(jnp.concatenate(tile, axis=0))
    inner = outs[0].shape[0]
    for step, out_ref in enumerate(outs):
        out_ref[...] = message_ref[pl.ds((places_ref[6] ^ step) * inner, inner)]


def finish(shape_info, places_ref, part_ref, *refs):
    rows_b, rows_c, feature_rows, channel_rows, lines, split = shape_info
    if split:
        own_ref, got_ref, refs = refs[0], refs[1], refs[2:]
        weight_refs = [own_ref.at[0], got_ref.at[0], own_ref.at[1], got_ref.at[1]]
        bank_refs, first = weight_refs, rows_b + rows_c
    else:
        weight_refs, bank_refs, refs, first = refs[:1], refs[1:-14], refs[-14:], 0
    conv_a_ref, conv_b_ref, conv_c_ref, bank_out_ref, key_ref, value_ref = refs[:6]
    vectors = refs[6:]
    conv_a_ref[...] = wide(part_ref[...]).reshape(conv_a_ref.shape)
    channels = weight_refs[0].shape[1]
    width = channels // len(bank_refs)

    def spot(number, size):
        if not split:
            return pl.ds(number * size, size)
        return pl.ds(pl.multiple_of((places_ref[4] ^ number) * size, size), size)

    for number, ref in enumerate(weight_refs):
        conv_b_ref[spot(number, rows_b)] = wide(ref[:rows_b])
        for chunk in range(rows_c // LANE_ROWS):
            begin = rows_b + chunk * LANE_ROWS
            conv_c_ref[spot(number, LANE_ROWS), chunk * channels : (chunk + 1) * channels] = wide(
                ref[begin : begin + LANE_ROWS]
            )
    tile = None
    at = feature_rows + 2 * channel_rows
    for number, ref in enumerate(bank_refs):
        bank = wide(load_narrow(ref, first, lines, width))
        columns = spot(number, width)
        bank_out_ref[:, columns] = bank[:feature_rows]
        key_ref[:, columns] = bank[feature_rows : feature_rows + channel_rows]
        value_ref[:, columns] = bank[feature_rows + channel_rows : at]
        tile = bank[at:] if tile is None else tile + bank[at:]
    total = sum(ref.shape[1] for ref in vectors)
    row = jnp.concatenate([tile[line : line + 1] for line in range(-(-total // width))], axis=1)
    at = 0
    for ref in vectors:
        ref[...] = row[:, at : at + ref.shape[1]]
        at += ref.shape[1]


def run_kernel(
    kernel, places, arrays, shapes, name, micros, scratch=(), raw_in=(), raw_out=(), fetched=(), limit=8
):
    count_in, count_out, fetched = len(arrays), len(shapes), list(fetched)

    def wrapped(*refs):
        places_ref, ins = refs[0], list(refs[1 : 1 + count_in])
        out_places, outs = refs[1 + count_in], refs[2 + count_in : 2 + count_in + count_out]
        extra = refs[2 + count_in + count_out :]
        if fetched:
            held, sems, extra = extra[: len(fetched)], extra[len(fetched)], extra[len(fetched) + 1 :]
            copies = start_all(
                [pltpu.make_async_copy(ins[number], held[slot], sems.at[slot]) for slot, number in enumerate(fetched)]
            )
        for number in range(places.shape[0]):
            out_places[number] = places_ref[number]
        if fetched:
            wait_all(copies)
            for slot, number in enumerate(fetched):
                ins[number] = held[slot]
        kernel(places_ref, *ins, *outs, *extra)

    outside = [*raw_in, *fetched]
    buffers = [pltpu.VMEM(arrays[number].shape, arrays[number].dtype) for number in fetched]
    if fetched:
        buffers.append(pltpu.SemaphoreType.DMA((len(fetched),)))
    return pl.pallas_call(
        wrapped,
        out_shape=[shape_of(places.shape, jnp.int32)] + list(shapes),
        in_specs=[SCALAR] + [ANY if number in outside else HELD for number in range(count_in)],
        out_specs=[SCALAR] + [ANY if number in raw_out else HELD for number in range(count_out)],
        scratch_shapes=buffers + list(scratch),
        compiler_params=params(limit),
        cost_estimate=pl.CostEstimate(
            flops=int(micros * COST), bytes_accessed=int(micros * COST / 1000), transcendentals=0
        ),
        name=name,
    )(places, *arrays)


def run_first_conv(places, feature_map, sources, scale, shift):
    sites, channels = feature_map.shape[0], sources[0].shape[3]
    groups = sources[0].shape[1]
    blocks = sum(source.shape[0] for source in sources)
    return pl.pallas_call(
        first_conv,
        out_shape=[
            shape_of((sites, channels), F32),
            shape_of((sites, channels), BF16),
            shape_of((blocks * groups, LANE_ROWS, channels), BF16),
        ],
        in_specs=[SCALAR, HELD] + [ANY] * len(sources) + [HELD] * 2,
        out_specs=[ANY, HELD, ANY],
        scratch_shapes=[
            pltpu.VMEM((blocks * groups, LANE_ROWS, channels), BF16),
            pltpu.VMEM((sites, channels), F32),
            pltpu.SemaphoreType.DMA((blocks,)),
            pltpu.SemaphoreType.DMA((2,)),
        ],
        compiler_params=params(FIRST_LIMIT),
        cost_estimate=pl.CostEstimate(flops=int(6 * COST), bytes_accessed=int(6 * COST / 1000), transcendentals=0),
        name="first_conv",
    )(places, feature_map, *sources, scale.reshape(1, -1), shift.reshape(1, -1))


def run_later_convs(
    act_a, feature_map, packed, scale_b, shift_b, scale_c, shift_c, pooling, w_reduce, w_query, groups_b, groups_c
):
    sites, channels = act_a.shape
    features = feature_map.shape[1]
    blocks = packed.shape[0]
    own = pooling.shape[0]
    group = lax.axis_size("bank")
    return pl.pallas_call(
        later_convs,
        out_shape=[
            jax.ShapeDtypeStruct((sites, channels), jnp.float32),
            jax.ShapeDtypeStruct((sites, channels), jnp.bfloat16),
            jax.ShapeDtypeStruct((sites, features), jnp.float32),
            jax.ShapeDtypeStruct((own, features), jnp.bfloat16),
            jax.ShapeDtypeStruct((own, channels), jnp.float32),
            jax.ShapeDtypeStruct((group, own, channels), jnp.bfloat16),
        ],
        in_specs=[HELD] + [ANY] * 2 + [HELD] * 5 + [ANY] * 2,
        out_specs=[ANY] * 5 + [HELD],
        scratch_shapes=[
            pltpu.VMEM((blocks * groups_b, LANE_ROWS, channels), jnp.bfloat16),
            pltpu.VMEM((groups_c, blocks, LANE_ROWS, channels), jnp.bfloat16),
            pltpu.VMEM((sites, channels), jnp.bfloat16),
            pltpu.VMEM((sites, features), jnp.bfloat16),
            pltpu.VMEM((sites, features), jnp.float32),
            pltpu.VMEM(w_reduce.shape, jnp.bfloat16),
            pltpu.VMEM((sites, channels), jnp.float32),
            pltpu.VMEM((sites, channels), jnp.bfloat16),
            pltpu.VMEM((own, features), jnp.bfloat16),
            pltpu.VMEM((own, channels), jnp.float32),
            pltpu.VMEM(w_query.shape, jnp.bfloat16),
            pltpu.SemaphoreType.DMA((blocks,)),
            pltpu.SemaphoreType.DMA((blocks,)),
            pltpu.SemaphoreType.DMA((7 + groups_c,)),
        ],
        compiler_params=params(52),
        cost_estimate=pl.CostEstimate(flops=int(15 * COST), bytes_accessed=int(15 * COST / 1000), transcendentals=0),
        name="later_convs",
    )(
        act_a, feature_map, packed, scale_b.reshape(1, -1), shift_b.reshape(1, -1), scale_c.reshape(1, -1),
        shift_c.reshape(1, -1), pooling, w_reduce, w_query,
    )


def body(
    feature_map,
    bank,
    region_time,
    roi_index,
    roi_weight,
    conv_a,
    scale_a,
    shift_a,
    conv_b,
    scale_b,
    shift_b,
    conv_c,
    scale_c,
    shift_c,
    w_reduce,
    w_bank,
    w_query,
    w_key,
    w_value,
    ln_gain,
    ln_shift,
    w_out,
    w_head,
    logit_grad,
):
    site_count = feature_map.shape[0]
    feature_count = feature_map.shape[1]
    channels = w_query.shape[0]
    classes = w_head.shape[1]
    keys_here = bank.shape[0]
    own_count = roi_index.shape[0]
    bank_count = lax.axis_size("bank")
    bank_place = lax.axis_index("bank")
    dp_count = lax.axis_size("dp")
    dp_place = lax.axis_index("dp")
    first_row = bank_place * own_count
    half_span = keys_here * bank_count // 2
    group_rows = bank_count * own_count
    chunks = feature_count // channels
    shards = (conv_a, conv_b, conv_c)
    split = dp_count // 2 == 2 and bank_count // 2 == 4 and all(shard.shape[0] % (LANE_ROWS * dp_count) == 0 for shard in shards)
    axes = block_axes(split, dp_count, bank_count)
    outer, inner, across, last = axes
    outer_count = outer.size if split else 1
    blocks = bank_count * dp_count if split else bank_count
    halves = tuple(axis.size for axis in axes[:3])
    places_here = jnp.stack([across.place(), inner.place(), outer.place(), last.place(), dp_place, bank_place * keys_here, outer.place() if split else 0 * bank_place, inner.place(), first_row, dp_place if split else 0 * dp_place])

    parts = dp_count if split else 1
    rows_a, rows_b, rows_c = [shard.shape[0] // parts for shard in shards]
    groups_a, groups_b, groups_c = rows_a // LANE_ROWS, rows_b // LANE_ROWS, chunks
    places, own_a, own_packed = run_kernel(
        functools.partial(front_pack, groups_a, groups_b),
        places_here,
        [shard.reshape(-1, LANE_ROWS, shard.shape[1]) for shard in shards],
        [shape_of((groups_a, LANE_ROWS, channels), BF16), shape_of((groups_b + chunks, LANE_ROWS, channels), BF16)],
        "front_pack",
        1,
        scratch=[pltpu.SemaphoreType.DMA((2 + chunks,))],
        raw_in=(0, 1, 2),
        raw_out=(0, 1),
    )
    packed = lax.all_gather(own_packed, ("bank", "dp") if split else "bank", axis=0, tiled=False)
    packed = packed.reshape((blocks,) + own_packed.shape)
    spare = ((0, 0), (0, TILE - classes))
    wide_head, wide_logit_grad = jnp.pad(w_head, spare), jnp.pad(logit_grad, spare)
    front = {}

    def turn(places):
        places, front["turned_map"], front["turned_bank"] = run_kernel(
            front_turn,
            places,
            [feature_map, bank],
            [shape_of((feature_count, site_count), BF16), shape_of((feature_count, keys_here), BF16)],
            "front_turn",
            6,
            limit=16,
        )
        return places

    def project(places):
        inside = shape_of((keys_here, channels), BF16)
        places, front["keys"], front["values"], front["turned_memory"] = run_kernel(
            front_bank,
            places,
            [bank, w_bank, w_key, w_value],
            [inside, inside, shape_of((channels, keys_here), BF16)],
            "front_bank",
            6,
            limit=16,
        )
        return places

    def head(places):
        places, front["pooling"], front["joined_grad"], front["hidden_grad"], front["group_branch_grad"] = run_kernel(
            front_head,
            places,
            [roi_index, roi_weight, wide_logit_grad, wide_head, w_out],
            [
                shape_of((own_count, site_count), BF16),
                shape_of((own_count, w_head.shape[0]), F32),
                shape_of((own_count, channels), F32),
                shape_of((group_rows, channels), BF16),
            ],
            "front_head",
            4,
            limit=16,
        )
        return places

    if split:
        places, sources = gather_blocks(own_a, axes, places, [turn, project, head])
    else:
        places, sources = head(project(turn(places))), [lax.all_gather(own_a, "bank", axis=0, tiled=False)]
    turned_map, turned_bank, turned_memory = front["turned_map"], front["turned_bank"], front["turned_memory"]
    keys, values, pooling = front["keys"], front["values"], front["pooling"]
    joined_grad, hidden_grad, group_branch_grad = front["joined_grad"], front["hidden_grad"], front["group_branch_grad"]
    time_column = region_time.reshape(-1, 1)
    scales = jnp.stack([scale_b, shift_b, scale_a, shift_a])
    places, time_column, scales, *sources = lax.optimization_barrier((places, time_column, scales, *sources))

    pre_a, act_a, weight_a = run_first_conv(places, feature_map, sources, scale_a, shift_a)
    pre_b, act_b, pre_c, regions, reduced, own_queries = run_later_convs(
        act_a, feature_map, packed, scale_b, shift_b, scale_c, shift_c, pooling, w_reduce, w_query, groups_b, groups_c
    )
    queries = to_owners(own_queries).reshape(group_rows, channels)
    places, message, scores = run_kernel(
        functools.partial(attend, half_span),
        places,
        [queries, keys, values, time_column],
        [shape_of((group_rows, channels + TILE), BF16), shape_of((group_rows, keys_here), F32)],
        "attend",
        2,
    )
    arrived = to_owners(message.reshape(bank_count, own_count, channels + TILE))
    row = shape_of((1, channels), F32)
    places, message, hidden_low, gain_part, shift_part = run_kernel(
        merge_rows,
        places,
        [arrived, hidden_grad, ln_gain.reshape(1, -1), ln_shift.reshape(1, -1)],
        [shape_of(arrived.shape, BF16), shape_of((own_count, channels), BF16), row, row],
        "merge_rows",
        2,
    )
    arrived = to_owners(message).reshape(group_rows, channels + TILE)
    maps = (site_count, feature_count)
    inside = (site_count, channels)
    places, slope_c = run_kernel(
        slopes_outer,
        places,
        [scale_c.reshape(1, -1), shift_c.reshape(1, -1), pre_c, feature_map],
        [shape_of(maps, BF16)],
        "slopes_outer",
        WINDOW,
        scratch=[
            pltpu.VMEM(maps, F32), pltpu.VMEM(maps, BF16), pltpu.VMEM(maps, BF16), pltpu.SemaphoreType.DMA((3, chunks))
        ],
        raw_in=(2, 3),
        raw_out=(0,),
        limit=52,
    )
    places, query_part, key_value = run_kernel(
        attend_back,
        places,
        [arrived, scores, keys, values, queries],
        [shape_of((group_rows, channels), BF16), shape_of((2 * keys_here, channels), BF16)],
        "attend_back",
        2,
    )
    query_parts = to_owners(query_part.reshape(bank_count, own_count, channels))
    def dp_swap(value, step):
        return lax.ppermute(value, "dp", [(i, i ^ step) for i in range(dp_count)])

    key_value_got = dp_swap(key_value, 1)

    def summed_swap(places, own, got):
        places, own = run_kernel(
            sum_swap, places, [own, got], [shape_of(own.shape, BF16)], "sum_swap", 2
        )
        return places, own

    places, key_value = summed_swap(places, key_value, key_value_got)
    step = 2
    while step * 2 < dp_count:
        places, key_value = summed_swap(places, key_value, dp_swap(key_value, step))
        step *= 2
    key_value_got = dp_swap(key_value, step)
    own_shape = shape_of((own_count, channels), BF16)
    places, query_grad, reduced_grad, regions_grad = run_kernel(
        region_back,
        places,
        [query_parts, joined_grad, w_query, w_reduce],
        [own_shape, own_shape, shape_of((own_count, feature_count), BF16)],
        "region_back",
        3,
    )
    half_blocks = blocks // 2
    rows_bc = rows_b + groups_c * LANE_ROWS
    wide_row = shape_of((1, feature_count), F32)
    (
        places, send_bc, keep_bc, lin_c_grad, pre_a_grad,
        scale_c_part, shift_c_part, scale_b_part, shift_b_part, scale_a_part, shift_a_part,
    ) = run_kernel(
        functools.partial(later_back, 0, groups_b),
        places,
        [
            regions_grad, pooling, scale_c.reshape(1, -1), scales, pre_c, slope_c, act_b, pre_b, act_a, pre_a, packed,
        ],
        [shape_of((half_blocks, rows_bc, channels), BF16)] * 2
        + [shape_of(maps, BF16), shape_of(inside, BF16), wide_row, wide_row]
        + [row] * 4,
        "later_back",
        28,
        scratch=[
            pltpu.VMEM((blocks * groups_b, LANE_ROWS, channels), BF16),
            pltpu.VMEM((groups_c, blocks, LANE_ROWS, channels), BF16),
            pltpu.VMEM((2, half_blocks, rows_bc, channels), BF16),
            pltpu.VMEM(inside, F32),
            pltpu.VMEM(inside, BF16),
            pltpu.VMEM((channels, site_count), BF16),
            pltpu.VMEM(inside, F32),
            pltpu.VMEM(inside, F32),
            pltpu.VMEM(maps, F32),
            pltpu.VMEM(maps, BF16),
            pltpu.VMEM(inside, BF16),
            pltpu.VMEM(inside, F32),
            pltpu.VMEM(inside, BF16),
            pltpu.VMEM(inside, F32),
            pltpu.VMEM(maps, BF16),
            pltpu.SemaphoreType.DMA((blocks,)),
            pltpu.SemaphoreType.DMA((blocks,)),
            pltpu.SemaphoreType.DMA((2,)),
            pltpu.SemaphoreType.DMA((4 + 3 * chunks,)),
        ],
        raw_in=range(4, 11),
        raw_out=(0, 1, 2),
        limit=40,
    )
    got_bc = last.swap(send_bc, 1)

    def parted(value):
        return value.reshape(halves + value.shape[1:])

    places, send_a, keep_a, key_value = run_kernel(
        first_back,
        places,
        [pre_a_grad, key_value, key_value_got, turned_map],
        [shape_of((half_blocks, rows_a, channels), BF16)] * 2 + [shape_of(key_value.shape, BF16)],
        "first_back",
        6,
        scratch=[
            pltpu.VMEM((2, half_blocks, rows_a, channels), BF16),
            pltpu.VMEM(turned_map.shape, BF16),
            pltpu.SemaphoreType.DMA((chunks,)),
            pltpu.SemaphoreType.DMA((2,)),
        ],
        raw_in=(3,),
        raw_out=(0, 1),
        limit=20,
    )
    got_a = last.swap(send_a, 1)
    half = outer.size // 2
    plane_shape = (half, 2, rows_bc, channels)
    places, keep_one, send_one, keep_two, send_two = run_kernel(
        after_last, places, [parted(keep_bc), parted(got_bc)], [shape_of(plane_shape, BF16)] * 4, "round_one", 4
    )
    got_one, got_two = across.swap(send_one, 1), inner.swap(send_two, 1)
    feature_rows, channel_rows = feature_count // bank_count, channels // bank_count
    joined_rows = (feature_count + channels) // bank_count
    widths = (channels, channels, feature_rows, channel_rows, channel_rows, joined_rows)
    message_width = -(-sum(widths) // TILE) * TILE
    places, logits_out, message = run_kernel(
        region_pack,
        places,
        [regions, reduced, hidden_low, query_grad, reduced_grad, w_out, wide_head],
        [shape_of((own_count, classes), BF16), shape_of((bank_count, own_count, message_width), BF16)],
        "region_pack",
        WINDOW,
    )
    group = to_owners(message).reshape(group_rows, message_width)

    places, map_grad = run_kernel(
        map_back,
        places,
        [pre_a_grad, weight_a, lin_c_grad],
        [shape_of(maps, BF16)],
        "map_back",
        WINDOW,
        scratch=[
            pltpu.VMEM((3,) + inside, BF16),
            pltpu.VMEM(maps, BF16),
            pltpu.VMEM(maps, BF16),
            pltpu.SemaphoreType.DMA((1 + chunks,)),
        ],
        raw_in=(2,),
        raw_out=(0,),
        limit=12,
    )
    kept_shape = shape_of((2 * half * (2 * rows_a + rows_bc), channels), BF16)
    both = shape_of((half * (2 * rows_a + rows_bc), channels), BF16)
    places, held, send_across, send_inner = run_kernel(
        round_two,
        places,
        [keep_one, got_one, keep_two, got_two, parted(keep_a), parted(got_a)],
        [kept_shape, both, both],
        "round_two",
        5,
    )
    got_across, got_inner = across.swap(send_across, 1), inner.swap(send_inner, 1)
    vectors = [
        gain_part, shift_part, scale_a_part, shift_a_part, scale_b_part, shift_b_part, scale_c_part, shift_c_part
    ]
    width = channels // dp_count
    lines = -(-sum(vector.shape[1] for vector in vectors) // (bank_count * width))
    lines = -(-lines // LANE_ROWS) * LANE_ROWS
    bank_lines = feature_rows + 2 * channel_rows + lines
    bank_step = bank_spans(bank_lines, width, channels)[1]
    region_lines = feature_rows + 2 * channel_rows + bank_spans(joined_rows, TILE, channels)[1]
    places, bank_grad, *bank_pieces = run_kernel(
        bank_back,
        places,
        [key_value, w_key, w_value, w_bank, turned_bank, turned_memory] + vectors,
        [shape_of(bank.shape, BF16)]
        + [shape_of((bank_count // outer_count, bank_lines, width), BF16)] * outer_count,
        "bank_back",
        WINDOW,
        scratch=[
            pltpu.VMEM((bank_count, bank_lines, width), BF16),
            pltpu.VMEM((3 * keys_here, channels), BF16),
        ],
        limit=8,
    )
    places, region_parts = run_kernel(
        functools.partial(region_sums, widths),
        places,
        [group, group_branch_grad, wide_logit_grad],
        [shape_of((region_lines, channels), BF16)],
        "region_sums",
        WINDOW,
    )
    region_both = [region_parts, dp_swap(region_parts, 1)] if split else [lax.psum(region_parts, "dp")]
    if split:
        bank_parts = [bank_pieces[0]] + [outer.swap(piece, step + 1) for step, piece in enumerate(bank_pieces[1:])]
    else:
        bank_parts = [low(jnp.sum(wide(to_owners(bank_pieces[0])), axis=0, keepdims=True))]
    sizes = (half, rows_bc, rows_a)
    places, held, send_across, send_inner, *pieces_bc = run_kernel(
        functools.partial(round_three, sizes, outer.size, split),
        places,
        [held, got_across, got_inner] + region_both + bank_parts,
        [
            shape_of((rows_bc + 2 * half * rows_a + bank_step, channels), BF16),
            shape_of((half * rows_a + region_lines, channels), BF16),
            shape_of((half * rows_a + bank_step, channels), BF16),
        ]
        + [shape_of((rows_bc, channels), BF16)] * (outer.size - 1),
        "round_three",
        5,
    )
    got_across, got_inner = across.swap(send_across, 1), inner.swap(send_inner, 1)
    got_bc = [outer.swap(piece, step + 1) for step, piece in enumerate(pieces_bc)]
    row_block = shape_of((channel_rows, channels), F32)
    results = run_kernel(
        functools.partial(round_four, sizes, outer.size, split, widths),
        places,
        [held, *got_bc, send_across, got_across, got_inner],
        [shape_of((rows_bc + bank_step, channels), BF16)]
        + [shape_of((rows_a, channels), BF16)] * outer.size
        + [shape_of((feature_rows, channels), F32), row_block, row_block, shape_of((joined_rows, classes), F32)],
        "round_four",
        4,
    )
    places, done, kept_a, *pieces_a = results[: 2 + outer.size]
    reduce_weight_grad, query_weight_grad, out_weight_grad, head_weight_grad = results[2 + outer.size :]
    got_a = [outer.swap(piece, step + 1) for step, piece in enumerate(pieces_a)]
    done_both = [done, across.swap(done, 1)] if split else []
    row_block = shape_of((channel_rows, channels), F32)
    places, part_a, *both = run_kernel(
        functools.partial(round_last, outer.size),
        places,
        [kept_a, *got_a, *done_both],
        [shape_of((rows_a, channels), BF16)] + [shape_of((2,) + done.shape, BF16)] * len(done_both[1:]),
        "round_last",
        2,
    )
    if split:
        done_a = lax.all_gather(part_a, "dp", axis=0, tiled=False)
        done_all = [both[0], last.swap(both[0], 1)]
    else:
        done_a = lax.psum(part_a, "dp")
        bank_all = lax.all_gather(done[rows_bc:], "dp", axis=0, tiled=False)
        done_all = [lax.psum(done[:rows_bc], "dp")] + [bank_all[place] for place in range(dp_count)]
    info = (rows_b, groups_c * LANE_ROWS, feature_rows, channel_rows, bank_lines, split)
    results = run_kernel(
        functools.partial(finish, info),
        places,
        [done_a, *done_all],
        [shape_of(conv_a.shape, F32), shape_of(conv_b.shape, F32), shape_of(conv_c.shape, F32)]
        + [shape_of((feature_rows, channels), F32), row_block, row_block]
        + [shape_of((1, vector.shape[1] // bank_count), F32) for vector in vectors],
        "finish",
        3,
    )
    places, conv_a_grad, conv_b_grad, conv_c_grad, bank_weight_grad, key_weight_grad, value_weight_grad = results[:7]
    small = [value.reshape(-1) for value in results[7:]]
    gain_grad, shift_grad = small[:2]
    scale_a_grad, shift_a_grad, scale_b_grad, shift_b_grad, scale_c_grad, shift_c_grad = small[2:]
    return (
        logits_out,
        map_grad,
        bank_grad,
        conv_a_grad,
        scale_a_grad,
        shift_a_grad,
        conv_b_grad,
        scale_b_grad,
        shift_b_grad,
        conv_c_grad,
        scale_c_grad,
        shift_c_grad,
        reduce_weight_grad,
        bank_weight_grad,
        query_weight_grad,
        key_weight_grad,
        value_weight_grad,
        gain_grad,
        shift_grad,
        out_weight_grad,
        head_weight_grad,
    )


def solution(mesh):
    in_specs = (
        P(("dp", "bank"), None),
        P("bank", None),
        P("dp"),
        P(("dp", "bank"), None),
        P(("dp", "bank"), None),
        P("bank", None),
        P(),
        P(),
        P("bank", None),
        P(),
        P(),
        P("bank", None),
        P(),
        P(),
        P(),
        P(),
        P(),
        P(),
        P(),
        P(),
        P(),
        P(),
        P(),
        P("dp", None),
    )
    out_specs = (
        P(("dp", "bank"), None),
        P(("dp", "bank"), None),
        P("bank", None),
        P("bank", None),
        P("bank"),
        P("bank"),
        P("bank", None),
        P("bank"),
        P("bank"),
        P("bank", None),
        P("bank"),
        P("bank"),
        P("bank", None),
        P("bank", None),
        P("bank", None),
        P("bank", None),
        P("bank", None),
        P("bank"),
        P("bank"),
        P("bank", None),
        P("bank", None),
    )
    return jax.shard_map(body, mesh=mesh, in_specs=in_specs, out_specs=out_specs, check_vma=False)
```
